32 devices in a mesh: dp: 32 (over z, y, x, core).
Axes of the slice: x: 2, y: 2, z: 4, core: 2. Of those that a mesh axis runs over, the one named last changes fastest.
Arguments:
- block_input: bfloat16 [64, 512, 768], P('dp'), may hold values from -6 to 6
- memory: bfloat16 [64, 512, 768], P('dp'), may hold values from -6 to 6
- cotangent: bfloat16 [64, 512, 768], P('dp'), may hold values from -6 to 6
- segments: int32 [64, 512], P('dp'), may hold values from 0 to 3, as said below
- memory_segments: int32 [64, 512], P('dp'), may hold values from 0 to 3, as said below
- task_of_segment: int32 [64, 4], P('dp'), may hold values from 0 to 7
- self_query: bfloat16 [768, 768], P('dp'), may hold values from -0.21875 to 0.21875
- self_key: bfloat16 [768, 768], P('dp'), may hold values from -0.21875 to 0.21875
- self_value: bfloat16 [768, 768], P('dp'), may hold values from -0.21875 to 0.21875
- self_output: bfloat16 [768, 768], P('dp'), may hold values from -0.875 to 0.875
- cross_query: bfloat16 [768, 768], P('dp'), may hold values from -0.21875 to 0.21875
- cross_key: bfloat16 [768, 768], P('dp'), may hold values from -0.21875 to 0.21875
- cross_value: bfloat16 [768, 768], P('dp'), may hold values from -0.21875 to 0.21875
- cross_output: bfloat16 [768, 768], P('dp'), may hold values from -0.875 to 0.875
- hidden_in: bfloat16 [768, 3072], P('dp'), may hold values from -0.21875 to 0.21875
- hidden_out: bfloat16 [3072, 768], P('dp'), may hold values from -0.109375 to 0.109375
- task_table: float32 [8, 64], replicated, may hold values from -6 to 6
- task_weight: float32 [64, 128], replicated, may hold values from -0.75 to 0.75
- task_bias: float32 [128], replicated, may hold values from -3 to 3
- down_maker: bfloat16 [18432, 128], P('dp'), may hold values from -0.0390625 to 0.0390625
- up_maker: bfloat16 [18432, 128], P('dp'), may hold values from -0.21875 to 0.21875
- gain_maker: bfloat16 [2304, 128], P('dp'), may hold values from -0.25 to 0.25
Outputs:
- output: bfloat16 [64, 512, 768], P('dp')
- input_gradient: float32 [64, 512, 768], P('dp')
- memory_gradient: float32 [64, 512, 768], P('dp')
- self_query_gradient: float32 [768, 768], P('dp')
- self_key_gradient: float32 [768, 768], P('dp')
- self_value_gradient: float32 [768, 768], P('dp')
- self_output_gradient: float32 [768, 768], P('dp')
- cross_query_gradient: float32 [768, 768], P('dp')
- cross_key_gradient: float32 [768, 768], P('dp')
- cross_value_gradient: float32 [768, 768], P('dp')
- cross_output_gradient: float32 [768, 768], P('dp')
- hidden_in_gradient: float32 [768, 3072], P('dp')
- hidden_out_gradient: float32 [3072, 768], P('dp')
- task_table_gradient: float32 [8, 64], replicated
- task_weight_gradient: float32 [64, 128], replicated
- task_bias_gradient: float32 [128], replicated
- down_maker_gradient: float32 [18432, 128], P('dp')
- up_maker_gradient: float32 [18432, 128], P('dp')
- gain_maker_gradient: float32 [2304, 128], P('dp')
The draws below stay inside these ranges and needn't reach their ends.
Inputs may be any that keep to these rules, and one draw needn't show every extreme that they name: In each row segment numbers start at 0 and rise by one at each boundary; every segment holds one position or more; a row's memory holds as many segments as its targets, and some row holds 4. `memory_segments`: segment numbers of the memory, with the same rule and count as the row's targets. `task_of_segment`: entries past a row's last segment are not read.
All inputs are finite; a program needn't handle non-finite values.
Results may differ from the reference program's by a relative error of at most 0.025.
Values may be sent and summed in bfloat16 or wider, within the bound.
A program may use at most 256 MiB of HBM per device.

```python
import jax
import jax.numpy as jnp
from jax import lax

D = 768
HEADS = 12
HEAD = 64
FF = 3072
ADA = 24
EMB = 64
HYP = 128
NTASK = 8
LEN = 512
MEM = 512
SEGS = 4
ROWS = 64


def segment_counts(key):
    drawn = jax.random.randint(key, (ROWS,), 1, SEGS + 1)
    return jnp.where(jnp.arange(ROWS) == 0, SEGS, drawn).astype(jnp.int32)


def boundary_ids(key, counts, span):
    row_keys = jax.random.split(key, ROWS)

    def one_row(row_key, seg_total):
        cut_points = jax.random.permutation(row_key, span - 1)[:SEGS - 1] + 1
        in_use = jnp.arange(SEGS - 1) < seg_total - 1
        positions = jnp.arange(span)
        passed = in_use[None, :] & (cut_points[None, :] <= positions[:, None])
        return jnp.sum(passed.astype(jnp.int32), axis=1)
    return jax.vmap(one_row)(row_keys, counts).astype(jnp.int32)


def draw_segments(key, part):
    counts = segment_counts(key)
    key = jax.random.fold_in(key, 5)
    return boundary_ids(key, counts, LEN)


def draw_memory_segments(key, part):
    counts = segment_counts(key)
    key = jax.random.fold_in(key, 9)
    return boundary_ids(key, counts, MEM)


def with_ends(values, stream_key, low, high):
    shape = values.shape
    index_at = [jax.random.randint(jax.random.fold_in(stream_key, axis), (), 0, shape[axis]) for axis in range(len(shape))]
    values = values.at[tuple(index_at)].set(low)
    longest = shape.index(max(shape))
    index_at[longest] = (index_at[longest] + 1) % shape[longest]
    return values.at[tuple(index_at)].set(high)


def spiked(values, key, source, target, parts, factor):
    def block_of(dim):
        return (jnp.arange(values.shape[dim]) // (values.shape[dim] // parts)).reshape((-1,) + (1,) * (values.ndim - 1 - dim))

    one_side = jax.random.permutation(key, parts)[block_of(target)]
    second = (block_of(target) + parts // 2) % parts
    return jnp.where((block_of(source) == one_side) | (block_of(source) == second), factor * values, values)


def shard_levels(stream_key, shape, cuts, low, top_value):
    gain, own = 1.0, jax.random.fold_in(stream_key, 6)
    for dim, shards_of in cuts:
        draws = jnp.exp(jax.random.uniform(jax.random.fold_in(own, dim), (shards_of,), jnp.float32, low / len(cuts), top_value / len(cuts)))
        gain = gain * jnp.repeat(draws, shape[dim] // shards_of).reshape([-1 if axis == dim else 1 for axis in range(len(shape))])
    return gain


def normal_values(key, extent, scale, limit, pieces=(), kind=jnp.bfloat16):
    array = jax.random.normal(key, extent, jnp.float32) * scale
    if len(pieces) > 0:
        array = shard_levels(key, extent, pieces, -0.22, 0.18) * array
    return jnp.clip(array, min=-limit, max=limit).astype(kind)


def heavy_noise(stream_key, extent, width, bound, cuts, heavy, kind=jnp.bfloat16):
    entries = width * jax.random.normal(stream_key, extent, jnp.float32)
    if cuts:
        entries = entries * shard_levels(stream_key, extent, cuts, -0.22, 0.18)
    return jnp.clip(spiked(entries, jax.random.fold_in(stream_key, 3), *heavy), -bound, bound).astype(kind)


def setup_inputs(seed: int = 0) -> dict:
    streams_of = jax.random.split(jax.random.key(seed), 23)
    block_input = heavy_noise(streams_of[0], (ROWS, LEN, D), 1.0, 6.0, ((0, 32),), (0, 2, 32, 2.75))
    memory = normal_values(streams_of[1], (ROWS, MEM, D), 1.0, 6.0, ((0, 32),))
    cotangent = normal_values(streams_of[2], (ROWS, LEN, D), 1.0, 6.0, ((0, 32),))
    segments = draw_segments(jax.random.fold_in(streams_of[22], 71), 0)
    memory_segments = draw_memory_segments(jax.random.fold_in(streams_of[22], 71), 0)
    task_of_segment = with_ends(jax.random.randint(streams_of[5], (ROWS, SEGS), 0, NTASK), jax.random.fold_in(streams_of[5], 1), 0, NTASK - 1).astype(jnp.int32)
    self_query = normal_values(streams_of[6], (D, D), D ** -0.5, 0.21875, ((0, 32),))
    self_key = normal_values(streams_of[7], (D, D), D ** -0.5, 0.21875, ((0, 32),))
    self_value = normal_values(streams_of[8], (D, D), D ** -0.5, 0.21875, ((0, 32),))
    self_output = normal_values(streams_of[9], (D, D), (D // 16) ** -0.5, 0.875, ((0, 32),))
    cross_query = normal_values(streams_of[10], (D, D), D ** -0.5, 0.21875, ((0, 32),))
    cross_key = normal_values(streams_of[11], (D, D), D ** -0.5, 0.21875, ((0, 32),))
    cross_value = normal_values(streams_of[12], (D, D), D ** -0.5, 0.21875, ((0, 32),))
    cross_output = normal_values(streams_of[13], (D, D), (D // 16) ** -0.5, 0.875, ((0, 32),))
    hidden_in = normal_values(streams_of[14], (D, FF), D ** -0.5, 0.21875, ((0, 32),))
    hidden_out = normal_values(streams_of[15], (FF, D), FF ** -0.5, 0.109375, ((0, 32),))
    task_table = normal_values(streams_of[16], (NTASK, EMB), 1.0, 6.0, (), jnp.float32)
    task_weight = normal_values(streams_of[17], (EMB, HYP), EMB ** -0.5, 0.75, (), jnp.float32)
    task_bias = normal_values(streams_of[18], (HYP,), 0.5, 3.0, (), jnp.float32)
    down_maker = normal_values(streams_of[19], (D * ADA, HYP), (D * HYP // 4) ** -0.5, 0.0390625, ((0, 32),))
    up_maker = normal_values(streams_of[20], (ADA * D, HYP), (ADA * HYP // 4) ** -0.5, 0.21875, ((0, 32),))
    gain_maker = normal_values(streams_of[21], (3 * D, HYP), (4 * HYP) ** -0.5, 0.25, ((0, 32),))
    return {"block_input": block_input, "memory": memory, "cotangent": cotangent, "segments": segments, "memory_segments": memory_segments, "task_of_segment": task_of_segment, "self_query": self_query, "self_key": self_key, "self_value": self_value, "self_output": self_output, "cross_query": cross_query, "cross_key": cross_key, "cross_value": cross_value, "cross_output": cross_output, "hidden_in": hidden_in, "hidden_out": hidden_out, "task_table": task_table, "task_weight": task_weight, "task_bias": task_bias, "down_maker": down_maker, "up_maker": up_maker, "gain_maker": gain_maker}


@jax.custom_vjp
def low(v):
    return lax.optimization_barrier(v.astype(jnp.bfloat16)).astype(jnp.float32)

@jax.custom_vjp
def low_back(v):
    return v

def low_keep(v):
    return (low(v), None)

def low_pass(kept, grad):
    return (grad,)

def back_keep(v):
    return (v, None)

def back_low(kept, grad):
    return (low(grad),)
low.defvjp(low_keep, low_pass)
low_back.defvjp(back_keep, back_low)
exact_mode = lax.Precision.HIGHEST
norm_eps = 1e-06
masked_score = -1e+30

def matmul(left_side, right_side):
    return jnp.dot(left_side, right_side, precision=exact_mode, preferred_element_type=jnp.float32)

def gelu_exact(operand):
    return jax.nn.gelu(operand, approximate=False)

def rms_norm(stream, gain_row):
    return stream * lax.rsqrt(lax.optimization_barrier(jnp.mean(stream * stream, axis=-1, keepdims=True)) + norm_eps) * gain_row

def attend_row(inputs):
    queries, key_rows, value_rows, allowed = inputs
    scores = jnp.einsum('qhe,khe->hqk', queries, key_rows, precision=exact_mode) * queries.shape[-1] ** (-0.5)
    scores = low_back(scores)
    scores = jnp.where(allowed[None], scores, masked_score)
    mix_weights = low(jax.nn.softmax(scores, axis=-1))
    return jnp.einsum('hqk,khe->qhe', mix_weights, value_rows, precision=exact_mode)

def attention(queries, key_rows, value_rows, allowed):
    return lax.map(jax.checkpoint(attend_row), (queries, key_rows, value_rows, allowed))

def forward(params, segments, memory_segments, task_of_segment):
    block_input, memory, self_query, self_key, self_value, self_output, cross_query, cross_key, cross_value, cross_output, hidden_in, hidden_out, task_table, task_weight, task_bias, down_maker, up_maker, gain_maker = params
    row_count, seq_len, model_width = block_input.shape
    mem_len = memory.shape[1]
    task_count = task_table.shape[0]
    token_count = row_count * seq_len
    task_state = low(gelu_exact(matmul(task_table, task_weight) + task_bias))
    made_down = low(low_back(matmul(task_state, down_maker.T)))
    made_up = low(low_back(matmul(task_state, up_maker.T)))
    gain_table = 1.0 + matmul(task_state, gain_maker.T)
    down_all = made_down.reshape(task_count, model_width, ADA).transpose(1, 0, 2).reshape(model_width, task_count * ADA)
    up_all = made_up.reshape(task_count * ADA, model_width)
    seg_match = segments[:, :, None] == jnp.arange(SEGS, dtype=jnp.int32)[None, None, :]
    token_task = lax.optimization_barrier(jnp.sum(jnp.where(seg_match, task_of_segment[:, None, :], 0), axis=-1)).reshape(token_count)
    task_hot = (token_task[:, None] == jnp.arange(task_count, dtype=jnp.int32)[None, :]).astype(jnp.float32)
    token_gain = matmul(task_hot, gain_table)
    position = jnp.arange(seq_len, dtype=jnp.int32)
    self_allow = (segments[:, :, None] == segments[:, None, :]) & (position[:, None] >= position[None, :])[None]
    cross_allow = segments[:, :, None] == memory_segments[:, None, :]

    def project(source, weight_full):
        return low(low_back(matmul(source, weight_full)))

    def split_heads(flat_rows, length):
        return flat_rows.reshape(row_count, length, HEADS, HEAD)
    stream_in = block_input.reshape(token_count, model_width)
    normed_one = low(rms_norm(stream_in, token_gain[:, :model_width]))
    mixed_one = attention(split_heads(project(normed_one, self_query), seq_len), split_heads(project(normed_one, self_key), seq_len), split_heads(project(normed_one, self_value), seq_len), self_allow)
    mixed_one = low(low_back(mixed_one.reshape(token_count, model_width)))
    stream_one = stream_in + low_back(matmul(mixed_one, self_output))
    normed_two = low(rms_norm(stream_one, token_gain[:, model_width:2 * model_width]))
    memory_flat = memory.reshape(row_count * mem_len, model_width)
    mixed_two = attention(split_heads(project(normed_two, cross_query), seq_len), split_heads(project(memory_flat, cross_key), mem_len), split_heads(project(memory_flat, cross_value), mem_len), cross_allow)
    mixed_two = low(low_back(mixed_two.reshape(token_count, model_width)))
    stream_two = stream_one + low_back(matmul(mixed_two, cross_output))
    normed_three = low(rms_norm(stream_two, token_gain[:, 2 * model_width:]))
    hidden_units = low_back(matmul(normed_three, hidden_in))
    activated = low(gelu_exact(hidden_units))
    feed_result = low_back(matmul(activated, hidden_out))
    feed_low = low(feed_result)
    task_mask = jnp.repeat(task_hot, ADA, axis=1)
    bottleneck = low_back(matmul(feed_low, down_all) * task_mask)
    adapter_out = low_back(matmul(low(gelu_exact(bottleneck)), up_all))
    result = stream_two + feed_result + adapter_out
    return result.reshape(row_count, seq_len, model_width)

def reference(block_input, memory, cotangent, segments, memory_segments, task_of_segment, self_query, self_key, self_value, self_output, cross_query, cross_key, cross_value, cross_output, hidden_in, hidden_out, task_table, task_weight, task_bias, down_maker, up_maker, gain_maker):
    params = tuple((array_in.astype(jnp.float32) for array_in in (block_input, memory, self_query, self_key, self_value, self_output, cross_query, cross_key, cross_value, cross_output, hidden_in, hidden_out, task_table, task_weight, task_bias, down_maker, up_maker, gain_maker)))

    def apply_layer(*flat_params):
        return forward(flat_params, segments, memory_segments, task_of_segment)
    result, pullback = jax.vjp(apply_layer, *params)
    gradients = pullback(cotangent.astype(jnp.float32))
    return (result.astype(jnp.bfloat16), gradients[0], gradients[1], gradients[2], gradients[3], gradients[4], gradients[5], gradients[6], gradients[7], gradients[8], gradients[9], gradients[10], gradients[11], gradients[12], gradients[13], gradients[14], gradients[15], gradients[16], gradients[17])
```

```python
import jax
import jax.numpy as jnp
from jax import lax
from jax.sharding import PartitionSpec as P

HEADS = 12
HEAD = 64
ADA = 24


exact_mode = lax.Precision.HIGHEST
norm_eps = 1e-06
masked_score = -1e30


def plain_dot(left_side, right_side):
    return jnp.dot(left_side, right_side, preferred_element_type=jnp.float32)


def exact_dot(left_side, right_side):
    return jnp.dot(left_side, right_side, precision=exact_mode, preferred_element_type=jnp.float32)


def inner_rows(left_side, right_side):
    return lax.dot_general(
        left_side, right_side, (((1,), (1,)), ((), ())), preferred_element_type=jnp.float32
    )


def inner_cols(left_side, right_side, precision_mode=None):
    return lax.dot_general(
        left_side,
        right_side,
        (((0,), (0,)), ((), ())),
        precision=precision_mode,
        preferred_element_type=jnp.float32,
    )


def gelu_exact(operand):
    return jax.nn.gelu(operand, approximate=False)


def gelu_back(operand, cotan):
    return jax.vjp(gelu_exact, operand)[1](cotan)[0]


def rms_norm(stream, gain_row):
    return (
        stream * lax.rsqrt(jnp.mean(stream * stream, axis=-1, keepdims=True) + norm_eps) * gain_row
    )


def norm_back(stream, gain_row, cotan):
    return jax.vjp(rms_norm, stream, gain_row)[1](cotan)


def task_network(table_rows, weight_in, bias_row):
    return gelu_exact(exact_dot(table_rows, weight_in) + bias_row)


def row_scores(queries, key_rows, allowed):
    scores = jnp.einsum("qhe,khe->hqk", queries, key_rows, preferred_element_type=jnp.float32)
    scores = scores * queries.shape[-1] ** (-0.5)
    return jnp.where(allowed[None], scores, masked_score)


def attend_forward(inputs):
    queries, key_rows, value_rows, allowed = inputs
    scores = row_scores(queries, key_rows, allowed)
    row_peak = jnp.max(scores, axis=-1, keepdims=True)
    shifted = jnp.exp(scores - row_peak)
    totals = jnp.sum(shifted, axis=-1, keepdims=True)
    mix_weights = (shifted / totals).astype(jnp.bfloat16)
    mixed_rows = jnp.einsum(
        "hqk,khe->qhe", mix_weights, value_rows, preferred_element_type=jnp.float32
    )
    return (mixed_rows.astype(jnp.bfloat16), (row_peak + jnp.log(totals))[..., 0])


def attend_backward(inputs):
    queries, key_rows, value_rows, allowed, log_totals, grad_mixed = inputs
    score_scale = queries.shape[-1] ** (-0.5)
    scores = row_scores(queries, key_rows, allowed)
    weights_full = jnp.exp(scores - log_totals[..., None])
    grad_values = jnp.einsum(
        "hqk,qhe->khe",
        weights_full.astype(jnp.bfloat16),
        grad_mixed,
        preferred_element_type=jnp.float32,
    )
    grad_weights = jnp.einsum(
        "qhe,khe->hqk", grad_mixed, value_rows, preferred_element_type=jnp.float32
    )
    inner_sum = jnp.sum(weights_full * grad_weights, axis=-1, keepdims=True)
    grad_scores = (weights_full * (grad_weights - inner_sum)).astype(jnp.bfloat16)
    grad_queries = (
        jnp.einsum("hqk,khe->qhe", grad_scores, key_rows, preferred_element_type=jnp.float32)
        * score_scale
    )
    grad_keys = (
        jnp.einsum("hqk,qhe->khe", grad_scores, queries, preferred_element_type=jnp.float32)
        * score_scale
    )
    return (
        grad_queries.astype(jnp.bfloat16),
        grad_keys.astype(jnp.bfloat16),
        grad_values.astype(jnp.bfloat16),
    )


def on_device(
    block_input,
    memory,
    cotangent,
    segments,
    memory_segments,
    task_of_segment,
    self_query,
    self_key,
    self_value,
    self_output,
    cross_query,
    cross_key,
    cross_value,
    cross_output,
    hidden_in,
    hidden_out,
    task_table,
    task_weight,
    task_bias,
    down_maker,
    up_maker,
    gain_maker,
):
    row_count, seq_len, model_width = block_input.shape
    mem_len = memory.shape[1]
    task_count = task_table.shape[0]
    token_count = row_count * seq_len
    parts = lax.axis_size("dp")
    own_rows = self_query.shape[0]
    squares = (
        self_query, self_key, self_value, self_output,
        cross_query, cross_key, cross_value, cross_output,
    )
    packed = jnp.concatenate(
        squares + (hidden_in.reshape(-1, model_width), hidden_out), axis=0
    )
    gathered = lax.all_gather(packed, "dp", axis=0, tiled=False)
    in_rows = hidden_in.size // model_width
    backbone = tuple(
        gathered[:, i * own_rows : (i + 1) * own_rows].reshape(-1, model_width) for i in range(8)
    ) + (
        gathered[:, 8 * own_rows : 8 * own_rows + in_rows].reshape(model_width, -1),
        gathered[:, 8 * own_rows + in_rows :].reshape(-1, model_width),
    )
    task_state, task_back = jax.vjp(task_network, task_table, task_weight, task_bias)
    task_low = task_state.astype(jnp.bfloat16)
    made = inner_rows(task_low, jnp.concatenate((down_maker, up_maker, gain_maker), axis=0))
    made = lax.all_gather(made, "dp", axis=0, tiled=False)
    down_own, gain_own = down_maker.shape[0], gain_maker.shape[0]

    def joined(block):
        return block.transpose(1, 0, 2).reshape(task_count, -1)

    made_down = joined(made[:, :, :down_own]).astype(jnp.bfloat16)
    made_up = joined(made[:, :, down_own : 2 * down_own]).astype(jnp.bfloat16)
    gain_table = 1.0 + joined(made[:, :, 2 * down_own :])
    down_all = (
        made_down.reshape(task_count, model_width, ADA)
        .transpose(1, 0, 2)
        .reshape(model_width, task_count * ADA)
    )
    up_all = made_up.reshape(task_count * ADA, model_width)
    seg_match = (
        segments[:, :, None] == jnp.arange(task_of_segment.shape[1], dtype=jnp.int32)[None, None, :]
    )
    token_task = jnp.sum(jnp.where(seg_match, task_of_segment[:, None, :], 0), axis=-1).reshape(
        token_count
    )
    task_hot = (token_task[:, None] == jnp.arange(task_count, dtype=jnp.int32)[None, :]).astype(
        jnp.float32
    )
    token_gain = exact_dot(task_hot, gain_table)
    gain_one = token_gain[:, :model_width]
    gain_two = token_gain[:, model_width : 2 * model_width]
    gain_three = token_gain[:, 2 * model_width :]
    position = jnp.arange(seq_len, dtype=jnp.int32)
    self_allow = (segments[:, :, None] == segments[:, None, :]) & (
        position[:, None] >= position[None, :]
    )[None]
    cross_allow = segments[:, :, None] == memory_segments[:, None, :]

    def split_heads(flat_rows, length):
        return flat_rows.reshape(row_count, length, HEADS, HEAD)

    def project(source, weight_full, length):
        return split_heads(plain_dot(source, weight_full).astype(jnp.bfloat16), length)

    (
        self_query_full,
        self_key_full,
        self_value_full,
        self_output_full,
        cross_query_full,
        cross_key_full,
        cross_value_full,
        cross_output_full,
        hidden_in_full,
        hidden_out_full,
    ) = backbone
    stream_in = block_input.reshape(token_count, model_width).astype(jnp.float32)
    normed_one = rms_norm(stream_in, gain_one).astype(jnp.bfloat16)
    queries_one = project(normed_one, self_query_full, seq_len)
    keys_one = project(normed_one, self_key_full, seq_len)
    values_one = project(normed_one, self_value_full, seq_len)
    mixed_one, totals_one = lax.map(attend_forward, (queries_one, keys_one, values_one, self_allow))
    mixed_one = mixed_one.reshape(token_count, model_width)
    stream_one = stream_in + plain_dot(mixed_one, self_output_full)
    normed_two = rms_norm(stream_one, gain_two).astype(jnp.bfloat16)
    memory_flat = memory.reshape(row_count * mem_len, model_width)
    queries_two = project(normed_two, cross_query_full, seq_len)
    keys_two = project(memory_flat, cross_key_full, mem_len)
    values_two = project(memory_flat, cross_value_full, mem_len)
    mixed_two, totals_two = lax.map(
        attend_forward, (queries_two, keys_two, values_two, cross_allow)
    )
    mixed_two = mixed_two.reshape(token_count, model_width)
    stream_two = stream_one + plain_dot(mixed_two, cross_output_full)
    normed_three = rms_norm(stream_two, gain_three).astype(jnp.bfloat16)
    hidden_units = plain_dot(normed_three, hidden_in_full)
    activated = gelu_exact(hidden_units).astype(jnp.bfloat16)
    feed_result = plain_dot(activated, hidden_out_full)
    feed_low = feed_result.astype(jnp.bfloat16)
    task_mask = jnp.repeat(task_hot, ADA, axis=1)
    bottleneck = plain_dot(feed_low, down_all) * task_mask
    narrow_low = gelu_exact(bottleneck).astype(jnp.bfloat16)
    adapter_out = plain_dot(narrow_low, up_all)
    output = (
        (stream_two + feed_result + adapter_out)
        .astype(jnp.bfloat16)
        .reshape(row_count, seq_len, model_width)
    )
    grad_out = cotangent.reshape(token_count, model_width).astype(jnp.float32)
    grad_adapter = cotangent.reshape(token_count, model_width)
    up_all_grad = inner_cols(narrow_low, grad_adapter)
    grad_narrow = inner_rows(grad_adapter, up_all)
    grad_bottleneck = (gelu_back(bottleneck, grad_narrow) * task_mask).astype(jnp.bfloat16)
    down_all_grad = inner_cols(feed_low, grad_bottleneck)
    grad_feed = (grad_out + inner_rows(grad_bottleneck, down_all)).astype(jnp.bfloat16)
    hidden_out_grad = inner_cols(activated, grad_feed)
    grad_units = gelu_back(hidden_units, inner_rows(grad_feed, hidden_out_full)).astype(
        jnp.bfloat16
    )
    hidden_in_grad = inner_cols(normed_three, grad_units)
    down_rows = (
        down_all_grad.reshape(model_width, task_count, ADA)
        .transpose(0, 2, 1)
        .reshape(model_width * ADA, task_count)
    )
    up_rows = (
        up_all_grad.reshape(task_count, ADA, model_width)
        .transpose(1, 2, 0)
        .reshape(ADA * model_width, task_count)
    )
    grad_normed_three = inner_rows(grad_units, hidden_in_full)
    stream_grad_three, gain_grad_three = norm_back(stream_two, gain_three, grad_normed_three)
    grad_two = grad_out + stream_grad_three
    grad_two_low = grad_two.astype(jnp.bfloat16)
    cross_output_grad = inner_cols(mixed_two, grad_two_low)
    grad_mixed_two = split_heads(
        inner_rows(grad_two_low, cross_output_full).astype(jnp.bfloat16), seq_len
    )
    grad_queries_two, grad_keys_two, grad_values_two = lax.map(
        attend_backward,
        (queries_two, keys_two, values_two, cross_allow, totals_two, grad_mixed_two),
    )
    grad_queries_two = grad_queries_two.reshape(token_count, model_width)
    grad_keys_two = grad_keys_two.reshape(row_count * mem_len, model_width)
    grad_values_two = grad_values_two.reshape(row_count * mem_len, model_width)
    cross_query_grad = inner_cols(normed_two, grad_queries_two)
    cross_key_grad = inner_cols(memory_flat, grad_keys_two)
    cross_value_grad = inner_cols(memory_flat, grad_values_two)
    memory_grad = inner_rows(grad_keys_two, cross_key_full) + inner_rows(
        grad_values_two, cross_value_full
    )
    grad_normed_two = inner_rows(grad_queries_two, cross_query_full)
    stream_grad_two, gain_grad_two = norm_back(stream_one, gain_two, grad_normed_two)
    grad_one = grad_two + stream_grad_two
    grad_one_low = grad_one.astype(jnp.bfloat16)
    self_output_grad = inner_cols(mixed_one, grad_one_low)
    grad_mixed_one = split_heads(
        inner_rows(grad_one_low, self_output_full).astype(jnp.bfloat16), seq_len
    )
    grad_queries_one, grad_keys_one, grad_values_one = lax.map(
        attend_backward, (queries_one, keys_one, values_one, self_allow, totals_one, grad_mixed_one)
    )
    grad_queries_one = grad_queries_one.reshape(token_count, model_width)
    grad_keys_one = grad_keys_one.reshape(token_count, model_width)
    grad_values_one = grad_values_one.reshape(token_count, model_width)
    self_query_grad = inner_cols(normed_one, grad_queries_one)
    self_key_grad = inner_cols(normed_one, grad_keys_one)
    self_value_grad = inner_cols(normed_one, grad_values_one)
    grad_normed_one = (
        inner_rows(grad_queries_one, self_query_full)
        + inner_rows(grad_keys_one, self_key_full)
        + inner_rows(grad_values_one, self_value_full)
    )
    stream_grad_one, gain_grad_one = norm_back(stream_in, gain_one, grad_normed_one)
    input_grad = grad_one + stream_grad_one
    gain_grads = jnp.concatenate((gain_grad_one, gain_grad_two, gain_grad_three), axis=1)
    gain_rows = inner_cols(gain_grads, task_hot, exact_mode)
    def blocks(grad):
        return grad.reshape(parts, -1, model_width).astype(jnp.bfloat16)

    grads = (
        self_query_grad, self_key_grad, self_value_grad, self_output_grad,
        cross_query_grad, cross_key_grad, cross_value_grad, cross_output_grad,
        hidden_in_grad, hidden_out_grad,
    )
    summed = lax.psum_scatter(
        jnp.concatenate([blocks(g) for g in grads], axis=1), "dp", scatter_dimension=0, tiled=False
    ).astype(jnp.float32)
    shares = tuple(summed[i * own_rows : (i + 1) * own_rows] for i in range(8)) + (
        summed[8 * own_rows : 8 * own_rows + in_rows].reshape(hidden_in.shape),
        summed[8 * own_rows + in_rows :],
    )
    small = jnp.concatenate(
        [r.reshape(parts, -1, task_count) for r in (down_rows, up_rows, gain_rows)], axis=1
    )
    small = lax.psum_scatter(small, "dp", scatter_dimension=0, tiled=False)
    shares = shares + (
        small[:down_own], small[down_own : 2 * down_own], small[2 * down_own :],
    )
    own_down = shares[10].astype(jnp.bfloat16)
    own_up = shares[11].astype(jnp.bfloat16)
    own_gain = shares[12]
    down_maker_grad = plain_dot(own_down, task_low)
    up_maker_grad = plain_dot(own_up, task_low)
    gain_maker_grad = exact_dot(own_gain, task_low.astype(jnp.float32))
    state_partial = (
        inner_cols(own_down, down_maker)
        + inner_cols(own_up, up_maker)
        + inner_cols(own_gain, gain_maker.astype(jnp.float32), exact_mode)
    )
    state_grad = lax.psum(state_partial, "dp")
    table_grad, weight_grad, bias_grad = task_back(state_grad)
    return (
        output,
        input_grad.reshape(row_count, seq_len, model_width),
        memory_grad.reshape(row_count, mem_len, model_width),
        shares[0],
        shares[1],
        shares[2],
        shares[3],
        shares[4],
        shares[5],
        shares[6],
        shares[7],
        shares[8],
        shares[9],
        table_grad,
        weight_grad,
        bias_grad,
        down_maker_grad,
        up_maker_grad,
        gain_maker_grad,
    )


def solution(mesh):
    in_specs = (
        P("dp", None, None),
        P("dp", None, None),
        P("dp", None, None),
        P("dp", None),
        P("dp", None),
        P("dp", None),
        P("dp", None),
        P("dp", None),
        P("dp", None),
        P("dp", None),
        P("dp", None),
        P("dp", None),
        P("dp", None),
        P("dp", None),
        P("dp", None),
        P("dp", None),
        P(),
        P(),
        P(),
        P("dp", None),
        P("dp", None),
        P("dp", None),
    )
    out_specs = (
        P("dp", None, None),
        P("dp", None, None),
        P("dp", None, None),
        P("dp", None),
        P("dp", None),
        P("dp", None),
        P("dp", None),
        P("dp", None),
        P("dp", None),
        P("dp", None),
        P("dp", None),
        P("dp", None),
        P("dp", None),
        P(),
        P(),
        P(),
        P("dp", None),
        P("dp", None),
        P("dp", None),
    )
    return jax.shard_map(
        on_device, mesh=mesh, in_specs=in_specs, out_specs=out_specs, check_vma=False
    )
```

```python
import functools

import jax
import jax.numpy as jnp
from jax import lax
from jax.experimental import pallas as pl
from jax.experimental.pallas import tpu as pltpu
from jax.sharding import PartitionSpec as P

HEADS = 12
HEAD = 64
ADA = 24
PAIR = 2 * HEAD

exact_mode = lax.Precision.HIGHEST
norm_eps = 1e-06
masked_score = -1e30
bf16 = jnp.bfloat16
f32 = jnp.float32
VMEM_BYTES = 56 << 20


def plain_dot(left_side, right_side):
    return jnp.dot(left_side, right_side, preferred_element_type=f32)


def exact_dot(left_side, right_side):
    return jnp.dot(left_side, right_side, precision=exact_mode, preferred_element_type=f32)


def inner_rows(left_side, right_side):
    return lax.dot_general(
        left_side, right_side, (((1,), (1,)), ((), ())), preferred_element_type=f32
    )


def inner_cols(left_side, right_side, precision_mode=None):
    return lax.dot_general(
        left_side,
        right_side,
        (((0,), (0,)), ((), ())),
        precision=precision_mode,
        preferred_element_type=f32,
    )


def gelu_exact(operand):
    return jax.nn.gelu(operand, approximate=False)


def task_network(table_rows, weight_in, bias_row):
    return gelu_exact(exact_dot(table_rows, weight_in) + bias_row)


def gelu_both(v):
    phi = 0.5 * lax.erf(v * 0.7071067811865476) + 0.5
    slope = phi + v * (jnp.exp(v * v * -0.5) * 0.3989422804014327)
    return v * phi, slope


def token_gain(task_column, gain):
    high = gain.astype(bf16).astype(f32)
    rest = gain - high
    middle = rest.astype(bf16).astype(f32)
    table = jnp.concatenate((high, middle, rest - middle), axis=0).astype(bf16)
    which = lax.broadcasted_iota(jnp.int32, (task_column.shape[0], 24), 1) & 7
    hot = jnp.where(which == task_column, 1.0, 0.0).astype(bf16)
    return plain_dot(hot, table)


def gain_rows(task_column, grads):
    which = lax.broadcasted_iota(jnp.int32, (task_column.shape[0], 8), 1)
    hot = jnp.where(which == task_column, 1.0, 0.0).astype(bf16)
    high = grads.astype(bf16)
    low = (grads - high.astype(f32)).astype(bf16)
    return inner_cols(hot, high) + inner_cols(hot, low)


def inverse_rms(stream):
    return lax.rsqrt(jnp.mean(stream * stream, axis=-1, keepdims=True) + norm_eps)


def norm_back(stream, gain, cotan):
    r = inverse_rms(stream)
    scaled = cotan * gain
    inner = jnp.mean(scaled * stream, axis=-1, keepdims=True)
    return r * (scaled - stream * (r * r * inner)), cotan * (stream * r)


def call(kernel, grid, ins, outs, scratch=(), flops=0, name=None):
    size = sum(a.size * a.dtype.itemsize for a, _, _ in ins)
    size += sum(functools.reduce(lambda p, q: p * q, s, 1) * jnp.dtype(d).itemsize for s, d, _, _ in outs)
    return pl.pallas_call(
        kernel,
        grid=grid,
        in_specs=[pl.BlockSpec(b, m) for _, b, m in ins],
        out_specs=[pl.BlockSpec(b, m) for _, _, b, m in outs],
        out_shape=[jax.ShapeDtypeStruct(s, d) for s, d, _, _ in outs],
        scratch_shapes=list(scratch),
        compiler_params=pltpu.CompilerParams(vmem_limit_bytes=VMEM_BYTES),
        cost_estimate=pl.CostEstimate(flops=flops, bytes_accessed=size, transcendentals=0),
        name=name,
    )(*[a for a, _, _ in ins])


def whole(array):
    return (array, array.shape, lambda *_: (0,) * array.ndim)


def by_row(array, rows):
    return (array, (rows,) + array.shape[1:], lambda i: (i,) + (0,) * (array.ndim - 1))


def out_row(shape, dtype, rows):
    return (shape, dtype, (rows,) + shape[1:], lambda i: (i,) + (0,) * (len(shape) - 1))


def out_whole(shape, dtype):
    return (shape, dtype, shape, lambda *_: (0,) * len(shape))


def pre_kernel(x, task, gain, wq, wk, wv, normed, q, k, v):
    stream = x[...].astype(f32)
    n = (stream * inverse_rms(stream) * token_gain(task[...], gain[...])).astype(bf16)
    normed[...] = n
    q[...] = (plain_dot(n, wq[...]).astype(bf16).astype(f32) * HEAD**-0.5).astype(bf16)
    k[...] = plain_dot(n, wk[...]).astype(bf16)
    v[...] = plain_dot(n, wv[...]).astype(bf16)


def memory_kernel(x, wk, wv, k, v):
    k[...] = plain_dot(x[...], wk[...]).astype(bf16)
    v[...] = plain_dot(x[...], wv[...]).astype(bf16)


def middle_kernel(x, mixed, wo, task, gain, wq, stream_out, normed, q):
    stream = x[...].astype(f32) + plain_dot(mixed[...], wo[...])
    stream_out[...] = stream
    n = (stream * inverse_rms(stream) * token_gain(task[...], gain[...])).astype(bf16)
    normed[...] = n
    q[...] = (plain_dot(n, wq[...]).astype(bf16).astype(f32) * HEAD**-0.5).astype(bf16)


def half_masks():
    lane = lax.broadcasted_iota(jnp.int32, (1, PAIR), 1)
    first = jnp.where(lane < HEAD, 1.0, 0.0)
    return first.astype(bf16), (1.0 - first).astype(bf16)


def attend_forward_kernel(causal, q_ref, k_ref, v_ref, seg_q, seg_k, mixed_ref, p_ref, bias):
    length, keys_all = q_ref.shape[0], k_ref.shape[0]
    step = length // 2 if causal else length

    @pl.when(pl.program_id(1) == 0)
    def _():
        same = seg_q[...] == seg_k[0]
        if causal:
            at_q = lax.broadcasted_iota(jnp.int32, (length, keys_all), 0)
            at_k = lax.broadcasted_iota(jnp.int32, (length, keys_all), 1)
            same = same & (at_q >= at_k)
        bias[...] = jnp.where(same, 0.0, masked_score)

    masks = half_masks()
    for first in range(0, length, step):
        rows = pl.ds(first, step)
        keys = first + step if causal else keys_all
        q = q_ref[rows, :]
        k = k_ref[:keys, :]
        v = v_ref[:keys, :]
        out = None
        for h, mask in enumerate(masks):
            s = inner_rows(q * mask, k) + bias[rows, :keys]
            e = jnp.exp(s - jnp.max(s, axis=-1, keepdims=True))
            p = (e * (1.0 / jnp.sum(e, axis=-1, keepdims=True))).astype(bf16)
            p_ref[0, h, rows, :keys] = p
            part = plain_dot(p, v * mask)
            out = part if out is None else out + part
        mixed_ref[rows, :] = out.astype(bf16)


def attend_backward_kernel(
    causal, q_ref, k_ref, v_ref, mixed_ref, gm_ref, p_ref, gq_ref, gk_ref, gv_ref
):
    length, keys_all = q_ref.shape[0], k_ref.shape[0]
    step = length // 2 if causal else length
    masks = half_masks()
    gk_parts, gv_parts = [], []
    for first in range(0, length, step):
        rows = pl.ds(first, step)
        keys = first + step if causal else keys_all
        q = q_ref[rows, :]
        k = k_ref[:keys, :]
        v = v_ref[:keys, :]
        gm = gm_ref[rows, :]
        product = gm.astype(f32) * mixed_ref[rows, :].astype(f32)
        gq = gk = gv = 0.0
        for h, mask in enumerate(masks):
            inner = jnp.sum(product * mask.astype(f32), axis=-1, keepdims=True)
            p = p_ref[0, h, rows, :keys]
            gm_half = gm * mask
            gw = inner_rows(gm_half, v)
            gs = (p.astype(f32) * (gw - inner)).astype(bf16)
            gv = gv + inner_cols(p, gm_half)
            gq = gq + plain_dot(gs, k * mask)
            gk = gk + inner_cols(gs, q * mask)
        gq_ref[rows, :] = (gq * HEAD**-0.5).astype(bf16)
        gk_parts.append(gk)
        gv_parts.append(gv)
    for ref, terms in ((gk_ref, gk_parts), (gv_ref, gv_parts)):
        if not causal:
            ref[...] = terms[0].astype(bf16)
        else:
            ref[:step, :] = (terms[0] + terms[1][:step]).astype(bf16)
            ref[step:, :] = terms[1][step:].astype(bf16)


def attention_specs(rows, length, arrays):
    return [(a, (length, PAIR), lambda r, p: (r, p)) for a in arrays]


def attend_forward(causal, rows, length, q, k, v, seg_q, seg_k):
    mem_len = k.shape[0] // rows
    mixed, probs = call(
        functools.partial(attend_forward_kernel, causal),
        (rows, HEADS // 2),
        attention_specs(rows, length, (q,))
        + attention_specs(rows, mem_len, (k, v))
        + [
            (seg_q.reshape(rows * length, 1), (length, 1), lambda r, p: (r, 0)),
            (seg_k.reshape(rows, 1, mem_len), (1, 1, mem_len), lambda r, p: (r, 0, 0)),
        ],
        [
            (q.shape, bf16, (length, PAIR), lambda r, p: (r, p)),
            (
                (rows, HEADS, length, mem_len),
                bf16,
                (1, 2, length, mem_len),
                lambda r, p: (r, p, 0, 0),
            ),
        ],
        scratch=[pltpu.VMEM((length, mem_len), f32)],
        flops=4 * rows * HEADS * length * mem_len * PAIR,
        name="attend_forward",
    )
    return mixed, probs


def attend_backward(causal, rows, length, q, k, v, mixed, grad_mixed, probs):
    mem_len = k.shape[0] // rows
    return call(
        functools.partial(attend_backward_kernel, causal),
        (rows, HEADS // 2),
        attention_specs(rows, length, (q,))
        + attention_specs(rows, mem_len, (k, v))
        + attention_specs(rows, length, (mixed, grad_mixed))
        + [(probs, (1, 2, length, mem_len), lambda r, p: (r, p, 0, 0))],
        [
            (q.shape, bf16, (length, PAIR), lambda r, p: (r, p)),
            (k.shape, bf16, (mem_len, PAIR), lambda r, p: (r, p)),
            (k.shape, bf16, (mem_len, PAIR), lambda r, p: (r, p)),
        ],
        flops=8 * rows * HEADS * length * mem_len * PAIR,
        name="attend_backward",
    )


CHUNK = 768


def feed_kernel(
    s1, mixed, wo, task, gain, w_in, w_out, down_all, up_all, cot,
    output, n3, act, gu, gfeed, g2, g2_low, gmix, up_grad, down_grad, gain_grad,
    slope, total,
):
    first = pl.program_id(0) == 0
    units = w_in.shape[1]
    stream = s1[...] + plain_dot(mixed[...], wo[...])
    picked = token_gain(task[...], gain[...])
    n3[...] = (stream * inverse_rms(stream) * picked).astype(bf16)
    total[...] = jnp.zeros_like(total)

    @pl.loop(0, units // CHUNK)
    def _(j):
        cols = pl.ds(pl.multiple_of(j * CHUNK, CHUNK), CHUNK)
        value, rate = gelu_both(plain_dot(n3[...], w_in[:, cols]))
        value = value.astype(bf16)
        act[:, cols] = value
        slope[:, cols] = rate.astype(bf16)
        total[...] += plain_dot(value, w_out[cols, :])

    feed = total[...]
    feed_low = feed.astype(bf16)
    tokens, wide = stream.shape[0], down_all.shape[1]
    owner = lax.broadcasted_iota(jnp.int32, (tokens, wide), 1) - task[...] * ADA
    mask = jnp.where((owner >= 0) & (owner < ADA), 1.0, 0.0)
    narrow, narrow_slope = gelu_both(plain_dot(feed_low, down_all[...]) * mask)
    narrow = narrow.astype(bf16)
    output[...] = (stream + feed + plain_dot(narrow, up_all[...])).astype(bf16)
    cotan = cot[...]
    gb = (narrow_slope * inner_rows(cotan, up_all[...]) * mask).astype(bf16)
    grad_feed = (cotan.astype(f32) + inner_rows(gb, down_all[...])).astype(bf16)
    gfeed[...] = grad_feed
    up_now = inner_cols(narrow, cotan)
    down_now = inner_cols(feed_low, gb)
    total[...] = jnp.zeros_like(total)

    @pl.loop(0, units // CHUNK)
    def _(j):
        cols = pl.ds(pl.multiple_of(j * CHUNK, CHUNK), CHUNK)
        grad = slope[:, cols].astype(f32) * inner_rows(gfeed[...], w_out[cols, :])
        grad = grad.astype(bf16)
        gu[:, cols] = grad
        total[...] += inner_rows(grad, w_in[:, cols])

    stream_grad, gain_tokens = norm_back(stream, picked, total[...])
    grad_two = cotan.astype(f32) + stream_grad
    g2[...] = grad_two
    low = grad_two.astype(bf16)
    g2_low[...] = low
    gmix[...] = inner_rows(low, wo[...]).astype(bf16)
    gain_now = gain_rows(task[...], gain_tokens)

    @pl.when(first)
    def _():
        up_grad[...] = up_now
        down_grad[...] = down_now
        gain_grad[...] = gain_now

    @pl.when(jnp.logical_not(first))
    def _():
        up_grad[...] += up_now
        down_grad[...] += down_now
        gain_grad[...] += gain_now


def cross_back_kernel(gq, wq, s1, task, gain, g2, wo, g1, g1_low, gmix, gain_grad):
    stream = s1[...]
    picked = token_gain(task[...], gain[...])
    stream_grad, gain_tokens = norm_back(stream, picked, inner_rows(gq[...], wq[...]))
    grad_one = g2[...] + stream_grad
    g1[...] = grad_one
    low = grad_one.astype(bf16)
    g1_low[...] = low
    gmix[...] = inner_rows(low, wo[...]).astype(bf16)
    accumulate(gain_grad, gain_rows(task[...], gain_tokens))


def accumulate(ref, value):
    @pl.when(pl.program_id(0) == 0)
    def _():
        ref[...] = value

    @pl.when(pl.program_id(0) != 0)
    def _():
        ref[...] += value


def memory_back_kernel(gk, gv, wk, wv, out):
    out[...] = inner_rows(gk[...], wk[...]) + inner_rows(gv[...], wv[...])


def input_back_kernel(gq, gk, gv, wq, wk, wv, x, task, gain, g1, out, gain_grad):
    stream = x[...].astype(f32)
    picked = token_gain(task[...], gain[...])
    cotan = inner_rows(gq[...], wq[...]) + inner_rows(gk[...], wk[...])
    cotan = cotan + inner_rows(gv[...], wv[...])
    stream_grad, gain_tokens = norm_back(stream, picked, cotan)
    out[...] = g1[...] + stream_grad
    accumulate(gain_grad, gain_rows(task[...], gain_tokens))


def outer_kernel(which, sources, *refs):
    left = refs[:sources]
    right = refs[sources : sources + len(which)]
    outs = refs[sources + len(which) :]
    for source, grad, out in zip(which, right, outs):
        for first in range(0, out.shape[1], CHUNK):
            cols = slice(first, first + CHUNK)
            out[:, cols] = inner_cols(left[source][...], grad[:, cols]).astype(bf16)


def outers(sources, grads, which, name):
    tokens, width = sources[0].shape
    block = 256
    return call(
        functools.partial(outer_kernel, which, len(sources)),
        (width // block,),
        [(s, (tokens, block), lambda i: (0, i)) for s in sources] + [whole(g) for g in grads],
        [((width, g.shape[1]), bf16, (block, g.shape[1]), lambda i: (i, 0)) for g in grads],
        flops=sum(2 * tokens * width * g.shape[1] for g in grads),
        name=name,
    )


def layer(x, mem, cot, segments, mem_segments, task, weights, gain_table, down_all, up_all):
    rows, length = segments.shape
    mem_len = mem_segments.shape[1]
    tokens, width = x.shape
    wq1, wk1, wv1, wo1, wq2, wk2, wv2, wo2, w_in, w_out = weights
    gain_one, gain_two, gain_three = (gain_table[:, i * width : (i + 1) * width] for i in range(3))
    block = 512
    grid = (tokens // block,)
    act_shape = (tokens, width)

    def low_out():
        return out_row(act_shape, bf16, block)

    def full_out():
        return out_row(act_shape, f32, block)

    square = 2 * tokens * width * width
    n1, q1, k1, v1 = call(
        pre_kernel,
        grid,
        [by_row(x, block), by_row(task, block)] + [whole(a) for a in (gain_one, wq1, wk1, wv1)],
        [low_out() for _ in range(4)],
        flops=3 * square,
        name="self_projections",
    )
    m1, p1 = attend_forward(True, rows, length, q1, k1, v1, segments, segments)
    s1, n2, q2 = call(
        middle_kernel,
        grid,
        [by_row(x, block), by_row(m1, block), whole(wo1), by_row(task, block), whole(gain_two), whole(wq2)],
        [full_out(), low_out(), low_out()],
        flops=2 * square,
        name="middle",
    )
    k2, v2 = call(
        memory_kernel,
        grid,
        [by_row(mem, block), whole(wk2), whole(wv2)],
        [low_out(), low_out()],
        flops=2 * square,
        name="memory_projections",
    )
    m2, p2 = attend_forward(False, rows, length, q2, k2, v2, segments, mem_segments)
    units = w_in.shape[1]
    wide = up_all.shape[0]
    tasks = gain_table.shape[0]
    output, n3, act, gu, gfeed, g2, g2_low, gmix2, up_grad, down_grad, gain3 = call(
        feed_kernel,
        grid,
        [
            by_row(s1, block), by_row(m2, block), whole(wo2), by_row(task, block), whole(gain_three),
            whole(w_in), whole(w_out), whole(down_all), whole(up_all), by_row(cot, block),
        ],
        [
            low_out(), low_out(), out_row((tokens, units), bf16, block), out_row((tokens, units), bf16, block),
            low_out(), full_out(), low_out(), low_out(),
            out_whole((wide, width), f32), out_whole((width, wide), f32), out_whole((tasks, width), f32),
        ],
        scratch=[pltpu.VMEM((block, units), bf16), pltpu.VMEM((block, width), f32)],
        flops=2 * square + 8 * tokens * width * units,
        name="feed_forward_and_back",
    )
    (hidden_in_grad,) = outers((n3,), (gu,), (0,), "hidden_in_grad")
    (hidden_out_grad,) = outers((act,), (gfeed,), (0,), "hidden_out_grad")
    gq2, gk2, gv2 = attend_backward(False, rows, length, q2, k2, v2, m2, gmix2, p2)
    g1, g1_low, gmix1, gain2 = call(
        cross_back_kernel,
        grid,
        [
            by_row(gq2, block), whole(wq2), by_row(s1, block), by_row(task, block), whole(gain_two),
            by_row(g2, block), whole(wo1),
        ],
        [full_out(), low_out(), low_out(), out_whole((tasks, width), f32)],
        flops=2 * square,
        name="cross_back",
    )
    (mem_grad,) = call(
        memory_back_kernel,
        grid,
        [by_row(gk2, block), by_row(gv2, block), whole(wk2), whole(wv2)],
        [full_out()],
        flops=2 * square,
        name="memory_back",
    )
    wo2_grad, wq2_grad, wk2_grad, wv2_grad = outers(
        (m2, n2, mem), (g2_low, gq2, gk2, gv2), (0, 1, 2, 2), "cross_grads"
    )
    gq1, gk1, gv1 = attend_backward(True, rows, length, q1, k1, v1, m1, gmix1, p1)
    input_grad, gain1 = call(
        input_back_kernel,
        grid,
        [
            by_row(gq1, block), by_row(gk1, block), by_row(gv1, block), whole(wq1), whole(wk1), whole(wv1),
            by_row(x, block), by_row(task, block), whole(gain_one), by_row(g1, block),
        ],
        [full_out(), out_whole((tasks, width), f32)],
        flops=3 * square,
        name="input_back",
    )
    wo1_grad, wq1_grad, wk1_grad, wv1_grad = outers(
        (m1, n1), (g1_low, gq1, gk1, gv1), (0, 1, 1, 1), "self_grads"
    )
    gain_grad = jnp.concatenate((gain1, gain2, gain3), axis=1)
    grads = (
        wq1_grad, wk1_grad, wv1_grad, wo1_grad, wq2_grad, wk2_grad, wv2_grad, wo2_grad,
        hidden_in_grad, hidden_out_grad,
    )
    return output, input_grad, mem_grad, grads, up_grad, down_grad, gain_grad


def on_device(
    block_input, memory, cotangent, segments, memory_segments, task_of_segment,
    self_query, self_key, self_value, self_output,
    cross_query, cross_key, cross_value, cross_output,
    hidden_in, hidden_out, task_table, task_weight, task_bias,
    down_maker, up_maker, gain_maker,
):
    row_count, seq_len, model_width = block_input.shape
    mem_len = memory.shape[1]
    task_count = task_table.shape[0]
    token_count = row_count * seq_len
    parts = lax.axis_size("dp")
    own_rows = self_query.shape[0]
    squares = (
        self_query, self_key, self_value, self_output,
        cross_query, cross_key, cross_value, cross_output,
    )
    packed = jnp.concatenate(
        squares + (hidden_in.reshape(-1, model_width), hidden_out), axis=0
    )
    gathered = lax.all_gather(packed, "dp", axis=0, tiled=False)
    in_rows = hidden_in.size // model_width
    backbone = tuple(
        gathered[:, i * own_rows : (i + 1) * own_rows].reshape(-1, model_width) for i in range(8)
    ) + (
        gathered[:, 8 * own_rows : 8 * own_rows + in_rows].reshape(model_width, -1),
        gathered[:, 8 * own_rows + in_rows :].reshape(-1, model_width),
    )
    task_state, task_back = jax.vjp(task_network, task_table, task_weight, task_bias)
    task_low = task_state.astype(bf16)
    made = inner_rows(task_low, jnp.concatenate((down_maker, up_maker, gain_maker), axis=0))
    made = lax.all_gather(made, "dp", axis=0, tiled=False)
    down_own = down_maker.shape[0]

    def joined(block):
        return block.transpose(1, 0, 2).reshape(task_count, -1)

    made_down = joined(made[:, :, :down_own]).astype(bf16)
    made_up = joined(made[:, :, down_own : 2 * down_own]).astype(bf16)
    gain_table = 1.0 + joined(made[:, :, 2 * down_own :])
    down_all = (
        made_down.reshape(task_count, model_width, ADA)
        .transpose(1, 0, 2)
        .reshape(model_width, task_count * ADA)
    )
    up_all = made_up.reshape(task_count * ADA, model_width)
    seg_match = (
        segments[:, :, None] == jnp.arange(task_of_segment.shape[1], dtype=jnp.int32)[None, None, :]
    )
    token_task = jnp.sum(jnp.where(seg_match, task_of_segment[:, None, :], 0), axis=-1).reshape(
        token_count, 1
    )
    output, input_grad, mem_grad, grads, up_all_grad, down_all_grad, gain_grad = layer(
        block_input.reshape(token_count, model_width),
        memory.reshape(row_count * mem_len, model_width),
        cotangent.reshape(token_count, model_width),
        segments, memory_segments, token_task, backbone, gain_table, down_all, up_all,
    )
    down_rows = (
        down_all_grad.reshape(model_width, task_count, ADA)
        .transpose(0, 2, 1)
        .reshape(model_width * ADA, task_count)
    )
    up_rows = (
        up_all_grad.reshape(task_count, ADA, model_width)
        .transpose(1, 2, 0)
        .reshape(ADA * model_width, task_count)
    )
    gain_rows_all = gain_grad.T

    def blocks(grad):
        return grad.reshape(parts, -1, model_width)

    summed = lax.psum_scatter(
        jnp.concatenate([blocks(g) for g in grads], axis=1), "dp", scatter_dimension=0, tiled=False
    ).astype(f32)
    shares = tuple(summed[i * own_rows : (i + 1) * own_rows] for i in range(8)) + (
        summed[8 * own_rows : 8 * own_rows + in_rows].reshape(hidden_in.shape),
        summed[8 * own_rows + in_rows :],
    )
    small = jnp.concatenate(
        [r.reshape(parts, -1, task_count) for r in (down_rows, up_rows, gain_rows_all)], axis=1
    )
    small = lax.psum_scatter(small, "dp", scatter_dimension=0, tiled=False)
    own_down = small[:down_own].astype(bf16)
    own_up = small[down_own : 2 * down_own].astype(bf16)
    own_gain = small[2 * down_own :]
    down_maker_grad = plain_dot(own_down, task_low)
    up_maker_grad = plain_dot(own_up, task_low)
    gain_maker_grad = exact_dot(own_gain, task_low.astype(f32))
    state_partial = (
        inner_cols(own_down, down_maker)
        + inner_cols(own_up, up_maker)
        + inner_cols(own_gain, gain_maker.astype(f32), exact_mode)
    )
    state_grad = lax.psum(state_partial, "dp")
    table_grad, weight_grad, bias_grad = task_back(state_grad)
    return (
        output.reshape(row_count, seq_len, model_width),
        input_grad.reshape(row_count, seq_len, model_width),
        mem_grad.reshape(row_count, mem_len, model_width),
        *shares,
        table_grad,
        weight_grad,
        bias_grad,
        down_maker_grad,
        up_maker_grad,
        gain_maker_grad,
    )


def solution(mesh):
    rows, whole_copy = P("dp"), P()
    return jax.shard_map(
        on_device,
        mesh=mesh,
        in_specs=(rows,) * 16 + (whole_copy,) * 3 + (rows,) * 3,
        out_specs=(rows,) * 13 + (whole_copy,) * 3 + (rows,) * 3,
        check_vma=False,
    )
```

```python
import functools

import jax
import jax.numpy as jnp
from jax import lax
from jax.experimental import pallas as pl
from jax.experimental.pallas import tpu as pltpu
from jax.sharding import PartitionSpec as P

HEADS = 12
HEAD = 64
ADA = 24
PAIR = 2 * HEAD

exact_mode = lax.Precision.HIGHEST
norm_eps = 1e-06
masked_score = -1e30
bf16 = jnp.bfloat16
f32 = jnp.float32
VMEM_BYTES = 56 << 20


def plain_dot(left_side, right_side):
    return jnp.dot(left_side, right_side, preferred_element_type=f32)


def exact_dot(left_side, right_side):
    return jnp.dot(left_side, right_side, precision=exact_mode, preferred_element_type=f32)


def inner_rows(left_side, right_side):
    return lax.dot_general(
        left_side, right_side, (((1,), (1,)), ((), ())), preferred_element_type=f32
    )


def inner_cols(left_side, right_side, precision_mode=None):
    return lax.dot_general(
        left_side,
        right_side,
        (((0,), (0,)), ((), ())),
        precision=precision_mode,
        preferred_element_type=f32,
    )


def gelu_exact(operand):
    return jax.nn.gelu(operand, approximate=False)


def task_network(table_rows, weight_in, bias_row):
    return gelu_exact(exact_dot(table_rows, weight_in) + bias_row)


def gelu_both(v):
    phi = 0.5 * lax.erf(v * 0.7071067811865476) + 0.5
    slope = phi + v * (jnp.exp(v * v * -0.5) * 0.3989422804014327)
    return v * phi, slope


def token_gain(task_column, gain):
    high = gain.astype(bf16).astype(f32)
    rest = gain - high
    middle = rest.astype(bf16).astype(f32)
    table = jnp.concatenate((high, middle, rest - middle), axis=0).astype(bf16)
    which = lax.broadcasted_iota(jnp.int32, (task_column.shape[0], 24), 1) & 7
    hot = jnp.where(which == task_column, 1.0, 0.0).astype(bf16)
    return plain_dot(hot, table)


def gain_rows(task_column, grads):
    which = lax.broadcasted_iota(jnp.int32, (task_column.shape[0], 8), 1)
    hot = jnp.where(which == task_column, 1.0, 0.0).astype(bf16)
    high = grads.astype(bf16)
    low = (grads - high.astype(f32)).astype(bf16)
    return inner_cols(hot, high) + inner_cols(hot, low)


def inverse_rms(stream):
    return lax.rsqrt(jnp.mean(stream * stream, axis=-1, keepdims=True) + norm_eps)


def norm_back(stream, gain, cotan):
    r = inverse_rms(stream)
    scaled = cotan * gain
    inner = jnp.mean(scaled * stream, axis=-1, keepdims=True)
    return r * (scaled - stream * (r * r * inner)), cotan * (stream * r)


def call(kernel, grid, ins, outs, scratch=(), flops=0, name=None):
    size = sum(a.size * a.dtype.itemsize for a, _, _ in ins)
    size += sum(functools.reduce(lambda p, q: p * q, s, 1) * jnp.dtype(d).itemsize for s, d, _, _ in outs)
    return pl.pallas_call(
        kernel,
        grid=grid,
        in_specs=[pl.BlockSpec(b, m) for _, b, m in ins],
        out_specs=[pl.BlockSpec(b, m) for _, _, b, m in outs],
        out_shape=[jax.ShapeDtypeStruct(s, d) for s, d, _, _ in outs],
        scratch_shapes=list(scratch),
        compiler_params=pltpu.CompilerParams(vmem_limit_bytes=VMEM_BYTES),
        cost_estimate=pl.CostEstimate(flops=flops, bytes_accessed=size, transcendentals=0),
        name=name,
    )(*[a for a, _, _ in ins])


def whole(array):
    return (array, array.shape, lambda *_: (0,) * array.ndim)


def by_row(array, rows):
    return (array, (rows,) + array.shape[1:], lambda i: (i,) + (0,) * (array.ndim - 1))


def out_row(shape, dtype, rows):
    return (shape, dtype, (rows,) + shape[1:], lambda i: (i,) + (0,) * (len(shape) - 1))


def out_whole(shape, dtype):
    return (shape, dtype, shape, lambda *_: (0,) * len(shape))


def pre_kernel(x, task, gain, wq, wk, wv, normed, q, k, v):
    stream = x[...].astype(f32)
    n = (stream * inverse_rms(stream) * token_gain(task[...], gain[...])).astype(bf16)
    normed[...] = n
    q[...] = (plain_dot(n, wq[...]).astype(bf16).astype(f32) * HEAD**-0.5).astype(bf16)
    k[...] = plain_dot(n, wk[...]).astype(bf16)
    v[...] = plain_dot(n, wv[...]).astype(bf16)


def memory_kernel(x, wk, wv, k, v):
    k[...] = plain_dot(x[...], wk[...]).astype(bf16)
    v[...] = plain_dot(x[...], wv[...]).astype(bf16)


def middle_kernel(x, mixed, wo, task, gain, wq, stream_out, normed, q):
    stream = x[...].astype(f32) + plain_dot(mixed[...], wo[...])
    stream_out[...] = stream
    n = (stream * inverse_rms(stream) * token_gain(task[...], gain[...])).astype(bf16)
    normed[...] = n
    q[...] = (plain_dot(n, wq[...]).astype(bf16).astype(f32) * HEAD**-0.5).astype(bf16)


def half_masks():
    lane = lax.broadcasted_iota(jnp.int32, (1, PAIR), 1)
    first = jnp.where(lane < HEAD, 1.0, 0.0)
    return first.astype(bf16), (1.0 - first).astype(bf16)


def attend_forward_kernel(causal, q_ref, k_ref, v_ref, seg_q, seg_k, mixed_ref, p_ref, bias):
    length, keys_all = q_ref.shape[0], k_ref.shape[0]
    step = length // 2 if causal else length

    @pl.when(pl.program_id(1) == 0)
    def _():
        same = seg_q[...] == seg_k[0]
        if causal:
            at_q = lax.broadcasted_iota(jnp.int32, (length, keys_all), 0)
            at_k = lax.broadcasted_iota(jnp.int32, (length, keys_all), 1)
            same = same & (at_q >= at_k)
        bias[...] = jnp.where(same, 0.0, masked_score)

    masks = half_masks()
    for first in range(0, length, step):
        rows = pl.ds(first, step)
        keys = first + step if causal else keys_all
        q = q_ref[rows, :]
        k = k_ref[:keys, :]
        v = v_ref[:keys, :]
        out = None
        for h, mask in enumerate(masks):
            s = inner_rows(q * mask, k) + bias[rows, :keys]
            e = jnp.exp(s - jnp.max(s, axis=-1, keepdims=True))
            p = (e * (1.0 / jnp.sum(e, axis=-1, keepdims=True))).astype(bf16)
            p_ref[0, h, rows, :keys] = p
            part = plain_dot(p, v * mask)
            out = part if out is None else out + part
        mixed_ref[rows, :] = out.astype(bf16)


def attend_backward_kernel(
    causal, q_ref, k_ref, v_ref, mixed_ref, gm_ref, p_ref, gq_ref, gk_ref, gv_ref
):
    length, keys_all = q_ref.shape[0], k_ref.shape[0]
    step = length // 2 if causal else length
    masks = half_masks()
    gk_parts, gv_parts = [], []
    for first in range(0, length, step):
        rows = pl.ds(first, step)
        keys = first + step if causal else keys_all
        q = q_ref[rows, :]
        k = k_ref[:keys, :]
        v = v_ref[:keys, :]
        gm = gm_ref[rows, :]
        product = gm.astype(f32) * mixed_ref[rows, :].astype(f32)
        gq = gk = gv = 0.0
        for h, mask in enumerate(masks):
            inner = jnp.sum(product * mask.astype(f32), axis=-1, keepdims=True)
            p = p_ref[0, h, rows, :keys]
            gm_half = gm * mask
            gw = inner_rows(gm_half, v)
            gs = (p.astype(f32) * (gw - inner)).astype(bf16)
            gv = gv + inner_cols(p, gm_half)
            gq = gq + plain_dot(gs, k * mask)
            gk = gk + inner_cols(gs, q * mask)
        gq_ref[rows, :] = (gq * HEAD**-0.5).astype(bf16)
        gk_parts.append(gk)
        gv_parts.append(gv)
    for ref, terms in ((gk_ref, gk_parts), (gv_ref, gv_parts)):
        if not causal:
            ref[...] = terms[0].astype(bf16)
        else:
            ref[:step, :] = (terms[0] + terms[1][:step]).astype(bf16)
            ref[step:, :] = terms[1][step:].astype(bf16)


def attention_specs(rows, length, arrays):
    return [(a, (length, PAIR), lambda r, p: (r, p)) for a in arrays]


def attend_forward(causal, rows, length, q, k, v, seg_q, seg_k):
    mem_len = k.shape[0] // rows
    mixed, probs = call(
        functools.partial(attend_forward_kernel, causal),
        (rows, HEADS // 2),
        attention_specs(rows, length, (q,))
        + attention_specs(rows, mem_len, (k, v))
        + [
            (seg_q.reshape(rows * length, 1), (length, 1), lambda r, p: (r, 0)),
            (seg_k.reshape(rows, 1, mem_len), (1, 1, mem_len), lambda r, p: (r, 0, 0)),
        ],
        [
            (q.shape, bf16, (length, PAIR), lambda r, p: (r, p)),
            (
                (rows, HEADS, length, mem_len),
                bf16,
                (1, 2, length, mem_len),
                lambda r, p: (r, p, 0, 0),
            ),
        ],
        scratch=[pltpu.VMEM((length, mem_len), f32)],
        flops=4 * rows * HEADS * length * mem_len * PAIR,
        name="attend_forward",
    )
    return mixed, probs


def attend_backward(causal, rows, length, q, k, v, mixed, grad_mixed, probs):
    mem_len = k.shape[0] // rows
    return call(
        functools.partial(attend_backward_kernel, causal),
        (rows, HEADS // 2),
        attention_specs(rows, length, (q,))
        + attention_specs(rows, mem_len, (k, v))
        + attention_specs(rows, length, (mixed, grad_mixed))
        + [(probs, (1, 2, length, mem_len), lambda r, p: (r, p, 0, 0))],
        [
            (q.shape, bf16, (length, PAIR), lambda r, p: (r, p)),
            (k.shape, bf16, (mem_len, PAIR), lambda r, p: (r, p)),
            (k.shape, bf16, (mem_len, PAIR), lambda r, p: (r, p)),
        ],
        flops=8 * rows * HEADS * length * mem_len * PAIR,
        name="attend_backward",
    )


CHUNK = 768


def feed_kernel(
    s1, mixed, wo, task, gain, w_in, w_out, down_all, up_all, cot,
    output, n3, act, gu, gfeed, g2, g2_low, gmix, up_grad, down_grad, gain_grad,
    slope, total,
):
    first = pl.program_id(0) == 0
    units = w_in.shape[1]
    stream = s1[...] + plain_dot(mixed[...], wo[...])
    picked = token_gain(task[...], gain[...])
    n3[...] = (stream * inverse_rms(stream) * picked).astype(bf16)
    total[...] = jnp.zeros_like(total)

    @pl.loop(0, units // CHUNK)
    def _(j):
        cols = pl.ds(pl.multiple_of(j * CHUNK, CHUNK), CHUNK)
        value, rate = gelu_both(plain_dot(n3[...], w_in[:, cols]))
        value = value.astype(bf16)
        act[:, cols] = value
        slope[:, cols] = rate.astype(bf16)
        total[...] += plain_dot(value, w_out[cols, :])

    feed = total[...]
    feed_low = feed.astype(bf16)
    tokens, wide = stream.shape[0], down_all.shape[1]
    owner = lax.broadcasted_iota(jnp.int32, (tokens, wide), 1) - task[...] * ADA
    mask = jnp.where((owner >= 0) & (owner < ADA), 1.0, 0.0)
    narrow, narrow_slope = gelu_both(plain_dot(feed_low, down_all[...]) * mask)
    narrow = narrow.astype(bf16)
    output[...] = (stream + feed + plain_dot(narrow, up_all[...])).astype(bf16)
    cotan = cot[...]
    gb = (narrow_slope * inner_rows(cotan, up_all[...]) * mask).astype(bf16)
    grad_feed = (cotan.astype(f32) + inner_rows(gb, down_all[...])).astype(bf16)
    gfeed[...] = grad_feed
    up_now = inner_cols(narrow, cotan)
    down_now = inner_cols(feed_low, gb)
    total[...] = jnp.zeros_like(total)

    @pl.loop(0, units // CHUNK)
    def _(j):
        cols = pl.ds(pl.multiple_of(j * CHUNK, CHUNK), CHUNK)
        grad = slope[:, cols].astype(f32) * inner_rows(gfeed[...], w_out[cols, :])
        grad = grad.astype(bf16)
        gu[:, cols] = grad
        total[...] += inner_rows(grad, w_in[:, cols])

    stream_grad, gain_tokens = norm_back(stream, picked, total[...])
    grad_two = cotan.astype(f32) + stream_grad
    g2[...] = grad_two
    low = grad_two.astype(bf16)
    g2_low[...] = low
    gmix[...] = inner_rows(low, wo[...]).astype(bf16)
    gain_now = gain_rows(task[...], gain_tokens)

    @pl.when(first)
    def _():
        up_grad[...] = up_now
        down_grad[...] = down_now
        gain_grad[...] = gain_now

    @pl.when(jnp.logical_not(first))
    def _():
        up_grad[...] += up_now
        down_grad[...] += down_now
        gain_grad[...] += gain_now


def cross_back_kernel(gq, wq, s1, task, gain, g2, wo, g1, g1_low, gmix, gain_grad):
    stream = s1[...]
    picked = token_gain(task[...], gain[...])
    stream_grad, gain_tokens = norm_back(stream, picked, inner_rows(gq[...], wq[...]))
    grad_one = g2[...] + stream_grad
    g1[...] = grad_one
    low = grad_one.astype(bf16)
    g1_low[...] = low
    gmix[...] = inner_rows(low, wo[...]).astype(bf16)
    accumulate(gain_grad, gain_rows(task[...], gain_tokens))


def accumulate(ref, value):
    @pl.when(pl.program_id(0) == 0)
    def _():
        ref[...] = value

    @pl.when(pl.program_id(0) != 0)
    def _():
        ref[...] += value


def memory_back_kernel(gk, gv, wk, wv, out):
    out[...] = inner_rows(gk[...], wk[...]) + inner_rows(gv[...], wv[...])


def input_back_kernel(gq, gk, gv, wq, wk, wv, x, task, gain, g1, out, gain_grad):
    stream = x[...].astype(f32)
    picked = token_gain(task[...], gain[...])
    cotan = inner_rows(gq[...], wq[...]) + inner_rows(gk[...], wk[...])
    cotan = cotan + inner_rows(gv[...], wv[...])
    stream_grad, gain_tokens = norm_back(stream, picked, cotan)
    out[...] = g1[...] + stream_grad
    accumulate(gain_grad, gain_rows(task[...], gain_tokens))


def outer_kernel(which, sources, *refs):
    left = refs[:sources]
    right = refs[sources : sources + len(which)]
    outs = refs[sources + len(which) :]
    for source, grad, out in zip(which, right, outs):
        for first in range(0, out.shape[1], CHUNK):
            cols = slice(first, first + CHUNK)
            out[:, cols] = inner_cols(left[source][...], grad[:, cols]).astype(bf16)


def outers(sources, grads, which, name):
    tokens, width = sources[0].shape
    block = 256
    return call(
        functools.partial(outer_kernel, which, len(sources)),
        (width // block,),
        [(s, (tokens, block), lambda i: (0, i)) for s in sources] + [whole(g) for g in grads],
        [((width, g.shape[1]), bf16, (block, g.shape[1]), lambda i: (i, 0)) for g in grads],
        flops=sum(2 * tokens * width * g.shape[1] for g in grads),
        name=name,
    )


def layer(x, mem, cot, segments, mem_segments, task, weights, gain_table, down_all, up_all):
    rows, length = segments.shape
    mem_len = mem_segments.shape[1]
    tokens, width = x.shape
    wq1, wk1, wv1, wo1, wq2, wk2, wv2, wo2, w_in, w_out = weights
    gain_one, gain_two, gain_three = (gain_table[:, i * width : (i + 1) * width] for i in range(3))
    block = 512
    grid = (tokens // block,)
    act_shape = (tokens, width)

    def low_out():
        return out_row(act_shape, bf16, block)

    def full_out():
        return out_row(act_shape, f32, block)

    square = 2 * tokens * width * width
    n1, q1, k1, v1 = call(
        pre_kernel,
        grid,
        [by_row(x, block), by_row(task, block)] + [whole(a) for a in (gain_one, wq1, wk1, wv1)],
        [low_out() for _ in range(4)],
        flops=3 * square,
        name="self_projections",
    )
    m1, p1 = attend_forward(True, rows, length, q1, k1, v1, segments, segments)
    s1, n2, q2 = call(
        middle_kernel,
        grid,
        [by_row(x, block), by_row(m1, block), whole(wo1), by_row(task, block), whole(gain_two), whole(wq2)],
        [full_out(), low_out(), low_out()],
        flops=2 * square,
        name="middle",
    )
    k2, v2 = call(
        memory_kernel,
        grid,
        [by_row(mem, block), whole(wk2), whole(wv2)],
        [low_out(), low_out()],
        flops=2 * square,
        name="memory_projections",
    )
    m2, p2 = attend_forward(False, rows, length, q2, k2, v2, segments, mem_segments)
    units = w_in.shape[1]
    wide = up_all.shape[0]
    tasks = gain_table.shape[0]
    output, n3, act, gu, gfeed, g2, g2_low, gmix2, up_grad, down_grad, gain3 = call(
        feed_kernel,
        grid,
        [
            by_row(s1, block), by_row(m2, block), whole(wo2), by_row(task, block), whole(gain_three),
            whole(w_in), whole(w_out), whole(down_all), whole(up_all), by_row(cot, block),
        ],
        [
            low_out(), low_out(), out_row((tokens, units), bf16, block), out_row((tokens, units), bf16, block),
            low_out(), full_out(), low_out(), low_out(),
            out_whole((wide, width), f32), out_whole((width, wide), f32), out_whole((tasks, width), f32),
        ],
        scratch=[pltpu.VMEM((block, units), bf16), pltpu.VMEM((block, width), f32)],
        flops=2 * square + 8 * tokens * width * units,
        name="feed_forward_and_back",
    )
    (hidden_in_grad,) = outers((n3,), (gu,), (0,), "hidden_in_grad")
    (hidden_out_grad,) = outers((act,), (gfeed,), (0,), "hidden_out_grad")
    gq2, gk2, gv2 = attend_backward(False, rows, length, q2, k2, v2, m2, gmix2, p2)
    g1, g1_low, gmix1, gain2 = call(
        cross_back_kernel,
        grid,
        [
            by_row(gq2, block), whole(wq2), by_row(s1, block), by_row(task, block), whole(gain_two),
            by_row(g2, block), whole(wo1),
        ],
        [full_out(), low_out(), low_out(), out_whole((tasks, width), f32)],
        flops=2 * square,
        name="cross_back",
    )
    (mem_grad,) = call(
        memory_back_kernel,
        grid,
        [by_row(gk2, block), by_row(gv2, block), whole(wk2), whole(wv2)],
        [full_out()],
        flops=2 * square,
        name="memory_back",
    )
    wo2_grad, wq2_grad, wk2_grad, wv2_grad = outers(
        (m2, n2, mem), (g2_low, gq2, gk2, gv2), (0, 1, 2, 2), "cross_grads"
    )
    gq1, gk1, gv1 = attend_backward(True, rows, length, q1, k1, v1, m1, gmix1, p1)
    input_grad, gain1 = call(
        input_back_kernel,
        grid,
        [
            by_row(gq1, block), by_row(gk1, block), by_row(gv1, block), whole(wq1), whole(wk1), whole(wv1),
            by_row(x, block), by_row(task, block), whole(gain_one), by_row(g1, block),
        ],
        [full_out(), out_whole((tasks, width), f32)],
        flops=3 * square,
        name="input_back",
    )
    wo1_grad, wq1_grad, wk1_grad, wv1_grad = outers(
        (m1, n1), (g1_low, gq1, gk1, gv1), (0, 1, 1, 1), "self_grads"
    )
    gain_grad = jnp.concatenate((gain1, gain2, gain3), axis=1)
    grads = (
        wq1_grad, wk1_grad, wv1_grad, wo1_grad, wq2_grad, wk2_grad, wv2_grad, wo2_grad,
        hidden_in_grad, hidden_out_grad,
    )
    return output, input_grad, mem_grad, grads, up_grad, down_grad, gain_grad


LINE = 4
MESH = pl.DeviceIdType.MESH


class Place:
    def __init__(self):
        me = lax.axis_index("dp")
        self.core = lax.rem(me, 2)
        self.x = lax.rem(me // 2, 2)
        self.y = lax.rem(me // 4, 2)
        self.z = me // 8

    def at(self, z=None, y=None, x=None, core=None):
        z = self.z if z is None else z
        y = self.y if y is None else y
        x = self.x if x is None else x
        core = self.core if core is None else core
        return (((z * 2 + y) * 2 + x) * 2 + core,)

    def sibling(self):
        return self.at(core=1 - self.core)

    def over_x(self):
        return self.at(x=1 - self.x)

    def over_y(self):
        return self.at(y=1 - self.y)

    def along_z(self, k):
        return self.at(z=lax.rem(self.z + k, LINE))

    def partners(self):
        return [self.sibling(), self.over_x(), self.over_y()] + [self.along_z(k) for k in (1, 2, 3)]


def meet(place):
    barrier = pltpu.get_barrier_semaphore()
    partners = place.partners()
    for partner in partners:
        pl.semaphore_signal(barrier, inc=1, device_id=partner, device_id_type=MESH)
    pl.semaphore_wait(barrier, len(partners))


class Copies:
    def __init__(self, send, recv):
        self.send, self.recv, self.used, self.open = send, recv, 0, []

    def remote(self, source, target, device):
        copy = pltpu.make_async_remote_copy(
            src_ref=source,
            dst_ref=target,
            send_sem=self.send.at[self.used],
            recv_sem=self.recv.at[self.used],
            device_id=device,
            device_id_type=MESH,
        )
        self.used += 1
        copy.start()
        self.open.append(copy)
        return copy

    def local(self, source, target):
        copy = pltpu.make_async_copy(source, target, self.recv.at[self.used])
        self.used += 1
        copy.start()
        return copy

    def finish(self):
        for copy in self.open:
            copy.wait_send()


def shares(rows, turn):
    cut = rows // 2 if rows % 32 == 0 else (rows // 32 + turn % 2) * 16
    return slice(0, cut), slice(cut, rows)


def stepped(count, stages):
    for turn in range(count + len(stages) - 1):
        for late, stage in enumerate(stages):
            if 0 <= turn - late < count:
                stage(turn - late)


def gather_kernel(count, *refs):
    own, made = refs[:count], refs[count]
    outs, made_out = refs[count + 1 : 2 * count + 1], refs[2 * count + 1]
    scratch = refs[2 * count + 2 :]
    whole_rows, halves, blocks = scratch[:count], scratch[count : 2 * count], scratch[2 * count : 3 * count]
    send, recv = scratch[3 * count :]
    here = Place()
    copies = Copies(send, recv)
    z, y, x, c = here.z, here.y, here.x, here.core

    def half(i, core):
        width = outs[i].shape[-1] // 2
        return pl.ds(pl.multiple_of(core * width, 128), width)

    for i in range(count):
        whole_rows[i][...] = own[i][...].astype(f32)
    meet(here)
    pair, first, second, third, last = {}, {}, {}, {}, {}
    half_made = made_out.shape[-1] // 2
    made_cols = (pl.ds(0, half_made), pl.ds(half_made, half_made))
    made_first = [copies.local(made, made_out.at[z, y, x, c])]
    made_first += [
        copies.remote(made, made_out.at[z, y, x, c], here.along_z(k)) for k in (1, 2, 3)
    ]
    for i in range(count):
        rows = own[i].shape[0]
        mine = pl.ds(pl.multiple_of(c * rows, 8), rows)
        pair[i] = copies.remote(
            whole_rows[i].at[:, half(i, 1 - c)], halves[i].at[mine, :], here.sibling()
        )
        halves[i][mine, :] = whole_rows[i][:, half(i, c)]
    for i in range(count):
        pair[i].wait_recv()
        blocks[i][...] = halves[i][...].astype(bf16)
        target = outs[i].at[z, y, x, :, half(i, c)]
        first[i] = [copies.remote(blocks[i], target, here.along_z(k)) for k in (1, 2, 3)]
        first[i].append(copies.local(blocks[i], target))

    made_first[0].wait()
    for copy in made_first[1:]:
        copy.wait_recv()
    made_second = []
    for cols, device in zip(made_cols, (here.over_x(), here.over_y())):
        part = made_out.at[:, y, x, c, :, cols]
        made_second.append(copies.remote(part, part, device))
    for copy in made_second:
        copy.wait_recv()
    made_third = []
    for part, device in (
        (made_out.at[:, y, :, c, :, made_cols[0]], here.over_y()),
        (made_out.at[:, :, x, c, :, made_cols[1]], here.over_x()),
    ):
        made_third.append(copies.remote(part, part, device))

    def along_first(i):
        for copy in first[i][:3]:
            copy.wait_recv()
        first[i][3].wait()
        second[i] = []
        for rows, device in zip(shares(outs[i].shape[3], i), (here.over_x(), here.over_y())):
            part = outs[i].at[:, y, x, rows, half(i, c)]
            second[i].append(copies.remote(part, part, device))

    def along_second(i):
        for copy in second[i]:
            copy.wait_recv()
        one, two = shares(outs[i].shape[3], i)
        third[i] = []
        for part, device in (
            (outs[i].at[:, y, :, one, half(i, c)], here.over_y()),
            (outs[i].at[:, :, x, two, half(i, c)], here.over_x()),
        ):
            third[i].append(copies.remote(part, part, device))

    def to_sibling(i):
        for copy in third[i]:
            copy.wait_recv()
        part = outs[i].at[:, :, :, :, half(i, c)]
        last[i] = copies.remote(part, part, here.sibling())

    stepped(count, (along_first, along_second, to_sibling))
    for copy in made_third:
        copy.wait_recv()
    part = made_out.at[:, :, :, c]
    made_last = copies.remote(part, part, here.sibling())
    for i in range(count):
        last[i].wait_recv()
    made_last.wait_recv()
    copies.finish()


def gather(own, made):
    count = len(own)
    spaces = LINE, 2, 2
    copies = 10 * count + 12
    any_space = pl.BlockSpec(memory_space=pl.ANY)
    vmem = pl.BlockSpec(memory_space=pltpu.VMEM)
    return pl.pallas_call(
        functools.partial(gather_kernel, count),
        in_specs=[vmem] * (count + 1),
        out_specs=[any_space] * (count + 1),
        out_shape=[
            jax.ShapeDtypeStruct(spaces + (2 * a.shape[0], a.shape[1]), bf16) for a in own
        ]
        + [jax.ShapeDtypeStruct(spaces + (2,) + made.shape, f32)],
        scratch_shapes=[pltpu.VMEM(a.shape, f32) for a in own]
        + [pltpu.VMEM((2 * a.shape[0], a.shape[1] // 2), f32) for a in own]
        + [pltpu.VMEM((2 * a.shape[0], a.shape[1] // 2), bf16) for a in own]
        + [pltpu.SemaphoreType.DMA((copies,)), pltpu.SemaphoreType.DMA((copies,))],
        compiler_params=pltpu.CompilerParams(
            collective_id=0, has_side_effects=True, vmem_limit_bytes=VMEM_BYTES
        ),
        name="gather_weights",
    )(*own, made)


def scatter_kernel(count, makers, *refs):
    grads, maker_refs = refs[:count], refs[count : count + makers]
    outs, state_out = refs[count + makers : 2 * count + makers], refs[2 * count + makers]
    scratch = refs[2 * count + makers + 1 :]
    held, from_core, from_a, from_b, from_c, from_d, from_z, final = (
        scratch[k * count : (k + 1) * count] for k in range(8)
    )
    totals, arriving, send, recv = scratch[8 * count :]
    here = Place()
    copies = Copies(send, recv)
    z, y, x, c = here.z, here.y, here.x, here.core
    local, core, one, two, three, last = {}, {}, {}, {}, {}, {}

    def half(i, which):
        width = grads[i].shape[-1] // 2
        return pl.ds(pl.multiple_of(which * width, 128), width)

    for i in range(count):
        local[i] = copies.local(grads[i].at[:, :, :, :, half(i, c)], held[i])
    meet(here)
    for i in range(count):
        core[i] = copies.remote(
            grads[i].at[:, :, :, :, half(i, 1 - c)], from_core[i], here.sibling()
        )

    def cuts(i):
        return shares(grads[i].shape[3], i)

    def over_first(i):
        local[i].wait()
        core[i].wait_recv()
        held[i][...] += from_core[i][...]
        first, second = cuts(i)
        one[i] = (
            copies.remote(held[i].at[:, 1 - y, :, first, :], from_a[i], here.over_y()),
            copies.remote(held[i].at[:, :, 1 - x, second, :], from_b[i], here.over_x()),
        )

    def over_second(i):
        first, second = cuts(i)
        one[i][0].wait_recv()
        held[i][:, y, :, first, :] += from_a[i][...]
        one[i][1].wait_recv()
        held[i][:, :, x, second, :] += from_b[i][...]
        two[i] = (
            copies.remote(held[i].at[:, y, 1 - x, first, :], from_c[i], here.over_x()),
            copies.remote(held[i].at[:, 1 - y, x, second, :], from_d[i], here.over_y()),
        )

    def over_line(i):
        first, second = cuts(i)
        two[i][0].wait_recv()
        held[i][:, y, x, first, :] += from_c[i][...]
        two[i][1].wait_recv()
        held[i][:, y, x, second, :] += from_d[i][...]
        three[i] = [
            copies.remote(
                held[i].at[lax.rem(z + k, LINE), y, x], from_z[i].at[k - 1], here.along_z(k)
            )
            for k in (1, 2, 3)
        ]

    def to_owner(i):
        total = held[i][z, y, x].astype(f32)
        for k, copy in enumerate(three[i]):
            copy.wait_recv()
            total = total + from_z[i][k].astype(f32)
        final[i][...] = total
        rows = outs[i].shape[0]
        theirs = pl.ds(pl.multiple_of((1 - c) * rows, 8), rows)
        last[i] = copies.remote(
            final[i].at[theirs, :], outs[i].at[:, half(i, c)], here.sibling()
        )
        outs[i][:, half(i, c)] = final[i][pl.ds(pl.multiple_of(c * rows, 8), rows), :]

    stepped(count, (over_first, over_second, over_line, to_owner))
    last[count - 1].wait_recv()
    down, up, gain = maker_refs
    small = outs[count - 1]
    made = down.shape[0]
    gains = gain.shape[0]
    state = plain_dot(small[0:8, :made].astype(bf16), down[...])
    state = state + plain_dot(small[8:16, :made].astype(bf16), up[...])
    state = state + exact_dot(small[0:8, made : made + gains], gain[...].astype(f32))
    for turn, device in enumerate((here.sibling(), here.over_x(), here.over_y())):
        totals[turn] = state
        copy = copies.remote(totals.at[turn], arriving.at[turn], device)
        copy.wait_recv()
        state = state + arriving[turn]
    totals[3] = state
    around = [copies.remote(totals.at[3], arriving.at[2 + k], here.along_z(k)) for k in (1, 2, 3)]
    terms = {}
    for k, copy in enumerate(around):
        copy.wait_recv()
    total = jnp.zeros_like(state)
    for line in range(LINE):
        for k in range(LINE):
            term = state if k == 0 else arriving[2 + k]
            total = total + jnp.where(lax.rem(z - k + LINE, LINE) == line, term, 0.0)
    state_out[...] = total
    for i in range(count - 1):
        last[i].wait_recv()
    copies.finish()


def scatter(grads, makers):
    count = len(grads)
    copies = 12 * count + 8
    any_space = pl.BlockSpec(memory_space=pl.ANY)
    vmem = pl.BlockSpec(memory_space=pltpu.VMEM)

    def slots(shape_of):
        return [pltpu.VMEM(shape_of(g, i), bf16) for i, g in enumerate(grads)]

    def rows_of(g, i, which):
        cut = shares(g.shape[3], i)[which]
        return cut.stop - cut.start

    scratch = slots(lambda g, i: g.shape[:4] + (g.shape[4] // 2,)) * 1
    scratch += slots(lambda g, i: g.shape[:4] + (g.shape[4] // 2,))
    scratch += slots(lambda g, i: (LINE, 2, rows_of(g, i, 0), g.shape[4] // 2))
    scratch += slots(lambda g, i: (LINE, 2, rows_of(g, i, 1), g.shape[4] // 2))
    scratch += slots(lambda g, i: (LINE, rows_of(g, i, 0), g.shape[4] // 2))
    scratch += slots(lambda g, i: (LINE, rows_of(g, i, 1), g.shape[4] // 2))
    scratch += slots(lambda g, i: (LINE - 1, g.shape[3], g.shape[4] // 2))
    scratch += [pltpu.VMEM((g.shape[3], g.shape[4] // 2), f32) for g in grads]
    tasks, hidden = 8, makers[0].shape[1]
    scratch += [pltpu.VMEM((4, tasks, hidden), f32), pltpu.VMEM((6, tasks, hidden), f32)]
    scratch += [pltpu.SemaphoreType.DMA((copies,)), pltpu.SemaphoreType.DMA((copies,))]
    return pl.pallas_call(
        functools.partial(scatter_kernel, count, len(makers)),
        in_specs=[any_space] * count + [vmem] * len(makers),
        out_specs=[vmem] * (count + 1),
        out_shape=[jax.ShapeDtypeStruct((g.shape[3] // 2, g.shape[4]), f32) for g in grads]
        + [jax.ShapeDtypeStruct((tasks, hidden), f32)],
        scratch_shapes=scratch,
        compiler_params=pltpu.CompilerParams(
            collective_id=1, has_side_effects=True, vmem_limit_bytes=60 << 20
        ),
        name="scatter_gradients",
    )(*grads, *makers)


def on_device(
    block_input, memory, cotangent, segments, memory_segments, task_of_segment,
    self_query, self_key, self_value, self_output,
    cross_query, cross_key, cross_value, cross_output,
    hidden_in, hidden_out, task_table, task_weight, task_bias,
    down_maker, up_maker, gain_maker,
):
    row_count, seq_len, model_width = block_input.shape
    mem_len = memory.shape[1]
    task_count = task_table.shape[0]
    token_count = row_count * seq_len
    parts = lax.axis_size("dp")
    weights = (
        self_query, self_key, self_value, self_output,
        cross_query, cross_key, cross_value, cross_output, hidden_in, hidden_out,
    )
    task_state, task_back = jax.vjp(task_network, task_table, task_weight, task_bias)
    task_low = task_state.astype(bf16)
    made = inner_rows(task_low, jnp.concatenate((down_maker, up_maker, gain_maker), axis=0))
    down_own, gain_own = down_maker.shape[0], gain_maker.shape[0]
    if parts == 32:
        made = jnp.pad(made, ((0, 0), (0, -made.shape[1] % 256)))
        *backbone, made = gather(weights, made)
        backbone = [w.reshape(-1, w.shape[-1]) for w in backbone]
        made = made.reshape((parts,) + made.shape[4:])
    else:
        backbone = [lax.all_gather(w, "dp", axis=0, tiled=True) for w in weights]
        made = lax.all_gather(made, "dp", axis=0, tiled=False)

    def joined(block):
        return block.transpose(1, 0, 2).reshape(task_count, -1)

    made_down = joined(made[:, :, :down_own]).astype(bf16)
    made_up = joined(made[:, :, down_own : 2 * down_own]).astype(bf16)
    gain_table = 1.0 + joined(made[:, :, 2 * down_own : 2 * down_own + gain_own])
    down_all = (
        made_down.reshape(task_count, model_width, ADA)
        .transpose(1, 0, 2)
        .reshape(model_width, task_count * ADA)
    )
    up_all = made_up.reshape(task_count * ADA, model_width)
    seg_match = (
        segments[:, :, None] == jnp.arange(task_of_segment.shape[1], dtype=jnp.int32)[None, None, :]
    )
    token_task = jnp.sum(jnp.where(seg_match, task_of_segment[:, None, :], 0), axis=-1).reshape(
        token_count, 1
    )
    output, input_grad, mem_grad, grads, up_all_grad, down_all_grad, gain_grad = layer(
        block_input.reshape(token_count, model_width),
        memory.reshape(row_count * mem_len, model_width),
        cotangent.reshape(token_count, model_width),
        segments, memory_segments, token_task, backbone, gain_table, down_all, up_all,
    )
    down_rows = (
        down_all_grad.reshape(parts, -1, task_count, ADA)
        .transpose(0, 2, 1, 3)
        .reshape(parts, task_count, down_own)
    )
    up_rows = up_all_grad.reshape(task_count, parts, -1).transpose(1, 0, 2)
    gain_rows_all = gain_grad.reshape(task_count, parts, -1).transpose(1, 0, 2)
    if parts == 32:
        small = jnp.concatenate((down_rows, gain_rows_all), axis=2)
        wide = small.shape[2] + (-small.shape[2] % 256)
        small = jnp.concatenate(
            (
                jnp.pad(small, ((0, 0), (0, 0), (0, wide - small.shape[2]))),
                jnp.pad(up_rows, ((0, 0), (0, 0), (0, wide - up_rows.shape[2]))),
            ),
            axis=1,
        ).astype(bf16)
        units = [
            g.reshape((LINE, 2, 2, 2 * w.shape[0], w.shape[1])) for g, w in zip(grads, weights)
        ]
        units.append(small.reshape(LINE, 2, 2, 4 * task_count, wide))
        *shared, small, state_grad = scatter(units, (down_maker, up_maker, gain_maker))
        own_down = small[:task_count, :down_own].astype(bf16)
        own_up = small[task_count:, :down_own].astype(bf16)
        own_gain = small[:task_count, down_own : down_own + gain_own]
    else:
        shared = [
            lax.psum_scatter(g, "dp", scatter_dimension=0, tiled=True).astype(f32) for g in grads
        ]
        small = jnp.concatenate((down_rows, up_rows, gain_rows_all), axis=2)
        small = lax.psum_scatter(small, "dp", scatter_dimension=0, tiled=False)
        own_down = small[:, :down_own].astype(bf16)
        own_up = small[:, down_own : 2 * down_own].astype(bf16)
        own_gain = small[:, 2 * down_own :]
        state_grad = lax.psum(
            plain_dot(own_down, down_maker)
            + plain_dot(own_up, up_maker)
            + exact_dot(own_gain, gain_maker.astype(f32)),
            "dp",
        )
    down_maker_grad = inner_cols(own_down, task_low)
    up_maker_grad = inner_cols(own_up, task_low)
    gain_maker_grad = inner_cols(own_gain, task_low.astype(f32), exact_mode)
    table_grad, weight_grad, bias_grad = task_back(state_grad)
    return (
        output.reshape(row_count, seq_len, model_width),
        input_grad.reshape(row_count, seq_len, model_width),
        mem_grad.reshape(row_count, mem_len, model_width),
        *shared,
        table_grad,
        weight_grad,
        bias_grad,
        down_maker_grad,
        up_maker_grad,
        gain_maker_grad,
    )


def solution(mesh):
    rows, whole_copy = P("dp"), P()
    return jax.shard_map(
        on_device,
        mesh=mesh,
        in_specs=(rows,) * 16 + (whole_copy,) * 3 + (rows,) * 3,
        out_specs=(rows,) * 13 + (whole_copy,) * 3 + (rows,) * 3,
        check_vma=False,
    )
```

```python
import functools

import jax
import jax.numpy as jnp
from jax import lax
from jax.experimental import pallas as pl
from jax.experimental.pallas import tpu as pltpu
from jax.sharding import PartitionSpec as P

HEADS = 12
HEAD = 64
ADA = 24
PAIR = 2 * HEAD

exact_mode = lax.Precision.HIGHEST
norm_eps = 1e-06
masked_score = -1e30
bf16 = jnp.bfloat16
f32 = jnp.float32
VMEM_BYTES = 56 << 20


def plain_dot(left_side, right_side):
    return jnp.dot(left_side, right_side, preferred_element_type=f32)


def exact_dot(left_side, right_side):
    return jnp.dot(left_side, right_side, precision=exact_mode, preferred_element_type=f32)


def inner_rows(left_side, right_side):
    return lax.dot_general(
        left_side, right_side, (((1,), (1,)), ((), ())), preferred_element_type=f32
    )


def inner_cols(left_side, right_side, precision_mode=None):
    return lax.dot_general(
        left_side,
        right_side,
        (((0,), (0,)), ((), ())),
        precision=precision_mode,
        preferred_element_type=f32,
    )


def gelu_exact(operand):
    return jax.nn.gelu(operand, approximate=False)


def task_network(table_rows, weight_in, bias_row):
    return gelu_exact(exact_dot(table_rows, weight_in) + bias_row)


def gelu_both(v):
    phi = 0.5 * lax.erf(v * 0.7071067811865476) + 0.5
    slope = phi + v * (jnp.exp(v * v * -0.5) * 0.3989422804014327)
    return v * phi, slope


def token_gain(task_column, gain):
    high = gain.astype(bf16).astype(f32)
    rest = gain - high
    middle = rest.astype(bf16).astype(f32)
    table = jnp.concatenate((high, middle, rest - middle), axis=0).astype(bf16)
    which = lax.broadcasted_iota(jnp.int32, (task_column.shape[0], 24), 1) & 7
    hot = jnp.where(which == task_column, 1.0, 0.0).astype(bf16)
    return plain_dot(hot, table)


def gain_rows(task_column, grads):
    which = lax.broadcasted_iota(jnp.int32, (task_column.shape[0], 8), 1)
    hot = jnp.where(which == task_column, 1.0, 0.0).astype(bf16)
    high = grads.astype(bf16)
    low = (grads - high.astype(f32)).astype(bf16)
    return inner_cols(hot, high) + inner_cols(hot, low)


def inverse_rms(stream):
    return lax.rsqrt(jnp.mean(stream * stream, axis=-1, keepdims=True) + norm_eps)


def norm_back(stream, gain, cotan):
    r = inverse_rms(stream)
    scaled = cotan * gain
    inner = jnp.mean(scaled * stream, axis=-1, keepdims=True)
    return r * (scaled - stream * (r * r * inner)), cotan * (stream * r)


def call(kernel, grid, ins, outs, scratch=(), flops=0, name=None):
    size = sum(a.size * a.dtype.itemsize for a, _, _ in ins)
    size += sum(functools.reduce(lambda p, q: p * q, s, 1) * jnp.dtype(d).itemsize for s, d, _, _ in outs)
    return pl.pallas_call(
        kernel,
        grid=grid,
        in_specs=[pl.BlockSpec(b, m) for _, b, m in ins],
        out_specs=[pl.BlockSpec(b, m) for _, _, b, m in outs],
        out_shape=[jax.ShapeDtypeStruct(s, d) for s, d, _, _ in outs],
        scratch_shapes=list(scratch),
        compiler_params=pltpu.CompilerParams(vmem_limit_bytes=VMEM_BYTES),
        cost_estimate=pl.CostEstimate(flops=flops, bytes_accessed=size, transcendentals=0),
        name=name,
    )(*[a for a, _, _ in ins])


def whole(array):
    return (array, array.shape, lambda *_: (0,) * array.ndim)


def by_row(array, rows):
    return (array, (rows,) + array.shape[1:], lambda i: (i,) + (0,) * (array.ndim - 1))


def out_row(shape, dtype, rows):
    return (shape, dtype, (rows,) + shape[1:], lambda i: (i,) + (0,) * (len(shape) - 1))


def out_whole(shape, dtype):
    return (shape, dtype, shape, lambda *_: (0,) * len(shape))


def pre_kernel(x, task, gain, wq, wk, wv, normed, q, k, v):
    stream = x[...].astype(f32)
    n = (stream * inverse_rms(stream) * token_gain(task[...], gain[...])).astype(bf16)
    normed[...] = n
    q[...] = (plain_dot(n, wq[...]).astype(bf16).astype(f32) * HEAD**-0.5).astype(bf16)
    k[...] = plain_dot(n, wk[...]).astype(bf16)
    v[...] = plain_dot(n, wv[...]).astype(bf16)


def memory_kernel(x, wk, wv, k, v):
    k[...] = plain_dot(x[...], wk[...]).astype(bf16)
    v[...] = plain_dot(x[...], wv[...]).astype(bf16)


def middle_kernel(x, mixed, wo, task, gain, wq, stream_out, normed, q):
    stream = x[...].astype(f32) + plain_dot(mixed[...], wo[...])
    stream_out[...] = stream
    n = (stream * inverse_rms(stream) * token_gain(task[...], gain[...])).astype(bf16)
    normed[...] = n
    q[...] = (plain_dot(n, wq[...]).astype(bf16).astype(f32) * HEAD**-0.5).astype(bf16)


def half_masks():
    lane = lax.broadcasted_iota(jnp.int32, (1, PAIR), 1)
    first = jnp.where(lane < HEAD, 1.0, 0.0)
    return first.astype(bf16), (1.0 - first).astype(bf16)


def attend_forward_kernel(causal, q_ref, k_ref, v_ref, seg_q, seg_k, mixed_ref, p_ref, bias):
    length, keys_all = q_ref.shape[0], k_ref.shape[0]
    step = length // 2 if causal else length

    @pl.when(pl.program_id(1) == 0)
    def _():
        same = seg_q[...] == seg_k[0]
        if causal:
            at_q = lax.broadcasted_iota(jnp.int32, (length, keys_all), 0)
            at_k = lax.broadcasted_iota(jnp.int32, (length, keys_all), 1)
            same = same & (at_q >= at_k)
        bias[...] = jnp.where(same, 0.0, masked_score)

    masks = half_masks()
    for first in range(0, length, step):
        rows = pl.ds(first, step)
        keys = first + step if causal else keys_all
        q = q_ref[rows, :]
        k = k_ref[:keys, :]
        v = v_ref[:keys, :]
        out = None
        for h, mask in enumerate(masks):
            s = inner_rows(q * mask, k) + bias[rows, :keys]
            e = jnp.exp(s - jnp.max(s, axis=-1, keepdims=True))
            p = (e * (1.0 / jnp.sum(e, axis=-1, keepdims=True))).astype(bf16)
            p_ref[0, h, rows, :keys] = p
            part = plain_dot(p, v * mask)
            out = part if out is None else out + part
        mixed_ref[rows, :] = out.astype(bf16)


def attend_backward_kernel(
    causal, q_ref, k_ref, v_ref, mixed_ref, gm_ref, p_ref, gq_ref, gk_ref, gv_ref
):
    length, keys_all = q_ref.shape[0], k_ref.shape[0]
    step = length // 2 if causal else length
    masks = half_masks()
    gk_parts, gv_parts = [], []
    for first in range(0, length, step):
        rows = pl.ds(first, step)
        keys = first + step if causal else keys_all
        q = q_ref[rows, :]
        k = k_ref[:keys, :]
        v = v_ref[:keys, :]
        gm = gm_ref[rows, :]
        product = gm.astype(f32) * mixed_ref[rows, :].astype(f32)
        gq = gk = gv = 0.0
        for h, mask in enumerate(masks):
            inner = jnp.sum(product * mask.astype(f32), axis=-1, keepdims=True)
            p = p_ref[0, h, rows, :keys]
            gm_half = gm * mask
            gw = inner_rows(gm_half, v)
            gs = (p.astype(f32) * (gw - inner)).astype(bf16)
            gv = gv + inner_cols(p, gm_half)
            gq = gq + plain_dot(gs, k * mask)
            gk = gk + inner_cols(gs, q * mask)
        gq_ref[rows, :] = (gq * HEAD**-0.5).astype(bf16)
        gk_parts.append(gk)
        gv_parts.append(gv)
    for ref, terms in ((gk_ref, gk_parts), (gv_ref, gv_parts)):
        if not causal:
            ref[...] = terms[0].astype(bf16)
        else:
            ref[:step, :] = (terms[0] + terms[1][:step]).astype(bf16)
            ref[step:, :] = terms[1][step:].astype(bf16)


def attention_specs(rows, length, arrays):
    return [(a, (length, PAIR), lambda r, p: (r, p)) for a in arrays]


def attend_forward(causal, rows, length, q, k, v, seg_q, seg_k):
    mem_len = k.shape[0] // rows
    mixed, probs = call(
        functools.partial(attend_forward_kernel, causal),
        (rows, HEADS // 2),
        attention_specs(rows, length, (q,))
        + attention_specs(rows, mem_len, (k, v))
        + [
            (seg_q.reshape(rows * length, 1), (length, 1), lambda r, p: (r, 0)),
            (seg_k.reshape(rows, 1, mem_len), (1, 1, mem_len), lambda r, p: (r, 0, 0)),
        ],
        [
            (q.shape, bf16, (length, PAIR), lambda r, p: (r, p)),
            (
                (rows, HEADS, length, mem_len),
                bf16,
                (1, 2, length, mem_len),
                lambda r, p: (r, p, 0, 0),
            ),
        ],
        scratch=[pltpu.VMEM((length, mem_len), f32)],
        flops=4 * rows * HEADS * length * mem_len * PAIR,
        name="attend_forward",
    )
    return mixed, probs


def attend_backward(causal, rows, length, q, k, v, mixed, grad_mixed, probs):
    mem_len = k.shape[0] // rows
    return call(
        functools.partial(attend_backward_kernel, causal),
        (rows, HEADS // 2),
        attention_specs(rows, length, (q,))
        + attention_specs(rows, mem_len, (k, v))
        + attention_specs(rows, length, (mixed, grad_mixed))
        + [(probs, (1, 2, length, mem_len), lambda r, p: (r, p, 0, 0))],
        [
            (q.shape, bf16, (length, PAIR), lambda r, p: (r, p)),
            (k.shape, bf16, (mem_len, PAIR), lambda r, p: (r, p)),
            (k.shape, bf16, (mem_len, PAIR), lambda r, p: (r, p)),
        ],
        flops=8 * rows * HEADS * length * mem_len * PAIR,
        name="attend_backward",
    )


CHUNK = 768


def feed_kernel(
    s1, mixed, wo, task, gain, w_in, w_out, down_all, up_all, cot,
    output, n3, act, gu, gfeed, g2, g2_low, gmix, up_grad, down_grad, gain_grad,
    slope, total,
):
    first = pl.program_id(0) == 0
    units = w_in.shape[1]
    stream = s1[...] + plain_dot(mixed[...], wo[...])
    picked = token_gain(task[...], gain[...])
    n3[...] = (stream * inverse_rms(stream) * picked).astype(bf16)
    total[...] = jnp.zeros_like(total)

    @pl.loop(0, units // CHUNK)
    def _(j):
        cols = pl.ds(pl.multiple_of(j * CHUNK, CHUNK), CHUNK)
        value, rate = gelu_both(plain_dot(n3[...], w_in[:, cols]))
        value = value.astype(bf16)
        act[:, cols] = value
        slope[:, cols] = rate.astype(bf16)
        total[...] += plain_dot(value, w_out[cols, :])

    feed = total[...]
    feed_low = feed.astype(bf16)
    tokens, wide = stream.shape[0], down_all.shape[1]
    owner = lax.broadcasted_iota(jnp.int32, (tokens, wide), 1) - task[...] * ADA
    mask = jnp.where((owner >= 0) & (owner < ADA), 1.0, 0.0)
    narrow, narrow_slope = gelu_both(plain_dot(feed_low, down_all[...]) * mask)
    narrow = narrow.astype(bf16)
    output[...] = (stream + feed + plain_dot(narrow, up_all[...])).astype(bf16)
    cotan = cot[...]
    gb = (narrow_slope * inner_rows(cotan, up_all[...]) * mask).astype(bf16)
    grad_feed = (cotan.astype(f32) + inner_rows(gb, down_all[...])).astype(bf16)
    gfeed[...] = grad_feed
    up_now = inner_cols(narrow, cotan)
    down_now = inner_cols(feed_low, gb)
    total[...] = jnp.zeros_like(total)

    @pl.loop(0, units // CHUNK)
    def _(j):
        cols = pl.ds(pl.multiple_of(j * CHUNK, CHUNK), CHUNK)
        grad = slope[:, cols].astype(f32) * inner_rows(gfeed[...], w_out[cols, :])
        grad = grad.astype(bf16)
        gu[:, cols] = grad
        total[...] += inner_rows(grad, w_in[:, cols])

    stream_grad, gain_tokens = norm_back(stream, picked, total[...])
    grad_two = cotan.astype(f32) + stream_grad
    g2[...] = grad_two
    low = grad_two.astype(bf16)
    g2_low[...] = low
    gmix[...] = inner_rows(low, wo[...]).astype(bf16)
    gain_now = gain_rows(task[...], gain_tokens)

    @pl.when(first)
    def _():
        up_grad[...] = up_now
        down_grad[...] = down_now
        gain_grad[...] = gain_now

    @pl.when(jnp.logical_not(first))
    def _():
        up_grad[...] += up_now
        down_grad[...] += down_now
        gain_grad[...] += gain_now


def cross_back_kernel(gq, wq, s1, task, gain, g2, wo, g1, g1_low, gmix, gain_grad):
    stream = s1[...]
    picked = token_gain(task[...], gain[...])
    stream_grad, gain_tokens = norm_back(stream, picked, inner_rows(gq[...], wq[...]))
    grad_one = g2[...] + stream_grad
    g1[...] = grad_one
    low = grad_one.astype(bf16)
    g1_low[...] = low
    gmix[...] = inner_rows(low, wo[...]).astype(bf16)
    accumulate(gain_grad, gain_rows(task[...], gain_tokens))


def accumulate(ref, value):
    @pl.when(pl.program_id(0) == 0)
    def _():
        ref[...] = value

    @pl.when(pl.program_id(0) != 0)
    def _():
        ref[...] += value


def memory_back_kernel(gk, gv, wk, wv, out):
    out[...] = inner_rows(gk[...], wk[...]) + inner_rows(gv[...], wv[...])


def input_back_kernel(gq, gk, gv, wq, wk, wv, x, task, gain, g1, out, gain_grad):
    stream = x[...].astype(f32)
    picked = token_gain(task[...], gain[...])
    cotan = inner_rows(gq[...], wq[...]) + inner_rows(gk[...], wk[...])
    cotan = cotan + inner_rows(gv[...], wv[...])
    stream_grad, gain_tokens = norm_back(stream, picked, cotan)
    out[...] = g1[...] + stream_grad
    accumulate(gain_grad, gain_rows(task[...], gain_tokens))


def outer_kernel(which, sources, *refs):
    left = refs[:sources]
    right = refs[sources : sources + len(which)]
    outs = refs[sources + len(which) :]
    for source, grad, out in zip(which, right, outs):
        for first in range(0, out.shape[1], CHUNK):
            cols = slice(first, first + CHUNK)
            out[:, cols] = inner_cols(left[source][...], grad[:, cols]).astype(bf16)


def outers(sources, grads, which, name):
    tokens, width = sources[0].shape
    block = 256
    return call(
        functools.partial(outer_kernel, which, len(sources)),
        (width // block,),
        [(s, (tokens, block), lambda i: (0, i)) for s in sources] + [whole(g) for g in grads],
        [((width, g.shape[1]), bf16, (block, g.shape[1]), lambda i: (i, 0)) for g in grads],
        flops=sum(2 * tokens * width * g.shape[1] for g in grads),
        name=name,
    )


BLOCK = 512


def low_out(shape):
    return out_row(shape, bf16, BLOCK)


def full_out(shape):
    return out_row(shape, f32, BLOCK)


def attention_layers(x, mem, segments, mem_segments, task, weights, gain_table):
    rows, length = segments.shape
    tokens, width = x.shape
    wq1, wk1, wv1, wo1, wq2, wk2, wv2 = weights[:7]
    gain_one, gain_two = (gain_table[:, i * width : (i + 1) * width] for i in range(2))
    block = BLOCK
    grid = (tokens // block,)
    act_shape = (tokens, width)
    square = 2 * tokens * width * width
    n1, q1, k1, v1 = call(
        pre_kernel,
        grid,
        [by_row(x, block), by_row(task, block)] + [whole(a) for a in (gain_one, wq1, wk1, wv1)],
        [low_out(act_shape) for _ in range(4)],
        flops=3 * square,
        name="self_projections",
    )
    m1, p1 = attend_forward(True, rows, length, q1, k1, v1, segments, segments)
    s1, n2, q2 = call(
        middle_kernel,
        grid,
        [by_row(x, block), by_row(m1, block), whole(wo1), by_row(task, block), whole(gain_two), whole(wq2)],
        [full_out(act_shape), low_out(act_shape), low_out(act_shape)],
        flops=2 * square,
        name="middle",
    )
    k2, v2 = call(
        memory_kernel,
        grid,
        [by_row(mem, block), whole(wk2), whole(wv2)],
        [low_out(mem.shape), low_out(mem.shape)],
        flops=2 * square,
        name="memory_projections",
    )
    m2, p2 = attend_forward(False, rows, length, q2, k2, v2, segments, mem_segments)
    return (n1, q1, k1, v1, m1, s1, n2, q2, k2, v2, m2), p1, p2


def feed_and_back(x, mem, cot, rows, task, weights, gain_table, down_all, up_all, saved, p1, p2):
    n1, q1, k1, v1, m1, s1, n2, q2, k2, v2, m2 = saved
    tokens, width = x.shape
    length = tokens // rows
    wq1, wk1, wv1, wo1, wq2, wk2, wv2, wo2, w_in, w_out = weights
    gain_one, gain_two, gain_three = (gain_table[:, i * width : (i + 1) * width] for i in range(3))
    block = BLOCK
    grid = (tokens // block,)
    act_shape = (tokens, width)
    square = 2 * tokens * width * width
    units = w_in.shape[1]
    wide = up_all.shape[0]
    tasks = gain_table.shape[0]
    output, n3, act, gu, gfeed, g2, g2_low, gmix2, up_grad, down_grad, gain3 = call(
        feed_kernel,
        grid,
        [
            by_row(s1, block), by_row(m2, block), whole(wo2), by_row(task, block), whole(gain_three),
            whole(w_in), whole(w_out), whole(down_all), whole(up_all), by_row(cot, block),
        ],
        [
            low_out(act_shape), low_out(act_shape), out_row((tokens, units), bf16, block), out_row((tokens, units), bf16, block),
            low_out(act_shape), full_out(act_shape), low_out(act_shape), low_out(act_shape),
            out_whole((wide, width), f32), out_whole((width, wide), f32), out_whole((tasks, width), f32),
        ],
        scratch=[pltpu.VMEM((block, units), bf16), pltpu.VMEM((block, width), f32)],
        flops=2 * square + 8 * tokens * width * units,
        name="feed_forward_and_back",
    )
    (hidden_in_grad,) = outers((n3,), (gu,), (0,), "hidden_in_grad")
    (hidden_out_grad,) = outers((act,), (gfeed,), (0,), "hidden_out_grad")
    gq2, gk2, gv2 = attend_backward(False, rows, length, q2, k2, v2, m2, gmix2, p2)
    g1, g1_low, gmix1, gain2 = call(
        cross_back_kernel,
        grid,
        [
            by_row(gq2, block), whole(wq2), by_row(s1, block), by_row(task, block), whole(gain_two),
            by_row(g2, block), whole(wo1),
        ],
        [full_out(act_shape), low_out(act_shape), low_out(act_shape), out_whole((tasks, width), f32)],
        flops=2 * square,
        name="cross_back",
    )
    (mem_grad,) = call(
        memory_back_kernel,
        grid,
        [by_row(gk2, block), by_row(gv2, block), whole(wk2), whole(wv2)],
        [full_out(act_shape)],
        flops=2 * square,
        name="memory_back",
    )
    wo2_grad, wq2_grad, wk2_grad, wv2_grad = outers(
        (m2, n2, mem), (g2_low, gq2, gk2, gv2), (0, 1, 2, 2), "cross_grads"
    )
    gq1, gk1, gv1 = attend_backward(True, rows, length, q1, k1, v1, m1, gmix1, p1)
    input_grad, gain1 = call(
        input_back_kernel,
        grid,
        [
            by_row(gq1, block), by_row(gk1, block), by_row(gv1, block), whole(wq1), whole(wk1), whole(wv1),
            by_row(x, block), by_row(task, block), whole(gain_one), by_row(g1, block),
        ],
        [full_out(act_shape), out_whole((tasks, width), f32)],
        flops=3 * square,
        name="input_back",
    )
    wo1_grad, wq1_grad, wk1_grad, wv1_grad = outers(
        (m1, n1), (g1_low, gq1, gk1, gv1), (0, 1, 1, 1), "self_grads"
    )
    gain_grad = jnp.concatenate((gain1, gain2, gain3), axis=1)
    grads = (
        wq1_grad, wk1_grad, wv1_grad, wo1_grad, wq2_grad, wk2_grad, wv2_grad, wo2_grad,
        hidden_in_grad, hidden_out_grad,
    )
    return output, input_grad, mem_grad, grads, up_grad, down_grad, gain_grad


LINE = 4
MESH = pl.DeviceIdType.MESH


class Place:
    def __init__(self):
        me = lax.axis_index("dp")
        self.core = lax.rem(me, 2)
        self.x = lax.rem(me // 2, 2)
        self.y = lax.rem(me // 4, 2)
        self.z = me // 8

    def at(self, z=None, y=None, x=None, core=None):
        z = self.z if z is None else z
        y = self.y if y is None else y
        x = self.x if x is None else x
        core = self.core if core is None else core
        return (((z * 2 + y) * 2 + x) * 2 + core,)

    def sibling(self):
        return self.at(core=1 - self.core)

    def over_x(self):
        return self.at(x=1 - self.x)

    def over_y(self):
        return self.at(y=1 - self.y)

    def along_z(self, k):
        return self.at(z=lax.rem(self.z + k, LINE))

    def partners(self):
        return [self.sibling(), self.over_x(), self.over_y()] + [self.along_z(k) for k in (1, 2, 3)]


def meet(place):
    barrier = pltpu.get_barrier_semaphore()
    partners = place.partners()
    for partner in partners:
        pl.semaphore_signal(barrier, inc=1, device_id=partner, device_id_type=MESH)
    pl.semaphore_wait(barrier, len(partners))


class Copies:
    def __init__(self, send, recv):
        self.send, self.recv, self.used, self.open = send, recv, 0, []

    def remote(self, source, target, device):
        copy = pltpu.make_async_remote_copy(
            src_ref=source,
            dst_ref=target,
            send_sem=self.send.at[self.used],
            recv_sem=self.recv.at[self.used],
            device_id=device,
            device_id_type=MESH,
        )
        self.used += 1
        copy.start()
        self.open.append(copy)
        return copy

    def local(self, source, target):
        copy = pltpu.make_async_copy(source, target, self.recv.at[self.used])
        self.used += 1
        copy.start()
        return copy

    def finish(self):
        for copy in self.open:
            copy.wait_send()


def shares(rows, turn):
    cut = rows // 2 if rows % 32 == 0 else (rows // 32 + turn % 2) * 16
    return slice(0, cut), slice(cut, rows)


def stepped(count, stages):
    for turn in range(count + len(stages) - 1):
        for late, stage in enumerate(stages):
            if 0 <= turn - late < count:
                stage(turn - late)


def scatter_kernel(count, makers, *refs):
    grads, maker_refs = refs[:count], refs[count : count + makers]
    outs, state_out = refs[count + makers : 2 * count + makers], refs[2 * count + makers]
    scratch = refs[2 * count + makers + 1 :]
    held, from_core, from_a, from_b, from_c, from_d, from_z, final = (
        scratch[k * count : (k + 1) * count] for k in range(8)
    )
    totals, arriving, send, recv = scratch[8 * count :]
    here = Place()
    copies = Copies(send, recv)
    z, y, x, c = here.z, here.y, here.x, here.core
    local, core, one, two, three, last = {}, {}, {}, {}, {}, {}

    def half(i, which):
        width = grads[i].shape[-1] // 2
        return pl.ds(pl.multiple_of(which * width, 128), width)

    for i in range(count):
        local[i] = copies.local(grads[i].at[:, :, :, :, half(i, c)], held[i])
    meet(here)
    for i in range(count):
        core[i] = copies.remote(
            grads[i].at[:, :, :, :, half(i, 1 - c)], from_core[i], here.sibling()
        )

    def cuts(i):
        return shares(grads[i].shape[3], i)

    def over_first(i):
        local[i].wait()
        core[i].wait_recv()
        held[i][...] += from_core[i][...]
        first, second = cuts(i)
        one[i] = (
            copies.remote(held[i].at[:, 1 - y, :, first, :], from_a[i], here.over_y()),
            copies.remote(held[i].at[:, :, 1 - x, second, :], from_b[i], here.over_x()),
        )

    def over_second(i):
        first, second = cuts(i)
        one[i][0].wait_recv()
        held[i][:, y, :, first, :] += from_a[i][...]
        one[i][1].wait_recv()
        held[i][:, :, x, second, :] += from_b[i][...]
        two[i] = (
            copies.remote(held[i].at[:, y, 1 - x, first, :], from_c[i], here.over_x()),
            copies.remote(held[i].at[:, 1 - y, x, second, :], from_d[i], here.over_y()),
        )

    def over_line(i):
        first, second = cuts(i)
        two[i][0].wait_recv()
        held[i][:, y, x, first, :] += from_c[i][...]
        two[i][1].wait_recv()
        held[i][:, y, x, second, :] += from_d[i][...]
        three[i] = [
            copies.remote(
                held[i].at[lax.rem(z + k, LINE), y, x], from_z[i].at[k - 1], here.along_z(k)
            )
            for k in (1, 2, 3)
        ]

    def to_owner(i):
        total = held[i][z, y, x].astype(f32)
        for k, copy in enumerate(three[i]):
            copy.wait_recv()
            total = total + from_z[i][k].astype(f32)
        final[i][...] = total
        rows = outs[i].shape[0]
        theirs = pl.ds(pl.multiple_of((1 - c) * rows, 8), rows)
        last[i] = copies.remote(
            final[i].at[theirs, :], outs[i].at[:, half(i, c)], here.sibling()
        )
        outs[i][:, half(i, c)] = final[i][pl.ds(pl.multiple_of(c * rows, 8), rows), :]

    stepped(count, (over_first, over_second, over_line, to_owner))
    last[count - 1].wait_recv()
    down, up, gain = maker_refs
    small = outs[count - 1]
    made = down.shape[0]
    gains = gain.shape[0]
    state = plain_dot(small[0:8, :made].astype(bf16), down[...])
    state = state + plain_dot(small[8:16, :made].astype(bf16), up[...])
    state = state + exact_dot(small[0:8, made : made + gains], gain[...].astype(f32))
    for turn, device in enumerate((here.sibling(), here.over_x(), here.over_y())):
        totals[turn] = state
        copy = copies.remote(totals.at[turn], arriving.at[turn], device)
        copy.wait_recv()
        state = state + arriving[turn]
    totals[3] = state
    around = [copies.remote(totals.at[3], arriving.at[2 + k], here.along_z(k)) for k in (1, 2, 3)]
    terms = {}
    for k, copy in enumerate(around):
        copy.wait_recv()
    total = jnp.zeros_like(state)
    for line in range(LINE):
        for k in range(LINE):
            term = state if k == 0 else arriving[2 + k]
            total = total + jnp.where(lax.rem(z - k + LINE, LINE) == line, term, 0.0)
    state_out[...] = total
    for i in range(count - 1):
        last[i].wait_recv()
    copies.finish()


def scatter(grads, makers):
    count = len(grads)
    copies = 12 * count + 8
    any_space = pl.BlockSpec(memory_space=pl.ANY)
    vmem = pl.BlockSpec(memory_space=pltpu.VMEM)

    def slots(shape_of):
        return [pltpu.VMEM(shape_of(g, i), bf16) for i, g in enumerate(grads)]

    def rows_of(g, i, which):
        cut = shares(g.shape[3], i)[which]
        return cut.stop - cut.start

    scratch = slots(lambda g, i: g.shape[:4] + (g.shape[4] // 2,)) * 1
    scratch += slots(lambda g, i: g.shape[:4] + (g.shape[4] // 2,))
    scratch += slots(lambda g, i: (LINE, 2, rows_of(g, i, 0), g.shape[4] // 2))
    scratch += slots(lambda g, i: (LINE, 2, rows_of(g, i, 1), g.shape[4] // 2))
    scratch += slots(lambda g, i: (LINE, rows_of(g, i, 0), g.shape[4] // 2))
    scratch += slots(lambda g, i: (LINE, rows_of(g, i, 1), g.shape[4] // 2))
    scratch += slots(lambda g, i: (LINE - 1, g.shape[3], g.shape[4] // 2))
    scratch += [pltpu.VMEM((g.shape[3], g.shape[4] // 2), f32) for g in grads]
    tasks, hidden = 8, makers[0].shape[1]
    scratch += [pltpu.VMEM((4, tasks, hidden), f32), pltpu.VMEM((6, tasks, hidden), f32)]
    scratch += [pltpu.SemaphoreType.DMA((copies,)), pltpu.SemaphoreType.DMA((copies,))]
    return pl.pallas_call(
        functools.partial(scatter_kernel, count, len(makers)),
        in_specs=[any_space] * count + [vmem] * len(makers),
        out_specs=[vmem] * (count + 1),
        out_shape=[jax.ShapeDtypeStruct((g.shape[3] // 2, g.shape[4]), f32) for g in grads]
        + [jax.ShapeDtypeStruct((tasks, hidden), f32)],
        scratch_shapes=scratch,
        compiler_params=pltpu.CompilerParams(
            collective_id=1, has_side_effects=True, vmem_limit_bytes=60 << 20
        ),
        name="scatter_gradients",
    )(*grads, *makers)


class Unit:
    def __init__(self, here, copies, source, whole_array, index, first, second):
        self.here, self.copies = here, copies
        self.source, self.array = source, whole_array
        self.index, self.shares = index, (first, second)
        self.going = {}

    def window(self, zs, ys, xs, share=None):
        return self.array.at[(zs, ys, xs) + (self.index if share is None else self.shares[share])]

    def depart(self):
        here, copies = self.here, self.copies
        source = self.source()
        target = self.window(here.z, here.y, here.x)
        self.going["z"] = [copies.remote(source, target, here.along_z(k)) for k in (1, 2, 3)]
        self.own = copies.local(source, target)

    def turn(self):
        here = self.here
        for copy in self.going["z"]:
            copy.wait_recv()
        self.own.wait()
        one = self.window(slice(None), here.y, here.x, 0)
        two = self.window(slice(None), here.y, here.x, 1)
        self.going["1"] = [
            self.copies.remote(one, one, here.over_x()),
            self.copies.remote(two, two, here.over_y()),
        ]

    def turn_again(self):
        here = self.here
        for copy in self.going["1"]:
            copy.wait_recv()
        one = self.window(slice(None), here.y, slice(None), 0)
        two = self.window(slice(None), slice(None), here.x, 1)
        self.going["2"] = [
            self.copies.remote(one, one, here.over_y()),
            self.copies.remote(two, two, here.over_x()),
        ]

    def cross(self):
        for copy in self.going["2"]:
            copy.wait_recv()
        part = self.window(slice(None), slice(None), slice(None))
        self.going["c"] = self.copies.remote(part, part, self.here.sibling())

    def settle(self):
        self.going["c"].wait_recv()

    def stages(self):
        return (self.depart, self.turn, self.turn_again, self.cross, self.settle)


def column_of(row):
    length = row.shape[1]
    at_q = lax.broadcasted_iota(jnp.int32, (length, length), 0)
    at_k = lax.broadcasted_iota(jnp.int32, (length, length), 1)
    picked = jnp.where(at_q == at_k, row.astype(f32), 0.0)
    return jnp.sum(picked, axis=1, keepdims=True).astype(jnp.int32)


def forward_kernel(*refs):
    (
        x, mem, segments, mem_segments, tasks,
        sq, sk, sv, so, cq, ck, cv, co, w_in, w_out,
        table, weight, bias_row, down, up, gain,
    ) = refs[:21]
    outs, made_out, gains_out = refs[21:31], refs[31], refs[32]
    low_out, gain_out, task_out = refs[33:36]
    saved_out = refs[36:47]
    p1_out, p2_out = refs[47:49]
    scratch = refs[49:]
    wide, halves, blocks = scratch[:10], scratch[10:20], scratch[20:30]
    local_w = scratch[30:38]
    saved = scratch[38:49]
    n1, q1, k1, v1, m1, s1, n2, q2, k2, v2, m2 = saved
    made, gain_rows_all, bias, probs, send, recv, p_sem, load_sem, save_sem, gain_full = scratch[49:]
    own = (sq, sk, sv, so, cq, ck, cv, co, w_in, w_out)
    rows_total, length = segments.shape
    mem_len = mem_segments.shape[1]
    here = Place()
    copies = Copies(send, recv)
    c = here.core

    def half(i, core, first=0, width=None):
        full = own[i].shape[1] // 2
        width = full if width is None else width
        return pl.ds(pl.multiple_of(core * full + first, 128), width)

    for i in range(10):
        wide[i][...] = own[i][...].astype(f32)
    gain_rows_all[...] = gain[...].astype(f32)
    probs[...] = jnp.zeros_like(probs)
    meet(here)
    pair = {}
    order = (0, 1, 2, 5, 6, 3, 4, 7, 8, 9)
    for i in order:
        rows = own[i].shape[0]
        mine = pl.ds(pl.multiple_of(c * rows, 8), rows)
        pair[i] = copies.remote(
            wide[i].at[:, half(i, 1 - c)], halves[i].at[mine, :], here.sibling()
        )
        halves[i][mine, :] = wide[i][:, half(i, c)]

    opened = set()

    def piece(i, rows, first, width):
        def source():
            if i not in opened:
                opened.add(i)
                pair[i].wait_recv()
                blocks[i][...] = halves[i][...].astype(bf16)
            return blocks[i].at[rows, pl.ds(first, width)]

        at = half(i, c, first, width)
        count = rows.stop - rows.start
        if (width // 2) % 128 == 0:
            one = (rows, half(i, c, first, width // 2))
            two = (rows, half(i, c, first + width // 2, width // 2))
        else:
            cut = rows.start + (count // 2 if count % 32 == 0 else (count // 32 + i % 2) * 16)
            one = (slice(rows.start, cut), at)
            two = (slice(cut, rows.stop), at)
        return Unit(here, copies, source, outs[i], (rows, at), one, two)

    def square(i):
        return piece(i, slice(0, outs[i].shape[3]), 0, own[i].shape[1] // 2)

    gain_own = gain.shape[0]
    gain_cut = gain_own // 16 * 8
    made_cut = made.shape[1] // 2
    gain_unit = Unit(
        here, copies, lambda: gain_rows_all, gains_out, (c,),
        (c, pl.ds(0, gain_cut)), (c, pl.ds(gain_cut, gain_own - gain_cut)),
    )
    made_unit = Unit(
        here, copies, lambda: made, made_out, (c,),
        (c, slice(None), pl.ds(0, made_cut)), (c, slice(None), pl.ds(made_cut, made_cut)),
    )
    in_half = w_in.shape[1] // 4
    out_rows = outs[9].shape[3]
    units = [gain_unit] + [square(i) for i in (0, 1, 2, 5, 6, 3, 4, 7)]
    units += [piece(8, slice(0, outs[8].shape[3]), k * in_half, in_half) for k in (0, 1)]
    units += [made_unit]
    units += [
        piece(9, slice(k * out_rows // 2, (k + 1) * out_rows // 2), 0, w_out.shape[1] // 2)
        for k in (0, 1)
    ]
    loads = {}
    landing = {1: (0,), 2: (1,), 3: (2,), 4: (5,), 5: (6,), 6: (3,), 7: (4,), 8: (7,)}

    def tick(turn):
        for late in range(5):
            u = turn - late
            if 0 <= u < len(units):
                units[u].stages()[late]()
                if late == 4 and u in landing:
                    (i,) = landing[u]
                    loads[i] = pltpu.make_async_copy(outs[i], local_w[i], load_sem.at[i])
                    loads[i].start()
                if late == 4 and u == 0:
                    loads["gain"] = pltpu.make_async_copy(gains_out, gain_full, load_sem.at[8])
                    loads["gain"].start()


    def matrix(i):
        return local_w[i][...].reshape(-1, own[i].shape[1])

    state = gelu_in_kernel(exact_dot(table[...], weight[...]) + bias_row[...])
    low = state.astype(bf16)
    low_out[...] = low
    made[...] = jnp.zeros_like(made)
    made[:, : down.shape[0]] = inner_rows(low, down[...])
    made_at = made.shape[1] // 2
    made[:, made_at : made_at + up.shape[0]] = inner_rows(low, up[...])

    for now in range(8):
        tick(now)
    ticks = iter(range(8, len(units) + 4))

    def between():
        turn = next(ticks, None)
        if turn is not None:
            tick(turn)

    stores = []

    def store(which, part=None):
        source, target = saved[which], saved_out[which]
        copy = pltpu.make_async_copy(source, target, save_sem.at[which])
        copy.start()
        stores.append(copy)

    for r in range(rows_total):
        column = column_of(segments[r : r + 1, :])
        task = jnp.zeros_like(column)
        for s in range(tasks.shape[1]):
            task = task + jnp.where(column == s, tasks[r : r + 1, s : s + 1], 0)
        task_out[r * length : (r + 1) * length, :] = task
    loads["gain"].wait()
    width = x.shape[1]
    gain_out[...] = 1.0 + inner_rows(low, gain_full[...].reshape(-1, gain.shape[1]).astype(bf16))

    def picked(r, which):
        task = task_out[r * length : (r + 1) * length, :]
        return token_gain(task, gain_out[:, which * width : (which + 1) * width])

    def row(r, size=None):
        size = length if size is None else size
        return slice(r * size, (r + 1) * size)

    for i in (0, 1, 2):
        loads[i].wait()
    for r in range(rows_total):
        stream = x[row(r), :].astype(f32)
        n = (stream * inverse_rms(stream) * picked(r, 0)).astype(bf16)
        n1[row(r), :] = n
        q1[row(r), :] = (plain_dot(n, matrix(0)).astype(bf16).astype(f32) * HEAD**-0.5).astype(bf16)
        k1[row(r), :] = plain_dot(n, matrix(1)).astype(bf16)
        v1[row(r), :] = plain_dot(n, matrix(2)).astype(bf16)
        between()
    for which in (0, 1, 2, 3):
        store(which)


    def attend(causal, q, k, v, mixed, p_out, r, keys_row):
        column = column_of(segments[r : r + 1, :])
        same = column == keys_row
        if causal:
            at_q = lax.broadcasted_iota(jnp.int32, same.shape, 0)
            at_k = lax.broadcasted_iota(jnp.int32, same.shape, 1)
            same = same & (at_q >= at_k)
        bias[...] = jnp.where(same, 0.0, masked_score)
        keys_total = keys_row.shape[1]
        per_group = HEADS // 4
        for group in range(2):
            @pl.loop(group * per_group, (group + 1) * per_group)
            def _(p):
                slot = lax.rem(p, 2)
                at = pl.ds(pl.multiple_of(p * PAIR, PAIR), PAIR)

                @pl.when(p >= 2)
                def _():
                    pltpu.make_async_copy(
                        probs.at[slot], p_out.at[r, pl.ds(2 * p - 4, 2)], p_sem.at[slot]
                    ).wait()

                attend_pair(causal, q, k, v, mixed, probs.at[slot], bias, row(r), row(r, keys_total), at)
                pltpu.make_async_copy(
                    probs.at[slot], p_out.at[r, pl.ds(2 * p, 2)], p_sem.at[slot]
                ).start()

            between()
        for p in (HEADS // 2 - 2, HEADS // 2 - 1):
            pltpu.make_async_copy(
                probs.at[p % 2], p_out.at[r, pl.ds(2 * p, 2)], p_sem.at[p % 2]
            ).wait()

    for r in range(rows_total):
        attend(True, q1, k1, v1, m1, p1_out, r, segments[r : r + 1, :])
    store(4)
    for i in (5, 6):
        loads[i].wait()
    for r in range(rows_total):
        mine = row(r, mem_len)
        k2[mine, :] = plain_dot(mem[mine, :], matrix(5)).astype(bf16)
        v2[mine, :] = plain_dot(mem[mine, :], matrix(6)).astype(bf16)
        between()
    store(8)
    store(9)
    for i in (3, 4):
        loads[i].wait()
    for r in range(rows_total):
        stream = x[row(r), :].astype(f32) + plain_dot(m1[row(r), :], matrix(3))
        s1[row(r), :] = stream
        n = (stream * inverse_rms(stream) * picked(r, 1)).astype(bf16)
        n2[row(r), :] = n
        q2[row(r), :] = (plain_dot(n, matrix(4)).astype(bf16).astype(f32) * HEAD**-0.5).astype(bf16)
        between()
    for which in (5, 6, 7):
        store(which)
    for r in range(rows_total):
        attend(False, q2, k2, v2, m2, p2_out, r, mem_segments[r : r + 1, :])
    store(10)
    for turn in ticks:
        tick(turn)
    loads[7].wait()
    for copy in stores:
        copy.wait()
    copies.finish()


def gelu_in_kernel(v):
    return v * (0.5 * lax.erf(v * 0.7071067811865476) + 0.5)


def attend_pair(causal, q_ref, k_ref, v_ref, mixed_ref, p_ref, bias, q_rows, k_rows, at):
    length = q_rows.stop - q_rows.start
    keys_all = k_rows.stop - k_rows.start
    step = length // 2 if causal else length
    masks = half_masks()
    for first in range(0, length, step):
        rows = slice(q_rows.start + first, q_rows.start + first + step)
        keys = first + step if causal else keys_all
        q = q_ref[rows, at]
        k = k_ref[k_rows.start : k_rows.start + keys, at]
        v = v_ref[k_rows.start : k_rows.start + keys, at]
        out = None
        for h, mask in enumerate(masks):
            s = inner_rows(q * mask, k) + bias[first : first + step, :keys]
            e = jnp.exp(s - jnp.max(s, axis=-1, keepdims=True))
            p = (e * (1.0 / jnp.sum(e, axis=-1, keepdims=True))).astype(bf16)
            p_ref[h, first : first + step, :keys] = p
            part = plain_dot(p, v * mask)
            out = part if out is None else out + part
        mixed_ref[rows, at] = out.astype(bf16)


def forward(x, mem, segments, mem_segments, tasks, weights, table, weight, bias_row, makers):
    down, up, gain = makers
    own = weights
    tokens, width = x.shape
    mem_tokens = mem.shape[0]
    rows, length = segments.shape
    mem_len = mem_segments.shape[1]
    spaces = (LINE, 2, 2)
    any_space = pl.BlockSpec(memory_space=pl.ANY)
    vmem = pl.BlockSpec(memory_space=pltpu.VMEM)
    made_half = down.shape[0] + (-down.shape[0] % 128)
    n_tasks = table.shape[0]
    chip = [spaces + (2 * a.shape[0], a.shape[1]) for a in own]
    t_low, m_low, t_full = ((tokens, width), bf16), ((mem_tokens, width), bf16), ((tokens, width), f32)
    kept = [t_low, t_low, t_low, t_low, t_low, t_full, t_low, t_low, m_low, m_low, t_low]
    shape = jax.ShapeDtypeStruct
    probs = (rows, HEADS, length, mem_len)
    copies = 11 * 16 + 16
    outs = pl.pallas_call(
        forward_kernel,
        in_specs=[vmem] * 21,
        out_specs=[any_space] * 12 + [vmem] * 3 + [any_space] * 13,
        out_shape=[shape(s, bf16) for s in chip]
        + [
            shape(spaces + (2, n_tasks, 2 * made_half), f32),
            shape(spaces + (2,) + gain.shape, f32),
            shape((n_tasks, weight.shape[1]), bf16),
            shape((n_tasks, 3 * width), f32),
            shape((tokens, 1), jnp.int32),
        ]
        + [shape(s, d) for s, d in kept]
        + [shape((rows, HEADS, length, length), bf16), shape(probs, bf16)],
        scratch_shapes=[pltpu.VMEM(a.shape, f32) for a in own]
        + [pltpu.VMEM((2 * a.shape[0], a.shape[1] // 2), f32) for a in own]
        + [pltpu.VMEM((2 * a.shape[0], a.shape[1] // 2), bf16) for a in own]
        + [pltpu.VMEM(s, bf16) for s in chip[:8]]
        + [pltpu.VMEM(s, d) for s, d in kept]
        + [
            pltpu.VMEM((n_tasks, 2 * made_half), f32),
            pltpu.VMEM(gain.shape, f32),
            pltpu.VMEM((length, max(length, mem_len)), f32),
            pltpu.VMEM((2, 2, length, max(length, mem_len)), bf16),
            pltpu.SemaphoreType.DMA((copies,)),
            pltpu.SemaphoreType.DMA((copies,)),
            pltpu.SemaphoreType.DMA((2,)),
            pltpu.SemaphoreType.DMA((9,)),
            pltpu.SemaphoreType.DMA((11,)),
            pltpu.VMEM(spaces + (2,) + gain.shape, f32),
        ],
        compiler_params=pltpu.CompilerParams(
            collective_id=0, has_side_effects=True, vmem_limit_bytes=VMEM_BYTES
        ),
        name="forward_as_weights_arrive",
    )(x, mem, segments, mem_segments, tasks, *own, table, weight, bias_row, down, up, gain)
    return outs


def on_device(
    block_input, memory, cotangent, segments, memory_segments, task_of_segment,
    self_query, self_key, self_value, self_output,
    cross_query, cross_key, cross_value, cross_output,
    hidden_in, hidden_out, task_table, task_weight, task_bias,
    down_maker, up_maker, gain_maker,
):
    row_count, seq_len, model_width = block_input.shape
    mem_len = memory.shape[1]
    task_count = task_table.shape[0]
    token_count = row_count * seq_len
    parts = lax.axis_size("dp")
    weights = (
        self_query, self_key, self_value, self_output,
        cross_query, cross_key, cross_value, cross_output, hidden_in, hidden_out,
    )
    task_state, task_back = jax.vjp(task_network, task_table, task_weight, task_bias)
    task_low = task_state.astype(bf16)
    down_own, gain_own = down_maker.shape[0], gain_maker.shape[0]
    makers = (down_maker, up_maker, gain_maker)
    x = block_input.reshape(token_count, model_width)
    mem = memory.reshape(row_count * mem_len, model_width)

    def joined(block):
        return block.transpose(1, 0, 2).reshape(task_count, -1)

    if parts == 32:
        outs = forward(
            x, mem, segments, memory_segments, task_of_segment, weights,
            task_table, task_weight, task_bias.reshape(1, -1), makers,
        )
        backbone = [w.reshape(-1, w.shape[-1]) for w in outs[:10]]
        made = outs[10].reshape(parts, task_count, -1)
        task_low, gain_table, token_task = outs[12:15]
        saved, probs_one, probs_two = outs[15:26], outs[26], outs[27]
        made_up = joined(made[:, :, made.shape[2] // 2 :][:, :, :down_own]).astype(bf16)
    else:
        packed = jnp.concatenate([w.reshape(-1, model_width) for w in weights], axis=0)
        packed = lax.all_gather(packed, "dp", axis=0, tiled=False)
        backbone, at = [], 0
        for w in weights:
            count = w.size // model_width
            backbone.append(packed[:, at : at + count].reshape(-1, w.shape[1]))
            at += count
        made = inner_rows(task_low, jnp.concatenate(makers, axis=0))
        made = lax.all_gather(made, "dp", axis=0, tiled=False)
        gain_table = 1.0 + joined(made[:, :, 2 * down_own :])
        seg_match = segments[:, :, None] == jnp.arange(task_of_segment.shape[1], dtype=jnp.int32)
        token_task = jnp.sum(
            jnp.where(seg_match, task_of_segment[:, None, :], 0), axis=-1
        ).reshape(token_count, 1)
        saved, probs_one, probs_two = attention_layers(
            x, mem, segments, memory_segments, token_task, backbone, gain_table
        )
        made_up = joined(made[:, :, down_own : 2 * down_own]).astype(bf16)
    made_down = joined(made[:, :, :down_own]).astype(bf16)
    down_all = (
        made_down.reshape(task_count, model_width, ADA)
        .transpose(1, 0, 2)
        .reshape(model_width, task_count * ADA)
    )
    up_all = made_up.reshape(task_count * ADA, model_width)
    output, input_grad, mem_grad, grads, up_all_grad, down_all_grad, gain_grad = feed_and_back(
        x, mem, cotangent.reshape(token_count, model_width), row_count, token_task,
        backbone, gain_table, down_all, up_all, saved, probs_one, probs_two,
    )
    down_rows = (
        down_all_grad.reshape(parts, -1, task_count, ADA)
        .transpose(0, 2, 1, 3)
        .reshape(parts, task_count, down_own)
    )
    up_rows = up_all_grad.reshape(task_count, parts, -1).transpose(1, 0, 2)
    gain_rows_all = gain_grad.reshape(task_count, parts, -1).transpose(1, 0, 2)
    if parts == 32:
        small = jnp.concatenate((down_rows, gain_rows_all), axis=2)
        wide = small.shape[2] + (-small.shape[2] % 256)
        small = jnp.concatenate(
            (
                jnp.pad(small, ((0, 0), (0, 0), (0, wide - small.shape[2]))),
                jnp.pad(up_rows, ((0, 0), (0, 0), (0, wide - up_rows.shape[2]))),
            ),
            axis=1,
        ).astype(bf16)
        units = [
            g.reshape((LINE, 2, 2, 2 * w.shape[0], w.shape[1])) for g, w in zip(grads, weights)
        ]
        units.append(small.reshape(LINE, 2, 2, 4 * task_count, wide))
        *shared, small, state_grad = scatter(units, (down_maker, up_maker, gain_maker))
        own_down = small[:task_count, :down_own].astype(bf16)
        own_up = small[task_count:, :down_own].astype(bf16)
        own_gain = small[:task_count, down_own : down_own + gain_own]
    else:
        packed = jnp.concatenate([g.reshape(parts, -1, model_width) for g in grads], axis=1)
        packed = lax.psum_scatter(packed, "dp", scatter_dimension=0, tiled=False).astype(f32)
        shared, at = [], 0
        for w in weights:
            count = w.size // model_width
            shared.append(packed[at : at + count].reshape(w.shape))
            at += count
        small = jnp.concatenate((down_rows, up_rows, gain_rows_all), axis=2)
        small = lax.psum_scatter(small, "dp", scatter_dimension=0, tiled=False)
        own_down = small[:, :down_own].astype(bf16)
        own_up = small[:, down_own : 2 * down_own].astype(bf16)
        own_gain = small[:, 2 * down_own :]
        state_grad = lax.psum(
            plain_dot(own_down, down_maker)
            + plain_dot(own_up, up_maker)
            + exact_dot(own_gain, gain_maker.astype(f32)),
            "dp",
        )
    down_maker_grad = inner_cols(own_down, task_low)
    up_maker_grad = inner_cols(own_up, task_low)
    gain_maker_grad = inner_cols(own_gain, task_low.astype(f32), exact_mode)
    table_grad, weight_grad, bias_grad = task_back(state_grad)
    return (
        output.reshape(row_count, seq_len, model_width),
        input_grad.reshape(row_count, seq_len, model_width),
        mem_grad.reshape(row_count, mem_len, model_width),
        *shared,
        table_grad,
        weight_grad,
        bias_grad,
        down_maker_grad,
        up_maker_grad,
        gain_maker_grad,
    )


def solution(mesh):
    rows, whole_copy = P("dp"), P()
    return jax.shard_map(
        on_device,
        mesh=mesh,
        in_specs=(rows,) * 16 + (whole_copy,) * 3 + (rows,) * 3,
        out_specs=(rows,) * 13 + (whole_copy,) * 3 + (rows,) * 3,
        check_vma=False,
    )
```

```python
import functools

import jax
import jax.numpy as jnp
from jax import lax
from jax.experimental import pallas as pl
from jax.experimental.pallas import tpu as pltpu
from jax.sharding import PartitionSpec as P

HEADS = 12
HEAD = 64
ADA = 24
PAIR = 2 * HEAD

exact_mode = lax.Precision.HIGHEST
norm_eps = 1e-06
masked_score = -1e30
bf16 = jnp.bfloat16
f32 = jnp.float32
VMEM_BYTES = 56 << 20


def plain_dot(left_side, right_side):
    return jnp.dot(left_side, right_side, preferred_element_type=f32)


def exact_dot(left_side, right_side):
    return jnp.dot(left_side, right_side, precision=exact_mode, preferred_element_type=f32)


def inner_rows(left_side, right_side):
    return lax.dot_general(
        left_side, right_side, (((1,), (1,)), ((), ())), preferred_element_type=f32
    )


def inner_cols(left_side, right_side, precision_mode=None):
    return lax.dot_general(
        left_side,
        right_side,
        (((0,), (0,)), ((), ())),
        precision=precision_mode,
        preferred_element_type=f32,
    )


def gelu_exact(operand):
    return jax.nn.gelu(operand, approximate=False)


def task_network(table_rows, weight_in, bias_row):
    return gelu_exact(exact_dot(table_rows, weight_in) + bias_row)


def gelu_both(v):
    phi = 0.5 * lax.erf(v * 0.7071067811865476) + 0.5
    slope = phi + v * (jnp.exp(v * v * -0.5) * 0.3989422804014327)
    return v * phi, slope


def token_gain(task_column, gain):
    high = gain.astype(bf16).astype(f32)
    rest = gain - high
    middle = rest.astype(bf16).astype(f32)
    table = jnp.concatenate((high, middle, rest - middle), axis=0).astype(bf16)
    which = lax.broadcasted_iota(jnp.int32, (task_column.shape[0], 24), 1) & 7
    hot = jnp.where(which == task_column, 1.0, 0.0).astype(bf16)
    return plain_dot(hot, table)


def gain_rows(task_column, grads):
    which = lax.broadcasted_iota(jnp.int32, (task_column.shape[0], 8), 1)
    hot = jnp.where(which == task_column, 1.0, 0.0).astype(bf16)
    high = grads.astype(bf16)
    low = (grads - high.astype(f32)).astype(bf16)
    return inner_cols(hot, high) + inner_cols(hot, low)


def inverse_rms(stream):
    return lax.rsqrt(jnp.mean(stream * stream, axis=-1, keepdims=True) + norm_eps)


def norm_back(stream, gain, cotan):
    r = inverse_rms(stream)
    scaled = cotan * gain
    inner = jnp.mean(scaled * stream, axis=-1, keepdims=True)
    return r * (scaled - stream * (r * r * inner)), cotan * (stream * r)


def call(kernel, grid, ins, outs, scratch=(), flops=0, name=None):
    size = sum(a.size * a.dtype.itemsize for a, _, _ in ins)
    size += sum(functools.reduce(lambda p, q: p * q, s, 1) * jnp.dtype(d).itemsize for s, d, _, _ in outs)
    return pl.pallas_call(
        kernel,
        grid=grid,
        in_specs=[pl.BlockSpec(b, m) for _, b, m in ins],
        out_specs=[pl.BlockSpec(b, m) for _, _, b, m in outs],
        out_shape=[jax.ShapeDtypeStruct(s, d) for s, d, _, _ in outs],
        scratch_shapes=list(scratch),
        compiler_params=pltpu.CompilerParams(vmem_limit_bytes=VMEM_BYTES),
        cost_estimate=pl.CostEstimate(flops=flops, bytes_accessed=size, transcendentals=0),
        name=name,
    )(*[a for a, _, _ in ins])


def whole(array):
    return (array, array.shape, lambda *_: (0,) * array.ndim)


def by_row(array, rows):
    return (array, (rows,) + array.shape[1:], lambda i: (i,) + (0,) * (array.ndim - 1))


def out_row(shape, dtype, rows):
    return (shape, dtype, (rows,) + shape[1:], lambda i: (i,) + (0,) * (len(shape) - 1))


def out_whole(shape, dtype):
    return (shape, dtype, shape, lambda *_: (0,) * len(shape))


def pre_kernel(x, task, gain, wq, wk, wv, normed, q, k, v):
    stream = x[...].astype(f32)
    n = (stream * inverse_rms(stream) * token_gain(task[...], gain[...])).astype(bf16)
    normed[...] = n
    q[...] = (plain_dot(n, wq[...]).astype(bf16).astype(f32) * HEAD**-0.5).astype(bf16)
    k[...] = plain_dot(n, wk[...]).astype(bf16)
    v[...] = plain_dot(n, wv[...]).astype(bf16)


def memory_kernel(x, wk, wv, k, v):
    k[...] = plain_dot(x[...], wk[...]).astype(bf16)
    v[...] = plain_dot(x[...], wv[...]).astype(bf16)


def middle_kernel(x, mixed, wo, task, gain, wq, stream_out, normed, q):
    stream = x[...].astype(f32) + plain_dot(mixed[...], wo[...])
    stream_out[...] = stream
    n = (stream * inverse_rms(stream) * token_gain(task[...], gain[...])).astype(bf16)
    normed[...] = n
    q[...] = (plain_dot(n, wq[...]).astype(bf16).astype(f32) * HEAD**-0.5).astype(bf16)


def half_masks():
    lane = lax.broadcasted_iota(jnp.int32, (1, PAIR), 1)
    first = jnp.where(lane < HEAD, 1.0, 0.0)
    return first.astype(bf16), (1.0 - first).astype(bf16)


def attend_forward_kernel(causal, q_ref, k_ref, v_ref, seg_q, seg_k, mixed_ref, p_ref, bias):
    length, keys_all = q_ref.shape[0], k_ref.shape[0]
    step = length // 2 if causal else length

    @pl.when(pl.program_id(1) == 0)
    def _():
        same = seg_q[...] == seg_k[0]
        if causal:
            at_q = lax.broadcasted_iota(jnp.int32, (length, keys_all), 0)
            at_k = lax.broadcasted_iota(jnp.int32, (length, keys_all), 1)
            same = same & (at_q >= at_k)
        bias[...] = jnp.where(same, 0.0, masked_score)

    masks = half_masks()
    for first in range(0, length, step):
        rows = pl.ds(first, step)
        keys = first + step if causal else keys_all
        q = q_ref[rows, :]
        k = k_ref[:keys, :]
        v = v_ref[:keys, :]
        out = None
        for h, mask in enumerate(masks):
            s = inner_rows(q * mask, k) + bias[rows, :keys]
            e = jnp.exp(s - jnp.max(s, axis=-1, keepdims=True))
            p = (e * (1.0 / jnp.sum(e, axis=-1, keepdims=True))).astype(bf16)
            p_ref[0, h, rows, :keys] = p
            part = plain_dot(p, v * mask)
            out = part if out is None else out + part
        mixed_ref[rows, :] = out.astype(bf16)


def attend_backward_kernel(
    causal, q_ref, k_ref, v_ref, mixed_ref, gm_ref, p_ref, gq_ref, gk_ref, gv_ref
):
    length, keys_all = q_ref.shape[0], k_ref.shape[0]
    step = length // 2 if causal else length
    masks = half_masks()
    gk_parts, gv_parts = [], []
    for first in range(0, length, step):
        rows = pl.ds(first, step)
        keys = first + step if causal else keys_all
        q = q_ref[rows, :]
        k = k_ref[:keys, :]
        v = v_ref[:keys, :]
        gm = gm_ref[rows, :]
        product = gm.astype(f32) * mixed_ref[rows, :].astype(f32)
        gq = gk = gv = 0.0
        for h, mask in enumerate(masks):
            inner = jnp.sum(product * mask.astype(f32), axis=-1, keepdims=True)
            p = p_ref[0, h, rows, :keys]
            gm_half = gm * mask
            gw = inner_rows(gm_half, v)
            gs = (p.astype(f32) * (gw - inner)).astype(bf16)
            gv = gv + inner_cols(p, gm_half)
            gq = gq + plain_dot(gs, k * mask)
            gk = gk + inner_cols(gs, q * mask)
        gq_ref[rows, :] = (gq * HEAD**-0.5).astype(bf16)
        gk_parts.append(gk)
        gv_parts.append(gv)
    for ref, terms in ((gk_ref, gk_parts), (gv_ref, gv_parts)):
        if not causal:
            ref[...] = terms[0].astype(bf16)
        else:
            ref[:step, :] = (terms[0] + terms[1][:step]).astype(bf16)
            ref[step:, :] = terms[1][step:].astype(bf16)


def attention_specs(rows, length, arrays):
    return [(a, (length, PAIR), lambda r, p: (r, p)) for a in arrays]


def attend_forward(causal, rows, length, q, k, v, seg_q, seg_k):
    mem_len = k.shape[0] // rows
    mixed, probs = call(
        functools.partial(attend_forward_kernel, causal),
        (rows, HEADS // 2),
        attention_specs(rows, length, (q,))
        + attention_specs(rows, mem_len, (k, v))
        + [
            (seg_q.reshape(rows * length, 1), (length, 1), lambda r, p: (r, 0)),
            (seg_k.reshape(rows, 1, mem_len), (1, 1, mem_len), lambda r, p: (r, 0, 0)),
        ],
        [
            (q.shape, bf16, (length, PAIR), lambda r, p: (r, p)),
            (
                (rows, HEADS, length, mem_len),
                bf16,
                (1, 2, length, mem_len),
                lambda r, p: (r, p, 0, 0),
            ),
        ],
        scratch=[pltpu.VMEM((length, mem_len), f32)],
        flops=4 * rows * HEADS * length * mem_len * PAIR,
        name="attend_forward",
    )
    return mixed, probs


def attend_backward(causal, rows, length, q, k, v, mixed, grad_mixed, probs):
    mem_len = k.shape[0] // rows
    return call(
        functools.partial(attend_backward_kernel, causal),
        (rows, HEADS // 2),
        attention_specs(rows, length, (q,))
        + attention_specs(rows, mem_len, (k, v))
        + attention_specs(rows, length, (mixed, grad_mixed))
        + [(probs, (1, 2, length, mem_len), lambda r, p: (r, p, 0, 0))],
        [
            (q.shape, bf16, (length, PAIR), lambda r, p: (r, p)),
            (k.shape, bf16, (mem_len, PAIR), lambda r, p: (r, p)),
            (k.shape, bf16, (mem_len, PAIR), lambda r, p: (r, p)),
        ],
        flops=8 * rows * HEADS * length * mem_len * PAIR,
        name="attend_backward",
    )


CHUNK = 768


def feed_kernel(
    s1, mixed, wo, task, gain, w_in, w_out, down_all, up_all, cot,
    output, n3, act, gu, gfeed, g2, g2_low, gmix, up_grad, down_grad, gain_grad,
    slope, total,
):
    first = pl.program_id(0) == 0
    units = w_in.shape[1]
    stream = s1[...] + plain_dot(mixed[...], wo[...])
    picked = token_gain(task[...], gain[...])
    n3[...] = (stream * inverse_rms(stream) * picked).astype(bf16)
    total[...] = jnp.zeros_like(total)

    @pl.loop(0, units // CHUNK)
    def _(j):
        cols = pl.ds(pl.multiple_of(j * CHUNK, CHUNK), CHUNK)
        value, rate = gelu_both(plain_dot(n3[...], w_in[:, cols]))
        value = value.astype(bf16)
        act[:, cols] = value
        slope[:, cols] = rate.astype(bf16)
        total[...] += plain_dot(value, w_out[cols, :])

    feed = total[...]
    feed_low = feed.astype(bf16)
    tokens, wide = stream.shape[0], down_all.shape[1]
    owner = lax.broadcasted_iota(jnp.int32, (tokens, wide), 1) - task[...] * ADA
    mask = jnp.where((owner >= 0) & (owner < ADA), 1.0, 0.0)
    narrow, narrow_slope = gelu_both(plain_dot(feed_low, down_all[...]) * mask)
    narrow = narrow.astype(bf16)
    output[...] = (stream + feed + plain_dot(narrow, up_all[...])).astype(bf16)
    cotan = cot[...]
    gb = (narrow_slope * inner_rows(cotan, up_all[...]) * mask).astype(bf16)
    grad_feed = (cotan.astype(f32) + inner_rows(gb, down_all[...])).astype(bf16)
    gfeed[...] = grad_feed
    up_now = inner_cols(narrow, cotan)
    down_now = inner_cols(feed_low, gb)
    total[...] = jnp.zeros_like(total)

    @pl.loop(0, units // CHUNK)
    def _(j):
        cols = pl.ds(pl.multiple_of(j * CHUNK, CHUNK), CHUNK)
        grad = slope[:, cols].astype(f32) * inner_rows(gfeed[...], w_out[cols, :])
        grad = grad.astype(bf16)
        gu[:, cols] = grad
        total[...] += inner_rows(grad, w_in[:, cols])

    stream_grad, gain_tokens = norm_back(stream, picked, total[...])
    grad_two = cotan.astype(f32) + stream_grad
    g2[...] = grad_two
    low = grad_two.astype(bf16)
    g2_low[...] = low
    gmix[...] = inner_rows(low, wo[...]).astype(bf16)
    gain_now = gain_rows(task[...], gain_tokens)

    @pl.when(first)
    def _():
        up_grad[...] = up_now
        down_grad[...] = down_now
        gain_grad[...] = gain_now

    @pl.when(jnp.logical_not(first))
    def _():
        up_grad[...] += up_now
        down_grad[...] += down_now
        gain_grad[...] += gain_now


def cross_back_kernel(gq, wq, s1, task, gain, g2, wo, g1, g1_low, gmix, gain_grad):
    stream = s1[...]
    picked = token_gain(task[...], gain[...])
    stream_grad, gain_tokens = norm_back(stream, picked, inner_rows(gq[...], wq[...]))
    grad_one = g2[...] + stream_grad
    g1[...] = grad_one
    low = grad_one.astype(bf16)
    g1_low[...] = low
    gmix[...] = inner_rows(low, wo[...]).astype(bf16)
    accumulate(gain_grad, gain_rows(task[...], gain_tokens))


def accumulate(ref, value):
    @pl.when(pl.program_id(0) == 0)
    def _():
        ref[...] = value

    @pl.when(pl.program_id(0) != 0)
    def _():
        ref[...] += value


def memory_back_kernel(gk, gv, wk, wv, out):
    out[...] = inner_rows(gk[...], wk[...]) + inner_rows(gv[...], wv[...])


def input_back_kernel(gq, gk, gv, wq, wk, wv, x, task, gain, g1, out, gain_grad):
    stream = x[...].astype(f32)
    picked = token_gain(task[...], gain[...])
    cotan = inner_rows(gq[...], wq[...]) + inner_rows(gk[...], wk[...])
    cotan = cotan + inner_rows(gv[...], wv[...])
    stream_grad, gain_tokens = norm_back(stream, picked, cotan)
    out[...] = g1[...] + stream_grad
    accumulate(gain_grad, gain_rows(task[...], gain_tokens))


def outer_kernel(which, sources, *refs):
    left = refs[:sources]
    right = refs[sources : sources + len(which)]
    outs = refs[sources + len(which) :]
    for source, grad, out in zip(which, right, outs):
        for first in range(0, out.shape[1], CHUNK):
            cols = slice(first, first + CHUNK)
            out[:, cols] = inner_cols(left[source][...], grad[:, cols]).astype(bf16)


def outers(sources, grads, which, name):
    tokens, width = sources[0].shape
    block = 256
    return call(
        functools.partial(outer_kernel, which, len(sources)),
        (width // block,),
        [(s, (tokens, block), lambda i: (0, i)) for s in sources] + [whole(g) for g in grads],
        [((width, g.shape[1]), bf16, (block, g.shape[1]), lambda i: (i, 0)) for g in grads],
        flops=sum(2 * tokens * width * g.shape[1] for g in grads),
        name=name,
    )


BLOCK = 512


def low_out(shape):
    return out_row(shape, bf16, BLOCK)


def full_out(shape):
    return out_row(shape, f32, BLOCK)


def attention_layers(x, mem, segments, mem_segments, task, weights, gain_table):
    rows, length = segments.shape
    tokens, width = x.shape
    wq1, wk1, wv1, wo1, wq2, wk2, wv2 = weights[:7]
    gain_one, gain_two = (gain_table[:, i * width : (i + 1) * width] for i in range(2))
    block = BLOCK
    grid = (tokens // block,)
    act_shape = (tokens, width)
    square = 2 * tokens * width * width
    n1, q1, k1, v1 = call(
        pre_kernel,
        grid,
        [by_row(x, block), by_row(task, block)] + [whole(a) for a in (gain_one, wq1, wk1, wv1)],
        [low_out(act_shape) for _ in range(4)],
        flops=3 * square,
        name="self_projections",
    )
    m1, p1 = attend_forward(True, rows, length, q1, k1, v1, segments, segments)
    s1, n2, q2 = call(
        middle_kernel,
        grid,
        [by_row(x, block), by_row(m1, block), whole(wo1), by_row(task, block), whole(gain_two), whole(wq2)],
        [full_out(act_shape), low_out(act_shape), low_out(act_shape)],
        flops=2 * square,
        name="middle",
    )
    k2, v2 = call(
        memory_kernel,
        grid,
        [by_row(mem, block), whole(wk2), whole(wv2)],
        [low_out(mem.shape), low_out(mem.shape)],
        flops=2 * square,
        name="memory_projections",
    )
    m2, p2 = attend_forward(False, rows, length, q2, k2, v2, segments, mem_segments)
    return (n1, q1, k1, v1, m1, s1, n2, q2, k2, v2, m2), p1, p2


def feed_forward(s1, m2, cot, task, weights, gain_table, down_all, up_all):
    tokens, width = s1.shape
    wo2, w_in, w_out = weights[7:]
    gain_three = gain_table[:, 2 * width :]
    block = BLOCK
    grid = (tokens // block,)
    act_shape = (tokens, width)
    square = 2 * tokens * width * width
    units = w_in.shape[1]
    wide = up_all.shape[0]
    tasks = gain_table.shape[0]
    output, n3, act, gu, gfeed, g2, g2_low, gmix2, up_grad, down_grad, gain3 = call(
        feed_kernel,
        grid,
        [
            by_row(s1, block), by_row(m2, block), whole(wo2), by_row(task, block), whole(gain_three),
            whole(w_in), whole(w_out), whole(down_all), whole(up_all), by_row(cot, block),
        ],
        [
            low_out(act_shape), low_out(act_shape), out_row((tokens, units), bf16, block), out_row((tokens, units), bf16, block),
            low_out(act_shape), full_out(act_shape), low_out(act_shape), low_out(act_shape),
            out_whole((wide, width), f32), out_whole((width, wide), f32), out_whole((tasks, width), f32),
        ],
        scratch=[pltpu.VMEM((block, units), bf16), pltpu.VMEM((block, width), f32)],
        flops=2 * square + 8 * tokens * width * units,
        name="feed_forward_and_back",
    )
    (hidden_in_grad,) = outers((n3,), (gu,), (0,), "hidden_in_grad")
    (hidden_out_grad,) = outers((act,), (gfeed,), (0,), "hidden_out_grad")
    return output, g2, g2_low, gmix2, hidden_in_grad, hidden_out_grad, up_grad, down_grad, gain3


def attention_back(x, mem, rows, task, weights, gain_table, saved, p1, p2, g2, g2_low, gmix2):
    n1, q1, k1, v1, m1, s1, n2, q2, k2, v2, m2 = saved
    tokens, width = x.shape
    length = tokens // rows
    wq1, wk1, wv1, wo1, wq2, wk2, wv2 = weights[:7]
    gain_one, gain_two = (gain_table[:, i * width : (i + 1) * width] for i in range(2))
    tasks = gain_table.shape[0]
    block = BLOCK
    grid = (tokens // block,)
    act_shape = (tokens, width)
    square = 2 * tokens * width * width
    gq2, gk2, gv2 = attend_backward(False, rows, length, q2, k2, v2, m2, gmix2, p2)
    g1, g1_low, gmix1, gain2 = call(
        cross_back_kernel,
        grid,
        [
            by_row(gq2, block), whole(wq2), by_row(s1, block), by_row(task, block), whole(gain_two),
            by_row(g2, block), whole(wo1),
        ],
        [full_out(act_shape), low_out(act_shape), low_out(act_shape), out_whole((tasks, width), f32)],
        flops=2 * square,
        name="cross_back",
    )
    (mem_grad,) = call(
        memory_back_kernel,
        grid,
        [by_row(gk2, block), by_row(gv2, block), whole(wk2), whole(wv2)],
        [full_out(act_shape)],
        flops=2 * square,
        name="memory_back",
    )
    wo2_grad, wq2_grad, wk2_grad, wv2_grad = outers(
        (m2, n2, mem), (g2_low, gq2, gk2, gv2), (0, 1, 2, 2), "cross_grads"
    )
    gq1, gk1, gv1 = attend_backward(True, rows, length, q1, k1, v1, m1, gmix1, p1)
    input_grad, gain1 = call(
        input_back_kernel,
        grid,
        [
            by_row(gq1, block), by_row(gk1, block), by_row(gv1, block), whole(wq1), whole(wk1), whole(wv1),
            by_row(x, block), by_row(task, block), whole(gain_one), by_row(g1, block),
        ],
        [full_out(act_shape), out_whole((tasks, width), f32)],
        flops=3 * square,
        name="input_back",
    )
    wo1_grad, wq1_grad, wk1_grad, wv1_grad = outers(
        (m1, n1), (g1_low, gq1, gk1, gv1), (0, 1, 1, 1), "self_grads"
    )
    grads = (wq1_grad, wk1_grad, wv1_grad, wo1_grad, wq2_grad, wk2_grad, wv2_grad, wo2_grad)
    return input_grad, mem_grad, grads, gain1, gain2


LINE = 4
MESH = pl.DeviceIdType.MESH


class Place:
    def __init__(self):
        me = lax.axis_index("dp")
        self.core = lax.rem(me, 2)
        self.x = lax.rem(me // 2, 2)
        self.y = lax.rem(me // 4, 2)
        self.z = me // 8

    def at(self, z=None, y=None, x=None, core=None):
        z = self.z if z is None else z
        y = self.y if y is None else y
        x = self.x if x is None else x
        core = self.core if core is None else core
        return (((z * 2 + y) * 2 + x) * 2 + core,)

    def sibling(self):
        return self.at(core=1 - self.core)

    def over_x(self):
        return self.at(x=1 - self.x)

    def over_y(self):
        return self.at(y=1 - self.y)

    def along_z(self, k):
        return self.at(z=lax.rem(self.z + k, LINE))

    def partners(self):
        return [self.sibling(), self.over_x(), self.over_y()] + [self.along_z(k) for k in (1, 2, 3)]


def meet(place):
    barrier = pltpu.get_barrier_semaphore()
    partners = place.partners()
    for partner in partners:
        pl.semaphore_signal(barrier, inc=1, device_id=partner, device_id_type=MESH)
    pl.semaphore_wait(barrier, len(partners))


class Copies:
    def __init__(self, send, recv):
        self.send, self.recv, self.used, self.open = send, recv, 0, []

    def remote(self, source, target, device):
        copy = pltpu.make_async_remote_copy(
            src_ref=source,
            dst_ref=target,
            send_sem=self.send.at[self.used],
            recv_sem=self.recv.at[self.used],
            device_id=device,
            device_id_type=MESH,
        )
        self.used += 1
        copy.start()
        self.open.append(copy)
        return copy

    def local(self, source, target):
        copy = pltpu.make_async_copy(source, target, self.recv.at[self.used])
        self.used += 1
        copy.start()
        return copy

    def close(self, copy):
        copy.wait_send()
        self.open = [other for other in self.open if other is not copy]

    def finish(self):
        for copy in self.open:
            copy.wait_send()


class Unit:
    def __init__(self, here, copies, source, whole_array, index, first, second):
        self.here, self.copies = here, copies
        self.source, self.array = source, whole_array
        self.index, self.shares = index, (first, second)
        self.going = {}

    def window(self, zs, ys, xs, share=None):
        return self.array.at[(zs, ys, xs) + (self.index if share is None else self.shares[share])]

    def depart(self):
        here, copies = self.here, self.copies
        source = self.source()
        target = self.window(here.z, here.y, here.x)
        self.going["z"] = [copies.remote(source, target, here.along_z(k)) for k in (1, 2, 3)]
        self.own = copies.local(source, target)

    def turn(self):
        here = self.here
        for copy in self.going["z"]:
            copy.wait_recv()
        self.own.wait()
        one = self.window(slice(None), here.y, here.x, 0)
        two = self.window(slice(None), here.y, here.x, 1)
        self.going["1"] = [
            self.copies.remote(one, one, here.over_x()),
            self.copies.remote(two, two, here.over_y()),
        ]

    def turn_again(self):
        here = self.here
        for copy in self.going["1"]:
            copy.wait_recv()
        one = self.window(slice(None), here.y, slice(None), 0)
        two = self.window(slice(None), slice(None), here.x, 1)
        self.going["2"] = [
            self.copies.remote(one, one, here.over_y()),
            self.copies.remote(two, two, here.over_x()),
        ]

    def cross(self):
        for copy in self.going["2"]:
            copy.wait_recv()
        part = self.window(slice(None), slice(None), slice(None))
        self.going["c"] = self.copies.remote(part, part, self.here.sibling())

    def settle(self):
        self.going["c"].wait_recv()

    def stages(self):
        return (self.depart, self.turn, self.turn_again, self.cross, self.settle)


def column_of(row):
    length = row.shape[1]
    at_q = lax.broadcasted_iota(jnp.int32, (length, length), 0)
    at_k = lax.broadcasted_iota(jnp.int32, (length, length), 1)
    picked = jnp.where(at_q == at_k, row.astype(f32), 0.0)
    return jnp.sum(picked, axis=1, keepdims=True).astype(jnp.int32)


def forward_kernel(*refs):
    (
        x, mem, segments, mem_segments, tasks,
        sq, sk, sv, so, cq, ck, cv, co, w_in, w_out,
        table, weight, bias_row, down, up, gain,
    ) = refs[:21]
    outs, made_out, gains_out = refs[21:31], refs[31], refs[32]
    low_out, gain_out, task_out = refs[33:36]
    saved_out = refs[36:47]
    p1_out, p2_out = refs[47:49]
    scratch = refs[49:]
    wide, halves, blocks = scratch[:10], scratch[10:20], scratch[20:30]
    local_w = scratch[30:38]
    saved = scratch[38:49]
    n1, q1, k1, v1, m1, s1, n2, q2, k2, v2, m2 = saved
    made, gain_rows_all, bias, probs, send, recv, p_sem, load_sem, save_sem, gain_full = scratch[49:]
    own = (sq, sk, sv, so, cq, ck, cv, co, w_in, w_out)
    rows_total, length = segments.shape
    mem_len = mem_segments.shape[1]
    here = Place()
    copies = Copies(send, recv)
    c = here.core

    def half(i, core, first=0, width=None):
        full = own[i].shape[1] // 2
        width = full if width is None else width
        return pl.ds(pl.multiple_of(core * full + first, 128), width)

    for i in range(10):
        wide[i][...] = own[i][...].astype(f32)
    gain_rows_all[...] = gain[...].astype(f32)
    probs[...] = jnp.zeros_like(probs)
    meet(here)
    pair = {}
    order = (0, 1, 2, 5, 6, 3, 4, 7, 8, 9)
    for i in order:
        rows = own[i].shape[0]
        mine = pl.ds(pl.multiple_of(c * rows, 8), rows)
        pair[i] = copies.remote(
            wide[i].at[:, half(i, 1 - c)], halves[i].at[mine, :], here.sibling()
        )
        halves[i][mine, :] = wide[i][:, half(i, c)]

    opened = set()

    def piece(i, rows, first, width):
        def source():
            if i not in opened:
                opened.add(i)
                pair[i].wait_recv()
                blocks[i][...] = halves[i][...].astype(bf16)
            return blocks[i].at[rows, pl.ds(first, width)]

        at = half(i, c, first, width)
        count = rows.stop - rows.start
        if (width // 2) % 128 == 0:
            one = (rows, half(i, c, first, width // 2))
            two = (rows, half(i, c, first + width // 2, width // 2))
        else:
            cut = rows.start + (count // 2 if count % 32 == 0 else (count // 32 + i % 2) * 16)
            one = (slice(rows.start, cut), at)
            two = (slice(cut, rows.stop), at)
        return Unit(here, copies, source, outs[i], (rows, at), one, two)

    def square(i):
        return piece(i, slice(0, outs[i].shape[3]), 0, own[i].shape[1] // 2)

    gain_own = gain.shape[0]
    gain_cut = gain_own // 16 * 8
    made_cut = made.shape[1] // 2
    gain_unit = Unit(
        here, copies, lambda: gain_rows_all, gains_out, (c,),
        (c, pl.ds(0, gain_cut)), (c, pl.ds(gain_cut, gain_own - gain_cut)),
    )
    made_unit = Unit(
        here, copies, lambda: made, made_out, (c,),
        (c, slice(None), pl.ds(0, made_cut)), (c, slice(None), pl.ds(made_cut, made_cut)),
    )
    in_half = w_in.shape[1] // 4
    out_rows = outs[9].shape[3]
    units = [gain_unit] + [square(i) for i in (0, 1, 2, 5, 6, 3, 4, 7)]
    units += [piece(8, slice(0, outs[8].shape[3]), k * in_half, in_half) for k in (0, 1)]
    units += [made_unit]
    units += [
        piece(9, slice(k * out_rows // 2, (k + 1) * out_rows // 2), 0, w_out.shape[1] // 2)
        for k in (0, 1)
    ]
    loads = {}
    landing = {1: (0,), 2: (1,), 3: (2,), 4: (5,), 5: (6,), 6: (3,), 7: (4,), 8: (7,)}

    def tick(turn):
        for late in range(5):
            u = turn - late
            if 0 <= u < len(units):
                units[u].stages()[late]()
                if late == 4 and u in landing:
                    (i,) = landing[u]
                    loads[i] = pltpu.make_async_copy(outs[i], local_w[i], load_sem.at[i])
                    loads[i].start()
                if late == 4 and u == 0:
                    loads["gain"] = pltpu.make_async_copy(gains_out, gain_full, load_sem.at[8])
                    loads["gain"].start()


    def matrix(i):
        return local_w[i][...].reshape(-1, own[i].shape[1])

    state = gelu_in_kernel(exact_dot(table[...], weight[...]) + bias_row[...])
    low = state.astype(bf16)
    low_out[...] = low
    made[...] = jnp.zeros_like(made)
    made[:, : down.shape[0]] = inner_rows(low, down[...])
    made_at = made.shape[1] // 2
    made[:, made_at : made_at + up.shape[0]] = inner_rows(low, up[...])

    for now in range(8):
        tick(now)
    ticks = iter(range(8, len(units) + 4))

    def between():
        turn = next(ticks, None)
        if turn is not None:
            tick(turn)

    stores = []

    def store(which, part=None):
        source, target = saved[which], saved_out[which]
        copy = pltpu.make_async_copy(source, target, save_sem.at[which])
        copy.start()
        stores.append(copy)

    for r in range(rows_total):
        column = column_of(segments[r : r + 1, :])
        task = jnp.zeros_like(column)
        for s in range(tasks.shape[1]):
            task = task + jnp.where(column == s, tasks[r : r + 1, s : s + 1], 0)
        task_out[r * length : (r + 1) * length, :] = task
    loads["gain"].wait()
    width = x.shape[1]
    gain_out[...] = 1.0 + inner_rows(low, gain_full[...].reshape(-1, gain.shape[1]).astype(bf16))

    def picked(r, which):
        task = task_out[r * length : (r + 1) * length, :]
        return token_gain(task, gain_out[:, which * width : (which + 1) * width])

    def row(r, size=None):
        size = length if size is None else size
        return slice(r * size, (r + 1) * size)

    for i in (0, 1, 2):
        loads[i].wait()
    for r in range(rows_total):
        stream = x[row(r), :].astype(f32)
        n = (stream * inverse_rms(stream) * picked(r, 0)).astype(bf16)
        n1[row(r), :] = n
        q1[row(r), :] = (plain_dot(n, matrix(0)).astype(bf16).astype(f32) * HEAD**-0.5).astype(bf16)
        k1[row(r), :] = plain_dot(n, matrix(1)).astype(bf16)
        v1[row(r), :] = plain_dot(n, matrix(2)).astype(bf16)
        between()
    for which in (0, 1, 2, 3):
        store(which)


    def attend(causal, q, k, v, mixed, p_out, r, keys_row):
        column = column_of(segments[r : r + 1, :])
        same = column == keys_row
        if causal:
            at_q = lax.broadcasted_iota(jnp.int32, same.shape, 0)
            at_k = lax.broadcasted_iota(jnp.int32, same.shape, 1)
            same = same & (at_q >= at_k)
        bias[...] = jnp.where(same, 0.0, masked_score)
        keys_total = keys_row.shape[1]
        per_group = HEADS // 4
        for group in range(2):
            @pl.loop(group * per_group, (group + 1) * per_group)
            def _(p):
                slot = lax.rem(p, 2)
                at = pl.ds(pl.multiple_of(p * PAIR, PAIR), PAIR)

                @pl.when(p >= 2)
                def _():
                    pltpu.make_async_copy(
                        probs.at[slot], p_out.at[r, pl.ds(2 * p - 4, 2)], p_sem.at[slot]
                    ).wait()

                attend_pair(causal, q, k, v, mixed, probs.at[slot], bias, row(r), row(r, keys_total), at)
                pltpu.make_async_copy(
                    probs.at[slot], p_out.at[r, pl.ds(2 * p, 2)], p_sem.at[slot]
                ).start()

            between()
        for p in (HEADS // 2 - 2, HEADS // 2 - 1):
            pltpu.make_async_copy(
                probs.at[p % 2], p_out.at[r, pl.ds(2 * p, 2)], p_sem.at[p % 2]
            ).wait()

    for r in range(rows_total):
        attend(True, q1, k1, v1, m1, p1_out, r, segments[r : r + 1, :])
    store(4)
    for i in (5, 6):
        loads[i].wait()
    for r in range(rows_total):
        mine = row(r, mem_len)
        k2[mine, :] = plain_dot(mem[mine, :], matrix(5)).astype(bf16)
        v2[mine, :] = plain_dot(mem[mine, :], matrix(6)).astype(bf16)
        between()
    store(8)
    store(9)
    for i in (3, 4):
        loads[i].wait()
    for r in range(rows_total):
        stream = x[row(r), :].astype(f32) + plain_dot(m1[row(r), :], matrix(3))
        s1[row(r), :] = stream
        n = (stream * inverse_rms(stream) * picked(r, 1)).astype(bf16)
        n2[row(r), :] = n
        q2[row(r), :] = (plain_dot(n, matrix(4)).astype(bf16).astype(f32) * HEAD**-0.5).astype(bf16)
        between()
    for which in (5, 6, 7):
        store(which)
    for r in range(rows_total):
        attend(False, q2, k2, v2, m2, p2_out, r, mem_segments[r : r + 1, :])
    store(10)
    for turn in ticks:
        tick(turn)
    loads[7].wait()
    for copy in stores:
        copy.wait()
    copies.finish()


def gelu_in_kernel(v):
    return v * (0.5 * lax.erf(v * 0.7071067811865476) + 0.5)


def attend_pair(causal, q_ref, k_ref, v_ref, mixed_ref, p_ref, bias, q_rows, k_rows, at):
    length = q_rows.stop - q_rows.start
    keys_all = k_rows.stop - k_rows.start
    step = length // 2 if causal else length
    masks = half_masks()
    for first in range(0, length, step):
        rows = slice(q_rows.start + first, q_rows.start + first + step)
        keys = first + step if causal else keys_all
        q = q_ref[rows, at]
        k = k_ref[k_rows.start : k_rows.start + keys, at]
        v = v_ref[k_rows.start : k_rows.start + keys, at]
        out = None
        for h, mask in enumerate(masks):
            s = inner_rows(q * mask, k) + bias[first : first + step, :keys]
            e = jnp.exp(s - jnp.max(s, axis=-1, keepdims=True))
            p = (e * (1.0 / jnp.sum(e, axis=-1, keepdims=True))).astype(bf16)
            p_ref[h, first : first + step, :keys] = p
            part = plain_dot(p, v * mask)
            out = part if out is None else out + part
        mixed_ref[rows, at] = out.astype(bf16)


def forward(x, mem, segments, mem_segments, tasks, weights, table, weight, bias_row, makers):
    down, up, gain = makers
    own = weights
    tokens, width = x.shape
    mem_tokens = mem.shape[0]
    rows, length = segments.shape
    mem_len = mem_segments.shape[1]
    spaces = (LINE, 2, 2)
    any_space = pl.BlockSpec(memory_space=pl.ANY)
    vmem = pl.BlockSpec(memory_space=pltpu.VMEM)
    made_half = down.shape[0] + (-down.shape[0] % 128)
    n_tasks = table.shape[0]
    chip = [spaces + (2 * a.shape[0], a.shape[1]) for a in own]
    t_low, m_low, t_full = ((tokens, width), bf16), ((mem_tokens, width), bf16), ((tokens, width), f32)
    kept = [t_low, t_low, t_low, t_low, t_low, t_full, t_low, t_low, m_low, m_low, t_low]
    shape = jax.ShapeDtypeStruct
    probs = (rows, HEADS, length, mem_len)
    copies = 11 * 16 + 16
    outs = pl.pallas_call(
        forward_kernel,
        in_specs=[vmem] * 21,
        out_specs=[any_space] * 12 + [vmem] * 3 + [any_space] * 13,
        out_shape=[shape(s, bf16) for s in chip]
        + [
            shape(spaces + (2, n_tasks, 2 * made_half), f32),
            shape(spaces + (2,) + gain.shape, f32),
            shape((n_tasks, weight.shape[1]), bf16),
            shape((n_tasks, 3 * width), f32),
            shape((tokens, 1), jnp.int32),
        ]
        + [shape(s, d) for s, d in kept]
        + [shape((rows, HEADS, length, length), bf16), shape(probs, bf16)],
        scratch_shapes=[pltpu.VMEM(a.shape, f32) for a in own]
        + [pltpu.VMEM((2 * a.shape[0], a.shape[1] // 2), f32) for a in own]
        + [pltpu.VMEM((2 * a.shape[0], a.shape[1] // 2), bf16) for a in own]
        + [pltpu.VMEM(s, bf16) for s in chip[:8]]
        + [pltpu.VMEM(s, d) for s, d in kept]
        + [
            pltpu.VMEM((n_tasks, 2 * made_half), f32),
            pltpu.VMEM(gain.shape, f32),
            pltpu.VMEM((length, max(length, mem_len)), f32),
            pltpu.VMEM((2, 2, length, max(length, mem_len)), bf16),
            pltpu.SemaphoreType.DMA((copies,)),
            pltpu.SemaphoreType.DMA((copies,)),
            pltpu.SemaphoreType.DMA((2,)),
            pltpu.SemaphoreType.DMA((9,)),
            pltpu.SemaphoreType.DMA((11,)),
            pltpu.VMEM(spaces + (2,) + gain.shape, f32),
        ],
        compiler_params=pltpu.CompilerParams(
            collective_id=0, has_side_effects=True, vmem_limit_bytes=VMEM_BYTES
        ),
        name="forward_as_weights_arrive",
    )(x, mem, segments, mem_segments, tasks, *own, table, weight, bias_row, down, up, gain)
    return outs


class Stepwise:
    def __init__(self, stages):
        self.stages = list(stages)

    def advance(self):
        self.stages.pop(0)()


class Traffic:
    def __init__(self):
        self.ready, self.flying = [], []

    def add(self, item):
        self.ready.append(item)

    def tick(self):
        for item in list(self.flying):
            item.advance()
            if not item.stages:
                self.flying.remove(item)
        if self.ready:
            item = self.ready.pop(0)
            item.advance()
            self.flying.append(item)

    def drain(self):
        while self.ready or self.flying:
            self.tick()


class Summed(Stepwise):
    def __init__(self, here, copies, theirs, mine, shares, slots, out, out_first, fetch=None):
        super().__init__(
            [self.begin, self.over_first, self.over_second, self.over_line, self.to_owner, self.end]
        )
        self.here, self.copies = here, copies
        self.theirs, self.mine, self.fetch = theirs, mine, fetch
        self.shares, self.slots, self.out, self.out_first = shares, slots, out, out_first
        self.landed = None

    def begin(self):
        self.core = self.copies.remote(self.theirs, self.slots[0], self.here.sibling())
        if self.fetch is not None:
            self.local = self.copies.local(*self.fetch)

    def over_first(self):
        here, held = self.here, self.slots[0]
        if self.fetch is not None:
            self.local.wait()
        self.core.wait_recv()
        held[...] += self.mine()
        one, two = self.shares
        self.first = (
            self.copies.remote(held.at[(slice(None), 1 - here.y, slice(None)) + one], self.slots[1], here.over_y()),
            self.copies.remote(held.at[(slice(None), slice(None), 1 - here.x) + two], self.slots[2], here.over_x()),
        )

    def over_second(self):
        here, held = self.here, self.slots[0]
        one, two = self.shares
        self.first[0].wait_recv()
        held[(slice(None), here.y, slice(None)) + one] += self.slots[1][...]
        self.first[1].wait_recv()
        held[(slice(None), slice(None), here.x) + two] += self.slots[2][...]
        self.second = (
            self.copies.remote(held.at[(slice(None), here.y, 1 - here.x) + one], self.slots[3], here.over_x()),
            self.copies.remote(held.at[(slice(None), 1 - here.y, here.x) + two], self.slots[4], here.over_y()),
        )

    def over_line(self):
        here, held = self.here, self.slots[0]
        one, two = self.shares
        self.second[0].wait_recv()
        held[(slice(None), here.y, here.x) + one] += self.slots[3][...]
        self.second[1].wait_recv()
        held[(slice(None), here.y, here.x) + two] += self.slots[4][...]
        self.third = [
            self.copies.remote(
                held.at[lax.rem(here.z + k, LINE), here.y, here.x],
                self.slots[5].at[k - 1],
                here.along_z(k),
            )
            for k in (1, 2, 3)
        ]

    def window(self, core, width, full):
        return pl.ds(pl.multiple_of(core * full + self.out_first, 128), width)

    def to_owner(self):
        here, held, final = self.here, self.slots[0], self.slots[6]
        total = held[here.z, here.y, here.x].astype(f32)
        for k, copy in enumerate(self.third):
            copy.wait_recv()
            total = total + self.slots[5][k].astype(f32)
        final[...] = total
        rows, full = self.out.shape[0], self.out.shape[1] // 2
        c = here.core
        at = self.window(c, final.shape[1], full)
        theirs = pl.ds(pl.multiple_of((1 - c) * rows, 8), rows)
        self.last = self.copies.remote(final.at[theirs, :], self.out.at[:, at], here.sibling())
        self.out[:, at] = final[pl.ds(pl.multiple_of(c * rows, 8), rows), :]

    def end(self):
        self.last.wait_recv()
        if self.landed is not None:
            self.landed()


class Everywhere(Stepwise):
    def __init__(self, here, copies, value, sent, arriving, out):
        super().__init__([self.begin, self.step_x, self.step_y, self.step_z, self.end])
        self.here, self.copies, self.value = here, copies, value
        self.sent, self.arriving, self.out = sent, arriving, out

    def send(self, turn, device):
        self.sent[turn] = self.total
        self.copy = self.copies.remote(self.sent.at[turn], self.arriving.at[turn], device)

    def add(self, turn):
        self.copy.wait_recv()
        self.total = self.total + self.arriving[turn]

    def begin(self):
        self.total = self.value()
        self.send(0, self.here.sibling())

    def step_x(self):
        self.add(0)
        self.send(1, self.here.over_x())

    def step_y(self):
        self.add(1)
        self.send(2, self.here.over_y())

    def step_z(self):
        self.add(2)
        self.sent[3] = self.total
        self.around = [
            self.copies.remote(self.sent.at[3], self.arriving.at[2 + k], self.here.along_z(k))
            for k in (1, 2, 3)
        ]

    def end(self):
        for copy in self.around:
            copy.wait_recv()
        total = jnp.zeros_like(self.total)
        for line in range(LINE):
            for k in range(LINE):
                term = self.total if k == 0 else self.arriving[2 + k]
                here_now = lax.rem(self.here.z - k + LINE, LINE) == line
                total = total + jnp.where(here_now, term, 0.0)
        self.out[...] = total


def attend_pair_back(causal, q_ref, k_ref, v_ref, mixed_ref, gm_ref, p_ref, gq_ref, gk_ref, gv_ref, start, k_start, at, length, keys_all):
    step = length // 2 if causal else length
    masks = half_masks()
    gk_parts, gv_parts = [], []
    for first in range(0, length, step):
        rows = pl.ds(start + first, step)
        keys = first + step if causal else keys_all
        key_rows = pl.ds(k_start, keys)
        q, k, v = q_ref[rows, at], k_ref[key_rows, at], v_ref[key_rows, at]
        gm = gm_ref[rows, at]
        product = gm.astype(f32) * mixed_ref[rows, at].astype(f32)
        gq = gk = gv = 0.0
        for h, mask in enumerate(masks):
            inner = jnp.sum(product * mask.astype(f32), axis=-1, keepdims=True)
            p = p_ref[h, first : first + step, :keys]
            gm_half = gm * mask
            gw = inner_rows(gm_half, v)
            gs = (p.astype(f32) * (gw - inner)).astype(bf16)
            gv = gv + inner_cols(p, gm_half)
            gq = gq + plain_dot(gs, k * mask)
            gk = gk + inner_cols(gs, q * mask)
        gq_ref[rows, at] = (gq * HEAD**-0.5).astype(bf16)
        gk_parts.append(gk)
        gv_parts.append(gv)
    for ref, terms in ((gk_ref, gk_parts), (gv_ref, gv_parts)):
        if not causal:
            ref[pl.ds(k_start, keys_all), at] = terms[0].astype(bf16)
        else:
            ref[pl.ds(k_start, step), at] = (terms[0] + terms[1][:step]).astype(bf16)
            ref[pl.ds(k_start + step, step), at] = terms[1][step:].astype(bf16)


SUM_NAMES = ("q1", "k1", "v1", "o1", "q2", "k2", "v2", "o2", "in0", "in1", "out0", "out1", "small")


def sum_pieces(width, units, own):
    rows = 2 * own
    half = width // 2
    pieces = {}
    for turn, name in enumerate(SUM_NAMES[:8]):
        cut = rows // 2 if rows % 32 == 0 else (rows // 32 + turn % 2) * 16
        pieces[name] = (rows, half, 0, (slice(0, cut), slice(0, half)), (slice(cut, rows), slice(0, half)))
    part = units // 4
    for k in (0, 1):
        pieces[f"in{k}"] = (
            rows, part, k * part,
            (slice(0, rows), slice(0, part // 2)), (slice(0, rows), slice(part // 2, part)),
        )
    out_rows = rows * units // width
    third = half // 3
    for k, (first, size) in enumerate(((0, third), (third, half - third))):
        pieces[f"out{k}"] = (
            out_rows, size, first,
            (slice(0, out_rows // 2), slice(0, size)), (slice(out_rows // 2, out_rows), slice(0, size)),
        )
    pieces["small"] = (32, half, 0, (slice(0, 16), slice(0, half)), (slice(16, 32), slice(0, half)))
    return pieces


def backward_kernel(sizes, *refs):
    rows_total, length, mem_len, width, units, own_rows = sizes
    pieces = sum_pieces(width, units, own_rows)
    (
        p1, p2, q2h, k2h, v2h, m2h, gm2h, q1h, k1h, v1h, m1h, n1h, n2h, memh, xh, s1h, g2h, g2lowh,
        wq1h, wk1h, wv1h, wo1h, wq2h, wk2h, wv2h, g_in, g_out, g_small,
        task, gains, gain_three, down, up,
    ) = refs[:33]
    mem_out, input_out = refs[33:35]
    outs = refs[35:46]
    gain_out, state_out = refs[46:48]
    scratch = refs[48:]
    a = scratch[:5]
    gq, gk, gv = scratch[5:8]
    f0, f1, low = scratch[8:11]
    probs = scratch[11]
    w = scratch[12:16]
    grads = scratch[16:20]
    stage_in, stage_out, stage_small = scratch[20:23]
    slots = {}
    at_slot = 23
    for name in SUM_NAMES:
        slots[name] = scratch[at_slot : at_slot + 7]
        at_slot += 7
    state_sent, state_arriving, gain_sent, gain_arriving, gain_rows_ref = scratch[at_slot : at_slot + 5]
    send, recv, p_sem, load_sem = scratch[at_slot + 5 :]
    here = Place()
    copies = Copies(send, recv)
    traffic = Traffic()
    c = here.core
    loads = {}

    def fetch(name, source, target):
        loads[name] = pltpu.make_async_copy(source, target, load_sem.at[len(loads)])
        loads[name].start()

    def need(*names):
        for name in names:
            loads[name].wait()

    def half(which, first, size, full):
        return pl.ds(pl.multiple_of(which * full + first, 128), size)

    fetch("m2", m2h, a[3])
    fetch("g2low", g2lowh, low)
    fetch("q2", q2h, a[0])
    fetch("k2", k2h, a[1])
    fetch("v2", v2h, a[2])
    fetch("gm2", gm2h, a[4])

    def probs_copy(source, index):
        return pltpu.make_async_copy(source.at[index], probs.at[lax.rem(index, 2)], p_sem.at[lax.rem(index, 2)])

    pairs = HEADS // 2
    count = rows_total * pairs
    for index in (0, 1):
        probs_copy(p2, index).start()
    fetch("wq2", wq2h, w[0])
    fetch("wo1", wo1h, w[1])
    fetch("wk2", wk2h, w[2])
    fetch("wv2", wv2h, w[3])
    fetch("s1", s1h, f0)
    fetch("g2", g2h, f1)
    meet(here)

    def from_hbm(name, array, out, stage):
        rows, size, first, one, two = pieces[name]
        full = array.shape[4] // 2
        return Summed(
            here, copies, array.at[:, :, :, :, half(1 - c, first, size, full)], lambda: stage[...],
            (one, two), slots[name], out, first,
            fetch=(array.at[:, :, :, :, half(c, first, size, full)], stage),
        )

    for item in (
        from_hbm("out0", g_out, outs[9], stage_out.at[:, :, :, :, : pieces["out0"][1]]),
        from_hbm("out1", g_out, outs[9], stage_out),
        from_hbm("small", g_small, outs[10], stage_small),
        from_hbm("in0", g_in, outs[8], stage_in),
        from_hbm("in1", g_in, outs[8], stage_in),
    ):
        traffic.add(item)
        if item.out is outs[10]:
            small_item = item

    def small_landed():
        made = down.shape[0]
        small = outs[10]
        state = plain_dot(small[0:8, :made].astype(bf16), down[...])
        state = state + plain_dot(small[8:16, :made].astype(bf16), up[...])
        traffic.add(Everywhere(here, copies, lambda: state, state_sent, state_arriving, state_out))

    small_item.landed = small_landed
    users = {}

    def weight_gradient(name, index, source, grad, slot):
        if slot in users:
            copies.close(users[slot].core)
        buffer = grads[slot]
        rows, size, first, one, two = pieces[name]
        columns = width // 2
        for k in range(2):
            block = inner_cols(source[:, k * columns : (k + 1) * columns], grad[...]).astype(bf16)
            buffer[2 * k : 2 * k + 2] = block.reshape((2, 2, 2, rows, width))
        full = width // 2
        item = Summed(
            here, copies, buffer.at[:, :, :, :, half(1 - c, 0, size, full)],
            lambda: buffer[:, :, :, :, half(c, 0, size, full)],
            (one, two), slots[name], outs[index], 0,
        )
        users[slot] = item
        traffic.add(item)

    def matrix(k):
        return w[k][...].reshape(width, width)

    def row(r, size=None):
        size = length if size is None else size
        return slice(r * size, (r + 1) * size)

    def picked(r, which):
        return token_gain(task[row(r), :], gains[:, which * width : (which + 1) * width])

    def attention(causal, q, k, v, m, gm, source, keys_all):
        per_group = 2
        for group in range(count // per_group):
            @pl.loop(group * per_group, (group + 1) * per_group)
            def _(index):
                slot = lax.rem(index, 2)
                probs_copy(source, index).wait()
                r, p = index // pairs, lax.rem(index, pairs)
                at = pl.ds(pl.multiple_of(p * PAIR, PAIR), PAIR)
                attend_pair_back(
                    causal, q, k, v, m, gm, probs.at[slot], gq, gk, gv,
                    pl.multiple_of(r * length, length), pl.multiple_of(r * keys_all, keys_all), at, length, keys_all,
                )

                @pl.when(index + 2 < count)
                def _():
                    probs_copy(source, index + 2).start()

            traffic.tick()

    traffic.tick()
    need("m2", "g2low")
    weight_gradient("o2", 7, a[3], low, 0)
    traffic.tick()
    need("q2", "k2", "v2", "gm2")
    attention(False, a[0], a[1], a[2], a[3], a[4], p2, mem_len)
    for index in (0, 1):
        probs_copy(p1, index).start()
    fetch("n2", n2h, a[0])
    fetch("mem", memh, a[1])
    fetch("v1", v1h, a[2])
    fetch("m1", m1h, a[3])
    need("wq2", "wo1", "s1", "g2")
    gain_two = None
    for r in range(rows_total):
        stream = f0[row(r), :]
        stream_grad, gain_tokens = norm_back(stream, picked(r, 1), inner_rows(gq[row(r), :], matrix(0)))
        grad_one = f1[row(r), :] + stream_grad
        f1[row(r), :] = grad_one
        low_now = grad_one.astype(bf16)
        low[row(r), :] = low_now
        a[4][row(r), :] = inner_rows(low_now, matrix(1)).astype(bf16)
        now = gain_rows(task[row(r), :], gain_tokens)
        gain_two = now if gain_two is None else gain_two + now
        traffic.tick()
    fetch("wq1", wq1h, w[0])
    fetch("wk1", wk1h, w[1])
    need("n2", "mem")
    for name, index, source, grad, slot in (
        ("q2", 4, a[0], gq, 1), ("k2", 5, a[1], gk, 2), ("v2", 6, a[1], gv, 3)
    ):
        weight_gradient(name, index, source, grad, slot)
        traffic.tick()
    fetch("q1", q1h, a[0])
    fetch("k1", k1h, a[1])
    need("wk2", "wv2")
    for r in range(rows_total):
        mine = row(r, mem_len)
        f0[mine, :] = inner_rows(gk[mine, :], matrix(2)) + inner_rows(gv[mine, :], matrix(3))
        traffic.tick()
    fetch("mem_out", f0, mem_out)
    fetch("wv1", wv1h, w[2])
    need("m1")
    weight_gradient("o1", 3, a[3], low, 0)
    traffic.tick()
    need("q1", "k1", "v1")
    attention(True, a[0], a[1], a[2], a[3], a[4], p1, length)
    fetch("n1", n1h, a[0])
    fetch("x", xh, a[1])
    need("n1")
    for name, index, grad, slot in (("q1", 0, gq, 1), ("k1", 1, gk, 2), ("v1", 2, gv, 3)):
        weight_gradient(name, index, a[0], grad, slot)
        traffic.tick()
    need("x", "wq1", "wk1", "wv1")
    gain_one = None
    for r in range(rows_total):
        stream = a[1][row(r), :].astype(f32)
        cotan = inner_rows(gq[row(r), :], matrix(0)) + inner_rows(gk[row(r), :], matrix(1))
        cotan = cotan + inner_rows(gv[row(r), :], matrix(2))
        stream_grad, gain_tokens = norm_back(stream, picked(r, 0), cotan)
        f1[row(r), :] += stream_grad
        now = gain_rows(task[row(r), :], gain_tokens)
        gain_one = now if gain_one is None else gain_one + now
        traffic.tick()
    fetch("input_out", f1, input_out)
    gain_rows_ref[:, :width] = gain_one
    gain_rows_ref[:, width : 2 * width] = gain_two
    gain_rows_ref[:, 2 * width :] = gain_three[...]
    traffic.ready.insert(0, Everywhere(here, copies, lambda: gain_rows_ref[...], gain_sent, gain_arriving, gain_out))
    traffic.drain()
    need("mem_out", "input_out")
    copies.finish()


def backward(mem_len, saved, probs, x, mem, weights, g2, g2_low, gmix2, g_in, g_out, g_small, task, gains, gain_three, down, up, own):
    n1, q1, k1, v1, m1, s1, n2, q2, k2, v2, m2 = saved
    p1, p2 = (p.reshape((-1, 2) + p.shape[2:]) for p in probs)
    rows = probs[0].shape[0]
    tokens, width = x.shape
    length = tokens // rows
    units = own[8].shape[1]
    own_rows = own[0].shape[0]
    any_space = pl.BlockSpec(memory_space=pl.ANY)
    vmem = pl.BlockSpec(memory_space=pltpu.VMEM)
    shape = jax.ShapeDtypeStruct
    act, full = pltpu.VMEM((tokens, width), bf16), pltpu.VMEM((tokens, width), f32)
    mem_act = pltpu.VMEM((max(tokens, mem.shape[0]), width), bf16)
    square = pltpu.VMEM((LINE, 2, 2, 2 * own_rows, width), bf16)
    pieces = sum_pieces(width, units, own_rows)
    slots = []
    for name in SUM_NAMES:
        r, size, _, one, two = pieces[name]
        extent = [tuple(s.stop - s.start for s in share) for share in (one, two)]
        slots += [
            pltpu.VMEM((LINE, 2, 2, r, size), bf16),
            pltpu.VMEM((LINE, 2) + extent[0], bf16),
            pltpu.VMEM((LINE, 2) + extent[1], bf16),
            pltpu.VMEM((LINE,) + extent[0], bf16),
            pltpu.VMEM((LINE,) + extent[1], bf16),
            pltpu.VMEM((LINE - 1, r, size), bf16),
            pltpu.VMEM((r, size), f32),
        ]

    def stage(name):
        r, size = pieces[name][:2]
        return (LINE, 2, 2, r, size)

    tasks, hidden = gains.shape[0], down.shape[1]
    copies = 200
    ins_any = (
        p1, p2, q2, k2, v2, m2, gmix2, q1, k1, v1, m1, n1, n2, mem, x, s1, g2, g2_low,
        *(weights[i] for i in range(7)), g_in, g_out, g_small,
    )
    return pl.pallas_call(
        functools.partial(backward_kernel, (rows, length, mem_len, width, units, own_rows)),
        in_specs=[any_space] * len(ins_any) + [vmem] * 5,
        out_specs=[any_space] * 2 + [vmem] * 13,
        out_shape=[shape((mem.shape[0], width), f32), shape((tokens, width), f32)]
        + [shape(g.shape, f32) for g in own]
        + [shape((16, width), f32), shape(gains.shape, f32), shape((tasks, hidden), f32)],
        scratch_shapes=[act] * 5 + [act, mem_act, mem_act] + [full, full, act]
        + [pltpu.VMEM((2, 2, length, max(length, mem_len)), bf16)]
        + [square] * 4
        + [square] * 4
        + [
            pltpu.VMEM(stage("in0"), bf16),
            pltpu.VMEM(stage("out1"), bf16),
            pltpu.VMEM(stage("small"), bf16),
        ]
        + slots
        + [
            pltpu.VMEM((4, tasks, hidden), f32),
            pltpu.VMEM((6, tasks, hidden), f32),
            pltpu.VMEM((4,) + gains.shape, f32),
            pltpu.VMEM((6,) + gains.shape, f32),
            pltpu.VMEM(gains.shape, f32),
            pltpu.SemaphoreType.DMA((copies,)),
            pltpu.SemaphoreType.DMA((copies,)),
            pltpu.SemaphoreType.DMA((2,)),
            pltpu.SemaphoreType.DMA((32,)),
        ],
        compiler_params=pltpu.CompilerParams(
            collective_id=1, has_side_effects=True, vmem_limit_bytes=63 << 20
        ),
        name="backward_as_gradients_leave",
    )(*ins_any, task, gains, gain_three, down, up)


def finish_kernel(count, *refs):
    shards, small, gain_sum, state, gain_all, low, table, weight, bias_row = (
        refs[:count], *refs[count : count + 8]
    )
    outs = refs[count + 8 : 2 * count + 8]
    down_out, up_out, gain_out, table_out, weight_out, bias_out, rows = refs[2 * count + 8 :]
    for shard, out in zip(shards, outs):
        out[...] = shard[...]
    made = down_out.shape[0]
    low_now = low[...]
    down_out[...] = inner_cols(small[0:8, :made].astype(bf16), low_now)
    up_out[...] = inner_cols(small[8:16, :made].astype(bf16), low_now)
    rows[...] = inner_cols(gain_sum[...], low_now.astype(f32), exact_mode)
    owned = gain_out.shape[0]
    me = lax.axis_index("dp")
    gain_out[...] = rows[pl.ds(pl.multiple_of(me * owned, 8), owned), :]
    makers = gain_all[...].reshape(-1, gain_all.shape[-1])
    state_grad = state[...] + exact_dot(gain_sum[...], makers)
    before = exact_dot(table[...], weight[...]) + bias_row[...]
    pre_grad = gelu_both(before)[1] * state_grad
    bias_out[...] = jnp.sum(pre_grad, axis=0, keepdims=True)
    weight_out[...] = inner_cols(table[...], pre_grad, exact_mode)
    table_out[...] = lax.dot_general(
        pre_grad, weight[...], (((1,), (1,)), ((), ())), precision=exact_mode, preferred_element_type=f32
    )


def finish(shards, small, gain_sum, state, gain_all, low, table, weight, bias_row, makers):
    down, up, gain = makers
    shape = jax.ShapeDtypeStruct
    vmem = pl.BlockSpec(memory_space=pltpu.VMEM)
    ins = (*shards, small, gain_sum, state, gain_all, low, table, weight, bias_row)
    outs = [shape(s.shape, f32) for s in shards]
    outs += [shape(m.shape, f32) for m in makers] + [shape(a.shape, f32) for a in (table, weight, bias_row)]
    return pl.pallas_call(
        functools.partial(finish_kernel, len(shards)),
        in_specs=[vmem] * len(ins),
        out_specs=[vmem] * len(outs),
        out_shape=outs,
        scratch_shapes=[pltpu.VMEM((gain_sum.shape[1], low.shape[1]), f32)],
        compiler_params=pltpu.CompilerParams(vmem_limit_bytes=VMEM_BYTES),
        name="finish",
    )(*ins)


def on_device(
    block_input, memory, cotangent, segments, memory_segments, task_of_segment,
    self_query, self_key, self_value, self_output,
    cross_query, cross_key, cross_value, cross_output,
    hidden_in, hidden_out, task_table, task_weight, task_bias,
    down_maker, up_maker, gain_maker,
):
    row_count, seq_len, model_width = block_input.shape
    mem_len = memory.shape[1]
    task_count = task_table.shape[0]
    token_count = row_count * seq_len
    parts = lax.axis_size("dp")
    weights = (
        self_query, self_key, self_value, self_output,
        cross_query, cross_key, cross_value, cross_output, hidden_in, hidden_out,
    )
    task_state, task_back = jax.vjp(task_network, task_table, task_weight, task_bias)
    task_low = task_state.astype(bf16)
    down_own, gain_own = down_maker.shape[0], gain_maker.shape[0]
    makers = (down_maker, up_maker, gain_maker)
    x = block_input.reshape(token_count, model_width)
    mem = memory.reshape(row_count * mem_len, model_width)

    def joined(block):
        return block.transpose(1, 0, 2).reshape(task_count, -1)

    if parts == 32:
        outs = forward(
            x, mem, segments, memory_segments, task_of_segment, weights,
            task_table, task_weight, task_bias.reshape(1, -1), makers,
        )
        backbone = [w.reshape(-1, w.shape[-1]) for w in outs[:10]]
        made = outs[10].reshape(parts, task_count, -1)
        task_low, gain_table, token_task = outs[12:15]
        saved, probs_one, probs_two = outs[15:26], outs[26], outs[27]
        made_up = joined(made[:, :, made.shape[2] // 2 :][:, :, :down_own]).astype(bf16)
    else:
        packed = jnp.concatenate([w.reshape(-1, model_width) for w in weights], axis=0)
        packed = lax.all_gather(packed, "dp", axis=0, tiled=False)
        backbone, at = [], 0
        for w in weights:
            count = w.size // model_width
            backbone.append(packed[:, at : at + count].reshape(-1, w.shape[1]))
            at += count
        made = inner_rows(task_low, jnp.concatenate(makers, axis=0))
        made = lax.all_gather(made, "dp", axis=0, tiled=False)
        gain_table = 1.0 + joined(made[:, :, 2 * down_own :])
        seg_match = segments[:, :, None] == jnp.arange(task_of_segment.shape[1], dtype=jnp.int32)
        token_task = jnp.sum(
            jnp.where(seg_match, task_of_segment[:, None, :], 0), axis=-1
        ).reshape(token_count, 1)
        saved, probs_one, probs_two = attention_layers(
            x, mem, segments, memory_segments, token_task, backbone, gain_table
        )
        made_up = joined(made[:, :, down_own : 2 * down_own]).astype(bf16)
    made_down = joined(made[:, :, :down_own]).astype(bf16)
    down_all = (
        made_down.reshape(task_count, model_width, ADA)
        .transpose(1, 0, 2)
        .reshape(model_width, task_count * ADA)
    )
    up_all = made_up.reshape(task_count * ADA, model_width)
    cot = cotangent.reshape(token_count, model_width)
    output, g2, g2_low, gmix2, hidden_in_grad, hidden_out_grad, up_grad, down_grad, gain_three = feed_forward(
        saved[5], saved[10], cot, token_task, backbone, gain_table, down_all, up_all
    )
    down_rows = (
        down_grad.reshape(parts, -1, task_count, ADA)
        .transpose(0, 2, 1, 3)
        .reshape(parts, task_count, down_own)
    )
    up_rows = up_grad.reshape(task_count, parts, -1).transpose(1, 0, 2)
    if parts == 32:
        small = jnp.concatenate((down_rows, up_rows), axis=1).astype(bf16)
        small = jnp.pad(small, ((0, 0), (0, 0), (0, model_width - down_own)))
        in_grad = hidden_in_grad.reshape((LINE, 2, 2, -1, hidden_in.shape[1]))
        out_grad = hidden_out_grad.reshape((LINE, 2, 2, -1, model_width))
        mem_grad, input_grad, *shared, small, gain_sum, state = backward(
            mem_len, saved, (probs_one, probs_two), x, mem, outs[:7], g2, g2_low, gmix2, in_grad, out_grad,
            small.reshape(LINE, 2, 2, 4 * task_count, model_width), token_task, gain_table, gain_three,
            down_maker, up_maker, weights,
        )
        *shared, down_maker_grad, up_maker_grad, gain_maker_grad, table_grad, weight_grad, bias_grad = finish(
            shared, small, gain_sum, state, outs[11], task_low, task_table, task_weight,
            task_bias.reshape(1, -1), makers,
        )
        bias_grad = bias_grad.reshape(task_bias.shape)
    else:
        input_grad, mem_grad, grads, gain_one, gain_two = attention_back(
            x, mem, row_count, token_task, backbone, gain_table, saved, probs_one, probs_two, g2, g2_low, gmix2
        )
        grads = (*grads, hidden_in_grad, hidden_out_grad)
        packed = jnp.concatenate([g.reshape(parts, -1, model_width) for g in grads], axis=1)
        packed = lax.psum_scatter(packed, "dp", scatter_dimension=0, tiled=False).astype(f32)
        shared, at = [], 0
        for w in weights:
            count = w.size // model_width
            shared.append(packed[at : at + count].reshape(w.shape))
            at += count
        gain_grad = jnp.concatenate((gain_one, gain_two, gain_three), axis=1)
        gain_rows_all = gain_grad.reshape(task_count, parts, -1).transpose(1, 0, 2)
        small = jnp.concatenate((down_rows, up_rows, gain_rows_all), axis=2)
        small = lax.psum_scatter(small, "dp", scatter_dimension=0, tiled=False)
        own_down = small[:, :down_own].astype(bf16)
        own_up = small[:, down_own : 2 * down_own].astype(bf16)
        own_gain = small[:, 2 * down_own :]
        state_grad = lax.psum(
            plain_dot(own_down, down_maker)
            + plain_dot(own_up, up_maker)
            + exact_dot(own_gain, gain_maker.astype(f32)),
            "dp",
        )
        down_maker_grad = inner_cols(own_down, task_low)
        up_maker_grad = inner_cols(own_up, task_low)
        gain_maker_grad = inner_cols(own_gain, task_low.astype(f32), exact_mode)
        table_grad, weight_grad, bias_grad = task_back(state_grad)
    return (
        output.reshape(row_count, seq_len, model_width),
        input_grad.reshape(row_count, seq_len, model_width),
        mem_grad.reshape(row_count, mem_len, model_width),
        *shared,
        table_grad,
        weight_grad,
        bias_grad,
        down_maker_grad,
        up_maker_grad,
        gain_maker_grad,
    )


def solution(mesh):
    rows, whole_copy = P("dp"), P()
    return jax.shard_map(
        on_device,
        mesh=mesh,
        in_specs=(rows,) * 16 + (whole_copy,) * 3 + (rows,) * 3,
        out_specs=(rows,) * 13 + (whole_copy,) * 3 + (rows,) * 3,
        check_vma=False,
    )
```

```python
import functools

import jax
import jax.numpy as jnp
from jax import lax
from jax.experimental import pallas as pl
from jax.experimental.pallas import tpu as pltpu
from jax.sharding import PartitionSpec as P

HEADS = 12
HEAD = 64
ADA = 24
PAIR = 2 * HEAD

exact_mode = lax.Precision.HIGHEST
norm_eps = 1e-06
masked_score = -1e30
bf16 = jnp.bfloat16
f32 = jnp.float32
VMEM_BYTES = 56 << 20


def plain_dot(left_side, right_side):
    return jnp.dot(left_side, right_side, preferred_element_type=f32)


def exact_dot(left_side, right_side):
    return jnp.dot(left_side, right_side, precision=exact_mode, preferred_element_type=f32)


def inner_rows(left_side, right_side):
    return lax.dot_general(
        left_side, right_side, (((1,), (1,)), ((), ())), preferred_element_type=f32
    )


def inner_cols(left_side, right_side, precision_mode=None):
    return lax.dot_general(
        left_side,
        right_side,
        (((0,), (0,)), ((), ())),
        precision=precision_mode,
        preferred_element_type=f32,
    )


def gelu_exact(operand):
    return jax.nn.gelu(operand, approximate=False)


def task_network(table_rows, weight_in, bias_row):
    return gelu_exact(exact_dot(table_rows, weight_in) + bias_row)


def gelu_both(v):
    phi = 0.5 * lax.erf(v * 0.7071067811865476) + 0.5
    slope = phi + v * (jnp.exp(v * v * -0.5) * 0.3989422804014327)
    return v * phi, slope


def token_gain(task_column, gain):
    high = gain.astype(bf16).astype(f32)
    rest = gain - high
    middle = rest.astype(bf16).astype(f32)
    table = jnp.concatenate((high, middle, rest - middle), axis=0).astype(bf16)
    which = lax.broadcasted_iota(jnp.int32, (task_column.shape[0], 24), 1) & 7
    hot = jnp.where(which == task_column, 1.0, 0.0).astype(bf16)
    return plain_dot(hot, table)


def gain_rows(task_column, grads):
    which = lax.broadcasted_iota(jnp.int32, (task_column.shape[0], 8), 1)
    hot = jnp.where(which == task_column, 1.0, 0.0).astype(bf16)
    high = grads.astype(bf16)
    low = (grads - high.astype(f32)).astype(bf16)
    return inner_cols(hot, high) + inner_cols(hot, low)


def inverse_rms(stream):
    return lax.rsqrt(jnp.mean(stream * stream, axis=-1, keepdims=True) + norm_eps)


def norm_back(stream, gain, cotan):
    r = inverse_rms(stream)
    scaled = cotan * gain
    inner = jnp.mean(scaled * stream, axis=-1, keepdims=True)
    return r * (scaled - stream * (r * r * inner)), cotan * (stream * r)


def call(kernel, grid, ins, outs, scratch=(), flops=0, name=None):
    size = sum(a.size * a.dtype.itemsize for a, _, _ in ins)
    size += sum(functools.reduce(lambda p, q: p * q, s, 1) * jnp.dtype(d).itemsize for s, d, _, _ in outs)
    return pl.pallas_call(
        kernel,
        grid=grid,
        in_specs=[pl.BlockSpec(b, m) for _, b, m in ins],
        out_specs=[pl.BlockSpec(b, m) for _, _, b, m in outs],
        out_shape=[jax.ShapeDtypeStruct(s, d) for s, d, _, _ in outs],
        scratch_shapes=list(scratch),
        compiler_params=pltpu.CompilerParams(vmem_limit_bytes=VMEM_BYTES),
        cost_estimate=pl.CostEstimate(flops=flops, bytes_accessed=size, transcendentals=0),
        name=name,
    )(*[a for a, _, _ in ins])


def whole(array):
    return (array, array.shape, lambda *_: (0,) * array.ndim)


def by_row(array, rows):
    return (array, (rows,) + array.shape[1:], lambda i: (i,) + (0,) * (array.ndim - 1))


def out_row(shape, dtype, rows):
    return (shape, dtype, (rows,) + shape[1:], lambda i: (i,) + (0,) * (len(shape) - 1))


def out_whole(shape, dtype):
    return (shape, dtype, shape, lambda *_: (0,) * len(shape))


def pre_kernel(x, task, gain, wq, wk, wv, normed, q, k, v):
    stream = x[...].astype(f32)
    n = (stream * inverse_rms(stream) * token_gain(task[...], gain[...])).astype(bf16)
    normed[...] = n
    q[...] = (plain_dot(n, wq[...]).astype(bf16).astype(f32) * HEAD**-0.5).astype(bf16)
    k[...] = plain_dot(n, wk[...]).astype(bf16)
    v[...] = plain_dot(n, wv[...]).astype(bf16)


def memory_kernel(x, wk, wv, k, v):
    k[...] = plain_dot(x[...], wk[...]).astype(bf16)
    v[...] = plain_dot(x[...], wv[...]).astype(bf16)


def middle_kernel(x, mixed, wo, task, gain, wq, stream_out, normed, q):
    stream = x[...].astype(f32) + plain_dot(mixed[...], wo[...])
    stream_out[...] = stream
    n = (stream * inverse_rms(stream) * token_gain(task[...], gain[...])).astype(bf16)
    normed[...] = n
    q[...] = (plain_dot(n, wq[...]).astype(bf16).astype(f32) * HEAD**-0.5).astype(bf16)


def half_masks():
    lane = lax.broadcasted_iota(jnp.int32, (1, PAIR), 1)
    first = jnp.where(lane < HEAD, 1.0, 0.0)
    return first.astype(bf16), (1.0 - first).astype(bf16)


def attend_forward_kernel(causal, q_ref, k_ref, v_ref, seg_q, seg_k, mixed_ref, p_ref, bias):
    length, keys_all = q_ref.shape[0], k_ref.shape[0]
    step = length // 2 if causal else length

    @pl.when(pl.program_id(1) == 0)
    def _():
        same = seg_q[...] == seg_k[0]
        if causal:
            at_q = lax.broadcasted_iota(jnp.int32, (length, keys_all), 0)
            at_k = lax.broadcasted_iota(jnp.int32, (length, keys_all), 1)
            same = same & (at_q >= at_k)
        bias[...] = jnp.where(same, 0.0, masked_score)

    masks = half_masks()
    for first in range(0, length, step):
        rows = pl.ds(first, step)
        keys = first + step if causal else keys_all
        q = q_ref[rows, :]
        k = k_ref[:keys, :]
        v = v_ref[:keys, :]
        out = None
        for h, mask in enumerate(masks):
            s = inner_rows(q * mask, k) + bias[rows, :keys]
            e = jnp.exp(s - jnp.max(s, axis=-1, keepdims=True))
            p = (e * (1.0 / jnp.sum(e, axis=-1, keepdims=True))).astype(bf16)
            p_ref[0, h, rows, :keys] = p
            part = plain_dot(p, v * mask)
            out = part if out is None else out + part
        mixed_ref[rows, :] = out.astype(bf16)


def attend_backward_kernel(
    causal, q_ref, k_ref, v_ref, mixed_ref, gm_ref, p_ref, gq_ref, gk_ref, gv_ref
):
    length, keys_all = q_ref.shape[0], k_ref.shape[0]
    step = length // 2 if causal else length
    masks = half_masks()
    gk_parts, gv_parts = [], []
    for first in range(0, length, step):
        rows = pl.ds(first, step)
        keys = first + step if causal else keys_all
        q = q_ref[rows, :]
        k = k_ref[:keys, :]
        v = v_ref[:keys, :]
        gm = gm_ref[rows, :]
        product = gm.astype(f32) * mixed_ref[rows, :].astype(f32)
        gq = gk = gv = 0.0
        for h, mask in enumerate(masks):
            inner = jnp.sum(product * mask.astype(f32), axis=-1, keepdims=True)
            p = p_ref[0, h, rows, :keys]
            gm_half = gm * mask
            gw = inner_rows(gm_half, v)
            gs = (p.astype(f32) * (gw - inner)).astype(bf16)
            gv = gv + inner_cols(p, gm_half)
            gq = gq + plain_dot(gs, k * mask)
            gk = gk + inner_cols(gs, q * mask)
        gq_ref[rows, :] = (gq * HEAD**-0.5).astype(bf16)
        gk_parts.append(gk)
        gv_parts.append(gv)
    for ref, terms in ((gk_ref, gk_parts), (gv_ref, gv_parts)):
        if not causal:
            ref[...] = terms[0].astype(bf16)
        else:
            ref[:step, :] = (terms[0] + terms[1][:step]).astype(bf16)
            ref[step:, :] = terms[1][step:].astype(bf16)


def attention_specs(rows, length, arrays):
    return [(a, (length, PAIR), lambda r, p: (r, p)) for a in arrays]


def attend_forward(causal, rows, length, q, k, v, seg_q, seg_k):
    mem_len = k.shape[0] // rows
    mixed, probs = call(
        functools.partial(attend_forward_kernel, causal),
        (rows, HEADS // 2),
        attention_specs(rows, length, (q,))
        + attention_specs(rows, mem_len, (k, v))
        + [
            (seg_q.reshape(rows * length, 1), (length, 1), lambda r, p: (r, 0)),
            (seg_k.reshape(rows, 1, mem_len), (1, 1, mem_len), lambda r, p: (r, 0, 0)),
        ],
        [
            (q.shape, bf16, (length, PAIR), lambda r, p: (r, p)),
            (
                (rows, HEADS, length, mem_len),
                bf16,
                (1, 2, length, mem_len),
                lambda r, p: (r, p, 0, 0),
            ),
        ],
        scratch=[pltpu.VMEM((length, mem_len), f32)],
        flops=4 * rows * HEADS * length * mem_len * PAIR,
        name="attend_forward",
    )
    return mixed, probs


def attend_backward(causal, rows, length, q, k, v, mixed, grad_mixed, probs):
    mem_len = k.shape[0] // rows
    return call(
        functools.partial(attend_backward_kernel, causal),
        (rows, HEADS // 2),
        attention_specs(rows, length, (q,))
        + attention_specs(rows, mem_len, (k, v))
        + attention_specs(rows, length, (mixed, grad_mixed))
        + [(probs, (1, 2, length, mem_len), lambda r, p: (r, p, 0, 0))],
        [
            (q.shape, bf16, (length, PAIR), lambda r, p: (r, p)),
            (k.shape, bf16, (mem_len, PAIR), lambda r, p: (r, p)),
            (k.shape, bf16, (mem_len, PAIR), lambda r, p: (r, p)),
        ],
        flops=8 * rows * HEADS * length * mem_len * PAIR,
        name="attend_backward",
    )


CHUNK = 768


def feed_kernel(
    s1, mixed, wo, task, gain, w_in, w_out, down_all, up_all, cot,
    output, n3, act, gu, gfeed, g2, g2_low, gmix, up_grad, down_grad, gain_grad,
    slope, total,
):
    first = pl.program_id(0) == 0
    units = w_in.shape[1]
    stream = s1[...] + plain_dot(mixed[...], wo[...])
    picked = token_gain(task[...], gain[...])
    n3[...] = (stream * inverse_rms(stream) * picked).astype(bf16)
    total[...] = jnp.zeros_like(total)

    @pl.loop(0, units // CHUNK)
    def _(j):
        cols = pl.ds(pl.multiple_of(j * CHUNK, CHUNK), CHUNK)
        value, rate = gelu_both(plain_dot(n3[...], w_in[:, cols]))
        value = value.astype(bf16)
        act[:, cols] = value
        slope[:, cols] = rate.astype(bf16)
        total[...] += plain_dot(value, w_out[cols, :])

    feed = total[...]
    feed_low = feed.astype(bf16)
    tokens, wide = stream.shape[0], down_all.shape[1]
    owner = lax.broadcasted_iota(jnp.int32, (tokens, wide), 1) - task[...] * ADA
    mask = jnp.where((owner >= 0) & (owner < ADA), 1.0, 0.0)
    narrow, narrow_slope = gelu_both(plain_dot(feed_low, down_all[...]) * mask)
    narrow = narrow.astype(bf16)
    output[...] = (stream + feed + plain_dot(narrow, up_all[...])).astype(bf16)
    cotan = cot[...]
    gb = (narrow_slope * inner_rows(cotan, up_all[...]) * mask).astype(bf16)
    grad_feed = (cotan.astype(f32) + inner_rows(gb, down_all[...])).astype(bf16)
    gfeed[...] = grad_feed
    up_now = inner_cols(narrow, cotan)
    down_now = inner_cols(feed_low, gb)
    total[...] = jnp.zeros_like(total)

    @pl.loop(0, units // CHUNK)
    def _(j):
        cols = pl.ds(pl.multiple_of(j * CHUNK, CHUNK), CHUNK)
        grad = slope[:, cols].astype(f32) * inner_rows(gfeed[...], w_out[cols, :])
        grad = grad.astype(bf16)
        gu[:, cols] = grad
        total[...] += inner_rows(grad, w_in[:, cols])

    stream_grad, gain_tokens = norm_back(stream, picked, total[...])
    grad_two = cotan.astype(f32) + stream_grad
    g2[...] = grad_two
    low = grad_two.astype(bf16)
    g2_low[...] = low
    gmix[...] = inner_rows(low, wo[...]).astype(bf16)
    gain_now = gain_rows(task[...], gain_tokens)

    @pl.when(first)
    def _():
        up_grad[...] = up_now
        down_grad[...] = down_now
        gain_grad[...] = gain_now

    @pl.when(jnp.logical_not(first))
    def _():
        up_grad[...] += up_now
        down_grad[...] += down_now
        gain_grad[...] += gain_now


def cross_back_kernel(gq, wq, s1, task, gain, g2, wo, g1, g1_low, gmix, gain_grad):
    stream = s1[...]
    picked = token_gain(task[...], gain[...])
    stream_grad, gain_tokens = norm_back(stream, picked, inner_rows(gq[...], wq[...]))
    grad_one = g2[...] + stream_grad
    g1[...] = grad_one
    low = grad_one.astype(bf16)
    g1_low[...] = low
    gmix[...] = inner_rows(low, wo[...]).astype(bf16)
    accumulate(gain_grad, gain_rows(task[...], gain_tokens))


def accumulate(ref, value):
    @pl.when(pl.program_id(0) == 0)
    def _():
        ref[...] = value

    @pl.when(pl.program_id(0) != 0)
    def _():
        ref[...] += value


def memory_back_kernel(gk, gv, wk, wv, out):
    out[...] = inner_rows(gk[...], wk[...]) + inner_rows(gv[...], wv[...])


def input_back_kernel(gq, gk, gv, wq, wk, wv, x, task, gain, g1, out, gain_grad):
    stream = x[...].astype(f32)
    picked = token_gain(task[...], gain[...])
    cotan = inner_rows(gq[...], wq[...]) + inner_rows(gk[...], wk[...])
    cotan = cotan + inner_rows(gv[...], wv[...])
    stream_grad, gain_tokens = norm_back(stream, picked, cotan)
    out[...] = g1[...] + stream_grad
    accumulate(gain_grad, gain_rows(task[...], gain_tokens))


def outer_kernel(which, sources, *refs):
    left = refs[:sources]
    right = refs[sources : sources + len(which)]
    outs = refs[sources + len(which) :]
    for source, grad, out in zip(which, right, outs):
        for first in range(0, out.shape[1], CHUNK):
            cols = slice(first, first + CHUNK)
            out[:, cols] = inner_cols(left[source][...], grad[:, cols]).astype(bf16)


def outers(sources, grads, which, name):
    tokens, width = sources[0].shape
    block = 256
    return call(
        functools.partial(outer_kernel, which, len(sources)),
        (width // block,),
        [(s, (tokens, block), lambda i: (0, i)) for s in sources] + [whole(g) for g in grads],
        [((width, g.shape[1]), bf16, (block, g.shape[1]), lambda i: (i, 0)) for g in grads],
        flops=sum(2 * tokens * width * g.shape[1] for g in grads),
        name=name,
    )


BLOCK = 512


def low_out(shape):
    return out_row(shape, bf16, BLOCK)


def full_out(shape):
    return out_row(shape, f32, BLOCK)


def attention_layers(x, mem, segments, mem_segments, task, weights, gain_table):
    rows, length = segments.shape
    tokens, width = x.shape
    wq1, wk1, wv1, wo1, wq2, wk2, wv2 = weights[:7]
    gain_one, gain_two = (gain_table[:, i * width : (i + 1) * width] for i in range(2))
    block = BLOCK
    grid = (tokens // block,)
    act_shape = (tokens, width)
    square = 2 * tokens * width * width
    n1, q1, k1, v1 = call(
        pre_kernel,
        grid,
        [by_row(x, block), by_row(task, block)] + [whole(a) for a in (gain_one, wq1, wk1, wv1)],
        [low_out(act_shape) for _ in range(4)],
        flops=3 * square,
        name="self_projections",
    )
    m1, p1 = attend_forward(True, rows, length, q1, k1, v1, segments, segments)
    s1, n2, q2 = call(
        middle_kernel,
        grid,
        [by_row(x, block), by_row(m1, block), whole(wo1), by_row(task, block), whole(gain_two), whole(wq2)],
        [full_out(act_shape), low_out(act_shape), low_out(act_shape)],
        flops=2 * square,
        name="middle",
    )
    k2, v2 = call(
        memory_kernel,
        grid,
        [by_row(mem, block), whole(wk2), whole(wv2)],
        [low_out(mem.shape), low_out(mem.shape)],
        flops=2 * square,
        name="memory_projections",
    )
    m2, p2 = attend_forward(False, rows, length, q2, k2, v2, segments, mem_segments)
    return (n1, q1, k1, v1, m1, s1, n2, q2, k2, v2, m2), p1, p2


def feed_forward(s1, m2, cot, task, weights, gain_table, down_all, up_all):
    tokens, width = s1.shape
    wo2, w_in, w_out = weights[7:]
    gain_three = gain_table[:, 2 * width :]
    block = BLOCK
    grid = (tokens // block,)
    act_shape = (tokens, width)
    square = 2 * tokens * width * width
    units = w_in.shape[1]
    wide = up_all.shape[0]
    tasks = gain_table.shape[0]
    output, n3, act, gu, gfeed, g2, g2_low, gmix2, up_grad, down_grad, gain3 = call(
        feed_kernel,
        grid,
        [
            by_row(s1, block), by_row(m2, block), whole(wo2), by_row(task, block), whole(gain_three),
            whole(w_in), whole(w_out), whole(down_all), whole(up_all), by_row(cot, block),
        ],
        [
            low_out(act_shape), low_out(act_shape), out_row((tokens, units), bf16, block), out_row((tokens, units), bf16, block),
            low_out(act_shape), full_out(act_shape), low_out(act_shape), low_out(act_shape),
            out_whole((wide, width), f32), out_whole((width, wide), f32), out_whole((tasks, width), f32),
        ],
        scratch=[pltpu.VMEM((block, units), bf16), pltpu.VMEM((block, width), f32)],
        flops=2 * square + 8 * tokens * width * units,
        name="feed_forward_and_back",
    )
    (hidden_in_grad,) = outers((n3,), (gu,), (0,), "hidden_in_grad")
    (hidden_out_grad,) = outers((act,), (gfeed,), (0,), "hidden_out_grad")
    return output, g2, g2_low, gmix2, hidden_in_grad, hidden_out_grad, up_grad, down_grad, gain3


def attention_back(x, mem, rows, task, weights, gain_table, saved, p1, p2, g2, g2_low, gmix2):
    n1, q1, k1, v1, m1, s1, n2, q2, k2, v2, m2 = saved
    tokens, width = x.shape
    length = tokens // rows
    wq1, wk1, wv1, wo1, wq2, wk2, wv2 = weights[:7]
    gain_one, gain_two = (gain_table[:, i * width : (i + 1) * width] for i in range(2))
    tasks = gain_table.shape[0]
    block = BLOCK
    grid = (tokens // block,)
    act_shape = (tokens, width)
    square = 2 * tokens * width * width
    gq2, gk2, gv2 = attend_backward(False, rows, length, q2, k2, v2, m2, gmix2, p2)
    g1, g1_low, gmix1, gain2 = call(
        cross_back_kernel,
        grid,
        [
            by_row(gq2, block), whole(wq2), by_row(s1, block), by_row(task, block), whole(gain_two),
            by_row(g2, block), whole(wo1),
        ],
        [full_out(act_shape), low_out(act_shape), low_out(act_shape), out_whole((tasks, width), f32)],
        flops=2 * square,
        name="cross_back",
    )
    (mem_grad,) = call(
        memory_back_kernel,
        grid,
        [by_row(gk2, block), by_row(gv2, block), whole(wk2), whole(wv2)],
        [full_out(act_shape)],
        flops=2 * square,
        name="memory_back",
    )
    wo2_grad, wq2_grad, wk2_grad, wv2_grad = outers(
        (m2, n2, mem), (g2_low, gq2, gk2, gv2), (0, 1, 2, 2), "cross_grads"
    )
    gq1, gk1, gv1 = attend_backward(True, rows, length, q1, k1, v1, m1, gmix1, p1)
    input_grad, gain1 = call(
        input_back_kernel,
        grid,
        [
            by_row(gq1, block), by_row(gk1, block), by_row(gv1, block), whole(wq1), whole(wk1), whole(wv1),
            by_row(x, block), by_row(task, block), whole(gain_one), by_row(g1, block),
        ],
        [full_out(act_shape), out_whole((tasks, width), f32)],
        flops=3 * square,
        name="input_back",
    )
    wo1_grad, wq1_grad, wk1_grad, wv1_grad = outers(
        (m1, n1), (g1_low, gq1, gk1, gv1), (0, 1, 1, 1), "self_grads"
    )
    grads = (wq1_grad, wk1_grad, wv1_grad, wo1_grad, wq2_grad, wk2_grad, wv2_grad, wo2_grad)
    return input_grad, mem_grad, grads, gain1, gain2


LINE = 4
MESH = pl.DeviceIdType.MESH


class Place:
    def __init__(self):
        me = lax.axis_index("dp")
        self.core = lax.rem(me, 2)
        self.x = lax.rem(me // 2, 2)
        self.y = lax.rem(me // 4, 2)
        self.z = me // 8

    def at(self, z=None, y=None, x=None, core=None):
        z = self.z if z is None else z
        y = self.y if y is None else y
        x = self.x if x is None else x
        core = self.core if core is None else core
        return (((z * 2 + y) * 2 + x) * 2 + core,)

    def sibling(self):
        return self.at(core=1 - self.core)

    def over_x(self):
        return self.at(x=1 - self.x)

    def over_y(self):
        return self.at(y=1 - self.y)

    def along_z(self, k):
        return self.at(z=lax.rem(self.z + k, LINE))

    def partners(self):
        return [self.sibling(), self.over_x(), self.over_y()] + [self.along_z(k) for k in (1, 2, 3)]


def meet(place):
    barrier = pltpu.get_barrier_semaphore()
    partners = place.partners()
    for partner in partners:
        pl.semaphore_signal(barrier, inc=1, device_id=partner, device_id_type=MESH)
    pl.semaphore_wait(barrier, len(partners))


class Copies:
    def __init__(self, send, recv):
        self.send, self.recv, self.used, self.open = send, recv, 0, []

    def remote(self, source, target, device):
        copy = pltpu.make_async_remote_copy(
            src_ref=source,
            dst_ref=target,
            send_sem=self.send.at[self.used],
            recv_sem=self.recv.at[self.used],
            device_id=device,
            device_id_type=MESH,
        )
        self.used += 1
        copy.start()
        self.open.append(copy)
        return copy

    def local(self, source, target):
        copy = pltpu.make_async_copy(source, target, self.recv.at[self.used])
        self.used += 1
        copy.start()
        return copy

    def close(self, copy):
        copy.wait_send()
        self.open = [other for other in self.open if other is not copy]

    def finish(self):
        for copy in self.open:
            copy.wait_send()


ORDER = reversed
FIRST_PACE = 1
PACE = 2


class Unit:
    def __init__(self, here, copies, source, whole_array, index, first, second):
        self.here, self.copies = here, copies
        self.source, self.array = source, whole_array
        self.index, self.shares = index, (first, second)
        self.going = {}

    def window(self, zs, ys, xs, share=None):
        return self.array.at[(zs, ys, xs) + (self.index if share is None else self.shares[share])]

    def depart(self):
        here, copies = self.here, self.copies
        source = self.source(None)
        target = self.window(here.z, here.y, here.x)
        self.going["z"] = [copies.remote(source, target, here.along_z(k)) for k in (1, 2, 3)]
        self.own = copies.local(source, target)

    def turn(self):
        here = self.here
        for copy in self.going["z"]:
            copy.wait_recv()
        self.own.wait()
        one = self.window(slice(None), here.y, here.x, 0)
        two = self.window(slice(None), here.y, here.x, 1)
        self.going["1"] = [
            self.copies.remote(one, one, here.over_x()),
            self.copies.remote(two, two, here.over_y()),
        ]

    def turn_again(self):
        here = self.here
        for copy in self.going["1"]:
            copy.wait_recv()
        one = self.window(slice(None), here.y, slice(None), 0)
        two = self.window(slice(None), slice(None), here.x, 1)
        self.going["2"] = [
            self.copies.remote(one, one, here.over_y()),
            self.copies.remote(two, two, here.over_x()),
        ]

    def cross(self):
        for copy in self.going["2"]:
            copy.wait_recv()
        part = self.window(slice(None), slice(None), slice(None))
        self.going["c"] = self.copies.remote(part, part, self.here.sibling())

    def settle(self):
        self.going["c"].wait_recv()

    def stages(self):
        return (self.depart, self.turn, self.turn_again, self.cross, self.settle)


def column_of(row):
    length = row.shape[1]
    at_q = lax.broadcasted_iota(jnp.int32, (length, length), 0)
    at_k = lax.broadcasted_iota(jnp.int32, (length, length), 1)
    picked = jnp.where(at_q == at_k, row.astype(f32), 0.0)
    return jnp.sum(picked, axis=1, keepdims=True).astype(jnp.int32)


def forward_kernel(*refs):
    (
        x, mem, segments, mem_segments, tasks,
        sq, sk, sv, so, cq, ck, cv, co, w_in, w_out,
        table, weight, bias_row, down, up, gain,
    ) = refs[:21]
    outs, made_out, gains_out = refs[21:31], refs[31], refs[32]
    low_out, gain_out, task_out = refs[33:36]
    saved_out = refs[36:47]
    p1_out, p2_out = refs[47:49]
    scratch = refs[49:]
    wide, halves, blocks = scratch[:10], scratch[10:20], scratch[20:30]
    local_w = scratch[30:38]
    saved = scratch[38:49]
    n1, q1, k1, v1, m1, s1, n2, q2, k2, v2, m2 = saved
    made, gain_rows_all, bias, probs, send, recv, p_sem, load_sem, save_sem, gain_full = scratch[49:]
    own = (sq, sk, sv, so, cq, ck, cv, co, w_in, w_out)
    rows_total, length = segments.shape
    mem_len = mem_segments.shape[1]
    here = Place()
    copies = Copies(send, recv)
    c = here.core

    def half(i, core, first=0, width=None):
        full = own[i].shape[1] // 2
        width = full if width is None else width
        return pl.ds(pl.multiple_of(core * full + first, 128), width)

    for i in range(10):
        wide[i][...] = own[i][...].astype(f32)
    gain_rows_all[...] = gain[...].astype(f32)
    probs[...] = jnp.zeros_like(probs)
    meet(here)
    pair = {}
    order = (0, 1, 2, 5, 6, 3, 4, 7, 8, 9)
    for i in order:
        rows = own[i].shape[0]
        mine = pl.ds(pl.multiple_of(c * rows, 8), rows)
        pair[i] = copies.remote(
            wide[i].at[:, half(i, 1 - c)], halves[i].at[mine, :], here.sibling()
        )
        halves[i][mine, :] = wide[i][:, half(i, c)]

    opened = set()

    def piece(i, rows, first, width):
        at = half(i, c, first, width)
        count = rows.stop - rows.start
        if (width // 2) % 128 == 0:
            windows = (
                (rows, half(i, c, first, width // 2)),
                (rows, half(i, c, first + width // 2, width // 2)),
            )
            local = (
                (rows, pl.ds(first, width // 2)),
                (rows, pl.ds(first + width // 2, width // 2)),
            )
        else:
            cut = rows.start + (count // 2 if count % 32 == 0 else (count // 32 + i % 2) * 16)
            split = (slice(rows.start, cut), slice(cut, rows.stop))
            windows = tuple((part, at) for part in split)
            local = tuple((part, pl.ds(first, width)) for part in split)

        def source(share):
            if i not in opened:
                opened.add(i)
                pair[i].wait_recv()
                blocks[i][...] = halves[i][...].astype(bf16)
            return blocks[i].at[(rows, pl.ds(first, width)) if share is None else local[share]]

        return Unit(here, copies, source, outs[i], (rows, at), *windows)

    def square(i):
        return piece(i, slice(0, outs[i].shape[3]), 0, own[i].shape[1] // 2)

    gain_own = gain.shape[0]
    gain_cut = gain_own // 16 * 8
    made_cut = made.shape[1] // 256 * 128
    gain_unit = Unit(
        here, copies, lambda _: gain_rows_all, gains_out, (c,),
        (c, pl.ds(0, gain_cut)), (c, pl.ds(gain_cut, gain_own - gain_cut)),
    )
    made_unit = Unit(
        here, copies, lambda _: made, made_out, (c,),
        (c, slice(None), pl.ds(0, made_cut)), (c, slice(None), pl.ds(made_cut, made.shape[1] - made_cut)),
    )
    in_half = w_in.shape[1] // 4
    out_rows = outs[9].shape[3]
    units = [gain_unit] + [square(i) for i in (0, 1, 2, 5, 6, 3, 4, 7)]
    units += [
        piece(8, slice(0, outs[8].shape[3]), k * in_half, in_half) for k in (0, 1)
    ]
    units += [made_unit]
    units += [
        piece(
            9, slice(k * out_rows // 2, (k + 1) * out_rows // 2), 0, w_out.shape[1] // 2
        )
        for k in (0, 1)
    ]
    loads = {}
    landing = {1: (0,), 2: (1,), 3: (2,), 4: (5,), 5: (6,), 6: (3,), 7: (4,), 8: (7,)}

    def stage_at(u, turn):
        pace = FIRST_PACE if u < 4 else PACE
        return (turn - u) // pace if turn >= u and (turn - u) % pace == 0 else -1

    def tick(turn):
        for u in range(min(turn, len(units) - 1), -1, -1):
            if stage_at(u, turn) == 0:
                units[u].depart()
        for u in ORDER(range(len(units))):
            late = stage_at(u, turn)
            if not 0 < late < 5:
                continue
            units[u].stages()[late]()
            if late == 4 and u in landing:
                (i,) = landing[u]
                loads[i] = pltpu.make_async_copy(outs[i], local_w[i], load_sem.at[i])
                loads[i].start()
            if late == 4 and u == 0:
                loads["gain"] = pltpu.make_async_copy(gains_out, gain_full, load_sem.at[8])
                loads["gain"].start()

    def matrix(i):
        return local_w[i][...].reshape(-1, own[i].shape[1])

    state = gelu_in_kernel(exact_dot(table[...], weight[...]) + bias_row[...])
    low = state.astype(bf16)
    low_out[...] = low
    values = jnp.concatenate((inner_rows(low, down[...]), inner_rows(low, up[...])), axis=0)
    made[...] = jnp.zeros_like(made)
    made[:, : down.shape[0]] = values.astype(bf16)

    for turn in range(3 + 4 * FIRST_PACE + 1):
        tick(turn)
    ticks = iter(range(3 + 4 * FIRST_PACE + 1, len(units) + 4 * PACE))

    def between():
        turn = next(ticks, None)
        if turn is not None:
            tick(turn)

    stores = []

    def store(which, part=None):
        source, target = saved[which], saved_out[which]
        copy = pltpu.make_async_copy(source, target, save_sem.at[which])
        copy.start()
        stores.append(copy)

    for r in range(rows_total):
        column = column_of(segments[r : r + 1, :])
        task = jnp.zeros_like(column)
        for s in range(tasks.shape[1]):
            task = task + jnp.where(column == s, tasks[r : r + 1, s : s + 1], 0)
        task_out[r * length : (r + 1) * length, :] = task
    loads["gain"].wait()
    width = x.shape[1]
    gain_out[...] = 1.0 + inner_rows(low, gain_full[...].reshape(-1, gain.shape[1]).astype(bf16))

    def picked(r, which):
        task = task_out[r * length : (r + 1) * length, :]
        return token_gain(task, gain_out[:, which * width : (which + 1) * width])

    def row(r, size=None):
        size = length if size is None else size
        return slice(r * size, (r + 1) * size)

    for i in (0, 1, 2):
        loads[i].wait()
    for r in range(rows_total):
        stream = x[row(r), :].astype(f32)
        n = (stream * inverse_rms(stream) * picked(r, 0)).astype(bf16)
        n1[row(r), :] = n
        q1[row(r), :] = (plain_dot(n, matrix(0)).astype(bf16).astype(f32) * HEAD**-0.5).astype(bf16)
        k1[row(r), :] = plain_dot(n, matrix(1)).astype(bf16)
        v1[row(r), :] = plain_dot(n, matrix(2)).astype(bf16)
        between()
    for which in (0, 1, 2, 3):
        store(which)


    def attend(causal, q, k, v, mixed, p_out, r, keys_row):
        column = column_of(segments[r : r + 1, :])
        same = column == keys_row
        if causal:
            at_q = lax.broadcasted_iota(jnp.int32, same.shape, 0)
            at_k = lax.broadcasted_iota(jnp.int32, same.shape, 1)
            same = same & (at_q >= at_k)
        bias[...] = jnp.where(same, 0.0, masked_score)
        keys_total = keys_row.shape[1]
        per_group = HEADS // 4
        for group in range(2):
            @pl.loop(group * per_group, (group + 1) * per_group)
            def _(p):
                slot = lax.rem(p, 2)
                at = pl.ds(pl.multiple_of(p * PAIR, PAIR), PAIR)

                @pl.when(p >= 2)
                def _():
                    pltpu.make_async_copy(
                        probs.at[slot], p_out.at[r, pl.ds(2 * p - 4, 2)], p_sem.at[slot]
                    ).wait()

                attend_pair(causal, q, k, v, mixed, probs.at[slot], bias, row(r), row(r, keys_total), at)
                pltpu.make_async_copy(
                    probs.at[slot], p_out.at[r, pl.ds(2 * p, 2)], p_sem.at[slot]
                ).start()

            between()
        for p in (HEADS // 2 - 2, HEADS // 2 - 1):
            pltpu.make_async_copy(
                probs.at[p % 2], p_out.at[r, pl.ds(2 * p, 2)], p_sem.at[p % 2]
            ).wait()

    for r in range(rows_total):
        attend(True, q1, k1, v1, m1, p1_out, r, segments[r : r + 1, :])
    store(4)
    for i in (5, 6):
        loads[i].wait()
    for r in range(rows_total):
        mine = row(r, mem_len)
        k2[mine, :] = plain_dot(mem[mine, :], matrix(5)).astype(bf16)
        v2[mine, :] = plain_dot(mem[mine, :], matrix(6)).astype(bf16)
        between()
    store(8)
    store(9)
    for i in (3, 4):
        loads[i].wait()
    for r in range(rows_total):
        stream = x[row(r), :].astype(f32) + plain_dot(m1[row(r), :], matrix(3))
        s1[row(r), :] = stream
        n = (stream * inverse_rms(stream) * picked(r, 1)).astype(bf16)
        n2[row(r), :] = n
        q2[row(r), :] = (plain_dot(n, matrix(4)).astype(bf16).astype(f32) * HEAD**-0.5).astype(bf16)
        between()
    for which in (5, 6, 7):
        store(which)
    for r in range(rows_total):
        attend(False, q2, k2, v2, m2, p2_out, r, mem_segments[r : r + 1, :])
    store(10)
    for turn in ticks:
        tick(turn)
    loads[7].wait()
    for copy in stores:
        copy.wait()
    copies.finish()


def gelu_in_kernel(v):
    return v * (0.5 * lax.erf(v * 0.7071067811865476) + 0.5)


def attend_pair(causal, q_ref, k_ref, v_ref, mixed_ref, p_ref, bias, q_rows, k_rows, at):
    length = q_rows.stop - q_rows.start
    keys_all = k_rows.stop - k_rows.start
    step = length // 2 if causal else length
    masks = half_masks()
    for first in range(0, length, step):
        rows = slice(q_rows.start + first, q_rows.start + first + step)
        keys = first + step if causal else keys_all
        q = q_ref[rows, at]
        k = k_ref[k_rows.start : k_rows.start + keys, at]
        v = v_ref[k_rows.start : k_rows.start + keys, at]
        out = None
        for h, mask in enumerate(masks):
            s = inner_rows(q * mask, k) + bias[first : first + step, :keys]
            e = jnp.exp(s - jnp.max(s, axis=-1, keepdims=True))
            p = (e * (1.0 / jnp.sum(e, axis=-1, keepdims=True))).astype(bf16)
            p_ref[h, first : first + step, :keys] = p
            part = plain_dot(p, v * mask)
            out = part if out is None else out + part
        mixed_ref[rows, at] = out.astype(bf16)


def forward(x, mem, segments, mem_segments, tasks, weights, table, weight, bias_row, makers):
    down, up, gain = makers
    own = weights
    tokens, width = x.shape
    mem_tokens = mem.shape[0]
    rows, length = segments.shape
    mem_len = mem_segments.shape[1]
    spaces = (LINE, 2, 2)
    any_space = pl.BlockSpec(memory_space=pl.ANY)
    vmem = pl.BlockSpec(memory_space=pltpu.VMEM)
    made_half = down.shape[0] + (-down.shape[0] % 128)
    n_tasks = table.shape[0]
    chip = [spaces + (2 * a.shape[0], a.shape[1]) for a in own]
    t_low, m_low, t_full = ((tokens, width), bf16), ((mem_tokens, width), bf16), ((tokens, width), f32)
    kept = [t_low, t_low, t_low, t_low, t_low, t_full, t_low, t_low, m_low, m_low, t_low]
    shape = jax.ShapeDtypeStruct
    probs = (rows, HEADS, length, mem_len)
    copies = 11 * 16 + 32
    outs = pl.pallas_call(
        forward_kernel,
        in_specs=[vmem] * 21,
        out_specs=[any_space] * 12 + [vmem] * 3 + [any_space] * 13,
        out_shape=[shape(s, bf16) for s in chip]
        + [
            shape(spaces + (2, 2 * n_tasks, made_half), bf16),
            shape(spaces + (2,) + gain.shape, f32),
            shape((n_tasks, weight.shape[1]), bf16),
            shape((n_tasks, 3 * width), f32),
            shape((tokens, 1), jnp.int32),
        ]
        + [shape(s, d) for s, d in kept]
        + [shape((rows, HEADS, length, length), bf16), shape(probs, bf16)],
        scratch_shapes=[pltpu.VMEM(a.shape, f32) for a in own]
        + [pltpu.VMEM((2 * a.shape[0], a.shape[1] // 2), f32) for a in own]
        + [pltpu.VMEM((2 * a.shape[0], a.shape[1] // 2), bf16) for a in own]
        + [pltpu.VMEM(s, bf16) for s in chip[:8]]
        + [pltpu.VMEM(s, d) for s, d in kept]
        + [
            pltpu.VMEM((2 * n_tasks, made_half), bf16),
            pltpu.VMEM(gain.shape, f32),
            pltpu.VMEM((length, max(length, mem_len)), f32),
            pltpu.VMEM((2, 2, length, max(length, mem_len)), bf16),
            pltpu.SemaphoreType.DMA((copies,)),
            pltpu.SemaphoreType.DMA((copies,)),
            pltpu.SemaphoreType.DMA((2,)),
            pltpu.SemaphoreType.DMA((9,)),
            pltpu.SemaphoreType.DMA((11,)),
            pltpu.VMEM(spaces + (2,) + gain.shape, f32),
        ],
        compiler_params=pltpu.CompilerParams(
            collective_id=0, has_side_effects=True, vmem_limit_bytes=VMEM_BYTES
        ),
        name="forward_as_weights_arrive",
    )(x, mem, segments, mem_segments, tasks, *own, table, weight, bias_row, down, up, gain)
    return outs


BACK_ORDER = reversed
BACK_PACE = 3


class Stepwise:
    def __init__(self, stages):
        self.stages = list(stages)

    def advance(self):
        self.stages.pop(0)()


class Traffic:
    def __init__(self, pace):
        self.ready, self.flying, self.pace, self.now = [], [], pace, 0

    def add(self, item):
        self.ready.append(item)

    def tick(self):
        self.now += 1
        for item in BACK_ORDER(list(self.flying)):
            if (self.now - item.began) % self.pace:
                continue
            item.advance()
            if not item.stages:
                self.flying.remove(item)
        if self.ready:
            item = self.ready.pop(0)
            item.began = self.now
            item.advance()
            self.flying.append(item)

    def drain(self):
        while self.ready or self.flying:
            self.tick()


class Summed(Stepwise):
    def __init__(self, here, copies, theirs, mine, shares, slots, out, out_first, fetch=None):
        super().__init__(
            [self.begin, self.over_first, self.over_second, self.over_line, self.to_owner, self.end]
        )
        self.here, self.copies = here, copies
        self.theirs, self.mine, self.fetch = theirs, mine, fetch
        self.shares, self.slots, self.out, self.out_first = shares, slots, out, out_first
        self.landed = self.follower = None
        self.follows = False

    def begin(self):
        self.core = self.copies.remote(self.theirs, self.slots[0], self.here.sibling())
        if self.fetch is not None and not self.follows:
            self.start_fetch()

    def start_fetch(self):
        self.local = self.copies.local(*self.fetch)

    def over_first(self):
        here, held = self.here, self.slots[0]
        if self.fetch is not None:
            self.local.wait()
        self.core.wait_recv()
        held[...] += self.mine()
        if self.follower is not None:
            self.follower.start_fetch()
        one, two = self.shares
        self.first = (
            self.copies.remote(held.at[(slice(None), 1 - here.y, slice(None)) + one], self.slots[1], here.over_y()),
            self.copies.remote(held.at[(slice(None), slice(None), 1 - here.x) + two], self.slots[2], here.over_x()),
        )

    def over_second(self):
        here, held = self.here, self.slots[0]
        one, two = self.shares
        self.first[0].wait_recv()
        held[(slice(None), here.y, slice(None)) + one] += self.slots[1][...]
        self.first[1].wait_recv()
        held[(slice(None), slice(None), here.x) + two] += self.slots[2][...]
        self.second = (
            self.copies.remote(held.at[(slice(None), here.y, 1 - here.x) + one], self.slots[3], here.over_x()),
            self.copies.remote(held.at[(slice(None), 1 - here.y, here.x) + two], self.slots[4], here.over_y()),
        )

    def over_line(self):
        here, held = self.here, self.slots[0]
        one, two = self.shares
        self.second[0].wait_recv()
        held[(slice(None), here.y, here.x) + one] += self.slots[3][...]
        self.second[1].wait_recv()
        held[(slice(None), here.y, here.x) + two] += self.slots[4][...]
        self.third = [
            self.copies.remote(
                held.at[lax.rem(here.z + k, LINE), here.y, here.x],
                self.slots[5].at[k - 1],
                here.along_z(k),
            )
            for k in (1, 2, 3)
        ]

    def gathered(self):
        here = self.here
        total = self.slots[0][here.z, here.y, here.x].astype(f32)
        for k, copy in enumerate(self.third):
            copy.wait_recv()
            total = total + self.slots[5][k].astype(f32)
        return total

    def window(self, core, width, full):
        return pl.ds(pl.multiple_of(core * full + self.out_first, 128), width)

    def to_owner(self):
        here, final = self.here, self.slots[6]
        final[...] = self.gathered()
        rows, full = self.out.shape[0], self.out.shape[1] // 2
        c = here.core
        at = self.window(c, final.shape[1], full)
        theirs = pl.ds(pl.multiple_of((1 - c) * rows, 8), rows)
        self.last = self.copies.remote(final.at[theirs, :], self.out.at[:, at], here.sibling())
        self.out[:, at] = final[pl.ds(pl.multiple_of(c * rows, 8), rows), :]

    def end(self):
        self.last.wait_recv()
        if self.landed is not None:
            self.landed()


class Everywhere(Stepwise):
    def __init__(self, here, copies, value, sent, arriving, out):
        super().__init__([self.begin, self.step_x, self.step_y, self.step_z, self.end])
        self.here, self.copies, self.value = here, copies, value
        self.sent, self.arriving, self.out = sent, arriving, out

    def send(self, turn, device):
        self.sent[turn] = self.total
        self.copy = self.copies.remote(self.sent.at[turn], self.arriving.at[turn], device)

    def add(self, turn):
        self.copy.wait_recv()
        self.total = self.total + self.arriving[turn]

    def begin(self):
        self.total = self.value()
        self.send(0, self.here.sibling())

    def step_x(self):
        self.add(0)
        self.send(1, self.here.over_x())

    def step_y(self):
        self.add(1)
        self.send(2, self.here.over_y())

    def step_z(self):
        self.add(2)
        self.sent[3] = self.total
        self.around = [
            self.copies.remote(self.sent.at[3], self.arriving.at[2 + k], self.here.along_z(k))
            for k in (1, 2, 3)
        ]

    def end(self):
        for copy in self.around:
            copy.wait_recv()
        total = jnp.zeros_like(self.total)
        for line in range(LINE):
            for k in range(LINE):
                term = self.total if k == 0 else self.arriving[2 + k]
                here_now = lax.rem(self.here.z - k + LINE, LINE) == line
                total = total + jnp.where(here_now, term, 0.0)
        self.out[...] = total


def attend_pair_back(causal, q_ref, k_ref, v_ref, mixed_ref, gm_ref, p_ref, gq_ref, gk_ref, gv_ref, start, k_start, at, length, keys_all):
    step = length // 2 if causal else length
    masks = half_masks()
    gk_parts, gv_parts = [], []
    for first in range(0, length, step):
        rows = pl.ds(start + first, step)
        keys = first + step if causal else keys_all
        key_rows = pl.ds(k_start, keys)
        q, k, v = q_ref[rows, at], k_ref[key_rows, at], v_ref[key_rows, at]
        gm = gm_ref[rows, at]
        product = gm.astype(f32) * mixed_ref[rows, at].astype(f32)
        gq = gk = gv = 0.0
        for h, mask in enumerate(masks):
            inner = jnp.sum(product * mask.astype(f32), axis=-1, keepdims=True)
            p = p_ref[h, first : first + step, :keys]
            gm_half = gm * mask
            gw = inner_rows(gm_half, v)
            gs = (p.astype(f32) * (gw - inner)).astype(bf16)
            gv = gv + inner_cols(p, gm_half)
            gq = gq + plain_dot(gs, k * mask)
            gk = gk + inner_cols(gs, q * mask)
        gq_ref[rows, at] = (gq * HEAD**-0.5).astype(bf16)
        gk_parts.append(gk)
        gv_parts.append(gv)
    for ref, terms in ((gk_ref, gk_parts), (gv_ref, gv_parts)):
        if not causal:
            ref[pl.ds(k_start, keys_all), at] = terms[0].astype(bf16)
        else:
            ref[pl.ds(k_start, step), at] = (terms[0] + terms[1][:step]).astype(bf16)
            ref[pl.ds(k_start + step, step), at] = terms[1][step:].astype(bf16)


SUM_NAMES = ("q1", "k1", "v1", "o1", "q2", "k2", "v2", "o2", "in0", "in1", "out0", "out1", "small")


def sum_pieces(width, units, own):
    rows = 2 * own
    half = width // 2
    pieces = {}
    for turn, name in enumerate(SUM_NAMES[:8]):
        cut = rows // 2 if rows % 32 == 0 else (rows // 32 + turn % 2) * 16
        pieces[name] = (rows, half, 0, (slice(0, cut), slice(0, half)), (slice(cut, rows), slice(0, half)))
    part = units // 4
    for k in (0, 1):
        pieces[f"in{k}"] = (
            rows, part, k * part,
            (slice(0, rows), slice(0, part // 2)), (slice(0, rows), slice(part // 2, part)),
        )
    out_rows = rows * units // width
    third = half // 3
    for k, (first, size) in enumerate(((0, third), (third, half - third))):
        pieces[f"out{k}"] = (
            out_rows, size, first,
            (slice(0, out_rows // 2), slice(0, size)), (slice(out_rows // 2, out_rows), slice(0, size)),
        )
    pieces["small"] = (32, half, 0, (slice(0, 16), slice(0, half)), (slice(16, 32), slice(0, half)))
    return pieces


def backward_kernel(sizes, *refs):
    rows_total, length, mem_len, width, units, own_rows = sizes
    pieces = sum_pieces(width, units, own_rows)
    (
        p1, p2, q2h, k2h, v2h, m2h, gm2h, q1h, k1h, v1h, m1h, n1h, n2h, memh, xh, s1h, g2h, g2lowh,
        wq1h, wk1h, wv1h, wo1h, wq2h, wk2h, wv2h, g_in, g_out, g_small,
        task, gains, gain_three, down, up,
    ) = refs[:33]
    mem_out, input_out = refs[33:35]
    outs = refs[35:46]
    gain_out, state_out = refs[46:48]
    scratch = refs[48:]
    a = scratch[:5]
    gq, gk, gv = scratch[5:8]
    f0, f1, low = scratch[8:11]
    probs = scratch[11]
    w = scratch[12:16]
    grads = scratch[16:20]
    stage_in, stage_out, stage_small = scratch[20:23]
    slots = {}
    at_slot = 23
    for name in SUM_NAMES:
        slots[name] = scratch[at_slot : at_slot + 7]
        at_slot += 7
    state_sent, state_arriving, gain_sent, gain_arriving, gain_rows_ref = scratch[at_slot : at_slot + 5]
    send, recv, p_sem, load_sem = scratch[at_slot + 5 :]
    here = Place()
    copies = Copies(send, recv)
    traffic = Traffic(BACK_PACE)
    c = here.core
    loads = {}

    def fetch(name, source, target):
        loads[name] = pltpu.make_async_copy(source, target, load_sem.at[len(loads)])
        loads[name].start()

    def need(*names):
        for name in names:
            loads[name].wait()

    def half(which, first, size, full):
        return pl.ds(pl.multiple_of(which * full + first, 128), size)

    fetch("m2", m2h, a[3])
    fetch("g2low", g2lowh, low)
    fetch("q2", q2h, a[0])
    fetch("k2", k2h, a[1])
    fetch("v2", v2h, a[2])
    fetch("gm2", gm2h, a[4])

    def probs_copy(source, index):
        return pltpu.make_async_copy(source.at[index], probs.at[lax.rem(index, 2)], p_sem.at[lax.rem(index, 2)])

    pairs = HEADS // 2
    count = rows_total * pairs
    for index in (0, 1):
        probs_copy(p2, index).start()
    fetch("wq2", wq2h, w[0])
    fetch("wo1", wo1h, w[1])
    fetch("wk2", wk2h, w[2])
    fetch("wv2", wv2h, w[3])
    fetch("s1", s1h, f0)
    fetch("g2", g2h, f1)
    meet(here)

    def from_hbm(name, array, out, stage):
        rows, size, first, one, two = pieces[name]
        full = array.shape[4] // 2
        return Summed(
            here, copies, array.at[:, :, :, :, half(1 - c, first, size, full)], lambda: stage[...],
            (one, two), slots[name], out, first,
            fetch=(array.at[:, :, :, :, half(c, first, size, full)], stage),
        )

    out_one, out_two, small_item, in_one, in_two = flown = (
        from_hbm("out0", g_out, outs[9], stage_out.at[:, :, :, :, : pieces["out0"][1]]),
        from_hbm("out1", g_out, outs[9], stage_out),
        from_hbm("small", g_small, outs[10], stage_small),
        from_hbm("in0", g_in, outs[8], stage_in),
        from_hbm("in1", g_in, outs[8], stage_in),
    )
    for item in flown:
        traffic.add(item)
    for item, follower in ((out_one, out_two), (in_one, in_two)):
        item.follower, follower.follows = follower, True

    def small_landed():
        made = down.shape[0]
        small = outs[10]
        state = plain_dot(small[0:8, :made].astype(bf16), down[...])
        state = state + plain_dot(small[8:16, :made].astype(bf16), up[...])
        traffic.add(Everywhere(here, copies, lambda: state, state_sent, state_arriving, state_out))

    small_item.landed = small_landed
    users = {}

    def weight_gradient(name, index, source, grad, slot):
        if slot in users:
            copies.close(users[slot].core)
        buffer = grads[slot]
        rows, size, first, one, two = pieces[name]
        columns = width // 2
        for k in range(2):
            block = inner_cols(source[:, k * columns : (k + 1) * columns], grad[...]).astype(bf16)
            buffer[2 * k : 2 * k + 2] = block.reshape((2, 2, 2, rows, width))
        full = width // 2
        item = Summed(
            here, copies, buffer.at[:, :, :, :, half(1 - c, 0, size, full)],
            lambda: buffer[:, :, :, :, half(c, 0, size, full)],
            (one, two), slots[name], outs[index], 0,
        )
        users[slot] = item
        traffic.add(item)

    def matrix(k):
        return w[k][...].reshape(width, width)

    def row(r, size=None):
        size = length if size is None else size
        return slice(r * size, (r + 1) * size)

    def picked(r, which):
        return token_gain(task[row(r), :], gains[:, which * width : (which + 1) * width])

    def attention(causal, q, k, v, m, gm, source, keys_all):
        per_group = 2
        for group in range(count // per_group):
            @pl.loop(group * per_group, (group + 1) * per_group)
            def _(index):
                slot = lax.rem(index, 2)
                probs_copy(source, index).wait()
                r, p = index // pairs, lax.rem(index, pairs)
                at = pl.ds(pl.multiple_of(p * PAIR, PAIR), PAIR)
                attend_pair_back(
                    causal, q, k, v, m, gm, probs.at[slot], gq, gk, gv,
                    pl.multiple_of(r * length, length), pl.multiple_of(r * keys_all, keys_all), at, length, keys_all,
                )

                @pl.when(index + 2 < count)
                def _():
                    probs_copy(source, index + 2).start()

            traffic.tick()

    traffic.tick()
    need("m2", "g2low")
    weight_gradient("o2", 7, a[3], low, 0)
    traffic.tick()
    need("q2", "k2", "v2", "gm2")
    attention(False, a[0], a[1], a[2], a[3], a[4], p2, mem_len)
    for index in (0, 1):
        probs_copy(p1, index).start()
    fetch("n2", n2h, a[0])
    fetch("mem", memh, a[1])
    fetch("v1", v1h, a[2])
    fetch("m1", m1h, a[3])
    need("wq2", "wo1", "s1", "g2")
    gain_two = None
    for r in range(rows_total):
        stream = f0[row(r), :]
        stream_grad, gain_tokens = norm_back(stream, picked(r, 1), inner_rows(gq[row(r), :], matrix(0)))
        grad_one = f1[row(r), :] + stream_grad
        f1[row(r), :] = grad_one
        low_now = grad_one.astype(bf16)
        low[row(r), :] = low_now
        a[4][row(r), :] = inner_rows(low_now, matrix(1)).astype(bf16)
        now = gain_rows(task[row(r), :], gain_tokens)
        gain_two = now if gain_two is None else gain_two + now
        traffic.tick()
    fetch("wq1", wq1h, w[0])
    fetch("wk1", wk1h, w[1])
    need("n2", "mem")
    for name, index, source, grad, slot in (
        ("q2", 4, a[0], gq, 1), ("k2", 5, a[1], gk, 2), ("v2", 6, a[1], gv, 3)
    ):
        weight_gradient(name, index, source, grad, slot)
        traffic.tick()
    fetch("q1", q1h, a[0])
    fetch("k1", k1h, a[1])
    need("wk2", "wv2")
    for r in range(rows_total):
        mine = row(r, mem_len)
        f0[mine, :] = inner_rows(gk[mine, :], matrix(2)) + inner_rows(gv[mine, :], matrix(3))
        traffic.tick()
    fetch("mem_out", f0, mem_out)
    fetch("wv1", wv1h, w[2])
    need("m1")
    weight_gradient("o1", 3, a[3], low, 0)
    traffic.tick()
    need("q1", "k1", "v1")
    attention(True, a[0], a[1], a[2], a[3], a[4], p1, length)
    fetch("n1", n1h, a[0])
    fetch("x", xh, a[1])
    need("n1")
    for name, index, grad, slot in (("q1", 0, gq, 1), ("k1", 1, gk, 2), ("v1", 2, gv, 3)):
        weight_gradient(name, index, a[0], grad, slot)
        traffic.tick()
    need("x", "wq1", "wk1", "wv1")
    gain_one = None
    for r in range(rows_total):
        stream = a[1][row(r), :].astype(f32)
        cotan = inner_rows(gq[row(r), :], matrix(0)) + inner_rows(gk[row(r), :], matrix(1))
        cotan = cotan + inner_rows(gv[row(r), :], matrix(2))
        stream_grad, gain_tokens = norm_back(stream, picked(r, 0), cotan)
        f1[row(r), :] += stream_grad
        now = gain_rows(task[row(r), :], gain_tokens)
        gain_one = now if gain_one is None else gain_one + now
        traffic.tick()
    fetch("input_out", f1, input_out)
    gain_rows_ref[:, :width] = gain_one
    gain_rows_ref[:, width : 2 * width] = gain_two
    gain_rows_ref[:, 2 * width :] = gain_three[...]
    traffic.ready.insert(0, Everywhere(here, copies, lambda: gain_rows_ref[...], gain_sent, gain_arriving, gain_out))
    traffic.drain()
    need("mem_out", "input_out")
    copies.finish()


def backward(mem_len, saved, probs, x, mem, weights, g2, g2_low, gmix2, g_in, g_out, g_small, task, gains, gain_three, down, up, own):
    n1, q1, k1, v1, m1, s1, n2, q2, k2, v2, m2 = saved
    p1, p2 = (p.reshape((-1, 2) + p.shape[2:]) for p in probs)
    rows = probs[0].shape[0]
    tokens, width = x.shape
    length = tokens // rows
    units = own[8].shape[1]
    own_rows = own[0].shape[0]
    any_space = pl.BlockSpec(memory_space=pl.ANY)
    vmem = pl.BlockSpec(memory_space=pltpu.VMEM)
    shape = jax.ShapeDtypeStruct
    act, full = pltpu.VMEM((tokens, width), bf16), pltpu.VMEM((tokens, width), f32)
    mem_act = pltpu.VMEM((max(tokens, mem.shape[0]), width), bf16)
    square = pltpu.VMEM((LINE, 2, 2, 2 * own_rows, width), bf16)
    pieces = sum_pieces(width, units, own_rows)
    slots = []
    for name in SUM_NAMES:
        r, size, _, one, two = pieces[name]
        extent = [tuple(s.stop - s.start for s in share) for share in (one, two)]
        slots += [
            pltpu.VMEM((LINE, 2, 2, r, size), bf16),
            pltpu.VMEM((LINE, 2) + extent[0], bf16),
            pltpu.VMEM((LINE, 2) + extent[1], bf16),
            pltpu.VMEM((LINE,) + extent[0], bf16),
            pltpu.VMEM((LINE,) + extent[1], bf16),
            pltpu.VMEM((LINE - 1, r, size), bf16),
            pltpu.VMEM((r, size), f32),
        ]

    def stage(name):
        r, size = pieces[name][:2]
        return (LINE, 2, 2, r, size)

    tasks, hidden = gains.shape[0], down.shape[1]
    copies = 200
    ins_any = (
        p1, p2, q2, k2, v2, m2, gmix2, q1, k1, v1, m1, n1, n2, mem, x, s1, g2, g2_low,
        *(weights[i] for i in range(7)), g_in, g_out, g_small,
    )
    return pl.pallas_call(
        functools.partial(backward_kernel, (rows, length, mem_len, width, units, own_rows)),
        in_specs=[any_space] * len(ins_any) + [vmem] * 5,
        out_specs=[any_space] * 2 + [vmem] * 13,
        out_shape=[shape((mem.shape[0], width), f32), shape((tokens, width), f32)]
        + [shape(g.shape, f32) for g in own]
        + [shape((16, width), f32), shape(gains.shape, f32), shape((tasks, hidden), f32)],
        scratch_shapes=[act] * 5 + [act, mem_act, mem_act] + [full, full, act]
        + [pltpu.VMEM((2, 2, length, max(length, mem_len)), bf16)]
        + [square] * 4
        + [square] * 4
        + [
            pltpu.VMEM(stage("in0"), bf16),
            pltpu.VMEM(stage("out1"), bf16),
            pltpu.VMEM(stage("small"), bf16),
        ]
        + slots
        + [
            pltpu.VMEM((4, tasks, hidden), f32),
            pltpu.VMEM((6, tasks, hidden), f32),
            pltpu.VMEM((4,) + gains.shape, f32),
            pltpu.VMEM((6,) + gains.shape, f32),
            pltpu.VMEM(gains.shape, f32),
            pltpu.SemaphoreType.DMA((copies,)),
            pltpu.SemaphoreType.DMA((copies,)),
            pltpu.SemaphoreType.DMA((2,)),
            pltpu.SemaphoreType.DMA((32,)),
        ],
        compiler_params=pltpu.CompilerParams(
            collective_id=1, has_side_effects=True, vmem_limit_bytes=63 << 20
        ),
        name="backward_as_gradients_leave",
    )(*ins_any, task, gains, gain_three, down, up)


def finish_kernel(count, *refs):
    shards, small, gain_sum, state, gain_all, low, table, weight, bias_row = (
        refs[:count], *refs[count : count + 8]
    )
    large = refs[count + 8 : count + 10]
    outs = refs[count + 10 : 2 * count + 10]
    down_out, up_out, gain_out, table_out, weight_out, bias_out = refs[2 * count + 10 : 2 * count + 16]
    large_outs, (rows, held_a, held_b, sems) = (
        refs[2 * count + 16 : 2 * count + 18], refs[2 * count + 18 :]
    )
    held = (held_a, held_b)
    moves = [
        pltpu.make_async_copy(source, buffer, sems.at[k])
        for k, (source, buffer) in enumerate(zip(large, held))
    ]
    for move in moves:
        move.start()
    for shard, out in zip(shards, outs):
        out[...] = shard[...]
    made = down_out.shape[0]
    for move in moves:
        move.wait()
    moves = [
        pltpu.make_async_copy(buffer, target, sems.at[2 + k])
        for k, (buffer, target) in enumerate(zip(held, large_outs))
    ]
    for move in moves:
        move.start()
    low_now = low[...]
    down_out[...] = inner_cols(small[0:8, :made].astype(bf16), low_now)
    up_out[...] = inner_cols(small[8:16, :made].astype(bf16), low_now)
    rows[...] = inner_cols(gain_sum[...], low_now.astype(f32), exact_mode)
    owned = gain_out.shape[0]
    me = lax.axis_index("dp")
    gain_out[...] = rows[pl.ds(pl.multiple_of(me * owned, 8), owned), :]
    makers = gain_all[...].reshape(-1, gain_all.shape[-1])
    state_grad = state[...] + exact_dot(gain_sum[...], makers)
    before = exact_dot(table[...], weight[...]) + bias_row[...]
    pre_grad = gelu_both(before)[1] * state_grad
    bias_out[...] = jnp.sum(pre_grad, axis=0, keepdims=True)
    weight_out[...] = inner_cols(table[...], pre_grad, exact_mode)
    table_out[...] = lax.dot_general(
        pre_grad, weight[...], (((1,), (1,)), ((), ())), precision=exact_mode, preferred_element_type=f32
    )
    for move in moves:
        move.wait()


def finish(mem_grad, input_grad, shards, small, gain_sum, state, gain_all, low, table, weight, bias_row, makers):
    down, up, gain = makers
    shape = jax.ShapeDtypeStruct
    vmem = pl.BlockSpec(memory_space=pltpu.VMEM)
    ins = (*shards, small, gain_sum, state, gain_all, low, table, weight, bias_row)
    outs = [shape(s.shape, f32) for s in shards]
    outs += [shape(m.shape, f32) for m in makers] + [shape(a.shape, f32) for a in (table, weight, bias_row)]
    large = (mem_grad, input_grad)
    any_space = pl.BlockSpec(memory_space=pl.ANY)
    return pl.pallas_call(
        functools.partial(finish_kernel, len(shards)),
        in_specs=[vmem] * len(ins) + [any_space] * 2,
        out_specs=[vmem] * len(outs) + [any_space] * 2,
        out_shape=outs + [shape(a.shape, f32) for a in large],
        scratch_shapes=[
            pltpu.VMEM((gain_sum.shape[1], low.shape[1]), f32),
            *(pltpu.VMEM(a.shape, f32) for a in large),
            pltpu.SemaphoreType.DMA((4,)),
        ],
        compiler_params=pltpu.CompilerParams(vmem_limit_bytes=VMEM_BYTES),
        name="finish",
    )(*ins, *large)


def on_device(
    block_input, memory, cotangent, segments, memory_segments, task_of_segment,
    self_query, self_key, self_value, self_output,
    cross_query, cross_key, cross_value, cross_output,
    hidden_in, hidden_out, task_table, task_weight, task_bias,
    down_maker, up_maker, gain_maker,
):
    row_count, seq_len, model_width = block_input.shape
    mem_len = memory.shape[1]
    task_count = task_table.shape[0]
    token_count = row_count * seq_len
    parts = lax.axis_size("dp")
    weights = (
        self_query, self_key, self_value, self_output,
        cross_query, cross_key, cross_value, cross_output, hidden_in, hidden_out,
    )
    task_state, task_back = jax.vjp(task_network, task_table, task_weight, task_bias)
    task_low = task_state.astype(bf16)
    down_own, gain_own = down_maker.shape[0], gain_maker.shape[0]
    makers = (down_maker, up_maker, gain_maker)
    x = block_input.reshape(token_count, model_width)
    mem = memory.reshape(row_count * mem_len, model_width)

    def joined(block):
        return block.transpose(1, 0, 2).reshape(task_count, -1)

    if parts == 32:
        outs = forward(
            x, mem, segments, memory_segments, task_of_segment, weights,
            task_table, task_weight, task_bias.reshape(1, -1), makers,
        )
        backbone = [w.reshape(-1, w.shape[-1]) for w in outs[:10]]
        made = outs[10].reshape(parts, 2 * task_count, -1)
        task_low, gain_table, token_task = outs[12:15]
        saved, probs_one, probs_two = outs[15:26], outs[26], outs[27]
        made_up = joined(made[:, task_count:, :down_own])
        made = made[:, :task_count]
    else:
        packed = jnp.concatenate([w.reshape(-1, model_width) for w in weights], axis=0)
        packed = lax.all_gather(packed, "dp", axis=0, tiled=False)
        backbone, at = [], 0
        for w in weights:
            count = w.size // model_width
            backbone.append(packed[:, at : at + count].reshape(-1, w.shape[1]))
            at += count
        made = inner_rows(task_low, jnp.concatenate(makers, axis=0))
        made = lax.all_gather(made, "dp", axis=0, tiled=False)
        gain_table = 1.0 + joined(made[:, :, 2 * down_own :])
        seg_match = segments[:, :, None] == jnp.arange(task_of_segment.shape[1], dtype=jnp.int32)
        token_task = jnp.sum(
            jnp.where(seg_match, task_of_segment[:, None, :], 0), axis=-1
        ).reshape(token_count, 1)
        saved, probs_one, probs_two = attention_layers(
            x, mem, segments, memory_segments, token_task, backbone, gain_table
        )
        made_up = joined(made[:, :, down_own : 2 * down_own]).astype(bf16)
    made_down = joined(made[:, :, :down_own]).astype(bf16)
    down_all = (
        made_down.reshape(task_count, model_width, ADA)
        .transpose(1, 0, 2)
        .reshape(model_width, task_count * ADA)
    )
    up_all = made_up.reshape(task_count * ADA, model_width)
    cot = cotangent.reshape(token_count, model_width)
    output, g2, g2_low, gmix2, hidden_in_grad, hidden_out_grad, up_grad, down_grad, gain_three = feed_forward(
        saved[5], saved[10], cot, token_task, backbone, gain_table, down_all, up_all
    )
    down_rows = (
        down_grad.reshape(parts, -1, task_count, ADA)
        .transpose(0, 2, 1, 3)
        .reshape(parts, task_count, down_own)
    )
    up_rows = up_grad.reshape(task_count, parts, -1).transpose(1, 0, 2)
    if parts == 32:
        small = jnp.concatenate((down_rows, up_rows), axis=1).astype(bf16)
        small = jnp.pad(small, ((0, 0), (0, 0), (0, model_width - down_own)))
        in_grad = hidden_in_grad.reshape((LINE, 2, 2, -1, hidden_in.shape[1]))
        out_grad = hidden_out_grad.reshape((LINE, 2, 2, -1, model_width))
        mem_grad, input_grad, *shared, small, gain_sum, state = backward(
            mem_len, saved, (probs_one, probs_two), x, mem, outs[:7], g2, g2_low, gmix2, in_grad, out_grad,
            small.reshape(LINE, 2, 2, 4 * task_count, model_width), token_task, gain_table, gain_three,
            down_maker, up_maker, weights,
        )
        (
            *shared, down_maker_grad, up_maker_grad, gain_maker_grad,
            table_grad, weight_grad, bias_grad, mem_grad, input_grad,
        ) = finish(
            mem_grad, input_grad, shared, small, gain_sum, state, outs[11], task_low, task_table, task_weight,
            task_bias.reshape(1, -1), makers,
        )
        bias_grad = bias_grad.reshape(task_bias.shape)
    else:
        input_grad, mem_grad, grads, gain_one, gain_two = attention_back(
            x, mem, row_count, token_task, backbone, gain_table, saved, probs_one, probs_two, g2, g2_low, gmix2
        )
        grads = (*grads, hidden_in_grad, hidden_out_grad)
        packed = jnp.concatenate([g.reshape(parts, -1, model_width) for g in grads], axis=1)
        packed = lax.psum_scatter(packed, "dp", scatter_dimension=0, tiled=False).astype(f32)
        shared, at = [], 0
        for w in weights:
            count = w.size // model_width
            shared.append(packed[at : at + count].reshape(w.shape))
            at += count
        gain_grad = jnp.concatenate((gain_one, gain_two, gain_three), axis=1)
        gain_rows_all = gain_grad.reshape(task_count, parts, -1).transpose(1, 0, 2)
        small = jnp.concatenate((down_rows, up_rows, gain_rows_all), axis=2)
        small = lax.psum_scatter(small, "dp", scatter_dimension=0, tiled=False)
        own_down = small[:, :down_own].astype(bf16)
        own_up = small[:, down_own : 2 * down_own].astype(bf16)
        own_gain = small[:, 2 * down_own :]
        state_grad = lax.psum(
            plain_dot(own_down, down_maker)
            + plain_dot(own_up, up_maker)
            + exact_dot(own_gain, gain_maker.astype(f32)),
            "dp",
        )
        down_maker_grad = inner_cols(own_down, task_low)
        up_maker_grad = inner_cols(own_up, task_low)
        gain_maker_grad = inner_cols(own_gain, task_low.astype(f32), exact_mode)
        table_grad, weight_grad, bias_grad = task_back(state_grad)
    return (
        output.reshape(row_count, seq_len, model_width),
        input_grad.reshape(row_count, seq_len, model_width),
        mem_grad.reshape(row_count, mem_len, model_width),
        *shared,
        table_grad,
        weight_grad,
        bias_grad,
        down_maker_grad,
        up_maker_grad,
        gain_maker_grad,
    )


def solution(mesh):
    rows, whole_copy = P("dp"), P()
    return jax.shard_map(
        on_device,
        mesh=mesh,
        in_specs=(rows,) * 16 + (whole_copy,) * 3 + (rows,) * 3,
        out_specs=(rows,) * 13 + (whole_copy,) * 3 + (rows,) * 3,
        check_vma=False,
    )
```

```python
import functools

import jax
import jax.numpy as jnp
from jax import lax
from jax.experimental import pallas as pl
from jax.experimental.pallas import tpu as pltpu
from jax.sharding import PartitionSpec as P

HEADS = 12
HEAD = 64
ADA = 24
PAIR = 2 * HEAD

exact_mode = lax.Precision.HIGHEST
norm_eps = 1e-06
masked_score = -1e30
bf16 = jnp.bfloat16
f32 = jnp.float32
VMEM_BYTES = 56 << 20


def plain_dot(left_side, right_side):
    return jnp.dot(left_side, right_side, preferred_element_type=f32)


def exact_dot(left_side, right_side):
    return jnp.dot(left_side, right_side, precision=exact_mode, preferred_element_type=f32)


def inner_rows(left_side, right_side):
    return lax.dot_general(
        left_side, right_side, (((1,), (1,)), ((), ())), preferred_element_type=f32
    )


def inner_cols(left_side, right_side, precision_mode=None):
    return lax.dot_general(
        left_side,
        right_side,
        (((0,), (0,)), ((), ())),
        precision=precision_mode,
        preferred_element_type=f32,
    )


def gelu_exact(operand):
    return jax.nn.gelu(operand, approximate=False)


def task_network(table_rows, weight_in, bias_row):
    return gelu_exact(exact_dot(table_rows, weight_in) + bias_row)


def gelu_both(v):
    phi = 0.5 * lax.erf(v * 0.7071067811865476) + 0.5
    slope = phi + v * (jnp.exp(v * v * -0.5) * 0.3989422804014327)
    return v * phi, slope


def token_gain(task_column, gain):
    high = gain.astype(bf16).astype(f32)
    rest = gain - high
    middle = rest.astype(bf16).astype(f32)
    table = jnp.concatenate((high, middle, rest - middle), axis=0).astype(bf16)
    which = lax.broadcasted_iota(jnp.int32, (task_column.shape[0], 24), 1) & 7
    hot = jnp.where(which == task_column, 1.0, 0.0).astype(bf16)
    return plain_dot(hot, table)


def gain_rows(task_column, grads):
    which = lax.broadcasted_iota(jnp.int32, (task_column.shape[0], 8), 1)
    hot = jnp.where(which == task_column, 1.0, 0.0).astype(bf16)
    high = grads.astype(bf16)
    low = (grads - high.astype(f32)).astype(bf16)
    return inner_cols(hot, high) + inner_cols(hot, low)


def inverse_rms(stream):
    return lax.rsqrt(jnp.mean(stream * stream, axis=-1, keepdims=True) + norm_eps)


def norm_back(stream, gain, cotan):
    r = inverse_rms(stream)
    scaled = cotan * gain
    inner = jnp.mean(scaled * stream, axis=-1, keepdims=True)
    return r * (scaled - stream * (r * r * inner)), cotan * (stream * r)


def call(kernel, grid, ins, outs, scratch=(), flops=0, name=None):
    size = sum(a.size * a.dtype.itemsize for a, _, _ in ins)
    size += sum(functools.reduce(lambda p, q: p * q, s, 1) * jnp.dtype(d).itemsize for s, d, _, _ in outs)
    return pl.pallas_call(
        kernel,
        grid=grid,
        in_specs=[pl.BlockSpec(b, m) for _, b, m in ins],
        out_specs=[pl.BlockSpec(b, m) for _, _, b, m in outs],
        out_shape=[jax.ShapeDtypeStruct(s, d) for s, d, _, _ in outs],
        scratch_shapes=list(scratch),
        compiler_params=pltpu.CompilerParams(vmem_limit_bytes=VMEM_BYTES),
        cost_estimate=pl.CostEstimate(flops=flops, bytes_accessed=size, transcendentals=0),
        name=name,
    )(*[a for a, _, _ in ins])


def whole(array):
    return (array, array.shape, lambda *_: (0,) * array.ndim)


def by_row(array, rows):
    return (array, (rows,) + array.shape[1:], lambda i: (i,) + (0,) * (array.ndim - 1))


def out_row(shape, dtype, rows):
    return (shape, dtype, (rows,) + shape[1:], lambda i: (i,) + (0,) * (len(shape) - 1))


def out_whole(shape, dtype):
    return (shape, dtype, shape, lambda *_: (0,) * len(shape))


def pre_kernel(x, task, gain, wq, wk, wv, normed, q, k, v):
    stream = x[...].astype(f32)
    n = (stream * inverse_rms(stream) * token_gain(task[...], gain[...])).astype(bf16)
    normed[...] = n
    q[...] = (plain_dot(n, wq[...]).astype(bf16).astype(f32) * HEAD**-0.5).astype(bf16)
    k[...] = plain_dot(n, wk[...]).astype(bf16)
    v[...] = plain_dot(n, wv[...]).astype(bf16)


def memory_kernel(x, wk, wv, k, v):
    k[...] = plain_dot(x[...], wk[...]).astype(bf16)
    v[...] = plain_dot(x[...], wv[...]).astype(bf16)


def middle_kernel(x, mixed, wo, task, gain, wq, stream_out, normed, q):
    stream = x[...].astype(f32) + plain_dot(mixed[...], wo[...])
    stream_out[...] = stream
    n = (stream * inverse_rms(stream) * token_gain(task[...], gain[...])).astype(bf16)
    normed[...] = n
    q[...] = (plain_dot(n, wq[...]).astype(bf16).astype(f32) * HEAD**-0.5).astype(bf16)


def half_masks():
    lane = lax.broadcasted_iota(jnp.int32, (1, PAIR), 1)
    first = jnp.where(lane < HEAD, 1.0, 0.0)
    return first.astype(bf16), (1.0 - first).astype(bf16)


def attend_forward_kernel(causal, q_ref, k_ref, v_ref, seg_q, seg_k, mixed_ref, p_ref, bias):
    length, keys_all = q_ref.shape[0], k_ref.shape[0]
    step = length // 2 if causal else length

    @pl.when(pl.program_id(1) == 0)
    def _():
        same = seg_q[...] == seg_k[0]
        if causal:
            at_q = lax.broadcasted_iota(jnp.int32, (length, keys_all), 0)
            at_k = lax.broadcasted_iota(jnp.int32, (length, keys_all), 1)
            same = same & (at_q >= at_k)
        bias[...] = jnp.where(same, 0.0, masked_score)

    masks = half_masks()
    for first in range(0, length, step):
        rows = pl.ds(first, step)
        keys = first + step if causal else keys_all
        q = q_ref[rows, :]
        k = k_ref[:keys, :]
        v = v_ref[:keys, :]
        out = None
        for h, mask in enumerate(masks):
            s = inner_rows(q * mask, k) + bias[rows, :keys]
            e = jnp.exp(s - jnp.max(s, axis=-1, keepdims=True))
            p = (e * (1.0 / jnp.sum(e, axis=-1, keepdims=True))).astype(bf16)
            p_ref[0, h, rows, :keys] = p
            part = plain_dot(p, v * mask)
            out = part if out is None else out + part
        mixed_ref[rows, :] = out.astype(bf16)


def attend_backward_kernel(
    causal, q_ref, k_ref, v_ref, mixed_ref, gm_ref, p_ref, gq_ref, gk_ref, gv_ref
):
    length, keys_all = q_ref.shape[0], k_ref.shape[0]
    step = length // 2 if causal else length
    masks = half_masks()
    gk_parts, gv_parts = [], []
    for first in range(0, length, step):
        rows = pl.ds(first, step)
        keys = first + step if causal else keys_all
        q = q_ref[rows, :]
        k = k_ref[:keys, :]
        v = v_ref[:keys, :]
        gm = gm_ref[rows, :]
        product = gm.astype(f32) * mixed_ref[rows, :].astype(f32)
        gq = gk = gv = 0.0
        for h, mask in enumerate(masks):
            inner = jnp.sum(product * mask.astype(f32), axis=-1, keepdims=True)
            p = p_ref[0, h, rows, :keys]
            gm_half = gm * mask
            gw = inner_rows(gm_half, v)
            gs = (p.astype(f32) * (gw - inner)).astype(bf16)
            gv = gv + inner_cols(p, gm_half)
            gq = gq + plain_dot(gs, k * mask)
            gk = gk + inner_cols(gs, q * mask)
        gq_ref[rows, :] = (gq * HEAD**-0.5).astype(bf16)
        gk_parts.append(gk)
        gv_parts.append(gv)
    for ref, terms in ((gk_ref, gk_parts), (gv_ref, gv_parts)):
        if not causal:
            ref[...] = terms[0].astype(bf16)
        else:
            ref[:step, :] = (terms[0] + terms[1][:step]).astype(bf16)
            ref[step:, :] = terms[1][step:].astype(bf16)


def attention_specs(rows, length, arrays):
    return [(a, (length, PAIR), lambda r, p: (r, p)) for a in arrays]


def attend_forward(causal, rows, length, q, k, v, seg_q, seg_k):
    mem_len = k.shape[0] // rows
    mixed, probs = call(
        functools.partial(attend_forward_kernel, causal),
        (rows, HEADS // 2),
        attention_specs(rows, length, (q,))
        + attention_specs(rows, mem_len, (k, v))
        + [
            (seg_q.reshape(rows * length, 1), (length, 1), lambda r, p: (r, 0)),
            (seg_k.reshape(rows, 1, mem_len), (1, 1, mem_len), lambda r, p: (r, 0, 0)),
        ],
        [
            (q.shape, bf16, (length, PAIR), lambda r, p: (r, p)),
            (
                (rows, HEADS, length, mem_len),
                bf16,
                (1, 2, length, mem_len),
                lambda r, p: (r, p, 0, 0),
            ),
        ],
        scratch=[pltpu.VMEM((length, mem_len), f32)],
        flops=4 * rows * HEADS * length * mem_len * PAIR,
        name="attend_forward",
    )
    return mixed, probs


def attend_backward(causal, rows, length, q, k, v, mixed, grad_mixed, probs):
    mem_len = k.shape[0] // rows
    return call(
        functools.partial(attend_backward_kernel, causal),
        (rows, HEADS // 2),
        attention_specs(rows, length, (q,))
        + attention_specs(rows, mem_len, (k, v))
        + attention_specs(rows, length, (mixed, grad_mixed))
        + [(probs, (1, 2, length, mem_len), lambda r, p: (r, p, 0, 0))],
        [
            (q.shape, bf16, (length, PAIR), lambda r, p: (r, p)),
            (k.shape, bf16, (mem_len, PAIR), lambda r, p: (r, p)),
            (k.shape, bf16, (mem_len, PAIR), lambda r, p: (r, p)),
        ],
        flops=8 * rows * HEADS * length * mem_len * PAIR,
        name="attend_backward",
    )


CHUNK = 768
FEED_CHUNK = 768
OUTER_BLOCK = 768


def feed_kernel(
    s1, mixed, wo, task, gain, w_in, w_out, down_all, up_all, cot,
    output, n3, act, gu, gfeed, g2, g2_low, gmix, up_grad, down_grad, gain_grad,
    slope, total,
):
    first = pl.program_id(0) == 0
    units = w_in.shape[1]
    stream = s1[...] + plain_dot(mixed[...], wo[...])
    picked = token_gain(task[...], gain[...])
    n3[...] = (stream * inverse_rms(stream) * picked).astype(bf16)
    parts = [slice(k, k + FEED_CHUNK) for k in range(0, units, FEED_CHUNK)]
    normed = n3[...]
    hidden = plain_dot(normed, w_in[:, parts[0]])
    feed = None
    for k, cols in enumerate(parts):
        now = hidden
        if k + 1 < len(parts):
            hidden = plain_dot(normed, w_in[:, parts[k + 1]])
        value, rate = gelu_both(now)
        value = value.astype(bf16)
        act[:, cols] = value
        slope[:, cols] = rate.astype(bf16)
        term = plain_dot(value, w_out[cols, :])
        feed = term if feed is None else feed + term
    feed_low = feed.astype(bf16)
    tokens, wide = stream.shape[0], down_all.shape[1]
    owner = lax.broadcasted_iota(jnp.int32, (tokens, wide), 1) - task[...] * ADA
    mask = jnp.where((owner >= 0) & (owner < ADA), 1.0, 0.0)
    narrow, narrow_slope = gelu_both(plain_dot(feed_low, down_all[...]) * mask)
    narrow = narrow.astype(bf16)
    output[...] = (stream + feed + plain_dot(narrow, up_all[...])).astype(bf16)
    cotan = cot[...]
    gb = (narrow_slope * inner_rows(cotan, up_all[...]) * mask).astype(bf16)
    grad_feed = (cotan.astype(f32) + inner_rows(gb, down_all[...])).astype(bf16)
    gfeed[...] = grad_feed
    up_now = inner_cols(narrow, cotan)
    down_now = inner_cols(feed_low, gb)
    total[...] = jnp.zeros_like(total)

    @pl.loop(0, units // CHUNK)
    def _(j):
        cols = pl.ds(pl.multiple_of(j * CHUNK, CHUNK), CHUNK)
        grad = slope[:, cols].astype(f32) * inner_rows(gfeed[...], w_out[cols, :])
        grad = grad.astype(bf16)
        gu[:, cols] = grad
        total[...] += inner_rows(grad, w_in[:, cols])

    stream_grad, gain_tokens = norm_back(stream, picked, total[...])
    grad_two = cotan.astype(f32) + stream_grad
    g2[...] = grad_two
    low = grad_two.astype(bf16)
    g2_low[...] = low
    gmix[...] = inner_rows(low, wo[...]).astype(bf16)
    gain_now = gain_rows(task[...], gain_tokens)

    @pl.when(first)
    def _():
        up_grad[...] = up_now
        down_grad[...] = down_now
        gain_grad[...] = gain_now

    @pl.when(jnp.logical_not(first))
    def _():
        up_grad[...] += up_now
        down_grad[...] += down_now
        gain_grad[...] += gain_now


def cross_back_kernel(gq, wq, s1, task, gain, g2, wo, g1, g1_low, gmix, gain_grad):
    stream = s1[...]
    picked = token_gain(task[...], gain[...])
    stream_grad, gain_tokens = norm_back(stream, picked, inner_rows(gq[...], wq[...]))
    grad_one = g2[...] + stream_grad
    g1[...] = grad_one
    low = grad_one.astype(bf16)
    g1_low[...] = low
    gmix[...] = inner_rows(low, wo[...]).astype(bf16)
    accumulate(gain_grad, gain_rows(task[...], gain_tokens))


def accumulate(ref, value):
    @pl.when(pl.program_id(0) == 0)
    def _():
        ref[...] = value

    @pl.when(pl.program_id(0) != 0)
    def _():
        ref[...] += value


def memory_back_kernel(gk, gv, wk, wv, out):
    out[...] = inner_rows(gk[...], wk[...]) + inner_rows(gv[...], wv[...])


def input_back_kernel(gq, gk, gv, wq, wk, wv, x, task, gain, g1, out, gain_grad):
    stream = x[...].astype(f32)
    picked = token_gain(task[...], gain[...])
    cotan = inner_rows(gq[...], wq[...]) + inner_rows(gk[...], wk[...])
    cotan = cotan + inner_rows(gv[...], wv[...])
    stream_grad, gain_tokens = norm_back(stream, picked, cotan)
    out[...] = g1[...] + stream_grad
    accumulate(gain_grad, gain_rows(task[...], gain_tokens))


def outer_kernel(which, sources, *refs):
    left = refs[:sources]
    right = refs[sources : sources + len(which)]
    outs = refs[sources + len(which) :]
    for source, grad, out in zip(which, right, outs):
        for first in range(0, out.shape[1], CHUNK):
            cols = slice(first, first + CHUNK)
            out[:, cols] = inner_cols(left[source][...], grad[:, cols]).astype(bf16)


def outers(sources, grads, which, name):
    tokens, width = sources[0].shape
    block = OUTER_BLOCK if width > 768 else 256
    return call(
        functools.partial(outer_kernel, which, len(sources)),
        (width // block,),
        [(s, (tokens, block), lambda i: (0, i)) for s in sources] + [whole(g) for g in grads],
        [((width, g.shape[1]), bf16, (block, g.shape[1]), lambda i: (i, 0)) for g in grads],
        flops=sum(2 * tokens * width * g.shape[1] for g in grads),
        name=name,
    )


BLOCK = 512


def low_out(shape):
    return out_row(shape, bf16, BLOCK)


def full_out(shape):
    return out_row(shape, f32, BLOCK)


def attention_layers(x, mem, segments, mem_segments, task, weights, gain_table):
    rows, length = segments.shape
    tokens, width = x.shape
    wq1, wk1, wv1, wo1, wq2, wk2, wv2 = weights[:7]
    gain_one, gain_two = (gain_table[:, i * width : (i + 1) * width] for i in range(2))
    block = BLOCK
    grid = (tokens // block,)
    act_shape = (tokens, width)
    square = 2 * tokens * width * width
    n1, q1, k1, v1 = call(
        pre_kernel,
        grid,
        [by_row(x, block), by_row(task, block)] + [whole(a) for a in (gain_one, wq1, wk1, wv1)],
        [low_out(act_shape) for _ in range(4)],
        flops=3 * square,
        name="self_projections",
    )
    m1, p1 = attend_forward(True, rows, length, q1, k1, v1, segments, segments)
    s1, n2, q2 = call(
        middle_kernel,
        grid,
        [by_row(x, block), by_row(m1, block), whole(wo1), by_row(task, block), whole(gain_two), whole(wq2)],
        [full_out(act_shape), low_out(act_shape), low_out(act_shape)],
        flops=2 * square,
        name="middle",
    )
    k2, v2 = call(
        memory_kernel,
        grid,
        [by_row(mem, block), whole(wk2), whole(wv2)],
        [low_out(mem.shape), low_out(mem.shape)],
        flops=2 * square,
        name="memory_projections",
    )
    m2, p2 = attend_forward(False, rows, length, q2, k2, v2, segments, mem_segments)
    return (n1, q1, k1, v1, m1, s1, n2, q2, k2, v2, m2), p1, p2


def feed_forward(s1, m2, cot, task, weights, gain_table, down_all, up_all):
    tokens, width = s1.shape
    wo2, w_in, w_out = weights[7:]
    block = BLOCK
    grid = (tokens // block,)
    act_shape = (tokens, width)
    square = 2 * tokens * width * width
    units = w_in.shape[1]
    wide = up_all.shape[0]
    tasks = gain_table.shape[0]
    output, n3, act, gu, gfeed, g2, g2_low, gmix2, up_grad, down_grad, gain3 = call(
        feed_kernel,
        grid,
        [
            by_row(s1, block), by_row(m2, block), whole(wo2), by_row(task, block),
            (gain_table, (gain_table.shape[0], width), lambda *_: (0, 2)), whole(w_in), whole(w_out), whole(down_all), whole(up_all), by_row(cot, block),
        ],
        [
            low_out(act_shape), low_out(act_shape), out_row((tokens, units), bf16, block), out_row((tokens, units), bf16, block),
            low_out(act_shape), full_out(act_shape), low_out(act_shape), low_out(act_shape),
            out_whole((wide, width), f32), out_whole((width, wide), f32), out_whole((tasks, width), f32),
        ],
        scratch=[pltpu.VMEM((block, units), bf16), pltpu.VMEM((block, width), f32)],
        flops=2 * square + 8 * tokens * width * units,
        name="feed_forward_and_back",
    )
    (hidden_out_grad,) = outers((act,), (gfeed,), (0,), "hidden_out_grad")
    return output, g2, g2_low, gmix2, n3, gu, hidden_out_grad, up_grad, down_grad, gain3


def attention_back(x, mem, rows, task, weights, gain_table, saved, p1, p2, g2, g2_low, gmix2):
    n1, q1, k1, v1, m1, s1, n2, q2, k2, v2, m2 = saved
    tokens, width = x.shape
    length = tokens // rows
    wq1, wk1, wv1, wo1, wq2, wk2, wv2 = weights[:7]
    gain_one, gain_two = (gain_table[:, i * width : (i + 1) * width] for i in range(2))
    tasks = gain_table.shape[0]
    block = BLOCK
    grid = (tokens // block,)
    act_shape = (tokens, width)
    square = 2 * tokens * width * width
    gq2, gk2, gv2 = attend_backward(False, rows, length, q2, k2, v2, m2, gmix2, p2)
    g1, g1_low, gmix1, gain2 = call(
        cross_back_kernel,
        grid,
        [
            by_row(gq2, block), whole(wq2), by_row(s1, block), by_row(task, block), whole(gain_two),
            by_row(g2, block), whole(wo1),
        ],
        [full_out(act_shape), low_out(act_shape), low_out(act_shape), out_whole((tasks, width), f32)],
        flops=2 * square,
        name="cross_back",
    )
    (mem_grad,) = call(
        memory_back_kernel,
        grid,
        [by_row(gk2, block), by_row(gv2, block), whole(wk2), whole(wv2)],
        [full_out(act_shape)],
        flops=2 * square,
        name="memory_back",
    )
    wo2_grad, wq2_grad, wk2_grad, wv2_grad = outers(
        (m2, n2, mem), (g2_low, gq2, gk2, gv2), (0, 1, 2, 2), "cross_grads"
    )
    gq1, gk1, gv1 = attend_backward(True, rows, length, q1, k1, v1, m1, gmix1, p1)
    input_grad, gain1 = call(
        input_back_kernel,
        grid,
        [
            by_row(gq1, block), by_row(gk1, block), by_row(gv1, block), whole(wq1), whole(wk1), whole(wv1),
            by_row(x, block), by_row(task, block), whole(gain_one), by_row(g1, block),
        ],
        [full_out(act_shape), out_whole((tasks, width), f32)],
        flops=3 * square,
        name="input_back",
    )
    wo1_grad, wq1_grad, wk1_grad, wv1_grad = outers(
        (m1, n1), (g1_low, gq1, gk1, gv1), (0, 1, 1, 1), "self_grads"
    )
    grads = (wq1_grad, wk1_grad, wv1_grad, wo1_grad, wq2_grad, wk2_grad, wv2_grad, wo2_grad)
    return input_grad, mem_grad, grads, gain1, gain2


LINE = 4
MESH = pl.DeviceIdType.MESH


class Place:
    def __init__(self):
        me = lax.axis_index("dp")
        self.core = lax.rem(me, 2)
        self.x = lax.rem(me // 2, 2)
        self.y = lax.rem(me // 4, 2)
        self.z = me // 8

    def at(self, z=None, y=None, x=None, core=None):
        z = self.z if z is None else z
        y = self.y if y is None else y
        x = self.x if x is None else x
        core = self.core if core is None else core
        return (((z * 2 + y) * 2 + x) * 2 + core,)

    def sibling(self):
        return self.at(core=1 - self.core)

    def over_x(self):
        return self.at(x=1 - self.x)

    def over_y(self):
        return self.at(y=1 - self.y)

    def along_z(self, k):
        return self.at(z=lax.rem(self.z + k, LINE))

    def partners(self):
        return [self.sibling(), self.over_x(), self.over_y()] + [self.along_z(k) for k in (1, 2, 3)]


def meet(place):
    barrier = pltpu.get_barrier_semaphore()
    partners = place.partners()
    for partner in partners:
        pl.semaphore_signal(barrier, inc=1, device_id=partner, device_id_type=MESH)
    pl.semaphore_wait(barrier, len(partners))


class Copies:
    def __init__(self, send, recv):
        self.send, self.recv, self.used, self.open = send, recv, 0, []

    def remote(self, source, target, device):
        copy = pltpu.make_async_remote_copy(
            src_ref=source,
            dst_ref=target,
            send_sem=self.send.at[self.used],
            recv_sem=self.recv.at[self.used],
            device_id=device,
            device_id_type=MESH,
        )
        self.used += 1
        copy.start()
        self.open.append(copy)
        return copy

    def local(self, source, target):
        copy = pltpu.make_async_copy(source, target, self.recv.at[self.used])
        self.used += 1
        copy.start()
        return copy

    def close(self, copy):
        copy.wait_send()
        self.open = [other for other in self.open if other is not copy]

    def finish(self):
        for copy in self.open:
            copy.wait_send()


FIRST_PACE = 1
PACE = 2


class Unit:
    def __init__(self, here, copies, source, whole_array, index, first, second):
        self.here, self.copies = here, copies
        self.source, self.array = source, whole_array
        self.index, self.shares = index, (first, second)
        self.going = {}

    def window(self, zs, ys, xs, share=None):
        return self.array.at[(zs, ys, xs) + (self.index if share is None else self.shares[share])]

    def depart(self):
        here, copies = self.here, self.copies
        source = self.source(None)
        target = self.window(here.z, here.y, here.x)
        self.going["z"] = [copies.remote(source, target, here.along_z(k)) for k in (1, 2, 3)]
        self.own = copies.local(source, target)

    def turn(self):
        here = self.here
        for copy in self.going["z"]:
            copy.wait_recv()
        self.own.wait()
        one = self.window(slice(None), here.y, here.x, 0)
        two = self.window(slice(None), here.y, here.x, 1)
        self.going["1"] = [
            self.copies.remote(one, one, here.over_x()),
            self.copies.remote(two, two, here.over_y()),
        ]

    def turn_again(self):
        here = self.here
        for copy in self.going["1"]:
            copy.wait_recv()
        one = self.window(slice(None), here.y, slice(None), 0)
        two = self.window(slice(None), slice(None), here.x, 1)
        self.going["2"] = [
            self.copies.remote(one, one, here.over_y()),
            self.copies.remote(two, two, here.over_x()),
        ]

    def cross(self):
        for copy in self.going["2"]:
            copy.wait_recv()
        part = self.window(slice(None), slice(None), slice(None))
        self.going["c"] = self.copies.remote(part, part, self.here.sibling())

    def settle(self):
        self.going["c"].wait_recv()

    def stages(self):
        return (self.depart, self.turn, self.turn_again, self.cross, self.settle)


def column_of(row):
    length = row.shape[1]
    at_q = lax.broadcasted_iota(jnp.int32, (length, length), 0)
    at_k = lax.broadcasted_iota(jnp.int32, (length, length), 1)
    picked = jnp.where(at_q == at_k, row.astype(f32), 0.0)
    return jnp.sum(picked, axis=1, keepdims=True).astype(jnp.int32)


def forward_kernel(*refs):
    (
        x, mem, segments, mem_segments, tasks,
        sq, sk, sv, so, cq, ck, cv, co, w_in, w_out,
        table, weight, bias_row, down, up, gain,
    ) = refs[:21]
    outs, made_out, gains_out = refs[21:31], refs[31], refs[32]
    low_out, gain_out, task_out = refs[33:36]
    saved_out = refs[36:47]
    p1_out, p2_out = refs[47:49]
    scratch = refs[49:]
    wide, halves, blocks = scratch[:10], scratch[10:20], scratch[20:30]
    local_w = scratch[30:38]
    saved = scratch[38:49]
    n1, q1, k1, v1, m1, s1, n2, q2, k2, v2, m2 = saved
    made, gain_rows_all, bias, probs, send, recv, p_sem, load_sem, save_sem, gain_full = scratch[49:]
    own = (sq, sk, sv, so, cq, ck, cv, co, w_in, w_out)
    rows_total, length = segments.shape
    mem_len = mem_segments.shape[1]
    here = Place()
    copies = Copies(send, recv)
    c = here.core

    def half(i, core, first=0, width=None):
        full = own[i].shape[1] // 2
        width = full if width is None else width
        return pl.ds(pl.multiple_of(core * full + first, 128), width)

    for i in range(10):
        wide[i][...] = own[i][...].astype(f32)
    gain_rows_all[...] = gain[...].astype(f32)
    probs[...] = jnp.zeros_like(probs)
    meet(here)
    pair = {}
    order = (0, 1, 2, 5, 6, 3, 4, 7, 8, 9)
    for i in order:
        rows = own[i].shape[0]
        mine = pl.ds(pl.multiple_of(c * rows, 8), rows)
        pair[i] = copies.remote(
            wide[i].at[:, half(i, 1 - c)], halves[i].at[mine, :], here.sibling()
        )
        halves[i][mine, :] = wide[i][:, half(i, c)]

    opened = set()

    def piece(i, rows, first, width):
        at = half(i, c, first, width)
        count = rows.stop - rows.start
        if (width // 2) % 128 == 0:
            windows = (
                (rows, half(i, c, first, width // 2)),
                (rows, half(i, c, first + width // 2, width // 2)),
            )
            local = (
                (rows, pl.ds(first, width // 2)),
                (rows, pl.ds(first + width // 2, width // 2)),
            )
        else:
            cut = rows.start + (count // 2 if count % 32 == 0 else (count // 32 + i % 2) * 16)
            split = (slice(rows.start, cut), slice(cut, rows.stop))
            windows = tuple((part, at) for part in split)
            local = tuple((part, pl.ds(first, width)) for part in split)

        def source(share):
            if i not in opened:
                opened.add(i)
                pair[i].wait_recv()
                blocks[i][...] = halves[i][...].astype(bf16)
            return blocks[i].at[(rows, pl.ds(first, width)) if share is None else local[share]]

        return Unit(here, copies, source, outs[i], (rows, at), *windows)

    def square(i):
        return piece(i, slice(0, outs[i].shape[3]), 0, own[i].shape[1] // 2)

    gain_own = gain.shape[0]
    gain_cut = gain_own // 16 * 8
    made_cut = made.shape[1] // 256 * 128
    gain_unit = Unit(
        here, copies, lambda _: gain_rows_all, gains_out, (c,),
        (c, pl.ds(0, gain_cut)), (c, pl.ds(gain_cut, gain_own - gain_cut)),
    )
    made_unit = Unit(
        here, copies, lambda _: made, made_out, (c,),
        (c, slice(None), pl.ds(0, made_cut)), (c, slice(None), pl.ds(made_cut, made.shape[1] - made_cut)),
    )
    in_half = w_in.shape[1] // 4
    out_rows = outs[9].shape[3]
    units = [gain_unit] + [square(i) for i in (0, 1, 2, 5, 6, 3, 4, 7)]
    units += [
        piece(8, slice(0, outs[8].shape[3]), k * in_half, in_half) for k in (0, 1)
    ]
    units += [made_unit]
    units += [
        piece(
            9, slice(k * out_rows // 2, (k + 1) * out_rows // 2), 0, w_out.shape[1] // 2
        )
        for k in (0, 1)
    ]
    loads = {}
    landing = {1: (0,), 2: (1,), 3: (2,), 4: (5,), 5: (6,), 6: (3,), 7: (4,), 8: (7,)}

    def stage_at(u, turn):
        pace = FIRST_PACE if u < 4 else PACE
        return (turn - u) // pace if turn >= u and (turn - u) % pace == 0 else -1

    def tick(turn):
        for u in range(min(turn, len(units) - 1), -1, -1):
            if stage_at(u, turn) == 0:
                units[u].depart()
        for u in reversed(range(len(units))):
            late = stage_at(u, turn)
            if not 0 < late < 5:
                continue
            units[u].stages()[late]()
            if late == 4 and u in landing:
                (i,) = landing[u]
                loads[i] = pltpu.make_async_copy(outs[i], local_w[i], load_sem.at[i])
                loads[i].start()
            if late == 4 and u == 0:
                loads["gain"] = pltpu.make_async_copy(gains_out, gain_full, load_sem.at[8])
                loads["gain"].start()

    def matrix(i):
        return local_w[i][...].reshape(-1, own[i].shape[1])

    state = gelu_in_kernel(exact_dot(table[...], weight[...]) + bias_row[...])
    low = state.astype(bf16)
    low_out[...] = low
    values = jnp.concatenate((inner_rows(low, down[...]), inner_rows(low, up[...])), axis=0)
    made[...] = jnp.zeros_like(made)
    made[:, : down.shape[0]] = values.astype(bf16)

    for turn in range(3 + 4 * FIRST_PACE + 1):
        tick(turn)
    ticks = iter(range(3 + 4 * FIRST_PACE + 1, len(units) + 4 * PACE))

    def between():
        turn = next(ticks, None)
        if turn is not None:
            tick(turn)

    stores = []

    def store(which, part=None):
        source, target = saved[which], saved_out[which]
        copy = pltpu.make_async_copy(source, target, save_sem.at[which])
        copy.start()
        stores.append(copy)

    for r in range(rows_total):
        column = column_of(segments[r : r + 1, :])
        task = jnp.zeros_like(column)
        for s in range(tasks.shape[1]):
            task = task + jnp.where(column == s, tasks[r : r + 1, s : s + 1], 0)
        task_out[r * length : (r + 1) * length, :] = task
    loads["gain"].wait()
    width = x.shape[1]
    gain_out[...] = 1.0 + inner_rows(low, gain_full[...].reshape(-1, gain.shape[1]).astype(bf16))

    def picked(r, which):
        task = task_out[r * length : (r + 1) * length, :]
        return token_gain(task, gain_out[:, which * width : (which + 1) * width])

    def row(r, size=None):
        size = length if size is None else size
        return slice(r * size, (r + 1) * size)

    for i in (0, 1, 2):
        loads[i].wait()
    for r in range(rows_total):
        stream = x[row(r), :].astype(f32)
        n = (stream * inverse_rms(stream) * picked(r, 0)).astype(bf16)
        n1[row(r), :] = n
        q1[row(r), :] = (plain_dot(n, matrix(0)).astype(bf16).astype(f32) * HEAD**-0.5).astype(bf16)
        k1[row(r), :] = plain_dot(n, matrix(1)).astype(bf16)
        v1[row(r), :] = plain_dot(n, matrix(2)).astype(bf16)
        between()
    for which in (0, 1, 2, 3):
        store(which)


    def attend(causal, q, k, v, mixed, p_out, r, keys_row):
        column = column_of(segments[r : r + 1, :])
        same = column == keys_row
        if causal:
            at_q = lax.broadcasted_iota(jnp.int32, same.shape, 0)
            at_k = lax.broadcasted_iota(jnp.int32, same.shape, 1)
            same = same & (at_q >= at_k)
        bias[...] = jnp.where(same, 0.0, masked_score)
        keys_total = keys_row.shape[1]
        per_group = HEADS // 4
        for group in range(2):
            @pl.loop(group * per_group, (group + 1) * per_group)
            def _(p):
                slot = lax.rem(p, 2)
                at = pl.ds(pl.multiple_of(p * PAIR, PAIR), PAIR)

                @pl.when(p >= 2)
                def _():
                    pltpu.make_async_copy(
                        probs.at[slot], p_out.at[r, pl.ds(2 * p - 4, 2)], p_sem.at[slot]
                    ).wait()

                attend_pair(causal, q, k, v, mixed, probs.at[slot], bias, row(r), row(r, keys_total), at)
                pltpu.make_async_copy(
                    probs.at[slot], p_out.at[r, pl.ds(2 * p, 2)], p_sem.at[slot]
                ).start()

            between()
        for p in (HEADS // 2 - 2, HEADS // 2 - 1):
            pltpu.make_async_copy(
                probs.at[p % 2], p_out.at[r, pl.ds(2 * p, 2)], p_sem.at[p % 2]
            ).wait()

    for r in range(rows_total):
        attend(True, q1, k1, v1, m1, p1_out, r, segments[r : r + 1, :])
    store(4)
    for i in (5, 6):
        loads[i].wait()
    for r in range(rows_total):
        mine = row(r, mem_len)
        k2[mine, :] = plain_dot(mem[mine, :], matrix(5)).astype(bf16)
        v2[mine, :] = plain_dot(mem[mine, :], matrix(6)).astype(bf16)
        between()
    store(8)
    store(9)
    for i in (3, 4):
        loads[i].wait()
    for r in range(rows_total):
        stream = x[row(r), :].astype(f32) + plain_dot(m1[row(r), :], matrix(3))
        s1[row(r), :] = stream
        n = (stream * inverse_rms(stream) * picked(r, 1)).astype(bf16)
        n2[row(r), :] = n
        q2[row(r), :] = (plain_dot(n, matrix(4)).astype(bf16).astype(f32) * HEAD**-0.5).astype(bf16)
        between()
    for which in (5, 6, 7):
        store(which)
    for r in range(rows_total):
        attend(False, q2, k2, v2, m2, p2_out, r, mem_segments[r : r + 1, :])
    store(10)
    for turn in ticks:
        tick(turn)
    loads[7].wait()
    for copy in stores:
        copy.wait()
    copies.finish()


def gelu_in_kernel(v):
    return v * (0.5 * lax.erf(v * 0.7071067811865476) + 0.5)


def attend_pair(causal, q_ref, k_ref, v_ref, mixed_ref, p_ref, bias, q_rows, k_rows, at):
    length = q_rows.stop - q_rows.start
    keys_all = k_rows.stop - k_rows.start
    step = length // 2 if causal else length
    masks = half_masks()
    for first in range(0, length, step):
        rows = slice(q_rows.start + first, q_rows.start + first + step)
        keys = first + step if causal else keys_all
        q = q_ref[rows, at]
        k = k_ref[k_rows.start : k_rows.start + keys, at]
        v = v_ref[k_rows.start : k_rows.start + keys, at]
        out = None
        for h, mask in enumerate(masks):
            s = inner_rows(q * mask, k) + bias[first : first + step, :keys]
            e = jnp.exp(s - jnp.max(s, axis=-1, keepdims=True))
            p = (e * (1.0 / jnp.sum(e, axis=-1, keepdims=True))).astype(bf16)
            p_ref[h, first : first + step, :keys] = p
            part = plain_dot(p, v * mask)
            out = part if out is None else out + part
        mixed_ref[rows, at] = out.astype(bf16)


def forward(x, mem, segments, mem_segments, tasks, weights, table, weight, bias_row, makers):
    down, up, gain = makers
    own = weights
    tokens, width = x.shape
    mem_tokens = mem.shape[0]
    rows, length = segments.shape
    mem_len = mem_segments.shape[1]
    spaces = (LINE, 2, 2)
    any_space = pl.BlockSpec(memory_space=pl.ANY)
    vmem = pl.BlockSpec(memory_space=pltpu.VMEM)
    made_half = down.shape[0] + (-down.shape[0] % 128)
    n_tasks = table.shape[0]
    chip = [spaces + (2 * a.shape[0], a.shape[1]) for a in own]
    t_low, m_low, t_full = ((tokens, width), bf16), ((mem_tokens, width), bf16), ((tokens, width), f32)
    kept = [t_low, t_low, t_low, t_low, t_low, t_full, t_low, t_low, m_low, m_low, t_low]
    shape = jax.ShapeDtypeStruct
    probs = (rows, HEADS, length, mem_len)
    copies = 11 * 16 + 32
    outs = pl.pallas_call(
        forward_kernel,
        in_specs=[vmem] * 21,
        out_specs=[any_space] * 12 + [vmem] * 3 + [any_space] * 13,
        out_shape=[shape(s, bf16) for s in chip]
        + [
            shape(spaces + (2, 2 * n_tasks, made_half), bf16),
            shape(spaces + (2,) + gain.shape, f32),
            shape((n_tasks, weight.shape[1]), bf16),
            shape((n_tasks, 3 * width), f32),
            shape((tokens, 1), jnp.int32),
        ]
        + [shape(s, d) for s, d in kept]
        + [shape((rows, HEADS, length, length), bf16), shape(probs, bf16)],
        scratch_shapes=[pltpu.VMEM(a.shape, f32) for a in own]
        + [pltpu.VMEM((2 * a.shape[0], a.shape[1] // 2), f32) for a in own]
        + [pltpu.VMEM((2 * a.shape[0], a.shape[1] // 2), bf16) for a in own]
        + [pltpu.VMEM(s, bf16) for s in chip[:8]]
        + [pltpu.VMEM(s, d) for s, d in kept]
        + [
            pltpu.VMEM((2 * n_tasks, made_half), bf16),
            pltpu.VMEM(gain.shape, f32),
            pltpu.VMEM((length, max(length, mem_len)), f32),
            pltpu.VMEM((2, 2, length, max(length, mem_len)), bf16),
            pltpu.SemaphoreType.DMA((copies,)),
            pltpu.SemaphoreType.DMA((copies,)),
            pltpu.SemaphoreType.DMA((2,)),
            pltpu.SemaphoreType.DMA((9,)),
            pltpu.SemaphoreType.DMA((11,)),
            pltpu.VMEM(spaces + (2,) + gain.shape, f32),
        ],
        compiler_params=pltpu.CompilerParams(
            collective_id=0, has_side_effects=True, vmem_limit_bytes=VMEM_BYTES
        ),
        name="forward_as_weights_arrive",
    )(x, mem, segments, mem_segments, tasks, *own, table, weight, bias_row, down, up, gain)
    return outs


BACK_PACES = (2, 6, 6, 6, 3)
QUICK_PACES = (1, 1, 1, 1)
EARLY_TICKS = 3


class Stepwise:
    def __init__(self, stages, paces):
        self.stages, self.paces = list(stages), list(paces)

    def advance(self, now):
        self.stages.pop(0)()
        self.due = now + (self.paces.pop(0) if self.stages else 0)


class Traffic:
    def __init__(self):
        self.ready, self.flying, self.now = [], [], 0

    def add(self, item):
        self.ready.append(item)

    def tick(self):
        self.now += 1
        for item in reversed(list(self.flying)):
            if self.now >= item.due:
                item.advance(self.now)
        self.flying = [item for item in self.flying if item.stages]
        if self.ready:
            item = self.ready.pop(0)
            item.advance(self.now)
            self.flying.append(item)

    def drain(self):
        while self.ready or self.flying:
            self.tick()


class Summed(Stepwise):
    def __init__(self, here, copies, theirs, mine, shares, slots, out, out_first, fetch=None):
        super().__init__(
            [self.begin, self.over_first, self.over_second, self.over_line, self.to_owner, self.end],
            BACK_PACES,
        )
        self.here, self.copies = here, copies
        self.theirs, self.mine, self.fetch = theirs, mine, fetch
        self.shares, self.slots, self.out, self.out_first = shares, slots, out, out_first
        self.landed = self.follower = None
        self.follows = self.added = False

    def begin(self):
        self.core = self.copies.remote(self.theirs, self.slots[0], self.here.sibling())
        if self.fetch is not None and not self.follows:
            self.start_fetch()

    def start_fetch(self):
        self.local = self.copies.local(*self.fetch)

    def over_first(self):
        here, held = self.here, self.slots[0]
        if self.fetch is not None:
            self.local.wait()
        self.core.wait_recv()
        held[...] += self.mine()
        self.added = True
        if self.follower is not None:
            self.follower.start_fetch()
        one, two = self.shares
        self.first = (
            self.copies.remote(held.at[(slice(None), 1 - here.y, slice(None)) + one], self.slots[1], here.over_y()),
            self.copies.remote(held.at[(slice(None), slice(None), 1 - here.x) + two], self.slots[2], here.over_x()),
        )

    def over_second(self):
        here, held = self.here, self.slots[0]
        one, two = self.shares
        self.first[0].wait_recv()
        held[(slice(None), here.y, slice(None)) + one] += self.slots[1][...]
        self.first[1].wait_recv()
        held[(slice(None), slice(None), here.x) + two] += self.slots[2][...]
        self.second = (
            self.copies.remote(held.at[(slice(None), here.y, 1 - here.x) + one], self.slots[3], here.over_x()),
            self.copies.remote(held.at[(slice(None), 1 - here.y, here.x) + two], self.slots[4], here.over_y()),
        )

    def over_line(self):
        here, held = self.here, self.slots[0]
        one, two = self.shares
        self.second[0].wait_recv()
        held[(slice(None), here.y, here.x) + one] += self.slots[3][...]
        self.second[1].wait_recv()
        held[(slice(None), here.y, here.x) + two] += self.slots[4][...]
        self.third = [
            self.copies.remote(
                held.at[lax.rem(here.z + k, LINE), here.y, here.x],
                self.slots[5].at[k - 1],
                here.along_z(k),
            )
            for k in (1, 2, 3)
        ]

    def gathered(self):
        here = self.here
        total = self.slots[0][here.z, here.y, here.x].astype(f32)
        for k, copy in enumerate(self.third):
            copy.wait_recv()
            total = total + self.slots[5][k].astype(f32)
        return total

    def window(self, core, width, full):
        return pl.ds(pl.multiple_of(core * full + self.out_first, 128), width)

    def to_owner(self):
        here, final = self.here, self.slots[6]
        final[...] = self.gathered()
        rows, full = self.out.shape[0], self.out.shape[1] // 2
        c = here.core
        at = self.window(c, final.shape[1], full)
        theirs = pl.ds(pl.multiple_of((1 - c) * rows, 8), rows)
        self.last = self.copies.remote(final.at[theirs, :], self.out.at[:, at], here.sibling())
        self.out[:, at] = final[pl.ds(pl.multiple_of(c * rows, 8), rows), :]

    def end(self):
        self.last.wait_recv()
        if self.landed is not None:
            self.landed()


class Everywhere(Stepwise):
    def __init__(self, here, copies, value, sent, arriving, out):
        super().__init__([self.begin, self.step_x, self.step_y, self.step_z, self.end], QUICK_PACES)
        self.here, self.copies, self.value = here, copies, value
        self.sent, self.arriving, self.out = sent, arriving, out

    def send(self, turn, device):
        self.sent[turn] = self.total
        self.copy = self.copies.remote(self.sent.at[turn], self.arriving.at[turn], device)

    def add(self, turn):
        self.copy.wait_recv()
        self.total = self.total + self.arriving[turn]

    def begin(self):
        self.total = self.value()
        self.send(0, self.here.sibling())

    def step_x(self):
        self.add(0)
        self.send(1, self.here.over_x())

    def step_y(self):
        self.add(1)
        self.send(2, self.here.over_y())

    def step_z(self):
        self.add(2)
        self.sent[3] = self.total
        self.around = [
            self.copies.remote(self.sent.at[3], self.arriving.at[2 + k], self.here.along_z(k))
            for k in (1, 2, 3)
        ]

    def end(self):
        for copy in self.around:
            copy.wait_recv()
        total = jnp.zeros_like(self.total)
        for line in range(LINE):
            for k in range(LINE):
                term = self.total if k == 0 else self.arriving[2 + k]
                here_now = lax.rem(self.here.z - k + LINE, LINE) == line
                total = total + jnp.where(here_now, term, 0.0)
        self.out[...] = total


def attend_pair_back(causal, q_ref, k_ref, v_ref, mixed_ref, gm_ref, p_ref, gq_ref, gk_ref, gv_ref, start, k_start, at, length, keys_all):
    step = length // 2 if causal else length
    masks = half_masks()
    gk_parts, gv_parts = [], []
    for first in range(0, length, step):
        rows = pl.ds(start + first, step)
        keys = first + step if causal else keys_all
        key_rows = pl.ds(k_start, keys)
        q, k, v = q_ref[rows, at], k_ref[key_rows, at], v_ref[key_rows, at]
        gm = gm_ref[rows, at]
        product = gm.astype(f32) * mixed_ref[rows, at].astype(f32)
        gq = gk = gv = 0.0
        for h, mask in enumerate(masks):
            inner = jnp.sum(product * mask.astype(f32), axis=-1, keepdims=True)
            p = p_ref[h, first : first + step, :keys]
            gm_half = gm * mask
            gw = inner_rows(gm_half, v)
            gs = (p.astype(f32) * (gw - inner)).astype(bf16)
            gv = gv + inner_cols(p, gm_half)
            gq = gq + plain_dot(gs, k * mask)
            gk = gk + inner_cols(gs, q * mask)
        gq_ref[rows, at] = (gq * HEAD**-0.5).astype(bf16)
        gk_parts.append(gk)
        gv_parts.append(gv)
    for ref, terms in ((gk_ref, gk_parts), (gv_ref, gv_parts)):
        if not causal:
            ref[pl.ds(k_start, keys_all), at] = terms[0].astype(bf16)
        else:
            ref[pl.ds(k_start, step), at] = (terms[0] + terms[1][:step]).astype(bf16)
            ref[pl.ds(k_start + step, step), at] = terms[1][step:].astype(bf16)


SUM_NAMES = ("q1", "k1", "v1", "o1", "q2", "k2", "v2", "o2", "in0", "in1", "out0", "out1", "small")


def sum_pieces(width, units, own):
    rows = 2 * own
    half = width // 2
    pieces = {}
    for turn, name in enumerate(SUM_NAMES[:8]):
        cut = rows // 2 if rows % 32 == 0 else (rows // 32 + turn % 2) * 16
        pieces[name] = (rows, half, 0, (slice(0, cut), slice(0, half)), (slice(cut, rows), slice(0, half)))
    part = units // 4
    for k in (0, 1):
        pieces[f"in{k}"] = (
            rows, part, k * part,
            (slice(0, rows), slice(0, part // 2)), (slice(0, rows), slice(part // 2, part)),
        )
    out_rows = rows * units // width
    third = half // 3
    for k, (first, size) in enumerate(((0, third), (third, half - third))):
        pieces[f"out{k}"] = (
            out_rows, size, first,
            (slice(0, out_rows // 2), slice(0, size)), (slice(out_rows // 2, out_rows), slice(0, size)),
        )
    pieces["small"] = (32, half, 0, (slice(0, 16), slice(0, half)), (slice(16, 32), slice(0, half)))
    return pieces


def backward_kernel(sizes, *refs):
    rows_total, length, mem_len, width, units, own_rows = sizes
    pieces = sum_pieces(width, units, own_rows)
    (
        p1, p2, q2h, k2h, v2h, m2h, gm2h, q1h, k1h, v1h, m1h, n1h, n2h, memh, xh, s1h, g2h, g2lowh,
        wq1h, wk1h, wv1h, wo1h, wq2h, wk2h, wv2h, n3h, guh, g_out, g_small,
        task, gains, gain_three, down, up,
    ) = refs[:34]
    mem_out, input_out = refs[34:36]
    outs = refs[36:47]
    gain_out, state_out = refs[47:49]
    scratch = refs[49:]
    a = scratch[:5]
    gq, gk, gv = scratch[5:8]
    f0, f1, low = scratch[8:11]
    probs = scratch[11]
    w = scratch[12:16]
    grads = scratch[16:20]
    stage_out, stage_small = scratch[20:22]
    slots = {}
    at_slot = 22
    for name in SUM_NAMES:
        slots[name] = scratch[at_slot : at_slot + 7]
        at_slot += 7
    state_sent, state_arriving, gain_sent, gain_arriving, late_sent, late_arriving, gain_rows_ref = scratch[
        at_slot : at_slot + 7
    ]
    send, recv, p_sem, load_sem = scratch[at_slot + 7 :]
    here = Place()
    copies = Copies(send, recv)
    traffic = Traffic()
    c = here.core
    loads = {}

    def fetch(name, source, target):
        loads[name] = pltpu.make_async_copy(source, target, load_sem.at[len(loads)])
        loads[name].start()

    def need(*names):
        for name in names:
            loads[name].wait()

    def half(which, first, size, full):
        return pl.ds(pl.multiple_of(which * full + first, 128), size)

    full_in = units // 2
    panels = [(which, k) for k in (0, 1) for which in (1, 0)]

    def fetch_panel(turn):
        which, k = panels[turn]
        core = 1 - c if which else c
        cols = pl.ds(pl.multiple_of(core * full_in + k * width, 128), width)
        fetch(("panel", turn), guh.at[:, cols], (gq, gk)[turn % 2])

    fetch("n3", n3h, gv)
    fetch_panel(0)
    fetch_panel(1)
    fetch("m2", m2h, a[3])
    fetch("g2low", g2lowh, low)
    fetch("q2", q2h, a[0])
    fetch("k2", k2h, a[1])
    fetch("v2", v2h, a[2])
    fetch("gm2", gm2h, a[4])

    def probs_copy(source, index):
        return pltpu.make_async_copy(source.at[index], probs.at[lax.rem(index, 2)], p_sem.at[lax.rem(index, 2)])

    pairs = HEADS // 2
    count = rows_total * pairs
    for index in (0, 1):
        probs_copy(p2, index).start()
    fetch("wq2", wq2h, w[0])
    fetch("wo1", wo1h, w[1])
    fetch("wk2", wk2h, w[2])
    fetch("wv2", wv2h, w[3])
    fetch("s1", s1h, f0)
    fetch("g2", g2h, f1)
    meet(here)

    def from_hbm(name, array, out, stage):
        rows, size, first, one, two = pieces[name]
        full = array.shape[4] // 2
        return Summed(
            here, copies, array.at[:, :, :, :, half(1 - c, first, size, full)], lambda: stage[...],
            (one, two), slots[name], out, first,
            fetch=(array.at[:, :, :, :, half(c, first, size, full)], stage),
        )

    out_one, out_two, small_item = flown = (
        from_hbm("out0", g_out, outs[9], stage_out.at[:, :, :, :, : pieces["out0"][1]]),
        from_hbm("out1", g_out, outs[9], stage_out),
        from_hbm("small", g_small, outs[10], stage_small),
    )
    for item in flown:
        traffic.add(item)
    out_one.follower, out_two.follows = out_two, True

    def small_landed():
        made = down.shape[0]
        small = outs[10]
        state = plain_dot(small[0:8, :made].astype(bf16), down[...])
        state = state + plain_dot(small[8:16, :made].astype(bf16), up[...])
        traffic.add(Everywhere(here, copies, lambda: state, state_sent, state_arriving, state_out))

    small_item.landed = small_landed
    users = {}

    def free(slot):
        item = users.pop(slot, None)
        if item is not None:
            while not item.added:
                traffic.tick()
            if any(item.core is copy for copy in copies.open):
                copies.close(item.core)

    def product(source, grad, slot):
        free(slot)
        columns = width // 2
        for k in range(2):
            block = inner_cols(source[:, k * columns : (k + 1) * columns], grad[...]).astype(bf16)
            grads[slot][2 * k : 2 * k + 2] = block.reshape((2, 2, 2, 2 * own_rows, width))
        return grads[slot]

    def weight_gradient(name, index, source, grad, slot):
        buffer = product(source, grad, slot)
        rows, size, first, one, two = pieces[name]
        full = width // 2
        users[slot] = Summed(
            here, copies, buffer.at[:, :, :, :, half(1 - c, 0, size, full)],
            lambda: buffer[:, :, :, :, half(c, 0, size, full)],
            (one, two), slots[name], outs[index], 0,
        )
        traffic.add(users[slot])

    def matrix(k):
        return w[k][...].reshape(width, width)

    def row(r, size=None):
        size = length if size is None else size
        return slice(r * size, (r + 1) * size)

    def picked(r, which):
        return token_gain(task[row(r), :], gains[:, which * width : (which + 1) * width])

    def attention(causal, q, k, v, m, gm, source, keys_all):
        per_group = 2
        for group in range(count // per_group):
            @pl.loop(group * per_group, (group + 1) * per_group)
            def _(index):
                slot = lax.rem(index, 2)
                probs_copy(source, index).wait()
                r, p = index // pairs, lax.rem(index, pairs)
                at = pl.ds(pl.multiple_of(p * PAIR, PAIR), PAIR)
                attend_pair_back(
                    causal, q, k, v, m, gm, probs.at[slot], gq, gk, gv,
                    pl.multiple_of(r * length, length), pl.multiple_of(r * keys_all, keys_all), at, length, keys_all,
                )

                @pl.when(index + 2 < count)
                def _():
                    probs_copy(source, index + 2).start()

            traffic.tick()

    for _ in range(EARLY_TICKS):
        traffic.tick()
    need("n3")
    for turn, (which, k) in enumerate(panels):
        need(("panel", turn))
        buffer = product(gv, (gq, gk)[turn % 2], turn)
        if turn + 2 < len(panels):
            fetch_panel(turn + 2)
        if which == 0:
            _, _, first, one, two = pieces[f"in{k}"]
            mine = buffer
            item = Summed(
                here, copies, theirs, lambda mine=mine: mine[...], (one, two), slots[f"in{k}"], outs[8], first
            )
            users[turn - 1] = users[turn] = item
            traffic.add(item)
        theirs = buffer
        traffic.tick()
    need("m2", "g2low")
    weight_gradient("o2", 7, a[3], low, 0)
    traffic.tick()
    need("q2", "k2", "v2", "gm2")
    attention(False, a[0], a[1], a[2], a[3], a[4], p2, mem_len)
    for index in (0, 1):
        probs_copy(p1, index).start()
    fetch("n2", n2h, a[0])
    fetch("mem", memh, a[1])
    fetch("v1", v1h, a[2])
    fetch("m1", m1h, a[3])
    need("wq2", "wo1", "s1", "g2")
    gain_two = None
    for r in range(rows_total):
        stream = f0[row(r), :]
        stream_grad, gain_tokens = norm_back(stream, picked(r, 1), inner_rows(gq[row(r), :], matrix(0)))
        grad_one = f1[row(r), :] + stream_grad
        f1[row(r), :] = grad_one
        low_now = grad_one.astype(bf16)
        low[row(r), :] = low_now
        a[4][row(r), :] = inner_rows(low_now, matrix(1)).astype(bf16)
        now = gain_rows(task[row(r), :], gain_tokens)
        gain_two = now if gain_two is None else gain_two + now
        traffic.tick()
    gain_rows_ref[:, width : 2 * width] = gain_two
    gain_rows_ref[:, 2 * width :] = gain_three[...]
    traffic.add(
        Everywhere(here, copies, lambda: gain_rows_ref[:, width:], late_sent, late_arriving, gain_out.at[:, width:])
    )
    fetch("wq1", wq1h, w[0])
    fetch("wk1", wk1h, w[1])
    need("n2", "mem")
    for name, index, source, grad, slot in (
        ("q2", 4, a[0], gq, 1), ("k2", 5, a[1], gk, 2), ("v2", 6, a[1], gv, 3)
    ):
        weight_gradient(name, index, source, grad, slot)
        traffic.tick()
    fetch("q1", q1h, a[0])
    fetch("k1", k1h, a[1])
    need("wk2", "wv2")
    for r in range(rows_total):
        mine = row(r, mem_len)
        f0[mine, :] = inner_rows(gk[mine, :], matrix(2)) + inner_rows(gv[mine, :], matrix(3))
        traffic.tick()
    fetch("mem_out", f0, mem_out)
    fetch("wv1", wv1h, w[2])
    need("m1")
    weight_gradient("o1", 3, a[3], low, 0)
    traffic.tick()
    need("q1", "k1", "v1")
    attention(True, a[0], a[1], a[2], a[3], a[4], p1, length)
    fetch("n1", n1h, a[0])
    fetch("x", xh, a[1])
    need("n1")
    for name, index, grad, slot in (("q1", 0, gq, 1), ("k1", 1, gk, 2), ("v1", 2, gv, 3)):
        weight_gradient(name, index, a[0], grad, slot)
        traffic.tick()
    need("x", "wq1", "wk1", "wv1")
    gain_one = None
    for r in range(rows_total):
        stream = a[1][row(r), :].astype(f32)
        cotan = inner_rows(gq[row(r), :], matrix(0)) + inner_rows(gk[row(r), :], matrix(1))
        cotan = cotan + inner_rows(gv[row(r), :], matrix(2))
        stream_grad, gain_tokens = norm_back(stream, picked(r, 0), cotan)
        f1[row(r), :] += stream_grad
        now = gain_rows(task[row(r), :], gain_tokens)
        gain_one = now if gain_one is None else gain_one + now
        traffic.tick()
    fetch("input_out", f1, input_out)
    gain_rows_ref[:, :width] = gain_one
    traffic.ready.insert(
        0, Everywhere(here, copies, lambda: gain_rows_ref[:, :width], gain_sent, gain_arriving, gain_out.at[:, :width])
    )
    traffic.drain()
    need("mem_out", "input_out")
    copies.finish()


def backward(mem_len, saved, probs, x, mem, weights, g2, g2_low, gmix2, n3, gu, g_out, g_small, task, gains, gain_three, down, up, own):
    n1, q1, k1, v1, m1, s1, n2, q2, k2, v2, m2 = saved
    p1, p2 = (p.reshape((-1, 2) + p.shape[2:]) for p in probs)
    rows = probs[0].shape[0]
    tokens, width = x.shape
    length = tokens // rows
    units = own[8].shape[1]
    own_rows = own[0].shape[0]
    any_space = pl.BlockSpec(memory_space=pl.ANY)
    vmem = pl.BlockSpec(memory_space=pltpu.VMEM)
    shape = jax.ShapeDtypeStruct
    act, full = pltpu.VMEM((tokens, width), bf16), pltpu.VMEM((tokens, width), f32)
    mem_act = pltpu.VMEM((max(tokens, mem.shape[0]), width), bf16)
    square = pltpu.VMEM((LINE, 2, 2, 2 * own_rows, width), bf16)
    pieces = sum_pieces(width, units, own_rows)
    slots = []
    for name in SUM_NAMES:
        r, size, _, one, two = pieces[name]
        extent = [tuple(s.stop - s.start for s in share) for share in (one, two)]
        slots += [
            pltpu.VMEM((LINE, 2, 2, r, size), bf16),
            pltpu.VMEM((LINE, 2) + extent[0], bf16),
            pltpu.VMEM((LINE, 2) + extent[1], bf16),
            pltpu.VMEM((LINE,) + extent[0], bf16),
            pltpu.VMEM((LINE,) + extent[1], bf16),
            pltpu.VMEM((LINE - 1, r, size), bf16),
            pltpu.VMEM((r, size), f32),
        ]

    def stage(name):
        r, size = pieces[name][:2]
        return (LINE, 2, 2, r, size)

    tasks, hidden = gains.shape[0], down.shape[1]
    copies = 200
    ins_any = (
        p1, p2, q2, k2, v2, m2, gmix2, q1, k1, v1, m1, n1, n2, mem, x, s1, g2, g2_low,
        *(weights[i] for i in range(7)), n3, gu, g_out, g_small,
    )
    return pl.pallas_call(
        functools.partial(backward_kernel, (rows, length, mem_len, width, units, own_rows)),
        in_specs=[any_space] * len(ins_any) + [vmem] * 5,
        out_specs=[any_space] * 2 + [vmem] * 13,
        out_shape=[shape((mem.shape[0], width), f32), shape((tokens, width), f32)]
        + [shape(g.shape, f32) for g in own]
        + [shape((16, width), f32), shape(gains.shape, f32), shape((tasks, hidden), f32)],
        scratch_shapes=[act] * 5 + [act, mem_act, mem_act] + [full, full, act]
        + [pltpu.VMEM((2, 2, length, max(length, mem_len)), bf16)]
        + [square] * 4
        + [square] * 4
        + [
            pltpu.VMEM(stage("out1"), bf16),
            pltpu.VMEM(stage("small"), bf16),
        ]
        + slots
        + [
            pltpu.VMEM((4, tasks, hidden), f32),
            pltpu.VMEM((6, tasks, hidden), f32),
            pltpu.VMEM((4, tasks, width), f32),
            pltpu.VMEM((6, tasks, width), f32),
            pltpu.VMEM((4, tasks, 2 * width), f32),
            pltpu.VMEM((6, tasks, 2 * width), f32),
            pltpu.VMEM(gains.shape, f32),
            pltpu.SemaphoreType.DMA((copies,)),
            pltpu.SemaphoreType.DMA((copies,)),
            pltpu.SemaphoreType.DMA((2,)),
            pltpu.SemaphoreType.DMA((40,)),
        ],
        compiler_params=pltpu.CompilerParams(
            collective_id=1, has_side_effects=True, vmem_limit_bytes=63 << 20
        ),
        name="backward_as_gradients_leave",
    )(*ins_any, task, gains, gain_three, down, up)


def finish_kernel(count, *refs):
    shards, small, gain_sum, state, gain_all, low, table, weight, bias_row = (
        refs[:count], *refs[count : count + 8]
    )
    large = refs[count + 8 : count + 10]
    outs = refs[count + 10 : 2 * count + 10]
    down_out, up_out, gain_out, table_out, weight_out, bias_out = refs[2 * count + 10 : 2 * count + 16]
    large_outs, (rows, held_a, held_b, sems) = (
        refs[2 * count + 16 : 2 * count + 18], refs[2 * count + 18 :]
    )
    held = (held_a, held_b)
    moves = [
        pltpu.make_async_copy(source, buffer, sems.at[k])
        for k, (source, buffer) in enumerate(zip(large, held))
    ]
    for move in moves:
        move.start()
    for shard, out in zip(shards, outs):
        out[...] = shard[...]
    made = down_out.shape[0]
    for move in moves:
        move.wait()
    moves = [
        pltpu.make_async_copy(buffer, target, sems.at[2 + k])
        for k, (buffer, target) in enumerate(zip(held, large_outs))
    ]
    for move in moves:
        move.start()
    low_now = low[...]
    down_out[...] = inner_cols(small[0:8, :made].astype(bf16), low_now)
    up_out[...] = inner_cols(small[8:16, :made].astype(bf16), low_now)
    rows[...] = inner_cols(gain_sum[...], low_now.astype(f32), exact_mode)
    owned = gain_out.shape[0]
    me = lax.axis_index("dp")
    gain_out[...] = rows[pl.ds(pl.multiple_of(me * owned, 8), owned), :]
    makers = gain_all[...].reshape(-1, gain_all.shape[-1])
    state_grad = state[...] + exact_dot(gain_sum[...], makers)
    before = exact_dot(table[...], weight[...]) + bias_row[...]
    pre_grad = gelu_both(before)[1] * state_grad
    bias_out[...] = jnp.sum(pre_grad, axis=0, keepdims=True)
    weight_out[...] = inner_cols(table[...], pre_grad, exact_mode)
    table_out[...] = lax.dot_general(
        pre_grad, weight[...], (((1,), (1,)), ((), ())), precision=exact_mode, preferred_element_type=f32
    )
    for move in moves:
        move.wait()


def finish(mem_grad, input_grad, shards, small, gain_sum, state, gain_all, low, table, weight, bias_row, makers):
    down, up, gain = makers
    shape = jax.ShapeDtypeStruct
    vmem = pl.BlockSpec(memory_space=pltpu.VMEM)
    ins = (*shards, small, gain_sum, state, gain_all, low, table, weight, bias_row)
    outs = [shape(s.shape, f32) for s in shards]
    outs += [shape(m.shape, f32) for m in makers] + [shape(a.shape, f32) for a in (table, weight, bias_row)]
    large = (mem_grad, input_grad)
    any_space = pl.BlockSpec(memory_space=pl.ANY)
    return pl.pallas_call(
        functools.partial(finish_kernel, len(shards)),
        in_specs=[vmem] * len(ins) + [any_space] * 2,
        out_specs=[vmem] * len(outs) + [any_space] * 2,
        out_shape=outs + [shape(a.shape, f32) for a in large],
        scratch_shapes=[
            pltpu.VMEM((gain_sum.shape[1], low.shape[1]), f32),
            *(pltpu.VMEM(a.shape, f32) for a in large),
            pltpu.SemaphoreType.DMA((4,)),
        ],
        compiler_params=pltpu.CompilerParams(vmem_limit_bytes=VMEM_BYTES),
        name="finish",
    )(*ins, *large)


def on_device(
    block_input, memory, cotangent, segments, memory_segments, task_of_segment,
    self_query, self_key, self_value, self_output,
    cross_query, cross_key, cross_value, cross_output,
    hidden_in, hidden_out, task_table, task_weight, task_bias,
    down_maker, up_maker, gain_maker,
):
    row_count, seq_len, model_width = block_input.shape
    mem_len = memory.shape[1]
    task_count = task_table.shape[0]
    token_count = row_count * seq_len
    parts = lax.axis_size("dp")
    weights = (
        self_query, self_key, self_value, self_output,
        cross_query, cross_key, cross_value, cross_output, hidden_in, hidden_out,
    )
    task_state, task_back = jax.vjp(task_network, task_table, task_weight, task_bias)
    task_low = task_state.astype(bf16)
    down_own, gain_own = down_maker.shape[0], gain_maker.shape[0]
    makers = (down_maker, up_maker, gain_maker)
    x = block_input.reshape(token_count, model_width)
    mem = memory.reshape(row_count * mem_len, model_width)

    def joined(block):
        return block.transpose(1, 0, 2).reshape(task_count, -1)

    if parts == 32:
        outs = forward(
            x, mem, segments, memory_segments, task_of_segment, weights,
            task_table, task_weight, task_bias.reshape(1, -1), makers,
        )
        backbone = [w.reshape(-1, w.shape[-1]) for w in outs[:10]]
        made = outs[10].reshape(parts, 2 * task_count, -1)
        task_low, gain_table, token_task = outs[12:15]
        saved, probs_one, probs_two = outs[15:26], outs[26], outs[27]
        made_up = joined(made[:, task_count:, :down_own])
        made = made[:, :task_count]
    else:
        packed = jnp.concatenate([w.reshape(-1, model_width) for w in weights], axis=0)
        packed = lax.all_gather(packed, "dp", axis=0, tiled=False)
        backbone, at = [], 0
        for w in weights:
            count = w.size // model_width
            backbone.append(packed[:, at : at + count].reshape(-1, w.shape[1]))
            at += count
        made = inner_rows(task_low, jnp.concatenate(makers, axis=0))
        made = lax.all_gather(made, "dp", axis=0, tiled=False)
        gain_table = 1.0 + joined(made[:, :, 2 * down_own :])
        seg_match = segments[:, :, None] == jnp.arange(task_of_segment.shape[1], dtype=jnp.int32)
        token_task = jnp.sum(
            jnp.where(seg_match, task_of_segment[:, None, :], 0), axis=-1
        ).reshape(token_count, 1)
        saved, probs_one, probs_two = attention_layers(
            x, mem, segments, memory_segments, token_task, backbone, gain_table
        )
        made_up = joined(made[:, :, down_own : 2 * down_own]).astype(bf16)
    made_down = joined(made[:, :, :down_own]).astype(bf16)
    down_all = (
        made_down.reshape(task_count, model_width, ADA)
        .transpose(1, 0, 2)
        .reshape(model_width, task_count * ADA)
    )
    up_all = made_up.reshape(task_count * ADA, model_width)
    cot = cotangent.reshape(token_count, model_width)
    output, g2, g2_low, gmix2, n3, gu, hidden_out_grad, up_grad, down_grad, gain_three = feed_forward(
        saved[5], saved[10], cot, token_task, backbone, gain_table, down_all, up_all
    )
    down_rows = (
        down_grad.reshape(parts, -1, task_count, ADA)
        .transpose(0, 2, 1, 3)
        .reshape(parts, task_count, down_own)
    )
    up_rows = up_grad.reshape(task_count, parts, -1).transpose(1, 0, 2)
    if parts == 32:
        small = jnp.concatenate((down_rows, up_rows), axis=1).astype(bf16)
        small = jnp.pad(small, ((0, 0), (0, 0), (0, model_width - down_own)))
        out_grad = hidden_out_grad.reshape((LINE, 2, 2, -1, model_width))
        mem_grad, input_grad, *shared, small, gain_sum, state = backward(
            mem_len, saved, (probs_one, probs_two), x, mem, outs[:7], g2, g2_low, gmix2, n3, gu, out_grad,
            small.reshape(LINE, 2, 2, 4 * task_count, model_width), token_task, gain_table, gain_three,
            down_maker, up_maker, weights,
        )
        (
            *shared, down_maker_grad, up_maker_grad, gain_maker_grad,
            table_grad, weight_grad, bias_grad, mem_grad, input_grad,
        ) = finish(
            mem_grad, input_grad, shared, small, gain_sum, state, outs[11], task_low, task_table, task_weight,
            task_bias.reshape(1, -1), makers,
        )
        bias_grad = bias_grad.reshape(task_bias.shape)
    else:
        input_grad, mem_grad, grads, gain_one, gain_two = attention_back(
            x, mem, row_count, token_task, backbone, gain_table, saved, probs_one, probs_two, g2, g2_low, gmix2
        )
        grads = (*grads, *outers((n3,), (gu,), (0,), "hidden_in_grad"), hidden_out_grad)
        packed = jnp.concatenate([g.reshape(parts, -1, model_width) for g in grads], axis=1)
        packed = lax.psum_scatter(packed, "dp", scatter_dimension=0, tiled=False).astype(f32)
        shared, at = [], 0
        for w in weights:
            count = w.size // model_width
            shared.append(packed[at : at + count].reshape(w.shape))
            at += count
        gain_grad = jnp.concatenate((gain_one, gain_two, gain_three), axis=1)
        gain_rows_all = gain_grad.reshape(task_count, parts, -1).transpose(1, 0, 2)
        small = jnp.concatenate((down_rows, up_rows, gain_rows_all), axis=2)
        small = lax.psum_scatter(small, "dp", scatter_dimension=0, tiled=False)
        own_down = small[:, :down_own].astype(bf16)
        own_up = small[:, down_own : 2 * down_own].astype(bf16)
        own_gain = small[:, 2 * down_own :]
        state_grad = lax.psum(
            plain_dot(own_down, down_maker)
            + plain_dot(own_up, up_maker)
            + exact_dot(own_gain, gain_maker.astype(f32)),
            "dp",
        )
        down_maker_grad = inner_cols(own_down, task_low)
        up_maker_grad = inner_cols(own_up, task_low)
        gain_maker_grad = inner_cols(own_gain, task_low.astype(f32), exact_mode)
        table_grad, weight_grad, bias_grad = task_back(state_grad)
    return (
        output.reshape(row_count, seq_len, model_width),
        input_grad.reshape(row_count, seq_len, model_width),
        mem_grad.reshape(row_count, mem_len, model_width),
        *shared,
        table_grad,
        weight_grad,
        bias_grad,
        down_maker_grad,
        up_maker_grad,
        gain_maker_grad,
    )


def solution(mesh):
    rows, whole_copy = P("dp"), P()
    return jax.shard_map(
        on_device,
        mesh=mesh,
        in_specs=(rows,) * 16 + (whole_copy,) * 3 + (rows,) * 3,
        out_specs=(rows,) * 13 + (whole_copy,) * 3 + (rows,) * 3,
        check_vma=False,
    )
```

```python
import functools

import jax
import jax.numpy as jnp
from jax import lax
from jax.experimental import pallas as pl
from jax.experimental.pallas import tpu as pltpu
from jax.sharding import PartitionSpec as P

HEADS = 12
HEAD = 64
ADA = 24
PAIR = 2 * HEAD

exact_mode = lax.Precision.HIGHEST
norm_eps = 1e-06
masked_score = -1e30
bf16 = jnp.bfloat16
f32 = jnp.float32
VMEM_BYTES = 56 << 20


def plain_dot(left_side, right_side):
    return jnp.dot(left_side, right_side, preferred_element_type=f32)


def exact_dot(left_side, right_side):
    return jnp.dot(left_side, right_side, precision=exact_mode, preferred_element_type=f32)


def inner_rows(left_side, right_side):
    return lax.dot_general(
        left_side, right_side, (((1,), (1,)), ((), ())), preferred_element_type=f32
    )


def inner_cols(left_side, right_side, precision_mode=None):
    return lax.dot_general(
        left_side,
        right_side,
        (((0,), (0,)), ((), ())),
        precision=precision_mode,
        preferred_element_type=f32,
    )


def gelu_exact(operand):
    return jax.nn.gelu(operand, approximate=False)


def task_network(table_rows, weight_in, bias_row):
    return gelu_exact(exact_dot(table_rows, weight_in) + bias_row)


def gelu_both(v):
    phi = 0.5 * lax.erf(v * 0.7071067811865476) + 0.5
    slope = phi + v * (jnp.exp(v * v * -0.5) * 0.3989422804014327)
    return v * phi, slope


def token_gain(task_column, gain):
    high = gain.astype(bf16).astype(f32)
    rest = gain - high
    middle = rest.astype(bf16).astype(f32)
    table = jnp.concatenate((high, middle, rest - middle), axis=0).astype(bf16)
    which = lax.broadcasted_iota(jnp.int32, (task_column.shape[0], 24), 1) & 7
    hot = jnp.where(which == task_column, 1.0, 0.0).astype(bf16)
    return plain_dot(hot, table)


def gain_rows(task_column, grads):
    which = lax.broadcasted_iota(jnp.int32, (task_column.shape[0], 8), 1)
    hot = jnp.where(which == task_column, 1.0, 0.0).astype(bf16)
    high = grads.astype(bf16)
    low = (grads - high.astype(f32)).astype(bf16)
    return inner_cols(hot, high) + inner_cols(hot, low)


def inverse_rms(stream):
    return lax.rsqrt(jnp.mean(stream * stream, axis=-1, keepdims=True) + norm_eps)


def norm_back(stream, gain, cotan):
    r = inverse_rms(stream)
    scaled = cotan * gain
    inner = jnp.mean(scaled * stream, axis=-1, keepdims=True)
    return r * (scaled - stream * (r * r * inner)), cotan * (stream * r)


def call(kernel, grid, ins, outs, scratch=(), flops=0, name=None):
    size = sum(a.size * a.dtype.itemsize for a, _, _ in ins)
    size += sum(functools.reduce(lambda p, q: p * q, s, 1) * jnp.dtype(d).itemsize for s, d, _, _ in outs)
    return pl.pallas_call(
        kernel,
        grid=grid,
        in_specs=[pl.BlockSpec(b, m) for _, b, m in ins],
        out_specs=[pl.BlockSpec(b, m) for _, _, b, m in outs],
        out_shape=[jax.ShapeDtypeStruct(s, d) for s, d, _, _ in outs],
        scratch_shapes=list(scratch),
        compiler_params=pltpu.CompilerParams(vmem_limit_bytes=VMEM_BYTES),
        cost_estimate=pl.CostEstimate(flops=flops, bytes_accessed=size, transcendentals=0),
        name=name,
    )(*[a for a, _, _ in ins])


def whole(array):
    return (array, array.shape, lambda *_: (0,) * array.ndim)


def by_row(array, rows):
    return (array, (rows,) + array.shape[1:], lambda i: (i,) + (0,) * (array.ndim - 1))


def out_row(shape, dtype, rows):
    return (shape, dtype, (rows,) + shape[1:], lambda i: (i,) + (0,) * (len(shape) - 1))


def out_whole(shape, dtype):
    return (shape, dtype, shape, lambda *_: (0,) * len(shape))


def pre_kernel(x, task, gain, wq, wk, wv, normed, q, k, v):
    stream = x[...].astype(f32)
    n = (stream * inverse_rms(stream) * token_gain(task[...], gain[...])).astype(bf16)
    normed[...] = n
    q[...] = (plain_dot(n, wq[...]).astype(bf16).astype(f32) * HEAD**-0.5).astype(bf16)
    k[...] = plain_dot(n, wk[...]).astype(bf16)
    v[...] = plain_dot(n, wv[...]).astype(bf16)


def memory_kernel(x, wk, wv, k, v):
    k[...] = plain_dot(x[...], wk[...]).astype(bf16)
    v[...] = plain_dot(x[...], wv[...]).astype(bf16)


def middle_kernel(x, mixed, wo, task, gain, wq, stream_out, normed, q):
    stream = x[...].astype(f32) + plain_dot(mixed[...], wo[...])
    stream_out[...] = stream
    n = (stream * inverse_rms(stream) * token_gain(task[...], gain[...])).astype(bf16)
    normed[...] = n
    q[...] = (plain_dot(n, wq[...]).astype(bf16).astype(f32) * HEAD**-0.5).astype(bf16)


def half_masks():
    lane = lax.broadcasted_iota(jnp.int32, (1, PAIR), 1)
    first = jnp.where(lane < HEAD, 1.0, 0.0)
    return first.astype(bf16), (1.0 - first).astype(bf16)


def attend_forward_kernel(causal, q_ref, k_ref, v_ref, seg_q, seg_k, mixed_ref, p_ref, bias):
    length, keys_all = q_ref.shape[0], k_ref.shape[0]
    step = length // 2 if causal else length

    @pl.when(pl.program_id(1) == 0)
    def _():
        same = seg_q[...] == seg_k[0]
        if causal:
            at_q = lax.broadcasted_iota(jnp.int32, (length, keys_all), 0)
            at_k = lax.broadcasted_iota(jnp.int32, (length, keys_all), 1)
            same = same & (at_q >= at_k)
        bias[...] = jnp.where(same, 0.0, masked_score)

    masks = half_masks()
    for first in range(0, length, step):
        rows = pl.ds(first, step)
        keys = first + step if causal else keys_all
        q = q_ref[rows, :]
        k = k_ref[:keys, :]
        v = v_ref[:keys, :]
        out = None
        for h, mask in enumerate(masks):
            s = inner_rows(q * mask, k) + bias[rows, :keys]
            e = jnp.exp(s - jnp.max(s, axis=-1, keepdims=True))
            p = (e * (1.0 / jnp.sum(e, axis=-1, keepdims=True))).astype(bf16)
            p_ref[0, h, rows, :keys] = p
            part = plain_dot(p, v * mask)
            out = part if out is None else out + part
        mixed_ref[rows, :] = out.astype(bf16)


def attend_backward_kernel(
    causal, q_ref, k_ref, v_ref, mixed_ref, gm_ref, p_ref, gq_ref, gk_ref, gv_ref
):
    length, keys_all = q_ref.shape[0], k_ref.shape[0]
    step = length // 2 if causal else length
    masks = half_masks()
    gk_parts, gv_parts = [], []
    for first in range(0, length, step):
        rows = pl.ds(first, step)
        keys = first + step if causal else keys_all
        q = q_ref[rows, :]
        k = k_ref[:keys, :]
        v = v_ref[:keys, :]
        gm = gm_ref[rows, :]
        product = gm.astype(f32) * mixed_ref[rows, :].astype(f32)
        gq = gk = gv = 0.0
        for h, mask in enumerate(masks):
            inner = jnp.sum(product * mask.astype(f32), axis=-1, keepdims=True)
            p = p_ref[0, h, rows, :keys]
            gm_half = gm * mask
            gw = inner_rows(gm_half, v)
            gs = (p.astype(f32) * (gw - inner)).astype(bf16)
            gv = gv + inner_cols(p, gm_half)
            gq = gq + plain_dot(gs, k * mask)
            gk = gk + inner_cols(gs, q * mask)
        gq_ref[rows, :] = (gq * HEAD**-0.5).astype(bf16)
        gk_parts.append(gk)
        gv_parts.append(gv)
    for ref, terms in ((gk_ref, gk_parts), (gv_ref, gv_parts)):
        if not causal:
            ref[...] = terms[0].astype(bf16)
        else:
            ref[:step, :] = (terms[0] + terms[1][:step]).astype(bf16)
            ref[step:, :] = terms[1][step:].astype(bf16)


def attention_specs(rows, length, arrays):
    return [(a, (length, PAIR), lambda r, p: (r, p)) for a in arrays]


def attend_forward(causal, rows, length, q, k, v, seg_q, seg_k):
    mem_len = k.shape[0] // rows
    mixed, probs = call(
        functools.partial(attend_forward_kernel, causal),
        (rows, HEADS // 2),
        attention_specs(rows, length, (q,))
        + attention_specs(rows, mem_len, (k, v))
        + [
            (seg_q.reshape(rows * length, 1), (length, 1), lambda r, p: (r, 0)),
            (seg_k.reshape(rows, 1, mem_len), (1, 1, mem_len), lambda r, p: (r, 0, 0)),
        ],
        [
            (q.shape, bf16, (length, PAIR), lambda r, p: (r, p)),
            (
                (rows, HEADS, length, mem_len),
                bf16,
                (1, 2, length, mem_len),
                lambda r, p: (r, p, 0, 0),
            ),
        ],
        scratch=[pltpu.VMEM((length, mem_len), f32)],
        flops=4 * rows * HEADS * length * mem_len * PAIR,
        name="attend_forward",
    )
    return mixed, probs


def attend_backward(causal, rows, length, q, k, v, mixed, grad_mixed, probs):
    mem_len = k.shape[0] // rows
    return call(
        functools.partial(attend_backward_kernel, causal),
        (rows, HEADS // 2),
        attention_specs(rows, length, (q,))
        + attention_specs(rows, mem_len, (k, v))
        + attention_specs(rows, length, (mixed, grad_mixed))
        + [(probs, (1, 2, length, mem_len), lambda r, p: (r, p, 0, 0))],
        [
            (q.shape, bf16, (length, PAIR), lambda r, p: (r, p)),
            (k.shape, bf16, (mem_len, PAIR), lambda r, p: (r, p)),
            (k.shape, bf16, (mem_len, PAIR), lambda r, p: (r, p)),
        ],
        flops=8 * rows * HEADS * length * mem_len * PAIR,
        name="attend_backward",
    )


CHUNK = 768
FEED_CHUNK = 768
OUTER_BLOCK = 768


def feed_kernel(
    s1, mixed, wo, task, gain, w_in, w_out, down_all, up_all, cot,
    output, n3, act, gu, gfeed, g2, g2_low, gmix, up_grad, down_grad, gain_grad,
    slope,
):
    first = pl.program_id(0) == 0
    units = w_in.shape[1]
    stream = s1[...] + plain_dot(mixed[...], wo[...])
    picked = token_gain(task[...], gain[...])
    n3[...] = (stream * inverse_rms(stream) * picked).astype(bf16)
    parts = [slice(k, k + FEED_CHUNK) for k in range(0, units, FEED_CHUNK)]
    normed = n3[...]
    hidden = plain_dot(normed, w_in[:, parts[0]])
    feed = None
    for k, cols in enumerate(parts):
        now = hidden
        if k + 1 < len(parts):
            hidden = plain_dot(normed, w_in[:, parts[k + 1]])
        value, rate = gelu_both(now)
        value = value.astype(bf16)
        act[:, cols] = value
        slope[:, cols] = rate.astype(bf16)
        term = plain_dot(value, w_out[cols, :])
        feed = term if feed is None else feed + term
    feed_low = feed.astype(bf16)
    tokens, wide = stream.shape[0], down_all.shape[1]
    owner = lax.broadcasted_iota(jnp.int32, (tokens, wide), 1) - task[...] * ADA
    mask = jnp.where((owner >= 0) & (owner < ADA), 1.0, 0.0)
    narrow, narrow_slope = gelu_both(plain_dot(feed_low, down_all[...]) * mask)
    narrow = narrow.astype(bf16)
    output[...] = (stream + feed + plain_dot(narrow, up_all[...])).astype(bf16)
    cotan = cot[...]
    gb = (narrow_slope * inner_rows(cotan, up_all[...]) * mask).astype(bf16)
    grad_feed = (cotan.astype(f32) + inner_rows(gb, down_all[...])).astype(bf16)
    gfeed[...] = grad_feed
    up_now = inner_cols(narrow, cotan)
    down_now = inner_cols(feed_low, gb)
    grad_hidden = inner_rows(grad_feed, w_out[parts[0], :])
    total = None
    for k, cols in enumerate(parts):
        now = grad_hidden
        if k + 1 < len(parts):
            grad_hidden = inner_rows(grad_feed, w_out[parts[k + 1], :])
        grad = (slope[:, cols].astype(f32) * now).astype(bf16)
        gu[:, cols] = grad
        term = inner_rows(grad, w_in[:, cols])
        total = term if total is None else total + term

    stream_grad, gain_tokens = norm_back(stream, picked, total)
    grad_two = cotan.astype(f32) + stream_grad
    g2[...] = grad_two
    low = grad_two.astype(bf16)
    g2_low[...] = low
    gmix[...] = inner_rows(low, wo[...]).astype(bf16)
    gain_now = gain_rows(task[...], gain_tokens)

    @pl.when(first)
    def _():
        up_grad[...] = up_now
        down_grad[...] = down_now
        gain_grad[...] = gain_now

    @pl.when(jnp.logical_not(first))
    def _():
        up_grad[...] += up_now
        down_grad[...] += down_now
        gain_grad[...] += gain_now


def cross_back_kernel(gq, wq, s1, task, gain, g2, wo, g1, g1_low, gmix, gain_grad):
    stream = s1[...]
    picked = token_gain(task[...], gain[...])
    stream_grad, gain_tokens = norm_back(stream, picked, inner_rows(gq[...], wq[...]))
    grad_one = g2[...] + stream_grad
    g1[...] = grad_one
    low = grad_one.astype(bf16)
    g1_low[...] = low
    gmix[...] = inner_rows(low, wo[...]).astype(bf16)
    accumulate(gain_grad, gain_rows(task[...], gain_tokens))


def accumulate(ref, value):
    @pl.when(pl.program_id(0) == 0)
    def _():
        ref[...] = value

    @pl.when(pl.program_id(0) != 0)
    def _():
        ref[...] += value


def memory_back_kernel(gk, gv, wk, wv, out):
    out[...] = inner_rows(gk[...], wk[...]) + inner_rows(gv[...], wv[...])


def input_back_kernel(gq, gk, gv, wq, wk, wv, x, task, gain, g1, out, gain_grad):
    stream = x[...].astype(f32)
    picked = token_gain(task[...], gain[...])
    cotan = inner_rows(gq[...], wq[...]) + inner_rows(gk[...], wk[...])
    cotan = cotan + inner_rows(gv[...], wv[...])
    stream_grad, gain_tokens = norm_back(stream, picked, cotan)
    out[...] = g1[...] + stream_grad
    accumulate(gain_grad, gain_rows(task[...], gain_tokens))


def outer_kernel(which, sources, *refs):
    left = refs[:sources]
    right = refs[sources : sources + len(which)]
    outs = refs[sources + len(which) :]
    for source, grad, out in zip(which, right, outs):
        for first in range(0, out.shape[1], CHUNK):
            cols = slice(first, first + CHUNK)
            out[:, cols] = inner_cols(left[source][...], grad[:, cols]).astype(bf16)


def outers(sources, grads, which, name):
    tokens, width = sources[0].shape
    block = OUTER_BLOCK if width > 768 else 256
    return call(
        functools.partial(outer_kernel, which, len(sources)),
        (width // block,),
        [(s, (tokens, block), lambda i: (0, i)) for s in sources] + [whole(g) for g in grads],
        [((width, g.shape[1]), bf16, (block, g.shape[1]), lambda i: (i, 0)) for g in grads],
        flops=sum(2 * tokens * width * g.shape[1] for g in grads),
        name=name,
    )


BLOCK = 512


def low_out(shape):
    return out_row(shape, bf16, BLOCK)


def full_out(shape):
    return out_row(shape, f32, BLOCK)


def attention_layers(x, mem, segments, mem_segments, task, weights, gain_table):
    rows, length = segments.shape
    tokens, width = x.shape
    wq1, wk1, wv1, wo1, wq2, wk2, wv2 = weights[:7]
    gain_one, gain_two = (gain_table[:, i * width : (i + 1) * width] for i in range(2))
    block = BLOCK
    grid = (tokens // block,)
    act_shape = (tokens, width)
    square = 2 * tokens * width * width
    n1, q1, k1, v1 = call(
        pre_kernel,
        grid,
        [by_row(x, block), by_row(task, block)] + [whole(a) for a in (gain_one, wq1, wk1, wv1)],
        [low_out(act_shape) for _ in range(4)],
        flops=3 * square,
        name="self_projections",
    )
    m1, p1 = attend_forward(True, rows, length, q1, k1, v1, segments, segments)
    s1, n2, q2 = call(
        middle_kernel,
        grid,
        [by_row(x, block), by_row(m1, block), whole(wo1), by_row(task, block), whole(gain_two), whole(wq2)],
        [full_out(act_shape), low_out(act_shape), low_out(act_shape)],
        flops=2 * square,
        name="middle",
    )
    k2, v2 = call(
        memory_kernel,
        grid,
        [by_row(mem, block), whole(wk2), whole(wv2)],
        [low_out(mem.shape), low_out(mem.shape)],
        flops=2 * square,
        name="memory_projections",
    )
    m2, p2 = attend_forward(False, rows, length, q2, k2, v2, segments, mem_segments)
    return (n1, q1, k1, v1, m1, s1, n2, q2, k2, v2, m2), p1, p2


def feed_forward(s1, m2, cot, task, weights, gain_table, down_all, up_all):
    tokens, width = s1.shape
    wo2, w_in, w_out = weights[7:]
    block = BLOCK
    grid = (tokens // block,)
    act_shape = (tokens, width)
    square = 2 * tokens * width * width
    units = w_in.shape[1]
    wide = up_all.shape[0]
    tasks = gain_table.shape[0]
    output, n3, act, gu, gfeed, g2, g2_low, gmix2, up_grad, down_grad, gain3 = call(
        feed_kernel,
        grid,
        [
            by_row(s1, block), by_row(m2, block), whole(wo2), by_row(task, block),
            (gain_table, (gain_table.shape[0], width), lambda *_: (0, 2)), whole(w_in), whole(w_out), whole(down_all), whole(up_all), by_row(cot, block),
        ],
        [
            low_out(act_shape), low_out(act_shape), out_row((tokens, units), bf16, block), out_row((tokens, units), bf16, block),
            low_out(act_shape), full_out(act_shape), low_out(act_shape), low_out(act_shape),
            out_whole((wide, width), f32), out_whole((width, wide), f32), out_whole((tasks, width), f32),
        ],
        scratch=[pltpu.VMEM((block, units), bf16)],
        flops=2 * square + 8 * tokens * width * units,
        name="feed_forward_and_back",
    )
    (hidden_out_grad,) = outers((act,), (gfeed,), (0,), "hidden_out_grad")
    return output, g2, g2_low, gmix2, n3, gu, hidden_out_grad, up_grad, down_grad, gain3


def attention_back(x, mem, rows, task, weights, gain_table, saved, p1, p2, g2, g2_low, gmix2):
    n1, q1, k1, v1, m1, s1, n2, q2, k2, v2, m2 = saved
    tokens, width = x.shape
    length = tokens // rows
    wq1, wk1, wv1, wo1, wq2, wk2, wv2 = weights[:7]
    gain_one, gain_two = (gain_table[:, i * width : (i + 1) * width] for i in range(2))
    tasks = gain_table.shape[0]
    block = BLOCK
    grid = (tokens // block,)
    act_shape = (tokens, width)
    square = 2 * tokens * width * width
    gq2, gk2, gv2 = attend_backward(False, rows, length, q2, k2, v2, m2, gmix2, p2)
    g1, g1_low, gmix1, gain2 = call(
        cross_back_kernel,
        grid,
        [
            by_row(gq2, block), whole(wq2), by_row(s1, block), by_row(task, block), whole(gain_two),
            by_row(g2, block), whole(wo1),
        ],
        [full_out(act_shape), low_out(act_shape), low_out(act_shape), out_whole((tasks, width), f32)],
        flops=2 * square,
        name="cross_back",
    )
    (mem_grad,) = call(
        memory_back_kernel,
        grid,
        [by_row(gk2, block), by_row(gv2, block), whole(wk2), whole(wv2)],
        [full_out(act_shape)],
        flops=2 * square,
        name="memory_back",
    )
    wo2_grad, wq2_grad, wk2_grad, wv2_grad = outers(
        (m2, n2, mem), (g2_low, gq2, gk2, gv2), (0, 1, 2, 2), "cross_grads"
    )
    gq1, gk1, gv1 = attend_backward(True, rows, length, q1, k1, v1, m1, gmix1, p1)
    input_grad, gain1 = call(
        input_back_kernel,
        grid,
        [
            by_row(gq1, block), by_row(gk1, block), by_row(gv1, block), whole(wq1), whole(wk1), whole(wv1),
            by_row(x, block), by_row(task, block), whole(gain_one), by_row(g1, block),
        ],
        [full_out(act_shape), out_whole((tasks, width), f32)],
        flops=3 * square,
        name="input_back",
    )
    wo1_grad, wq1_grad, wk1_grad, wv1_grad = outers(
        (m1, n1), (g1_low, gq1, gk1, gv1), (0, 1, 1, 1), "self_grads"
    )
    grads = (wq1_grad, wk1_grad, wv1_grad, wo1_grad, wq2_grad, wk2_grad, wv2_grad, wo2_grad)
    return input_grad, mem_grad, grads, gain1, gain2


LINE = 4
MESH = pl.DeviceIdType.MESH


class Place:
    def __init__(self):
        me = lax.axis_index("dp")
        self.core = lax.rem(me, 2)
        self.x = lax.rem(me // 2, 2)
        self.y = lax.rem(me // 4, 2)
        self.z = me // 8

    def at(self, z=None, y=None, x=None, core=None):
        z = self.z if z is None else z
        y = self.y if y is None else y
        x = self.x if x is None else x
        core = self.core if core is None else core
        return (((z * 2 + y) * 2 + x) * 2 + core,)

    def sibling(self):
        return self.at(core=1 - self.core)

    def over_x(self):
        return self.at(x=1 - self.x)

    def over_y(self):
        return self.at(y=1 - self.y)

    def along_z(self, k):
        return self.at(z=lax.rem(self.z + k, LINE))

    def partners(self):
        return [self.sibling(), self.over_x(), self.over_y()] + [self.along_z(k) for k in (1, 2, 3)]


def meet(place):
    barrier = pltpu.get_barrier_semaphore()
    partners = place.partners()
    for partner in partners:
        pl.semaphore_signal(barrier, inc=1, device_id=partner, device_id_type=MESH)
    pl.semaphore_wait(barrier, len(partners))


class Copies:
    def __init__(self, send, recv):
        self.send, self.recv, self.used, self.open = send, recv, 0, []

    def remote(self, source, target, device):
        copy = pltpu.make_async_remote_copy(
            src_ref=source,
            dst_ref=target,
            send_sem=self.send.at[self.used],
            recv_sem=self.recv.at[self.used],
            device_id=device,
            device_id_type=MESH,
        )
        self.used += 1
        copy.start()
        self.open.append(copy)
        return copy

    def local(self, source, target):
        copy = pltpu.make_async_copy(source, target, self.recv.at[self.used])
        self.used += 1
        copy.start()
        return copy

    def close(self, copy):
        copy.wait_send()
        self.open = [other for other in self.open if other is not copy]

    def finish(self):
        for copy in self.open:
            copy.wait_send()


FIRST_PACE = 1
PACE = 2


class Unit:
    def __init__(self, here, copies, source, whole_array, index, first, second):
        self.here, self.copies = here, copies
        self.source, self.array = source, whole_array
        self.index, self.shares = index, (first, second)
        self.going = {}

    def window(self, zs, ys, xs, share=None):
        return self.array.at[(zs, ys, xs) + (self.index if share is None else self.shares[share])]

    def depart(self):
        here, copies = self.here, self.copies
        source = self.source(None)
        target = self.window(here.z, here.y, here.x)
        self.going["z"] = [copies.remote(source, target, here.along_z(k)) for k in (1, 2, 3)]
        self.own = copies.local(source, target)

    def turn(self):
        here = self.here
        for copy in self.going["z"]:
            copy.wait_recv()
        self.own.wait()
        one = self.window(slice(None), here.y, here.x, 0)
        two = self.window(slice(None), here.y, here.x, 1)
        self.going["1"] = [
            self.copies.remote(one, one, here.over_x()),
            self.copies.remote(two, two, here.over_y()),
        ]

    def turn_again(self):
        here = self.here
        for copy in self.going["1"]:
            copy.wait_recv()
        one = self.window(slice(None), here.y, slice(None), 0)
        two = self.window(slice(None), slice(None), here.x, 1)
        self.going["2"] = [
            self.copies.remote(one, one, here.over_y()),
            self.copies.remote(two, two, here.over_x()),
        ]

    def cross(self):
        for copy in self.going["2"]:
            copy.wait_recv()
        part = self.window(slice(None), slice(None), slice(None))
        self.going["c"] = self.copies.remote(part, part, self.here.sibling())

    def settle(self):
        self.going["c"].wait_recv()

    def stages(self):
        return (self.depart, self.turn, self.turn_again, self.cross, self.settle)


def column_of(row):
    length = row.shape[1]
    at_q = lax.broadcasted_iota(jnp.int32, (length, length), 0)
    at_k = lax.broadcasted_iota(jnp.int32, (length, length), 1)
    picked = jnp.where(at_q == at_k, row.astype(f32), 0.0)
    return jnp.sum(picked, axis=1, keepdims=True).astype(jnp.int32)


def forward_kernel(*refs):
    (
        x, mem, segments, mem_segments, tasks,
        sq, sk, sv, so, cq, ck, cv, co, w_in, w_out,
        table, weight, bias_row, down, up, gain,
    ) = refs[:21]
    outs, made_out, gains_out = refs[21:31], refs[31], refs[32]
    low_out, gain_out, task_out = refs[33:36]
    saved_out = refs[36:47]
    p1_out, p2_out = refs[47:49]
    scratch = refs[49:]
    wide, halves, blocks = scratch[:10], scratch[10:20], scratch[20:30]
    local_w = scratch[30:38]
    saved = scratch[38:49]
    n1, q1, k1, v1, m1, s1, n2, q2, k2, v2, m2 = saved
    made, gain_rows_all, bias, probs, send, recv, p_sem, load_sem, save_sem, gain_full = scratch[49:]
    own = (sq, sk, sv, so, cq, ck, cv, co, w_in, w_out)
    rows_total, length = segments.shape
    mem_len = mem_segments.shape[1]
    here = Place()
    copies = Copies(send, recv)
    c = here.core

    def half(i, core, first=0, width=None):
        full = own[i].shape[1] // 2
        width = full if width is None else width
        return pl.ds(pl.multiple_of(core * full + first, 128), width)

    for i in range(10):
        wide[i][...] = own[i][...].astype(f32)
    gain_rows_all[...] = gain[...].astype(f32)
    probs[...] = jnp.zeros_like(probs)
    meet(here)
    pair = {}
    order = (0, 1, 2, 5, 6, 3, 4, 7, 8, 9)
    for i in order:
        rows = own[i].shape[0]
        mine = pl.ds(pl.multiple_of(c * rows, 8), rows)
        pair[i] = copies.remote(
            wide[i].at[:, half(i, 1 - c)], halves[i].at[mine, :], here.sibling()
        )
        halves[i][mine, :] = wide[i][:, half(i, c)]

    opened = set()

    def piece(i, rows, first, width):
        at = half(i, c, first, width)
        count = rows.stop - rows.start
        if (width // 2) % 128 == 0:
            windows = (
                (rows, half(i, c, first, width // 2)),
                (rows, half(i, c, first + width // 2, width // 2)),
            )
            local = (
                (rows, pl.ds(first, width // 2)),
                (rows, pl.ds(first + width // 2, width // 2)),
            )
        else:
            cut = rows.start + (count // 2 if count % 32 == 0 else (count // 32 + i % 2) * 16)
            split = (slice(rows.start, cut), slice(cut, rows.stop))
            windows = tuple((part, at) for part in split)
            local = tuple((part, pl.ds(first, width)) for part in split)

        def source(share):
            if i not in opened:
                opened.add(i)
                pair[i].wait_recv()
                blocks[i][...] = halves[i][...].astype(bf16)
            return blocks[i].at[(rows, pl.ds(first, width)) if share is None else local[share]]

        return Unit(here, copies, source, outs[i], (rows, at), *windows)

    def square(i):
        return piece(i, slice(0, outs[i].shape[3]), 0, own[i].shape[1] // 2)

    gain_own = gain.shape[0]
    gain_cut = gain_own // 16 * 8
    made_cut = made.shape[1] // 256 * 128
    gain_unit = Unit(
        here, copies, lambda _: gain_rows_all, gains_out, (c,),
        (c, pl.ds(0, gain_cut)), (c, pl.ds(gain_cut, gain_own - gain_cut)),
    )
    made_unit = Unit(
        here, copies, lambda _: made, made_out, (c,),
        (c, slice(None), pl.ds(0, made_cut)), (c, slice(None), pl.ds(made_cut, made.shape[1] - made_cut)),
    )
    in_half = w_in.shape[1] // 4
    out_rows = outs[9].shape[3]
    units = [gain_unit] + [square(i) for i in (0, 1, 2, 5, 6, 3, 4, 7)]
    units += [
        piece(8, slice(0, outs[8].shape[3]), k * in_half, in_half) for k in (0, 1)
    ]
    units += [made_unit]
    units += [
        piece(
            9, slice(k * out_rows // 2, (k + 1) * out_rows // 2), 0, w_out.shape[1] // 2
        )
        for k in (0, 1)
    ]
    loads = {}
    landing = {1: (0,), 2: (1,), 3: (2,), 4: (5,), 5: (6,), 6: (3,), 7: (4,), 8: (7,)}

    def stage_at(u, turn):
        pace = FIRST_PACE if u < 4 else PACE
        return (turn - u) // pace if turn >= u and (turn - u) % pace == 0 else -1

    def tick(turn):
        for u in range(min(turn, len(units) - 1), -1, -1):
            if stage_at(u, turn) == 0:
                units[u].depart()
        for u in reversed(range(len(units))):
            late = stage_at(u, turn)
            if not 0 < late < 5:
                continue
            units[u].stages()[late]()
            if late == 4 and u in landing:
                (i,) = landing[u]
                loads[i] = pltpu.make_async_copy(outs[i], local_w[i], load_sem.at[i])
                loads[i].start()
            if late == 4 and u == 0:
                loads["gain"] = pltpu.make_async_copy(gains_out, gain_full, load_sem.at[8])
                loads["gain"].start()

    def matrix(i):
        return local_w[i][...].reshape(-1, own[i].shape[1])

    state = gelu_in_kernel(exact_dot(table[...], weight[...]) + bias_row[...])
    low = state.astype(bf16)
    low_out[...] = low
    values = jnp.concatenate((inner_rows(low, down[...]), inner_rows(low, up[...])), axis=0)
    made[...] = jnp.zeros_like(made)
    made[:, : down.shape[0]] = values.astype(bf16)

    for turn in range(3 + 4 * FIRST_PACE + 1):
        tick(turn)
    ticks = iter(range(3 + 4 * FIRST_PACE + 1, len(units) + 4 * PACE))

    def between():
        turn = next(ticks, None)
        if turn is not None:
            tick(turn)

    stores = []

    def store(which, part=None):
        source, target = saved[which], saved_out[which]
        copy = pltpu.make_async_copy(source, target, save_sem.at[which])
        copy.start()
        stores.append(copy)

    for r in range(rows_total):
        column = column_of(segments[r : r + 1, :])
        task = jnp.zeros_like(column)
        for s in range(tasks.shape[1]):
            task = task + jnp.where(column == s, tasks[r : r + 1, s : s + 1], 0)
        task_out[r * length : (r + 1) * length, :] = task
    loads["gain"].wait()
    width = x.shape[1]
    gain_out[...] = 1.0 + inner_rows(low, gain_full[...].reshape(-1, gain.shape[1]).astype(bf16))

    def picked(r, which):
        task = task_out[r * length : (r + 1) * length, :]
        return token_gain(task, gain_out[:, which * width : (which + 1) * width])

    def row(r, size=None):
        size = length if size is None else size
        return slice(r * size, (r + 1) * size)

    for i in (0, 1, 2):
        loads[i].wait()
    for r in range(rows_total):
        stream = x[row(r), :].astype(f32)
        n = (stream * inverse_rms(stream) * picked(r, 0)).astype(bf16)
        n1[row(r), :] = n
        q1[row(r), :] = (plain_dot(n, matrix(0)).astype(bf16).astype(f32) * HEAD**-0.5).astype(bf16)
        k1[row(r), :] = plain_dot(n, matrix(1)).astype(bf16)
        v1[row(r), :] = plain_dot(n, matrix(2)).astype(bf16)
        between()
    for which in (0, 1, 2, 3):
        store(which)


    def attend(causal, q, k, v, mixed, p_out, r, keys_row):
        column = column_of(segments[r : r + 1, :])
        same = column == keys_row
        if causal:
            at_q = lax.broadcasted_iota(jnp.int32, same.shape, 0)
            at_k = lax.broadcasted_iota(jnp.int32, same.shape, 1)
            same = same & (at_q >= at_k)
        bias[...] = jnp.where(same, 0.0, masked_score)
        keys_total = keys_row.shape[1]
        per_group = HEADS // 4
        for group in range(2):
            @pl.loop(group * per_group, (group + 1) * per_group)
            def _(p):
                slot = lax.rem(p, 2)
                at = pl.ds(pl.multiple_of(p * PAIR, PAIR), PAIR)

                @pl.when(p >= 2)
                def _():
                    pltpu.make_async_copy(
                        probs.at[slot], p_out.at[r, pl.ds(2 * p - 4, 2)], p_sem.at[slot]
                    ).wait()

                attend_pair(causal, q, k, v, mixed, probs.at[slot], bias, row(r), row(r, keys_total), at)
                pltpu.make_async_copy(
                    probs.at[slot], p_out.at[r, pl.ds(2 * p, 2)], p_sem.at[slot]
                ).start()

            between()
        for p in (HEADS // 2 - 2, HEADS // 2 - 1):
            pltpu.make_async_copy(
                probs.at[p % 2], p_out.at[r, pl.ds(2 * p, 2)], p_sem.at[p % 2]
            ).wait()

    for r in range(rows_total):
        attend(True, q1, k1, v1, m1, p1_out, r, segments[r : r + 1, :])
    store(4)
    for i in (5, 6):
        loads[i].wait()
    for r in range(rows_total):
        mine = row(r, mem_len)
        k2[mine, :] = plain_dot(mem[mine, :], matrix(5)).astype(bf16)
        v2[mine, :] = plain_dot(mem[mine, :], matrix(6)).astype(bf16)
        between()
    store(8)
    store(9)
    for i in (3, 4):
        loads[i].wait()
    for r in range(rows_total):
        stream = x[row(r), :].astype(f32) + plain_dot(m1[row(r), :], matrix(3))
        s1[row(r), :] = stream
        n = (stream * inverse_rms(stream) * picked(r, 1)).astype(bf16)
        n2[row(r), :] = n
        q2[row(r), :] = (plain_dot(n, matrix(4)).astype(bf16).astype(f32) * HEAD**-0.5).astype(bf16)
        between()
    for which in (5, 6, 7):
        store(which)
    for r in range(rows_total):
        attend(False, q2, k2, v2, m2, p2_out, r, mem_segments[r : r + 1, :])
    store(10)
    for turn in ticks:
        tick(turn)
    loads[7].wait()
    for copy in stores:
        copy.wait()
    copies.finish()


def gelu_in_kernel(v):
    return v * (0.5 * lax.erf(v * 0.7071067811865476) + 0.5)


def attend_pair(causal, q_ref, k_ref, v_ref, mixed_ref, p_ref, bias, q_rows, k_rows, at):
    length = q_rows.stop - q_rows.start
    keys_all = k_rows.stop - k_rows.start
    step = length // 2 if causal else length
    masks = half_masks()
    for first in range(0, length, step):
        rows = slice(q_rows.start + first, q_rows.start + first + step)
        keys = first + step if causal else keys_all
        q = q_ref[rows, at]
        k = k_ref[k_rows.start : k_rows.start + keys, at]
        v = v_ref[k_rows.start : k_rows.start + keys, at]
        out = None
        for h, mask in enumerate(masks):
            s = inner_rows(q * mask, k) + bias[first : first + step, :keys]
            e = jnp.exp(s - jnp.max(s, axis=-1, keepdims=True))
            p = (e * (1.0 / jnp.sum(e, axis=-1, keepdims=True))).astype(bf16)
            p_ref[h, first : first + step, :keys] = p
            part = plain_dot(p, v * mask)
            out = part if out is None else out + part
        mixed_ref[rows, at] = out.astype(bf16)


def forward(x, mem, segments, mem_segments, tasks, weights, table, weight, bias_row, makers):
    down, up, gain = makers
    own = weights
    tokens, width = x.shape
    mem_tokens = mem.shape[0]
    rows, length = segments.shape
    mem_len = mem_segments.shape[1]
    spaces = (LINE, 2, 2)
    any_space = pl.BlockSpec(memory_space=pl.ANY)
    vmem = pl.BlockSpec(memory_space=pltpu.VMEM)
    made_half = down.shape[0] + (-down.shape[0] % 128)
    n_tasks = table.shape[0]
    chip = [spaces + (2 * a.shape[0], a.shape[1]) for a in own]
    t_low, m_low, t_full = ((tokens, width), bf16), ((mem_tokens, width), bf16), ((tokens, width), f32)
    kept = [t_low, t_low, t_low, t_low, t_low, t_full, t_low, t_low, m_low, m_low, t_low]
    shape = jax.ShapeDtypeStruct
    probs = (rows, HEADS, length, mem_len)
    copies = 11 * 16 + 32
    outs = pl.pallas_call(
        forward_kernel,
        in_specs=[vmem] * 21,
        out_specs=[any_space] * 12 + [vmem] * 3 + [any_space] * 13,
        out_shape=[shape(s, bf16) for s in chip]
        + [
            shape(spaces + (2, 2 * n_tasks, made_half), bf16),
            shape(spaces + (2,) + gain.shape, f32),
            shape((n_tasks, weight.shape[1]), bf16),
            shape((n_tasks, 3 * width), f32),
            shape((tokens, 1), jnp.int32),
        ]
        + [shape(s, d) for s, d in kept]
        + [shape((rows, HEADS, length, length), bf16), shape(probs, bf16)],
        scratch_shapes=[pltpu.VMEM(a.shape, f32) for a in own]
        + [pltpu.VMEM((2 * a.shape[0], a.shape[1] // 2), f32) for a in own]
        + [pltpu.VMEM((2 * a.shape[0], a.shape[1] // 2), bf16) for a in own]
        + [pltpu.VMEM(s, bf16) for s in chip[:8]]
        + [pltpu.VMEM(s, d) for s, d in kept]
        + [
            pltpu.VMEM((2 * n_tasks, made_half), bf16),
            pltpu.VMEM(gain.shape, f32),
            pltpu.VMEM((length, max(length, mem_len)), f32),
            pltpu.VMEM((2, 2, length, max(length, mem_len)), bf16),
            pltpu.SemaphoreType.DMA((copies,)),
            pltpu.SemaphoreType.DMA((copies,)),
            pltpu.SemaphoreType.DMA((2,)),
            pltpu.SemaphoreType.DMA((9,)),
            pltpu.SemaphoreType.DMA((11,)),
            pltpu.VMEM(spaces + (2,) + gain.shape, f32),
        ],
        compiler_params=pltpu.CompilerParams(
            collective_id=0, has_side_effects=True, vmem_limit_bytes=VMEM_BYTES
        ),
        name="forward_as_weights_arrive",
    )(x, mem, segments, mem_segments, tasks, *own, table, weight, bias_row, down, up, gain)
    return outs


BACK_PACES = (2, 6, 6, 6, 3)
QUICK_PACES = (1, 1, 1, 1)
EARLY_TICKS = 3


class Stepwise:
    def __init__(self, stages, paces):
        self.stages, self.paces = list(stages), list(paces)

    def advance(self, now):
        self.stages.pop(0)()
        self.due = now + (self.paces.pop(0) if self.stages else 0)


class Traffic:
    def __init__(self):
        self.ready, self.flying, self.now = [], [], 0

    def add(self, item):
        self.ready.append(item)

    def tick(self):
        self.now += 1
        for item in reversed(list(self.flying)):
            if self.now >= item.due:
                item.advance(self.now)
        self.flying = [item for item in self.flying if item.stages]
        if self.ready:
            item = self.ready.pop(0)
            item.advance(self.now)
            self.flying.append(item)

    def drain(self):
        while self.ready or self.flying:
            self.tick()


class Summed(Stepwise):
    def __init__(self, here, copies, theirs, mine, shares, slots, out, out_first, fetch=None):
        super().__init__(
            [self.begin, self.over_first, self.over_second, self.over_line, self.to_owner, self.end],
            BACK_PACES,
        )
        self.here, self.copies = here, copies
        self.theirs, self.mine, self.fetch = theirs, mine, fetch
        self.shares, self.slots, self.out, self.out_first = shares, slots, out, out_first
        self.landed = self.follower = None
        self.follows = self.added = False

    def begin(self):
        self.core = self.copies.remote(self.theirs, self.slots[0], self.here.sibling())
        if self.fetch is not None and not self.follows:
            self.start_fetch()

    def start_fetch(self):
        self.local = self.copies.local(*self.fetch)

    def over_first(self):
        here, held = self.here, self.slots[0]
        if self.fetch is not None:
            self.local.wait()
        self.core.wait_recv()
        held[...] += self.mine()
        self.added = True
        if self.follower is not None:
            self.follower.start_fetch()
        one, two = self.shares
        self.first = (
            self.copies.remote(held.at[(slice(None), 1 - here.y, slice(None)) + one], self.slots[1], here.over_y()),
            self.copies.remote(held.at[(slice(None), slice(None), 1 - here.x) + two], self.slots[2], here.over_x()),
        )

    def over_second(self):
        here, held = self.here, self.slots[0]
        one, two = self.shares
        self.first[0].wait_recv()
        held[(slice(None), here.y, slice(None)) + one] += self.slots[1][...]
        self.first[1].wait_recv()
        held[(slice(None), slice(None), here.x) + two] += self.slots[2][...]
        self.second = (
            self.copies.remote(held.at[(slice(None), here.y, 1 - here.x) + one], self.slots[3], here.over_x()),
            self.copies.remote(held.at[(slice(None), 1 - here.y, here.x) + two], self.slots[4], here.over_y()),
        )

    def over_line(self):
        here, held = self.here, self.slots[0]
        one, two = self.shares
        self.second[0].wait_recv()
        held[(slice(None), here.y, here.x) + one] += self.slots[3][...]
        self.second[1].wait_recv()
        held[(slice(None), here.y, here.x) + two] += self.slots[4][...]
        self.third = [
            self.copies.remote(
                held.at[lax.rem(here.z + k, LINE), here.y, here.x],
                self.slots[5].at[k - 1],
                here.along_z(k),
            )
            for k in (1, 2, 3)
        ]

    def gathered(self):
        here = self.here
        total = self.slots[0][here.z, here.y, here.x].astype(f32)
        for k, copy in enumerate(self.third):
            copy.wait_recv()
            total = total + self.slots[5][k].astype(f32)
        return total

    def window(self, core, width, full):
        return pl.ds(pl.multiple_of(core * full + self.out_first, 128), width)

    def to_owner(self):
        here, final = self.here, self.slots[6]
        final[...] = self.gathered()
        rows, full = self.out.shape[0], self.out.shape[1] // 2
        c = here.core
        at = self.window(c, final.shape[1], full)
        theirs = pl.ds(pl.multiple_of((1 - c) * rows, 8), rows)
        self.last = self.copies.remote(final.at[theirs, :], self.out.at[:, at], here.sibling())
        self.out[:, at] = final[pl.ds(pl.multiple_of(c * rows, 8), rows), :]

    def end(self):
        self.last.wait_recv()
        if self.landed is not None:
            self.landed()


class Everywhere(Stepwise):
    def __init__(self, here, copies, value, sent, arriving, out):
        super().__init__([self.begin, self.step_x, self.step_y, self.step_z, self.end], QUICK_PACES)
        self.here, self.copies, self.value = here, copies, value
        self.sent, self.arriving, self.out = sent, arriving, out

    def send(self, turn, device):
        self.sent[turn] = self.total
        self.copy = self.copies.remote(self.sent.at[turn], self.arriving.at[turn], device)

    def add(self, turn):
        self.copy.wait_recv()
        self.total = self.total + self.arriving[turn]

    def begin(self):
        self.total = self.value()
        self.send(0, self.here.sibling())

    def step_x(self):
        self.add(0)
        self.send(1, self.here.over_x())

    def step_y(self):
        self.add(1)
        self.send(2, self.here.over_y())

    def step_z(self):
        self.add(2)
        self.sent[3] = self.total
        self.around = [
            self.copies.remote(self.sent.at[3], self.arriving.at[2 + k], self.here.along_z(k))
            for k in (1, 2, 3)
        ]

    def end(self):
        for copy in self.around:
            copy.wait_recv()
        total = jnp.zeros_like(self.total)
        for line in range(LINE):
            for k in range(LINE):
                term = self.total if k == 0 else self.arriving[2 + k]
                here_now = lax.rem(self.here.z - k + LINE, LINE) == line
                total = total + jnp.where(here_now, term, 0.0)
        self.out[...] = total


def attend_pair_back(causal, q_ref, k_ref, v_ref, mixed_ref, gm_ref, p_ref, gq_ref, gk_ref, gv_ref, start, k_start, at, length, keys_all):
    step = length // 2 if causal else length
    masks = half_masks()
    gk_parts, gv_parts = [], []
    for first in range(0, length, step):
        rows = pl.ds(start + first, step)
        keys = first + step if causal else keys_all
        key_rows = pl.ds(k_start, keys)
        q, k, v = q_ref[rows, at], k_ref[key_rows, at], v_ref[key_rows, at]
        gm = gm_ref[rows, at]
        product = gm.astype(f32) * mixed_ref[rows, at].astype(f32)
        gq = gk = gv = 0.0
        for h, mask in enumerate(masks):
            inner = jnp.sum(product * mask.astype(f32), axis=-1, keepdims=True)
            p = p_ref[h, first : first + step, :keys]
            gm_half = gm * mask
            gw = inner_rows(gm_half, v)
            gs = (p.astype(f32) * (gw - inner)).astype(bf16)
            gv = gv + inner_cols(p, gm_half)
            gq = gq + plain_dot(gs, k * mask)
            gk = gk + inner_cols(gs, q * mask)
        gq_ref[rows, at] = (gq * HEAD**-0.5).astype(bf16)
        gk_parts.append(gk)
        gv_parts.append(gv)
    for ref, terms in ((gk_ref, gk_parts), (gv_ref, gv_parts)):
        if not causal:
            ref[pl.ds(k_start, keys_all), at] = terms[0].astype(bf16)
        else:
            ref[pl.ds(k_start, step), at] = (terms[0] + terms[1][:step]).astype(bf16)
            ref[pl.ds(k_start + step, step), at] = terms[1][step:].astype(bf16)


SUM_NAMES = ("q1", "k1", "v1", "o1", "q2", "k2", "v2", "o2", "in0", "in1", "out0", "out1", "small")


def sum_pieces(width, units, own):
    rows = 2 * own
    half = width // 2
    pieces = {}
    for turn, name in enumerate(SUM_NAMES[:8]):
        cut = rows // 2 if rows % 32 == 0 else (rows // 32 + turn % 2) * 16
        pieces[name] = (rows, half, 0, (slice(0, cut), slice(0, half)), (slice(cut, rows), slice(0, half)))
    part = units // 4
    for k in (0, 1):
        pieces[f"in{k}"] = (
            rows, part, k * part,
            (slice(0, rows), slice(0, part // 2)), (slice(0, rows), slice(part // 2, part)),
        )
    out_rows = rows * units // width
    third = half // 3
    for k, (first, size) in enumerate(((0, third), (third, half - third))):
        pieces[f"out{k}"] = (
            out_rows, size, first,
            (slice(0, out_rows // 2), slice(0, size)), (slice(out_rows // 2, out_rows), slice(0, size)),
        )
    pieces["small"] = (32, half, 0, (slice(0, 16), slice(0, half)), (slice(16, 32), slice(0, half)))
    return pieces


def backward_kernel(sizes, *refs):
    rows_total, length, mem_len, width, units, own_rows = sizes
    pieces = sum_pieces(width, units, own_rows)
    (
        p1, p2, q2h, k2h, v2h, m2h, gm2h, q1h, k1h, v1h, m1h, n1h, n2h, memh, xh, s1h, g2h, g2lowh,
        wq1h, wk1h, wv1h, wo1h, wq2h, wk2h, wv2h, n3h, guh, g_out, g_small,
        task, gains, gain_three, down, up,
    ) = refs[:34]
    mem_out, input_out = refs[34:36]
    outs = refs[36:47]
    gain_out, state_out = refs[47:49]
    scratch = refs[49:]
    a = scratch[:5]
    gq, gk, gv = scratch[5:8]
    f0, f1, low = scratch[8:11]
    probs = scratch[11]
    w = scratch[12:16]
    grads = scratch[16:20]
    stage_out, stage_small = scratch[20:22]
    slots = {}
    at_slot = 22
    for name in SUM_NAMES:
        slots[name] = scratch[at_slot : at_slot + 7]
        at_slot += 7
    state_sent, state_arriving, gain_sent, gain_arriving, late_sent, late_arriving, gain_rows_ref = scratch[
        at_slot : at_slot + 7
    ]
    send, recv, p_sem, load_sem = scratch[at_slot + 7 :]
    here = Place()
    copies = Copies(send, recv)
    traffic = Traffic()
    c = here.core
    loads = {}

    def fetch(name, source, target):
        loads[name] = pltpu.make_async_copy(source, target, load_sem.at[len(loads)])
        loads[name].start()

    def need(*names):
        for name in names:
            loads[name].wait()

    def half(which, first, size, full):
        return pl.ds(pl.multiple_of(which * full + first, 128), size)

    full_in = units // 2
    panels = [(which, k) for k in (0, 1) for which in (1, 0)]

    def fetch_panel(turn):
        which, k = panels[turn]
        core = 1 - c if which else c
        cols = pl.ds(pl.multiple_of(core * full_in + k * width, 128), width)
        fetch(("panel", turn), guh.at[:, cols], (gq, gk)[turn % 2])

    fetch("n3", n3h, gv)
    fetch_panel(0)
    fetch_panel(1)
    fetch("m2", m2h, a[3])
    fetch("g2low", g2lowh, low)
    fetch("q2", q2h, a[0])
    fetch("k2", k2h, a[1])
    fetch("v2", v2h, a[2])
    fetch("gm2", gm2h, a[4])

    def probs_copy(source, index):
        return pltpu.make_async_copy(source.at[index], probs.at[lax.rem(index, 2)], p_sem.at[lax.rem(index, 2)])

    pairs = HEADS // 2
    count = rows_total * pairs
    for index in (0, 1):
        probs_copy(p2, index).start()
    fetch("wq2", wq2h, w[0])
    fetch("wo1", wo1h, w[1])
    fetch("wk2", wk2h, w[2])
    fetch("wv2", wv2h, w[3])
    fetch("s1", s1h, f0)
    fetch("g2", g2h, f1)
    meet(here)

    def from_hbm(name, array, out, stage):
        rows, size, first, one, two = pieces[name]
        full = array.shape[4] // 2
        return Summed(
            here, copies, array.at[:, :, :, :, half(1 - c, first, size, full)], lambda: stage[...],
            (one, two), slots[name], out, first,
            fetch=(array.at[:, :, :, :, half(c, first, size, full)], stage),
        )

    out_one, out_two, small_item = flown = (
        from_hbm("out0", g_out, outs[9], stage_out.at[:, :, :, :, : pieces["out0"][1]]),
        from_hbm("out1", g_out, outs[9], stage_out),
        from_hbm("small", g_small, outs[10], stage_small),
    )
    for item in flown:
        traffic.add(item)
    out_one.follower, out_two.follows = out_two, True

    def small_landed():
        made = down.shape[0]
        small = outs[10]
        state = plain_dot(small[0:8, :made].astype(bf16), down[...])
        state = state + plain_dot(small[8:16, :made].astype(bf16), up[...])
        traffic.add(Everywhere(here, copies, lambda: state, state_sent, state_arriving, state_out))

    small_item.landed = small_landed
    users = {}

    def free(slot):
        item = users.pop(slot, None)
        if item is not None:
            while not item.added:
                traffic.tick()
            if any(item.core is copy for copy in copies.open):
                copies.close(item.core)

    def product(source, grad, slot):
        free(slot)
        columns = width // 2
        for k in range(2):
            block = inner_cols(source[:, k * columns : (k + 1) * columns], grad[...]).astype(bf16)
            grads[slot][2 * k : 2 * k + 2] = block.reshape((2, 2, 2, 2 * own_rows, width))
        return grads[slot]

    def weight_gradient(name, index, source, grad, slot):
        buffer = product(source, grad, slot)
        rows, size, first, one, two = pieces[name]
        full = width // 2
        users[slot] = Summed(
            here, copies, buffer.at[:, :, :, :, half(1 - c, 0, size, full)],
            lambda: buffer[:, :, :, :, half(c, 0, size, full)],
            (one, two), slots[name], outs[index], 0,
        )
        traffic.add(users[slot])

    def matrix(k):
        return w[k][...].reshape(width, width)

    def row(r, size=None):
        size = length if size is None else size
        return slice(r * size, (r + 1) * size)

    def picked(r, which):
        return token_gain(task[row(r), :], gains[:, which * width : (which + 1) * width])

    def attention(causal, q, k, v, m, gm, source, keys_all):
        per_group = 2
        for group in range(count // per_group):
            @pl.loop(group * per_group, (group + 1) * per_group)
            def _(index):
                slot = lax.rem(index, 2)
                probs_copy(source, index).wait()
                r, p = index // pairs, lax.rem(index, pairs)
                at = pl.ds(pl.multiple_of(p * PAIR, PAIR), PAIR)
                attend_pair_back(
                    causal, q, k, v, m, gm, probs.at[slot], gq, gk, gv,
                    pl.multiple_of(r * length, length), pl.multiple_of(r * keys_all, keys_all), at, length, keys_all,
                )

                @pl.when(index + 2 < count)
                def _():
                    probs_copy(source, index + 2).start()

            traffic.tick()

    for _ in range(EARLY_TICKS):
        traffic.tick()
    need("n3")
    for turn, (which, k) in enumerate(panels):
        need(("panel", turn))
        buffer = product(gv, (gq, gk)[turn % 2], turn)
        if turn + 2 < len(panels):
            fetch_panel(turn + 2)
        if which == 0:
            _, _, first, one, two = pieces[f"in{k}"]
            mine = buffer
            item = Summed(
                here, copies, theirs, lambda mine=mine: mine[...], (one, two), slots[f"in{k}"], outs[8], first
            )
            users[turn - 1] = users[turn] = item
            traffic.add(item)
        theirs = buffer
        traffic.tick()
    need("m2", "g2low")
    weight_gradient("o2", 7, a[3], low, 0)
    traffic.tick()
    need("q2", "k2", "v2", "gm2")
    attention(False, a[0], a[1], a[2], a[3], a[4], p2, mem_len)
    for index in (0, 1):
        probs_copy(p1, index).start()
    fetch("n2", n2h, a[0])
    fetch("mem", memh, a[1])
    fetch("v1", v1h, a[2])
    fetch("m1", m1h, a[3])
    need("wq2", "wo1", "s1", "g2")
    gain_two = None
    for r in range(rows_total):
        stream = f0[row(r), :]
        stream_grad, gain_tokens = norm_back(stream, picked(r, 1), inner_rows(gq[row(r), :], matrix(0)))
        grad_one = f1[row(r), :] + stream_grad
        f1[row(r), :] = grad_one
        low_now = grad_one.astype(bf16)
        low[row(r), :] = low_now
        a[4][row(r), :] = inner_rows(low_now, matrix(1)).astype(bf16)
        now = gain_rows(task[row(r), :], gain_tokens)
        gain_two = now if gain_two is None else gain_two + now
        traffic.tick()
    gain_rows_ref[:, width : 2 * width] = gain_two
    gain_rows_ref[:, 2 * width :] = gain_three[...]
    traffic.add(
        Everywhere(here, copies, lambda: gain_rows_ref[:, width:], late_sent, late_arriving, gain_out.at[:, width:])
    )
    fetch("wq1", wq1h, w[0])
    fetch("wk1", wk1h, w[1])
    need("n2", "mem")
    for name, index, source, grad, slot in (
        ("q2", 4, a[0], gq, 1), ("k2", 5, a[1], gk, 2), ("v2", 6, a[1], gv, 3)
    ):
        weight_gradient(name, index, source, grad, slot)
        traffic.tick()
    fetch("q1", q1h, a[0])
    fetch("k1", k1h, a[1])
    need("wk2", "wv2")
    for r in range(rows_total):
        mine = row(r, mem_len)
        f0[mine, :] = inner_rows(gk[mine, :], matrix(2)) + inner_rows(gv[mine, :], matrix(3))
        traffic.tick()
    fetch("mem_out", f0, mem_out)
    fetch("wv1", wv1h, w[2])
    need("m1")
    weight_gradient("o1", 3, a[3], low, 0)
    traffic.tick()
    need("q1", "k1", "v1")
    attention(True, a[0], a[1], a[2], a[3], a[4], p1, length)
    fetch("n1", n1h, a[0])
    fetch("x", xh, a[1])
    need("n1")
    for name, index, grad, slot in (("q1", 0, gq, 1), ("k1", 1, gk, 2), ("v1", 2, gv, 3)):
        weight_gradient(name, index, a[0], grad, slot)
        traffic.tick()
    need("x", "wq1", "wk1", "wv1")
    gain_one = None
    for r in range(rows_total):
        stream = a[1][row(r), :].astype(f32)
        cotan = inner_rows(gq[row(r), :], matrix(0)) + inner_rows(gk[row(r), :], matrix(1))
        cotan = cotan + inner_rows(gv[row(r), :], matrix(2))
        stream_grad, gain_tokens = norm_back(stream, picked(r, 0), cotan)
        f1[row(r), :] += stream_grad
        now = gain_rows(task[row(r), :], gain_tokens)
        gain_one = now if gain_one is None else gain_one + now
        traffic.tick()
    fetch("input_out", f1, input_out)
    gain_rows_ref[:, :width] = gain_one
    traffic.ready.insert(
        0, Everywhere(here, copies, lambda: gain_rows_ref[:, :width], gain_sent, gain_arriving, gain_out.at[:, :width])
    )
    traffic.drain()
    need("mem_out", "input_out")
    copies.finish()


def backward(mem_len, saved, probs, x, mem, weights, g2, g2_low, gmix2, n3, gu, g_out, g_small, task, gains, gain_three, down, up, own):
    n1, q1, k1, v1, m1, s1, n2, q2, k2, v2, m2 = saved
    p1, p2 = (p.reshape((-1, 2) + p.shape[2:]) for p in probs)
    rows = probs[0].shape[0]
    tokens, width = x.shape
    length = tokens // rows
    units = own[8].shape[1]
    own_rows = own[0].shape[0]
    any_space = pl.BlockSpec(memory_space=pl.ANY)
    vmem = pl.BlockSpec(memory_space=pltpu.VMEM)
    shape = jax.ShapeDtypeStruct
    act, full = pltpu.VMEM((tokens, width), bf16), pltpu.VMEM((tokens, width), f32)
    mem_act = pltpu.VMEM((max(tokens, mem.shape[0]), width), bf16)
    square = pltpu.VMEM((LINE, 2, 2, 2 * own_rows, width), bf16)
    pieces = sum_pieces(width, units, own_rows)
    slots = []
    for name in SUM_NAMES:
        r, size, _, one, two = pieces[name]
        extent = [tuple(s.stop - s.start for s in share) for share in (one, two)]
        slots += [
            pltpu.VMEM((LINE, 2, 2, r, size), bf16),
            pltpu.VMEM((LINE, 2) + extent[0], bf16),
            pltpu.VMEM((LINE, 2) + extent[1], bf16),
            pltpu.VMEM((LINE,) + extent[0], bf16),
            pltpu.VMEM((LINE,) + extent[1], bf16),
            pltpu.VMEM((LINE - 1, r, size), bf16),
            pltpu.VMEM((r, size), f32),
        ]

    def stage(name):
        r, size = pieces[name][:2]
        return (LINE, 2, 2, r, size)

    tasks, hidden = gains.shape[0], down.shape[1]
    copies = 200
    ins_any = (
        p1, p2, q2, k2, v2, m2, gmix2, q1, k1, v1, m1, n1, n2, mem, x, s1, g2, g2_low,
        *(weights[i] for i in range(7)), n3, gu, g_out, g_small,
    )
    return pl.pallas_call(
        functools.partial(backward_kernel, (rows, length, mem_len, width, units, own_rows)),
        in_specs=[any_space] * len(ins_any) + [vmem] * 5,
        out_specs=[any_space] * 2 + [vmem] * 13,
        out_shape=[shape((mem.shape[0], width), f32), shape((tokens, width), f32)]
        + [shape(g.shape, f32) for g in own]
        + [shape((16, width), f32), shape(gains.shape, f32), shape((tasks, hidden), f32)],
        scratch_shapes=[act] * 5 + [act, mem_act, mem_act] + [full, full, act]
        + [pltpu.VMEM((2, 2, length, max(length, mem_len)), bf16)]
        + [square] * 4
        + [square] * 4
        + [
            pltpu.VMEM(stage("out1"), bf16),
            pltpu.VMEM(stage("small"), bf16),
        ]
        + slots
        + [
            pltpu.VMEM((4, tasks, hidden), f32),
            pltpu.VMEM((6, tasks, hidden), f32),
            pltpu.VMEM((4, tasks, width), f32),
            pltpu.VMEM((6, tasks, width), f32),
            pltpu.VMEM((4, tasks, 2 * width), f32),
            pltpu.VMEM((6, tasks, 2 * width), f32),
            pltpu.VMEM(gains.shape, f32),
            pltpu.SemaphoreType.DMA((copies,)),
            pltpu.SemaphoreType.DMA((copies,)),
            pltpu.SemaphoreType.DMA((2,)),
            pltpu.SemaphoreType.DMA((40,)),
        ],
        compiler_params=pltpu.CompilerParams(
            collective_id=1, has_side_effects=True, vmem_limit_bytes=63 << 20
        ),
        name="backward_as_gradients_leave",
    )(*ins_any, task, gains, gain_three, down, up)


def finish_kernel(count, *refs):
    shards, small, gain_sum, state, gain_all, low, table, weight, bias_row = (
        refs[:count], *refs[count : count + 8]
    )
    large = refs[count + 8 : count + 10]
    outs = refs[count + 10 : 2 * count + 10]
    down_out, up_out, gain_out, table_out, weight_out, bias_out = refs[2 * count + 10 : 2 * count + 16]
    large_outs, (rows, held_a, held_b, sems) = (
        refs[2 * count + 16 : 2 * count + 18], refs[2 * count + 18 :]
    )
    held = (held_a, held_b)
    moves = [
        pltpu.make_async_copy(source, buffer, sems.at[k])
        for k, (source, buffer) in enumerate(zip(large, held))
    ]
    for move in moves:
        move.start()
    for shard, out in zip(shards, outs):
        out[...] = shard[...]
    made = down_out.shape[0]
    for move in moves:
        move.wait()
    moves = [
        pltpu.make_async_copy(buffer, target, sems.at[2 + k])
        for k, (buffer, target) in enumerate(zip(held, large_outs))
    ]
    for move in moves:
        move.start()
    low_now = low[...]
    down_out[...] = inner_cols(small[0:8, :made].astype(bf16), low_now)
    up_out[...] = inner_cols(small[8:16, :made].astype(bf16), low_now)
    rows[...] = inner_cols(gain_sum[...], low_now.astype(f32), exact_mode)
    owned = gain_out.shape[0]
    me = lax.axis_index("dp")
    gain_out[...] = rows[pl.ds(pl.multiple_of(me * owned, 8), owned), :]
    makers = gain_all[...].reshape(-1, gain_all.shape[-1])
    state_grad = state[...] + exact_dot(gain_sum[...], makers)
    before = exact_dot(table[...], weight[...]) + bias_row[...]
    pre_grad = gelu_both(before)[1] * state_grad
    bias_out[...] = jnp.sum(pre_grad, axis=0, keepdims=True)
    weight_out[...] = inner_cols(table[...], pre_grad, exact_mode)
    table_out[...] = lax.dot_general(
        pre_grad, weight[...], (((1,), (1,)), ((), ())), precision=exact_mode, preferred_element_type=f32
    )
    for move in moves:
        move.wait()


def finish(mem_grad, input_grad, shards, small, gain_sum, state, gain_all, low, table, weight, bias_row, makers):
    down, up, gain = makers
    shape = jax.ShapeDtypeStruct
    vmem = pl.BlockSpec(memory_space=pltpu.VMEM)
    ins = (*shards, small, gain_sum, state, gain_all, low, table, weight, bias_row)
    outs = [shape(s.shape, f32) for s in shards]
    outs += [shape(m.shape, f32) for m in makers] + [shape(a.shape, f32) for a in (table, weight, bias_row)]
    large = (mem_grad, input_grad)
    any_space = pl.BlockSpec(memory_space=pl.ANY)
    return pl.pallas_call(
        functools.partial(finish_kernel, len(shards)),
        in_specs=[vmem] * len(ins) + [any_space] * 2,
        out_specs=[vmem] * len(outs) + [any_space] * 2,
        out_shape=outs + [shape(a.shape, f32) for a in large],
        scratch_shapes=[
            pltpu.VMEM((gain_sum.shape[1], low.shape[1]), f32),
            *(pltpu.VMEM(a.shape, f32) for a in large),
            pltpu.SemaphoreType.DMA((4,)),
        ],
        compiler_params=pltpu.CompilerParams(vmem_limit_bytes=VMEM_BYTES),
        name="finish",
    )(*ins, *large)


def on_device(
    block_input, memory, cotangent, segments, memory_segments, task_of_segment,
    self_query, self_key, self_value, self_output,
    cross_query, cross_key, cross_value, cross_output,
    hidden_in, hidden_out, task_table, task_weight, task_bias,
    down_maker, up_maker, gain_maker,
):
    row_count, seq_len, model_width = block_input.shape
    mem_len = memory.shape[1]
    task_count = task_table.shape[0]
    token_count = row_count * seq_len
    parts = lax.axis_size("dp")
    weights = (
        self_query, self_key, self_value, self_output,
        cross_query, cross_key, cross_value, cross_output, hidden_in, hidden_out,
    )
    task_state, task_back = jax.vjp(task_network, task_table, task_weight, task_bias)
    task_low = task_state.astype(bf16)
    down_own, gain_own = down_maker.shape[0], gain_maker.shape[0]
    makers = (down_maker, up_maker, gain_maker)
    x = block_input.reshape(token_count, model_width)
    mem = memory.reshape(row_count * mem_len, model_width)

    def joined(block):
        return block.transpose(1, 0, 2).reshape(task_count, -1)

    if parts == 32:
        outs = forward(
            x, mem, segments, memory_segments, task_of_segment, weights,
            task_table, task_weight, task_bias.reshape(1, -1), makers,
        )
        backbone = [w.reshape(-1, w.shape[-1]) for w in outs[:10]]
        made = outs[10].reshape(parts, 2 * task_count, -1)
        task_low, gain_table, token_task = outs[12:15]
        saved, probs_one, probs_two = outs[15:26], outs[26], outs[27]
        made_up = joined(made[:, task_count:, :down_own])
        made = made[:, :task_count]
    else:
        packed = jnp.concatenate([w.reshape(-1, model_width) for w in weights], axis=0)
        packed = lax.all_gather(packed, "dp", axis=0, tiled=False)
        backbone, at = [], 0
        for w in weights:
            count = w.size // model_width
            backbone.append(packed[:, at : at + count].reshape(-1, w.shape[1]))
            at += count
        made = inner_rows(task_low, jnp.concatenate(makers, axis=0))
        made = lax.all_gather(made, "dp", axis=0, tiled=False)
        gain_table = 1.0 + joined(made[:, :, 2 * down_own :])
        seg_match = segments[:, :, None] == jnp.arange(task_of_segment.shape[1], dtype=jnp.int32)
        token_task = jnp.sum(
            jnp.where(seg_match, task_of_segment[:, None, :], 0), axis=-1
        ).reshape(token_count, 1)
        saved, probs_one, probs_two = attention_layers(
            x, mem, segments, memory_segments, token_task, backbone, gain_table
        )
        made_up = joined(made[:, :, down_own : 2 * down_own]).astype(bf16)
    made_down = joined(made[:, :, :down_own]).astype(bf16)
    down_all = (
        made_down.reshape(task_count, model_width, ADA)
        .transpose(1, 0, 2)
        .reshape(model_width, task_count * ADA)
    )
    up_all = made_up.reshape(task_count * ADA, model_width)
    cot = cotangent.reshape(token_count, model_width)
    output, g2, g2_low, gmix2, n3, gu, hidden_out_grad, up_grad, down_grad, gain_three = feed_forward(
        saved[5], saved[10], cot, token_task, backbone, gain_table, down_all, up_all
    )
    down_rows = (
        down_grad.reshape(parts, -1, task_count, ADA)
        .transpose(0, 2, 1, 3)
        .reshape(parts, task_count, down_own)
    )
    up_rows = up_grad.reshape(task_count, parts, -1).transpose(1, 0, 2)
    if parts == 32:
        small = jnp.concatenate((down_rows, up_rows), axis=1).astype(bf16)
        small = jnp.pad(small, ((0, 0), (0, 0), (0, model_width - down_own)))
        out_grad = hidden_out_grad.reshape((LINE, 2, 2, -1, model_width))
        mem_grad, input_grad, *shared, small, gain_sum, state = backward(
            mem_len, saved, (probs_one, probs_two), x, mem, outs[:7], g2, g2_low, gmix2, n3, gu, out_grad,
            small.reshape(LINE, 2, 2, 4 * task_count, model_width), token_task, gain_table, gain_three,
            down_maker, up_maker, weights,
        )
        (
            *shared, down_maker_grad, up_maker_grad, gain_maker_grad,
            table_grad, weight_grad, bias_grad, mem_grad, input_grad,
        ) = finish(
            mem_grad, input_grad, shared, small, gain_sum, state, outs[11], task_low, task_table, task_weight,
            task_bias.reshape(1, -1), makers,
        )
        bias_grad = bias_grad.reshape(task_bias.shape)
    else:
        input_grad, mem_grad, grads, gain_one, gain_two = attention_back(
            x, mem, row_count, token_task, backbone, gain_table, saved, probs_one, probs_two, g2, g2_low, gmix2
        )
        grads = (*grads, *outers((n3,), (gu,), (0,), "hidden_in_grad"), hidden_out_grad)
        packed = jnp.concatenate([g.reshape(parts, -1, model_width) for g in grads], axis=1)
        packed = lax.psum_scatter(packed, "dp", scatter_dimension=0, tiled=False).astype(f32)
        shared, at = [], 0
        for w in weights:
            count = w.size // model_width
            shared.append(packed[at : at + count].reshape(w.shape))
            at += count
        gain_grad = jnp.concatenate((gain_one, gain_two, gain_three), axis=1)
        gain_rows_all = gain_grad.reshape(task_count, parts, -1).transpose(1, 0, 2)
        small = jnp.concatenate((down_rows, up_rows, gain_rows_all), axis=2)
        small = lax.psum_scatter(small, "dp", scatter_dimension=0, tiled=False)
        own_down = small[:, :down_own].astype(bf16)
        own_up = small[:, down_own : 2 * down_own].astype(bf16)
        own_gain = small[:, 2 * down_own :]
        state_grad = lax.psum(
            plain_dot(own_down, down_maker)
            + plain_dot(own_up, up_maker)
            + exact_dot(own_gain, gain_maker.astype(f32)),
            "dp",
        )
        down_maker_grad = inner_cols(own_down, task_low)
        up_maker_grad = inner_cols(own_up, task_low)
        gain_maker_grad = inner_cols(own_gain, task_low.astype(f32), exact_mode)
        table_grad, weight_grad, bias_grad = task_back(state_grad)
    return (
        output.reshape(row_count, seq_len, model_width),
        input_grad.reshape(row_count, seq_len, model_width),
        mem_grad.reshape(row_count, mem_len, model_width),
        *shared,
        table_grad,
        weight_grad,
        bias_grad,
        down_maker_grad,
        up_maker_grad,
        gain_maker_grad,
    )


def solution(mesh):
    rows, whole_copy = P("dp"), P()
    return jax.shard_map(
        on_device,
        mesh=mesh,
        in_specs=(rows,) * 16 + (whole_copy,) * 3 + (rows,) * 3,
        out_specs=(rows,) * 13 + (whole_copy,) * 3 + (rows,) * 3,
        check_vma=False,
    )
```
